256 devices in a mesh: dp: 8 (over z_hi, x), ep: 8 (over y, core), ctx: 4 (over z_lo).
Axes of the slice: x: 4, y: 4, z: 8 (z_hi: 2, z_lo: 4; z = z_hi * 4 + z_lo), core: 2. Of those that a mesh axis runs over, the one named last changes fastest.
Arguments:
- layer_input: bfloat16 [32768, 1024], P(('dp', 'ep', 'ctx')), may hold values from -24 to 24
- gain_attn: float32 [1024], replicated, may hold values from 0.5 to 1.5
- w_query: bfloat16 [1024, 1024], replicated, may hold values from -0.1875 to 0.1875
- w_key: bfloat16 [1024, 512], replicated, may hold values from -0.1875 to 0.1875
- w_value: bfloat16 [1024, 512], replicated, may hold values from -0.1875 to 0.1875
- w_proj: bfloat16 [1024, 1024], replicated, may hold values from -1 to 1
- gain_ffn: float32 [1024], replicated, may hold values from 0.5 to 1.5
- w_router: bfloat16 [1024, 32], replicated, may hold values from -0.09375 to 0.09375
- w_expert_in: bfloat16 [32, 1024, 1024], P('ep'), may hold values from -0.1875 to 0.1875
- w_expert_out: bfloat16 [32, 512, 1024], P('ep'), may hold values from -1 to 1
- segment_ids: int32 [8, 4096], P('dp'), may hold values from 0 to 127, never falling along the last dimension, each value on 1 to 3072 neighbouring positions
- expert_ids: int32 [32768, 8], P(('dp', 'ep', 'ctx')), may hold values from 0 to 31, all different within a row
- slot_order: int32 [256, 1024], P(('dp', 'ep', 'ctx')), may hold values from 0 to 1023, each once within a row
- out_grad: bfloat16 [32768, 1024], P(('dp', 'ep', 'ctx')), may hold values from -6 to 6
Outputs:
- layer_output: bfloat16 [32768, 1024], P(('dp', 'ep', 'ctx'))
- input_grad: bfloat16 [32768, 1024], P(('dp', 'ep', 'ctx'))
- grad_gain_attn: float32 [1024], P(('dp', 'ep', 'ctx'))
- grad_query: float32 [1024, 1024], P(('dp', 'ep', 'ctx'))
- grad_key: float32 [1024, 512], P(('dp', 'ep', 'ctx'))
- grad_value: float32 [1024, 512], P(('dp', 'ep', 'ctx'))
- grad_proj: float32 [1024, 1024], P(('dp', 'ep', 'ctx'))
- grad_gain_ffn: float32 [1024], P(('dp', 'ep', 'ctx'))
- grad_router: float32 [1024, 32], P(('dp', 'ep', 'ctx'))
- grad_expert_in: float32 [32, 1024, 1024], P('ep', ('dp', 'ctx'))
- grad_expert_out: float32 [32, 512, 1024], P('ep', ('dp', 'ctx'))
The draws below stay inside these ranges and needn't reach their ends.
Inputs may be any that keep to these rules, and one draw needn't show every extreme that they name: `segment_ids`: within a sequence the ids never fall; each document is at most 3072 tokens long and one is exactly that long. `expert_ids`: each row names 8 different experts. `slot_order`: each row holds every number below 1024 once.
All inputs are finite; a program needn't handle non-finite values.
Results may differ from the reference program's by a relative error of at most 0.025.
Values may be sent and summed in bfloat16 or wider, within the bound.
A program may use at most 192 MiB of HBM per device.

```python
import math
import jax
import jax.numpy as jnp
import numpy as np
from jax import lax

D = 1024
H = 16
KV = 8
HD = 64
FF = 512
TOP = 8
TOK_DEV = 128
EXPERTS = 32
SEQ = 4096
TOKENS = 32768
CAP = 40
N_DP = 8
N_EP = 8
N_CTX = 4


def raised(values, stream_key, source, target, blocks, factor):
    owner, partner = [(jnp.arange(values.shape[position]) // (values.shape[position] // blocks)).reshape([-1 if axis == position else 1 for axis in range(values.ndim)]) for position in (source, target)]
    chosen = jax.random.permutation(stream_key, blocks)[partner]
    strong = (owner == chosen) | (owner == (partner + blocks // 2) % blocks)
    return jnp.where(strong, factor * values, values)


def shard_levels(own_key, dims, shards, low, high):
    loudness = 1.0
    for dim, blocks in shards:
        heights = jax.random.uniform(jax.random.fold_in(jax.random.fold_in(own_key, 6), dim), (blocks,), jnp.float32, low / len(shards), high / len(shards))
        loudness = loudness * jnp.repeat(jnp.exp(heights), dims[dim] // blocks).reshape((-1,) + (1,) * (len(dims) - 1 - dim))
    return loudness


def picks_of(stream_key, rows, number_of, top, lift):
    sequence = jax.random.permutation(jax.random.fold_in(stream_key, 1), number_of)
    boost = sequence
    for power in range(3):
        boost = boost * boost // number_of
    boost = boost * lift // number_of
    tickets = jax.random.randint(jax.random.fold_in(stream_key, 2), (rows, number_of), 0, 4096) + boost
    holders = jax.random.permutation(jax.random.fold_in(stream_key, 3), rows)[jnp.arange(number_of) % rows]
    tickets = jnp.where(jnp.arange(rows)[:, None] == holders[None, :], 1 << 14, tickets)
    score = tickets * number_of + jnp.arange(number_of)
    return lax.top_k(score.astype(jnp.int32), top)[1].astype(jnp.int32)


def length_profile(number_of, total, most, slope):
    portions = [(1 << 20) // math.isqrt(standing ** slope) + 1 for standing in range(2, number_of + 1)]
    surplus, given = total - most - (number_of - 1), [1] * (number_of - 1)
    while surplus > 0:
        movable = [i for i in range(number_of - 1) if given[i] < most]
        whole, left = sum([portions[i] for i in movable]), surplus
        for i in movable:
            extra = min(most - given[i], max(1, left * portions[i] // whole), surplus)
            given[i] = given[i] + extra
            surplus = surplus - extra
    return np.array([most] + given)


def ragged_sizes(stream_key, number_of, total, reach, slope):
    if number_of == 2:
        one = jax.random.randint(stream_key, (), max(1, total - reach), min(reach, total - 1) + 1)
        return jnp.stack([one, total - one])
    sizes = jnp.asarray(length_profile(number_of, total, reach, slope), jnp.int32)
    pairs = (number_of - 1) // 2
    source_of, taker = sizes[1:1 + 2 * pairs:2], sizes[2:2 + 2 * pairs:2]
    margin = jnp.minimum(source_of - 1, reach - taker)
    passed = jax.random.randint(jax.random.fold_in(stream_key, 1), (pairs,), 0, 1 << 20) % (margin + 1)
    sizes = sizes.at[1:1 + 2 * pairs:2].set(source_of - passed).at[2:2 + 2 * pairs:2].set(taker + passed)
    return sizes[jax.random.permutation(jax.random.fold_in(stream_key, 2), number_of)]


def noise(rng, extent, width, limit, cuts=(), kind=jnp.bfloat16):
    values = jax.random.normal(rng, extent, jnp.float32) * width
    if len(cuts) > 0:
        values = shard_levels(rng, extent, cuts, -0.22, 0.18) * values
    return jnp.clip(values, min=-limit, max=limit).astype(kind)


def heavy_noise(key, extent, width, bound, pieces, heavy, kind=jnp.bfloat16):
    drawn = width * jax.random.normal(key, extent, jnp.float32)
    if pieces:
        drawn = drawn * shard_levels(key, extent, pieces, -0.22, 0.18)
    return jnp.clip(raised(drawn, jax.random.fold_in(key, 3), *heavy), -bound, bound).astype(kind)


def setup_inputs(seed: int = 0) -> dict:
    key_list = jax.random.split(jax.random.key(seed), 15)
    return {
        "layer_input": heavy_noise(key_list[0], (TOKENS, D), 1.0, 24.0, ((0, 256),), (0, 1, 256, 6.0)),
        "gain_attn": jnp.clip(1.0 + 0.1 * jax.random.normal(key_list[1], (D,), jnp.float32), 0.5, 1.5),
        "w_query": noise(key_list[2], (D, H * HD), D ** -0.5, 0.1875),
        "w_key": noise(key_list[3], (D, KV * HD), D ** -0.5, 0.1875),
        "w_value": noise(key_list[4], (D, KV * HD), D ** -0.5, 0.1875),
        "w_proj": noise(key_list[5], (H * HD, D), (H * HD // 32) ** -0.5, 1.0),
        "gain_ffn": jnp.clip(1.0 + 0.1 * jax.random.normal(key_list[6], (D,), jnp.float32), 0.5, 1.5),
        "w_router": noise(key_list[7], (D, EXPERTS), (4 * D) ** -0.5, 0.09375),
        "w_expert_in": noise(key_list[8], (EXPERTS, D, 2 * FF), D ** -0.5, 0.1875, ((0, 8),)),
        "w_expert_out": noise(key_list[9], (EXPERTS, FF, D), (FF // 16) ** -0.5, 1.0, ((0, 8),)),
        "segment_ids": jax.vmap(lambda own: jnp.searchsorted(jnp.cumsum(ragged_sizes(own, SEQ // 32, SEQ, 3 * SEQ // 4, 2)), jnp.arange(SEQ), side="right"))(jax.random.split(key_list[10], N_DP)).reshape((N_DP, SEQ)).astype(jnp.int32),
        "expert_ids": picks_of(key_list[11], TOKENS, EXPERTS, TOP, 2048),
        "slot_order": jax.vmap(lambda own: jax.random.permutation(own, TOK_DEV * TOP))(jax.random.split(key_list[12], (N_DP * N_EP * N_CTX))).reshape((N_DP * N_EP * N_CTX, TOK_DEV * TOP)).astype(jnp.int32),
        "out_grad": noise(key_list[13], (TOKENS, D), 1.0, 6.0, ((0, 256),)),
    }


@jax.custom_vjp
def low(v):
    return lax.optimization_barrier(v.astype(jnp.bfloat16)).astype(jnp.float32)

@jax.custom_vjp
def low_back(v):
    return v

def low_keep(v):
    return (low(v), None)

def low_pass(kept, grad):
    return (grad,)

def back_keep(v):
    return (v, None)

def back_low(kept, grad):
    return (low(grad),)
low.defvjp(low_keep, low_pass)
low_back.defvjp(back_keep, back_low)
EPSILON = 1e-06
PRECISE = lax.Precision.HIGHEST
MASKED = -1e+30

def rms_norm(values, norm_gain):
    return values * lax.rsqrt(lax.optimization_barrier(jnp.mean(values * values, axis=-1, keepdims=True)) + EPSILON) * norm_gain

def rotate(values, positions):
    middle = values.shape[-1] // 2
    frequency = 10000.0 ** (-jnp.arange(middle, dtype=jnp.float32) * 2.0 / values.shape[-1])
    angles = positions.astype(jnp.float32)[:, None] * frequency[None, :]
    cosine_part = jnp.cos(angles)[:, None, :]
    sine_part = jnp.sin(angles)[:, None, :]
    leading = values[..., :middle]
    trailing = values[..., middle:]
    return jnp.concatenate([leading * cosine_part - trailing * sine_part, trailing * cosine_part + leading * sine_part], axis=-1)

def swiglu(gate_up):
    middle = gate_up.shape[-1] // 2
    gating = gate_up[..., :middle]
    return gating / (1.0 + jnp.exp(-gating)) * gate_up[..., middle:]

def slot_table(expert_ids, slot_order):
    device_total = N_DP * N_EP * N_CTX
    pair_count = TOK_DEV * TOP
    block_ids = expert_ids.reshape(device_total, pair_count)

    def block_rank(packed):
        flat_ids, priority = packed
        earlier = (flat_ids[:, None] == flat_ids[None, :]) & (priority[None, :] < priority[:, None])
        return lax.optimization_barrier(jnp.sum(earlier.astype(jnp.int32), axis=1)).astype(jnp.int32)
    slot_rank = lax.map(block_rank, (block_ids, slot_order))
    device_ids = jnp.arange(device_total, dtype=jnp.int32)[:, None]
    pair_ids = device_ids * pair_count + jnp.arange(pair_count, dtype=jnp.int32)[None, :]
    slot_index = jnp.where(slot_rank < CAP, block_ids * (device_total * CAP) + device_ids * CAP + slot_rank, EXPERTS * device_total * CAP)
    table_flat = jnp.full((EXPERTS * device_total * CAP,), TOKENS * TOP, jnp.int32)
    table_flat = table_flat.at[slot_index.reshape(-1)].set(pair_ids.reshape(-1), mode='drop')
    return table_flat.reshape(EXPERTS, device_total * CAP)

def forward(layer_input, gain_attn, w_query, w_key, w_value, w_proj, gain_ffn, w_router, w_expert_in, w_expert_out, segment_ids, expert_ids, table):
    scaling = HD ** (-0.5)
    groups = H // KV
    positions = jnp.arange(TOKENS, dtype=jnp.int32) % SEQ
    normed = low(rms_norm(layer_input, gain_attn))
    query_pre = low_back(jnp.dot(normed, w_query, precision=PRECISE))
    key_pre = low_back(jnp.dot(normed, w_key, precision=PRECISE))
    value_rows = low(low_back(jnp.dot(normed, w_value, precision=PRECISE)))
    query = low(rotate(query_pre.reshape(TOKENS, H, HD), positions))
    keys = low(rotate(key_pre.reshape(TOKENS, KV, HD), positions))
    query_seq = query.reshape(N_DP, SEQ, KV, groups, HD).transpose(0, 2, 3, 1, 4)
    key_seq = keys.reshape(N_DP, SEQ, KV, HD).transpose(0, 2, 1, 3)
    value_seq = value_rows.reshape(N_DP, SEQ, KV, HD).transpose(0, 2, 1, 3)

    def attend_sequence(packed):
        query_one, key_one, value_one, doc_ids = packed
        places = jnp.arange(SEQ, dtype=jnp.int32)
        allowed = (places[:, None] >= places[None, :]) & (doc_ids[:, None] == doc_ids[None, :])

        def attend_group(inner):
            query_grp, key_head, value_head = inner
            scores = low_back(scaling * jnp.einsum('gqd,kd->gqk', query_grp, key_head, precision=PRECISE))
            scores = jnp.where(allowed[None], scores, MASKED)
            maxima = lax.optimization_barrier(jnp.max(scores, axis=-1, keepdims=True))
            exponent = jnp.exp(scores - maxima)
            attn_probs = low(exponent / lax.optimization_barrier(jnp.sum(exponent, axis=-1, keepdims=True)))
            return jnp.einsum('gqk,kd->gqd', attn_probs, value_head, precision=PRECISE)
        return lax.map(jax.checkpoint(attend_group), (query_one, key_one, value_one))
    attended = lax.map(jax.checkpoint(attend_sequence), (query_seq, key_seq, value_seq, segment_ids))
    attended = attended.transpose(0, 3, 1, 2, 4).reshape(TOKENS, H * HD)
    attended = low(low_back(attended))
    mixed = low_back(jnp.dot(attended, w_proj, precision=PRECISE))
    residual = layer_input + mixed
    normed_ffn = low(rms_norm(residual, gain_ffn))
    logits = jnp.dot(normed_ffn, w_router, precision=PRECISE)
    chosen = jnp.take_along_axis(logits, expert_ids, axis=1)
    maxima = lax.optimization_barrier(jnp.max(chosen, axis=1, keepdims=True))
    exponent = jnp.exp(chosen - maxima)
    gate_weights = exponent / lax.optimization_barrier(jnp.sum(exponent, axis=1, keepdims=True))
    padded_rows = jnp.concatenate([normed_ffn, jnp.zeros((1, D), jnp.float32)], axis=0)
    padded_gates = jnp.concatenate([gate_weights.reshape(-1), jnp.zeros((1,), jnp.float32)])

    def run_expert(packed):
        pair_ids, weight_in, weight_out = packed
        rows = low_back(padded_rows[pair_ids // TOP])
        gate_up = low_back(jnp.dot(rows, weight_in, precision=PRECISE))
        activated = low(swiglu(gate_up))
        result = low(low_back(jnp.dot(activated, weight_out, precision=PRECISE)))
        return result * padded_gates[pair_ids][:, None]
    weighted = lax.map(jax.checkpoint(run_expert), (table, w_expert_in, w_expert_out))
    token_ids = (table // TOP).reshape(-1)
    expert_sum = jnp.zeros((TOKENS + 1, D), jnp.float32).at[token_ids].add(weighted.reshape(-1, D))[:TOKENS]
    return residual + expert_sum

def reference(layer_input, gain_attn, w_query, w_key, w_value, w_proj, gain_ffn, w_router, w_expert_in, w_expert_out, segment_ids, expert_ids, slot_order, out_grad):
    table = slot_table(expert_ids, slot_order)

    def layer(inputs_f, gain_one, query_w, key_w, value_w, proj_w, gain_two, router_w, expert_in_w, expert_out_w):
        return forward(inputs_f, gain_one, query_w, key_w, value_w, proj_w, gain_two, router_w, expert_in_w, expert_out_w, segment_ids, expert_ids, table)
    output, pullback = jax.vjp(layer, layer_input.astype(jnp.float32), gain_attn.astype(jnp.float32), w_query.astype(jnp.float32), w_key.astype(jnp.float32), w_value.astype(jnp.float32), w_proj.astype(jnp.float32), gain_ffn.astype(jnp.float32), w_router.astype(jnp.float32), w_expert_in.astype(jnp.float32), w_expert_out.astype(jnp.float32))
    grads = pullback(out_grad.astype(jnp.float32))
    return (output.astype(jnp.bfloat16), grads[0].astype(jnp.bfloat16), grads[1], grads[2], grads[3], grads[4], grads[5], grads[6], grads[7], grads[8], grads[9])
```

```python
from functools import partial

import jax
import jax.numpy as jnp
import numpy as np
from jax import lax
from jax.experimental import pallas as pl
from jax.experimental.pallas import tpu as pltpu
from jax.sharding import PartitionSpec as P

HD = 64
EPSILON = 1e-06
MASKED = -1e30
CAP = 40
TOK = 128
BIG = 4096.0
MESH = pl.DeviceIdType.MESH
F32 = jnp.float32
BF16 = jnp.bfloat16
VMEM_LIMIT = 60 * 1024 * 1024

NT = (((1,), (1,)), ((), ()))
NN = (((1,), (0,)), ((), ()))
TN = (((0,), (0,)), ((), ()))


def mm(a, b, dims=NN):
    return lax.dot_general(a, b, dims, preferred_element_type=F32)


def mm3(a, b, dims=NN):
    high = a.astype(BF16)
    low = (a - high.astype(F32)).astype(BF16)
    return mm(high, b, dims) + mm(low, b, dims)


def where_am_i():
    dp, ep, ctx = lax.axis_index("dp"), lax.axis_index("ep"), lax.axis_index("ctx")
    return dp, ep, ctx


def remote(src, dst, send, recv, device):
    return pltpu.make_async_remote_copy(
        src_ref=src, dst_ref=dst, send_sem=send, recv_sem=recv, device_id=device, device_id_type=MESH
    )


def greet(barrier, device):
    pl.semaphore_signal(barrier, inc=1, device_id=device, device_id_type=MESH)


def rotate_half(values):
    lane = lax.broadcasted_iota(jnp.int32, values.shape, 1)
    return jnp.where(lane % HD < HD // 2, pltpu.roll(values, 96, 1), pltpu.roll(values, 32, 1))


def rope_block(block, ca_ref, sa_ref, cb_ref, sb_ref):
    ca, sa = ca_ref[pl.ds(block, 1), :], sa_ref[pl.ds(block, 1), :]
    cb, sb = cb_ref[...], sb_ref[...]
    cosine = ca * cb - sa * sb
    sine = sa * cb + ca * sb
    lane = lax.broadcasted_iota(jnp.int32, cosine.shape, 1)
    return cosine, jnp.where(lane % HD < HD // 2, -sine, sine)


def rope_tables():
    frequency = 10000.0 ** (-np.arange(HD // 2, dtype=np.float64) * 2.0 / HD)
    frequency = np.tile(frequency.astype(np.float32).astype(np.float64), 4)
    blocks = np.arange(32, dtype=np.float64)[:, None] * 128.0 * frequency[None, :]
    rows = np.arange(128, dtype=np.float64)[:, None] * frequency[None, :]
    return [t.astype(np.float32) for t in (np.cos(blocks), np.sin(blocks), np.cos(rows), np.sin(rows))]


class EpGather:
    COUNT = 13

    def __init__(self, ref, send, recv, place):
        self.ref, self.send, self.recv = ref, send, recv
        dp, ep, ctx = place
        y, k = ep // 2, ep % 2
        self.up = (dp, ((y + 1) % 4) * 2 + k, ctx)
        self.dn = (dp, ((y + 3) % 4) * 2 + k, ctx)
        self.sib = (dp, y * 2 + 1 - k, ctx)

        def at(dy, other):
            return ((y + dy) % 4) * 2 + ((1 - k) if other else k)

        u, s, d = self.up, self.sib, self.dn
        self.sends = [
            (at(0, 0), None, s), (at(0, 0), 0, u), (at(0, 0), 1, u), (at(0, 0), 1, d), (at(0, 0), 0, d),
            (at(3, 0), 0, u), (at(3, 0), 0, s), (at(1, 0), 1, d), (at(1, 0), 1, s),
            (at(3, 0), 1, s), (at(1, 0), 0, s), (at(2, 0), 0, s), (at(2, 0), 1, s),
        ]
        self.gets = [
            (at(0, 1), None), (at(3, 0), 0), (at(3, 0), 1), (at(1, 0), 1), (at(1, 0), 0),
            (at(2, 0), 0), (at(3, 1), 0), (at(2, 0), 1), (at(1, 1), 1),
            (at(3, 1), 1), (at(1, 1), 0), (at(2, 1), 0), (at(2, 1), 1),
        ]

    def view(self, block, half):
        if half is None:
            return self.ref.at[block]
        rows = self.ref.shape[1] // 2
        return self.ref.at[block, pl.ds(half * rows, rows)]

    def go(self, *which):
        for i in which:
            block, half, device = self.sends[i]
            v = self.view(block, half)
            remote(v, v, self.send.at[i], self.recv.at[i], device).start()

    def got(self, *which):
        for i in which:
            v = self.view(*self.gets[i])
            remote(v, v, self.send.at[i], self.recv.at[i], self.sends[i][2]).wait_recv()

    def sent(self):
        for i in range(self.COUNT):
            block, half, device = self.sends[i]
            v = self.view(block, half)
            remote(v, v, self.send.at[i], self.recv.at[i], device).wait_send()

    def whole(self):
        self.got(1)
        self.go(5, 6)
        self.got(3)
        self.go(7, 8)
        self.got(2)
        self.go(9)
        self.got(4)
        self.go(10)
        self.got(5)
        self.go(11)
        self.got(7)
        self.go(12)
        self.got(0, 6, 8, 9, 10, 11, 12)


class EpScatterSum:
    COUNT = 8

    def __init__(self, part, cbuf, fbuf, gbuf, send, recv, place):
        self.part, self.cbuf, self.fbuf, self.gbuf = part, cbuf, fbuf, gbuf
        self.send, self.recv = send, recv
        dp, ep, ctx = place
        self.y, self.k = ep // 2, ep % 2
        y, k = self.y, self.k
        self.up = (dp, ((y + 1) % 4) * 2 + k, ctx)
        self.dn = (dp, ((y + 3) % 4) * 2 + k, ctx)
        self.sib = (dp, y * 2 + 1 - k, ctx)

    def block(self, dy, other=False):
        return ((self.y + dy) % 4) * 2 + ((1 - self.k) if other else self.k)

    def copy(self, i):
        half = self.cbuf.shape[1] // 2
        lo, hi = pl.ds(0, half), pl.ds(half, half)
        s, r = self.send, self.recv
        if i < 4:
            away = self.block((2, 1, 3, 0)[i], True)
            return remote(self.part.at[away], self.cbuf.at[i], s.at[i], r.at[i], self.sib)
        src, dst, device = (
            (self.cbuf.at[0, lo], self.fbuf.at[0], self.up),
            (self.cbuf.at[0, hi], self.fbuf.at[1], self.dn),
            (self.cbuf.at[1], self.gbuf.at[0], self.up),
            (self.cbuf.at[2], self.gbuf.at[1], self.dn),
        )[i - 4]
        return remote(src, dst, s.at[i], r.at[i], device)

    def start(self):
        for i in range(4):
            self.copy(i).start()

    def far(self):
        self.copy(0).wait_recv()
        self.cbuf[0] = (self.cbuf[0].astype(F32) + self.part[self.block(2)].astype(F32)).astype(BF16)
        self.copy(4).start()
        self.copy(5).start()

    def near(self):
        half = self.cbuf.shape[1] // 2
        for slot, dy, far, rows, rest in ((1, 1, 0, pl.ds(0, half), pl.ds(half, half)), (2, 3, 1, pl.ds(half, half), pl.ds(0, half))):
            b = self.block(dy)
            self.copy(slot).wait_recv()
            self.copy(4 + far).wait_recv()
            self.cbuf[slot, rows] = (
                self.cbuf[slot, rows].astype(F32) + self.part[b, rows].astype(F32) + self.fbuf[far].astype(F32)
            ).astype(BF16)
            self.cbuf[slot, rest] = (self.cbuf[slot, rest].astype(F32) + self.part[b, rest].astype(F32)).astype(BF16)
            self.copy(6 + far).start()

    def last(self):
        for i in (3, 6, 7):
            self.copy(i).wait_recv()
        return (
            self.part[self.block(0)].astype(F32) + self.cbuf[3].astype(F32)
            + self.gbuf[0].astype(F32) + self.gbuf[1].astype(F32)
        )

    def sent(self):
        for i in range(self.COUNT):
            self.copy(i).wait_send()


def scatter_sum_scratch():
    return [
        pltpu.VMEM((4, TOK, 1024), BF16),
        pltpu.VMEM((2, TOK // 2, 1024), BF16),
        pltpu.VMEM((2, TOK, 1024), BF16),
        pltpu.SemaphoreType.DMA((8,)),
        pltpu.SemaphoreType.DMA((8,)),
    ]


def exchange(src, dst, send, recv, place, wait):
    dp, ep, ctx = place
    for r in range(1, 8):
        to, source = (ep + r) % 8, (ep + 8 - r) % 8
        if not wait:
            remote(src.at[to], dst.at[ep], send.at[r], recv.at[r], (dp, to, ctx)).start()
        else:
            remote(src.at[to], dst.at[source], send.at[r], recv.at[r], (dp, to, ctx)).wait_recv()


def exchange_sent(src, dst, send, recv, place):
    dp, ep, ctx = place
    for r in range(1, 8):
        to = (ep + r) % 8
        remote(src.at[to], dst.at[ep], send.at[r], recv.at[r], (dp, to, ctx)).wait_send()


def starts_of(docs):
    rows = lax.broadcasted_iota(jnp.int32, docs.shape, 0)
    lane = lax.broadcasted_iota(jnp.int32, docs.shape, 1)
    docs = docs.astype(F32)
    turned = pltpu.roll(docs, 1, 1)
    before = jnp.where(lane == 0, pltpu.roll(turned, 1, 0), turned)
    place = rows * 128 + lane
    fresh = (docs != before) | (place == 0)
    value = jnp.where(fresh, place.astype(F32), 0.0)
    for shift in (1, 2, 4, 8, 16, 32, 64):
        value = jnp.maximum(value, jnp.where(lane >= shift, pltpu.roll(value, shift, 1), 0.0))
    carry = jnp.broadcast_to(jnp.max(value, axis=1, keepdims=True), value.shape)
    for shift in (1, 2, 4, 8, 16):
        carry = jnp.maximum(carry, jnp.where(rows >= shift, pltpu.roll(carry, shift, 0), 0.0))
    above = jnp.where(rows >= 1, pltpu.roll(carry, 1, 0), 0.0)
    return jnp.maximum(value, above)


def slots_of(eid_ref, eidT_ref, so_ref, soT_ref, slot_scr, sel_ref):
    def expert(index):
        return jnp.where(index % 8 < 4, (index // 8) * 4 + index % 8, -1)

    row_expert = expert(lax.broadcasted_iota(jnp.int32, (64, TOK), 0))
    lane_expert = expert(lax.broadcasted_iota(jnp.int32, (TOK, 64), 1))
    by_row = jnp.full((64, TOK), BIG, F32)
    by_lane = jnp.full((TOK, 64), BIG, F32)
    for k in range(8):
        by_row = jnp.where(eidT_ref[k : k + 1, :] == row_expert, soT_ref[k : k + 1, :].astype(F32), by_row)
        by_lane = jnp.where(eid_ref[:, k : k + 1] == lane_expert, so_ref[:, k : k + 1].astype(F32), by_lane)
    sel_ref[...] = jnp.where(by_row < BIG, 1.0, 0.0)
    for g in range(8):
        for j in range(4):
            r = 8 * g + j
            row = by_row[r : r + 1, :]
            less = jnp.where(by_lane[:, r : r + 1] < row, 1.0, 0.0)
            rank = jnp.sum(less, axis=0, keepdims=True)
            slot_scr[g, j : j + 1, :] = jnp.where((row < BIG) & (rank < CAP), rank, -1.0)
        slot_scr[g, 4:8, :] = jnp.full((4, TOK), -1.0, F32)


def first_kernel(
    x_ref, gain_ref, og_ref, w_ref, ca_ref, sa_ref, cb_ref, sb_ref, eid_ref, eidT_ref, so_ref, soT_ref, doc_ref,
    nall_ref, q_ref, kv_ref, ogall_ref, slot_ref, sel_ref, start_ref,
    slot_scr, nsend, nrecv, osend, orecv, ssend, srecv, ksend, krecv,
):
    place = where_am_i()
    dp, ep, ctx = place
    y = ep // 2
    barrier = pltpu.get_barrier_semaphore()
    for r in range(1, 8):
        greet(barrier, (dp, (ep + r) % 8, ctx))

    @pl.when(ctx > 0)
    def _():
        greet(barrier, (dp, ep, ctx - 1))

    @pl.when(ctx < 3)
    def _():
        greet(barrier, (dp, ep, ctx + 1))

    x = x_ref[...].astype(F32)
    normed = x * lax.rsqrt(jnp.mean(x * x, axis=-1, keepdims=True) + EPSILON) * gain_ref[...]
    nall_ref[ep] = normed.astype(BF16)
    ogall_ref[ep] = og_ref[...]
    edges = jnp.where(ctx > 0, 1, 0) + jnp.where(ctx < 3, 1, 0)
    pl.semaphore_wait(barrier, 7 + edges)

    gather = EpGather(nall_ref, nsend, nrecv, place)
    grads = EpGather(ogall_ref, osend, orecv, place)
    gather.go(0, 1, 3, 2, 4)

    start_ref[...] = starts_of(doc_ref[...])
    slots_of(eid_ref, eidT_ref, so_ref, soT_ref, slot_scr, sel_ref)
    slot_ref[ep] = slot_scr[ep]
    exchange(slot_scr, slot_ref, ssend, srecv, place, False)

    lane = lax.broadcasted_iota(jnp.int32, (TOK, 128), 1)

    def project(dy):
        chip = (y + dy) % 4
        rows = jnp.concatenate([nall_ref[2 * chip], nall_ref[2 * chip + 1]], axis=0)
        out = mm(rows, w_ref[...])
        for i in range(2):
            b = 2 * chip + i
            cosine, sine = rope_block(4 * b + ctx, ca_ref, sa_ref, cb_ref, sb_ref)
            q = out[i * TOK : (i + 1) * TOK, :128]
            kv = out[i * TOK : (i + 1) * TOK, 128:]
            q_rot = (q * cosine + rotate_half(q) * sine).astype(BF16)
            q_ref[b] = (q_rot.astype(F32) * (HD**-0.5)).astype(BF16)
            cosine = jnp.where(lane < HD, cosine, 1.0)
            sine = jnp.where(lane < HD, sine, 0.0)
            kv_ref[b, ctx] = (kv * cosine + rotate_half(kv) * sine).astype(BF16)

    offsets = (0, 3, 1, 2)

    def hop(direction, h, g, action):
        chip = (y + offsets[g]) % 4
        back = h - 1
        own = ctx - back if direction == 0 else ctx + back
        come = ctx - h if direction == 0 else ctx + h
        to = ctx + 1 if direction == 0 else ctx - 1
        index = (direction * 3 + back) * 4 + g
        send, recv = ksend.at[index], krecv.at[index]
        if action == "recv":
            ok = come >= 0 if direction == 0 else come <= 3

            @pl.when(ok)
            def _():
                v = kv_ref.at[pl.ds(2 * chip, 2), come]
                remote(v, v, send, recv, (dp, ep, ctx)).wait_recv()

        else:
            ok = (own >= 0) & (ctx < 3) if direction == 0 else (own <= 3) & (ctx > 0)

            @pl.when(ok)
            def _():
                v = kv_ref.at[pl.ds(2 * chip, 2), own]
                c = remote(v, v, send, recv, (dp, ep, to))
                c.start() if action == "send" else c.wait_send()

    def hops(h, g):
        for direction in (0, 1):
            if h > 1:
                hop(direction, h - 1, g, "recv")
            hop(direction, h, g, "send")

    gather.got(0)
    project(0)
    hops(1, 0)
    gather.got(1)
    gather.go(5, 6)
    gather.got(3)
    gather.go(7, 8)
    gather.got(2)
    gather.go(9)
    gather.got(4)
    gather.go(10)
    grads.go(0, 1, 3, 2, 4)
    gather.got(6, 9)
    project(3)
    hops(1, 1)
    hops(2, 0)
    gather.got(8, 10)
    project(1)
    hops(1, 2)
    hops(2, 1)
    hops(3, 0)
    gather.got(5)
    gather.go(11)
    gather.got(7)
    gather.go(12)
    gather.got(11, 12)
    project(2)
    hops(1, 3)
    hops(2, 2)
    hops(3, 1)
    hops(2, 3)
    hops(3, 2)
    grads.whole()
    hops(3, 3)
    for g in range(4):
        for direction in (0, 1):
            hop(direction, 3, g, "recv")
    exchange(slot_scr, slot_ref, ssend, srecv, place, True)
    gather.sent()
    grads.sent()
    exchange_sent(slot_scr, slot_ref, ssend, srecv, place)
    for g in range(4):
        for h in (1, 2, 3):
            for direction in (0, 1):
                hop(direction, h, g, "sent")


CHUNK = 512


def key_mask(chunk, start_row, place_row):
    keys = (lax.broadcasted_iota(jnp.int32, (CHUNK, 256), 0) + chunk * CHUNK).astype(F32)
    return (keys >= start_row) & (keys <= place_row)


def query_rows(j, ctx, start_ref):
    block = 4 * j + ctx
    start = start_ref[pl.ds(block, 1), :]
    places = (lax.broadcasted_iota(jnp.int32, (1, 128), 1) + block * 128).astype(F32)
    return jnp.concatenate([start, start], axis=1), jnp.concatenate([places, places], axis=1)


def turned(block):
    return block.astype(F32).T.astype(BF16)


def heads_wide(tall):
    return jnp.concatenate([tall[:HD], tall[HD:]], axis=1)


def attend_kernel(first_ref, q_ref, kv_ref, start_ref, att_ref, attT_ref, lse_ref, kvT):
    ctx = lax.axis_index("ctx")

    for chunk in range(8):
        part = kv_ref[chunk * CHUNK : (chunk + 1) * CHUNK, :].astype(F32).T
        row = lax.broadcasted_iota(jnp.int32, part.shape, 0)
        kvT[:, chunk * CHUNK : (chunk + 1) * CHUNK] = jnp.where(row < HD, 1.0, part).astype(BF16)

    for j in range(8):
        start_row, place_row = query_rows(j, ctx, start_ref)
        wide = heads_wide(turned(q_ref[j]))
        q_pad = jnp.concatenate([wide, jnp.zeros_like(wide)], axis=0)

        def step(chunk, carry):
            top, total = carry
            rows = pl.ds(pl.multiple_of(chunk * CHUNK, CHUNK), CHUNK)
            scores = mm(kv_ref[rows, :], q_pad)
            scores = jnp.where(key_mask(chunk, start_row, place_row), scores, MASKED)
            new_top = jnp.maximum(top, jnp.max(scores, axis=0, keepdims=True))
            probs = jnp.exp(scores - new_top).astype(BF16)
            total = total * jnp.exp(top - new_top) + mm(kvT[:, rows], probs)
            return new_top, total

        top, total = lax.fori_loop(
            first_ref[j], j + 1, step, (jnp.full((1, 256), MASKED, F32), jnp.zeros((128, 256), F32))
        )
        norm = total[0:1]
        out = total[HD:] / norm
        tall = jnp.concatenate([out[:, :128], out[:, 128:]], axis=0)
        attT_ref[j] = tall
        att_ref[j] = tall.T.astype(BF16)
        lse_ref[j] = jnp.broadcast_to(top + jnp.log(norm), (8, 256))


def attend_back_kernel(
    first_ref, q_ref, kv_ref, start_ref, attT_ref, lse_ref, gm_ref, w_ref, ca_ref, sa_ref, cb_ref, sb_ref,
    dq_ref, dkv_ref, gproj_ref, kT, acc,
):
    ctx = lax.axis_index("ctx")
    for chunk in range(8):
        part = kv_ref[chunk * CHUNK : (chunk + 1) * CHUNK, :].astype(F32).T
        kT[:, chunk * CHUNK : (chunk + 1) * CHUNK] = part[:HD].astype(BF16)
        acc[chunk * CHUNK : (chunk + 1) * CHUNK, :] = jnp.zeros((CHUNK, 128), F32)
    gproj = jnp.zeros((128, 1024), F32)
    for j in range(8):
        gproj = gproj + mm(attT_ref[j].astype(BF16), gm_ref[j])
    gproj_ref[...] = gproj
    zero = jnp.zeros((HD, 256), BF16)
    lane = lax.broadcasted_iota(jnp.int32, (256, 128), 1)
    for j in range(8):
        start_row, place_row = query_rows(j, ctx, start_ref)
        grad_tall = mm(w_ref[...], gm_ref[j], NT).astype(BF16)
        delta = jnp.sum(
            heads_wide(grad_tall.astype(F32)) * heads_wide(attT_ref[j]), axis=0, keepdims=True
        )
        q_blk = q_ref[j]
        q_pad = jnp.concatenate([heads_wide(turned(q_blk)), zero], axis=0)
        g_pad = jnp.concatenate([zero, heads_wide(grad_tall)], axis=0)
        both = jnp.concatenate([q_pad, g_pad], axis=1)
        g_blk = turned(grad_tall)
        q_f, g_f = q_blk.astype(F32), g_blk.astype(F32)
        q_rows = jnp.concatenate([q_f, pltpu.roll(q_f, HD, 1)], axis=0)
        g_rows = jnp.concatenate([pltpu.roll(g_f, HD, 1), g_f], axis=0)
        stack = jnp.concatenate(
            [jnp.where(lane < HD, q_rows, 0.0), jnp.where(lane < HD, 0.0, g_rows)], axis=0
        ).astype(BF16)
        lse = lse_ref[j, 0:1, :]

        def step(chunk, dq):
            rows = pl.ds(pl.multiple_of(chunk * CHUNK, CHUNK), CHUNK)
            pair = mm(kv_ref[rows, :], both)
            scores = jnp.where(key_mask(chunk, start_row, place_row), pair[:, :256], MASKED)
            probs = jnp.exp(scores - lse)
            grad = (probs * (pair[:, 256:] - delta)).astype(BF16)
            acc[rows, :] += mm(jnp.concatenate([grad, probs.astype(BF16)], axis=1), stack)
            return dq + mm(kT[:, rows], grad)

        dq = lax.fori_loop(first_ref[j], j + 1, step, jnp.zeros((HD, 256), F32)) * (HD**-0.5)
        dq = jnp.concatenate([dq[:, :128], dq[:, 128:]], axis=0).T
        cosine, sine = rope_block(4 * j + ctx, ca_ref, sa_ref, cb_ref, sb_ref)
        dq_ref[j] = (dq * cosine - rotate_half(dq) * sine).astype(BF16)
    for chunk in range(8):
        rows = slice(chunk * CHUNK, (chunk + 1) * CHUNK)
        dkv_ref[rows, :] = acc[rows, :].astype(BF16)


def middle_kernel(
    att_ref, x_ref, gain_ref, w_ref, wr_ref, sel_ref,
    res_ref, nf_ref, gin_ref, gates_ref,
    abuf, gscr, asend, arecv, nsend, nrecv, gsend, grecv,
):
    place = where_am_i()
    dp, ep, ctx = place
    barrier = pltpu.get_barrier_semaphore()
    for r in range(1, 8):
        greet(barrier, (dp, (ep + r) % 8, ctx))
    pl.semaphore_wait(barrier, 7)
    exchange(att_ref, abuf, asend, arecv, place, False)
    abuf[ep] = att_ref[ep]
    exchange(att_ref, abuf, asend, arecv, place, True)
    attended = jnp.concatenate([abuf[p] for p in range(8)], axis=1)
    res = x_ref[...].astype(F32) + mm(attended, w_ref[...])
    res_ref[...] = res
    normed = res * lax.rsqrt(jnp.mean(res * res, axis=-1, keepdims=True) + EPSILON) * gain_ref[...]
    normed = normed.astype(BF16)
    nf_ref[ep] = normed
    gather = EpGather(nf_ref, nsend, nrecv, place)
    gather.go(0, 1, 3, 2, 4)
    logits = mm(wr_ref[...], normed, NT)
    chosen = sel_ref[...] > 0.5
    top = jnp.max(jnp.where(chosen, logits, MASKED), axis=0, keepdims=True)
    weight = jnp.where(chosen, jnp.exp(jnp.where(chosen, logits, MASKED) - top), 0.0)
    gates = weight / jnp.sum(weight, axis=0, keepdims=True)
    gates_ref[...] = gates
    for g in range(8):
        gscr[g] = gates[8 * g : 8 * g + 8, :]
    gin_ref[ep] = gscr[ep]
    exchange(gscr, gin_ref, gsend, grecv, place, False)
    gather.whole()
    exchange(gscr, gin_ref, gsend, grecv, place, True)
    gather.sent()
    exchange_sent(gscr, gin_ref, gsend, grecv, place)
    exchange_sent(att_ref, abuf, asend, arecv, place)


def expert_kernel(
    nf_ref, og_ref, slot_ref, gate_ref, win_ref, wout_ref,
    y_ref, d_ref, dg_ref, gw_ref,
    rows_scr, grad_scr,
):
    j = pl.program_id(0)
    slot = lax.broadcasted_iota(jnp.int32, (CAP, TOK), 0).astype(F32)

    def picks(s, e):
        return slot == slot_ref[s, pl.ds(e, 1), :]

    @pl.when(j == 0)
    def _():
        def load(s, carry):
            pick = jnp.concatenate([jnp.where(picks(s, e), 1.0, 0.0) for e in range(4)], axis=0).astype(BF16)
            got = mm(pick, nf_ref[s])
            grad = mm(pick, og_ref[s])
            for e in range(4):
                rows = pl.ds(pl.multiple_of(s * CAP, 8), CAP)
                rows_scr[e, rows, :] = got[e * CAP : (e + 1) * CAP]
                grad_scr[e, rows, :] = grad[e * CAP : (e + 1) * CAP]
            return carry

        lax.fori_loop(0, 8, load, 0)

    gates = jnp.concatenate(
        [jnp.sum(jnp.where(picks(s, j), gate_ref[s, pl.ds(j, 1), :], 0.0), axis=1, keepdims=True) for s in range(8)],
        axis=0,
    )
    received = rows_scr[j].astype(BF16)
    grad_tok = grad_scr[j]
    gate_up = mm(received, win_ref[0])
    gating, up = gate_up[:, :512], gate_up[:, 512:]
    sig = 1.0 / (1.0 + jnp.exp(-gating))
    silu = gating * sig
    act = (silu * up).astype(BF16)
    result = mm(act, wout_ref[0]).astype(BF16).astype(F32)
    dots = jnp.sum(grad_tok * result, axis=1, keepdims=True)
    grad_res = (grad_tok * gates).astype(BF16)
    grad_scr[j] = result * gates
    for s in range(8):
        dg_ref[s, pl.ds(j, 1), :] = jnp.sum(
            jnp.where(picks(s, j), dots[s * CAP : (s + 1) * CAP], 0.0), axis=0, keepdims=True
        )
    gw_ref[0, :, 32:48, :] = mm(act, grad_res, TN).astype(BF16).reshape(32, 16, 1024)
    grad_act = mm(grad_res, wout_ref[0], NT)
    grad_up = (grad_act * silu).astype(BF16)
    grad_gate = (grad_act * up * sig * (1.0 + gating * (1.0 - sig))).astype(BF16)
    grad_gu = jnp.concatenate([grad_gate, grad_up], axis=1)
    gw_ref[0, :, 0:32, :] = mm(received, grad_gu, TN).astype(BF16).reshape(32, 32, 1024)
    rows_scr[j] = mm(grad_gu, win_ref[0], NT)

    @pl.when(j == 3)
    def _():
        def store(s, carry):
            pick = jnp.concatenate([jnp.where(picks(s, e), 1.0, 0.0) for e in range(4)], axis=0).astype(BF16)
            rows = pl.ds(pl.multiple_of(s * CAP, 8), CAP)
            weighted = jnp.concatenate([grad_scr[e, rows, :] for e in range(4)], axis=0).astype(BF16)
            y_ref[s] = mm(pick, weighted, TN).astype(BF16)
            back = jnp.concatenate([rows_scr[e, rows, :] for e in range(4)], axis=0).astype(BF16)
            d_ref[s] = mm(pick, back, TN).astype(BF16)
            dg_ref[s, 4:8, :] = jnp.zeros((4, TOK), F32)
            return carry

        lax.fori_loop(0, 8, store, 0)


def turn_kernel(
    part_ref, dg_ref, gates_ref, res_ref, nf_ref, og_ref, gain_ref, wr_ref,
    gm_ref, gres_ref, grouter_ref, ggain_ref,
    dbuf, cbuf, fbuf, gbuf, csend, crecv, dsend, drecv, gsend, grecv,
):
    place = where_am_i()
    dp, ep, ctx = place
    barrier = pltpu.get_barrier_semaphore()
    for r in range(1, 8):
        greet(barrier, (dp, (ep + r) % 8, ctx))
    pl.semaphore_wait(barrier, 7)
    total = EpScatterSum(part_ref, cbuf, fbuf, gbuf, csend, crecv, place)
    total.start()
    exchange(dg_ref, dbuf, dsend, drecv, place, False)
    dbuf[ep] = dg_ref[ep]
    total.far()
    total.near()
    exchange(dg_ref, dbuf, dsend, drecv, place, True)
    gates = gates_ref[...]
    grad_gates = jnp.concatenate([dbuf[p] for p in range(8)], axis=0)
    grad_logits = gates * (grad_gates - jnp.sum(gates * grad_gates, axis=0, keepdims=True))
    high = grad_logits.astype(BF16)
    low = (grad_logits - high.astype(F32)).astype(BF16)
    grouter_ref[...] = mm(high, nf_ref[...]) + mm(low, nf_ref[...])
    from_router = mm(high, wr_ref[...], TN) + mm(low, wr_ref[...], TN)
    res = res_ref[...]
    scale = lax.rsqrt(jnp.mean(res * res, axis=-1, keepdims=True) + EPSILON)
    grad_normed = total.last() + from_router
    scaled = res * scale
    ggain_ref[...] = jnp.broadcast_to(jnp.sum(grad_normed * scaled, axis=0, keepdims=True), (8, 1024))
    grad_normed = grad_normed * gain_ref[...]
    mean = jnp.mean(grad_normed * scaled, axis=-1, keepdims=True)
    gres = og_ref[...].astype(F32) + scale * (grad_normed - scaled * mean)
    gres_ref[...] = gres
    gm_ref[ep] = gres.astype(BF16)
    gather = EpGather(gm_ref, gsend, grecv, place)
    gather.go(0, 1, 3, 2, 4)
    gather.whole()
    gather.sent()
    exchange_sent(dg_ref, dbuf, dsend, drecv, place)
    total.sent()


def final_kernel(
    dq_ref, dkv_ref, part_ref, res_ref, x_ref, gain_ref, nall_ref, wq_ref, wk_ref, wv_ref, gres_ref,
    ca_ref, sa_ref, cb_ref, sb_ref, grouter_ref, ggain_ref, gproj_ref,
    out_ref, ing_ref, dense_ref,
    kbuf, dqkv, pieces, cbuf, fbuf, gbuf, csend, crecv, ksend, krecv, psend, precv,
):
    place = where_am_i()
    dp, ep, ctx = place
    barrier = pltpu.get_barrier_semaphore()
    for r in range(1, 8):
        greet(barrier, (dp, (ep + r) % 8, ctx))

    @pl.when(ctx > 0)
    def _():
        greet(barrier, (dp, ep, ctx - 1))

    @pl.when(ctx < 3)
    def _():
        greet(barrier, (dp, ep, ctx + 1))

    edges = jnp.where(ctx > 0, 1, 0) + jnp.where(ctx < 3, 1, 0)
    pl.semaphore_wait(barrier, 7 + edges)
    total = EpScatterSum(part_ref, cbuf, fbuf, gbuf, csend, crecv, place)

    def link(direction, shard, half, action):
        blocks = pl.ds(half * 4, 4)
        index = (direction * 4 + shard) * 2 + half
        send, recv = ksend.at[index], krecv.at[index]
        to = ctx + 1 if direction == 0 else ctx - 1
        first = ctx == (0 if direction == 0 else 3)
        if direction == 0:
            passes, middle, here = ctx < shard, (ctx < shard) & (ctx > 0), (ctx == shard) & (ctx > 0)
        else:
            passes, middle, here = ctx > shard, (ctx > shard) & (ctx < 3), (ctx == shard) & (ctx < 3)
        slot = kbuf.at[direction, shard, blocks]
        own = dkv_ref.at[blocks, shard]

        def copy(src):
            return remote(src, slot, send, recv, (dp, ep, to))

        if action == "send":

            @pl.when(passes & first)
            def _():
                copy(own).start()

            @pl.when(middle)
            def _():
                copy(slot).wait_recv()

                def add(b, carry):
                    b = b + half * 4
                    kbuf[direction, shard, b] = (
                        kbuf[direction, shard, b].astype(F32) + dkv_ref[b, shard].astype(F32)
                    ).astype(BF16)
                    return carry

                lax.fori_loop(0, 4, add, 0)
                copy(slot).start()

        elif action == "recv":

            @pl.when(here)
            def _():
                copy(slot).wait_recv()

        else:

            @pl.when(passes)
            def _():
                copy(slot).wait_send()

    for half in (0, 1):
        link(0, 3, half, "send")
        link(1, 0, half, "send")
    total.start()
    total.far()
    for half in (0, 1):
        link(0, 2, half, "send")
        link(1, 1, half, "send")
    for half in (0, 1):
        link(0, 1, half, "send")
        link(1, 2, half, "send")
    total.near()
    for shard in range(4):
        for half in (0, 1):
            link(0, shard, half, "recv")
            link(1, shard, half, "recv")

    lane = lax.broadcasted_iota(jnp.int32, (TOK, 128), 1)

    def own_block(b, carry):
        left = jnp.where(ctx > 0, 1.0, 0.0)
        right = jnp.where(ctx < 3, 1.0, 0.0)

        @pl.when(ctx == 0)
        def _():
            kbuf[0, 0, b] = jnp.zeros((TOK, 128), BF16)

        @pl.when(ctx == 3)
        def _():
            kbuf[1, 3, b] = jnp.zeros((TOK, 128), BF16)

        grad = dkv_ref[b, ctx].astype(F32) + kbuf[0, ctx, b].astype(F32) * left + kbuf[1, ctx, b].astype(F32) * right
        cosine, sine = rope_block(4 * b + ctx, ca_ref, sa_ref, cb_ref, sb_ref)
        cosine = jnp.where(lane < HD, cosine, 1.0)
        sine = jnp.where(lane < HD, sine, 0.0)
        dqkv[b, :, 0:128] = dq_ref[b]
        dqkv[b, :, 128:256] = (grad * cosine - rotate_half(grad) * sine).astype(BF16)
        return carry

    lax.fori_loop(0, 8, own_block, 0)
    exchange(dqkv, pieces, psend, precv, place, False)
    pieces[ep] = dqkv[ep]
    weights = mm(nall_ref[...].reshape(1024, 1024), dqkv[...].reshape(1024, 256), TN)
    dense_ref[:, :, 0:256] = weights.astype(BF16).reshape(32, 32, 256)
    gproj = gproj_ref[...].astype(BF16)
    for d in range(8):
        for c in range(4):
            dense_ref[d * 4 + c, :, 384:512] = gproj[32 * c : 32 * c + 32, 128 * d : 128 * d + 128]
    out_ref[...] = (res_ref[...] + total.last()).astype(BF16)
    exchange(dqkv, pieces, psend, precv, place, True)
    grad_q = jnp.concatenate([pieces[p, :, 0:128] for p in range(8)], axis=1)
    grad_k = jnp.concatenate([pieces[p, :, 128:192] for p in range(8)], axis=1)
    grad_v = jnp.concatenate([pieces[p, :, 192:256] for p in range(8)], axis=1)
    grad_normed = mm(grad_q, wq_ref[...], NT) + mm(grad_k, wk_ref[...], NT) + mm(grad_v, wv_ref[...], NT)
    x = x_ref[...].astype(F32)
    scale = lax.rsqrt(jnp.mean(x * x, axis=-1, keepdims=True) + EPSILON)
    scaled = x * scale
    ggain = jnp.sum(grad_normed * scaled, axis=0, keepdims=True)
    grad_normed = grad_normed * gain_ref[...]
    mean = jnp.mean(grad_normed * scaled, axis=-1, keepdims=True)
    ing_ref[...] = (gres_ref[...] + scale * (grad_normed - scaled * mean)).astype(BF16)
    side = jnp.concatenate(
        [grouter_ref[...], jnp.broadcast_to(ggain, (8, 1024)), ggain_ref[...], jnp.zeros((48, 1024), F32)], axis=0
    )
    for t in range(8):
        tile = side[:, t * 128 : (t + 1) * 128].T.astype(BF16)
        dense_ref[4 * t : 4 * t + 4, :, 256:384] = tile.reshape(4, 32, 128)
    total.sent()
    exchange_sent(dqkv, pieces, psend, precv, place)
    for shard in range(4):
        for half in (0, 1):
            for direction in (0, 1):
                link(direction, shard, half, "sent")


class Ring:
    def __init__(self, n, pos, direction, own, slots, device, send, recv, rows):
        self.n, self.pos, self.direction, self.own, self.slots = n, pos, direction, own, slots
        self.device, self.send, self.recv, self.rows = device, send, recv, rows

    def chunk(self, s):
        if self.direction > 0:
            return (self.pos + 2 * self.n - 1 - s) % self.n
        return (self.pos + 1 + s) % self.n

    def copy(self, s):
        src = self.own(self.chunk(0)) if s == 0 else self.slots.at[s - 1]
        return remote(src, self.slots.at[s], self.send.at[s], self.recv.at[s], self.device)

    def add(self, s):
        own = self.own(self.chunk(s))
        held = self.slots.at[s - 1]

        def one(i, carry):
            index = self.rows(i)
            held[index] = (held[index].astype(F32) + own[index].astype(F32)).astype(BF16)
            return carry

        lax.fori_loop(0, self.count(), one, 0)

    def count(self):
        c = 1
        for size in self.slots.shape[1:-2]:
            c *= size
        return c

    def step(self, s):
        if s > 0:
            self.copy(s - 1).wait_recv()
            self.add(s)
        self.copy(s).start()

    def sent(self):
        for s in range(self.n - 1):
            self.copy(s).wait_send()


def sums_kernel(
    gw_ref, dense_ref,
    gin_ref, gout_ref, gq_ref, gk_ref, gv_ref, gside_ref, gproj_ref,
    xa, za, zb, xb, xd, zd, ra, rb, rd, fin, rq, rp,
    xas, xar, zas, zar, zbs, zbr, xbs, xbr, xds, xdr, zds, zdr, fsend, frecv, hsend, hrecv,
):
    dp, ep, ctx = where_am_i()
    zh, x = dp // 4, dp % 4
    z = zh * 4 + ctx

    def at_x(v):
        return (zh * 4 + v % 4, ep, ctx)

    def at_z(v):
        v = v % 8
        return ((v // 4) * 4 + x, ep, v % 4)

    x_up, x_dn = at_x(x + 1), at_x(x + 3)
    z_up, z_dn = at_z(z + 1), at_z(z + 7)

    def send_to(g, h):
        return (dp, 2 * ctx + g // 2, 2 * (g % 2) + h), (ep, 2 * ctx + g // 2, 2 * (g % 2) + h)

    def is_me(device):
        return (device[0] == dp) & (device[1] == ep) & (device[2] == ctx)

    barrier = pltpu.get_barrier_semaphore()
    for device in (x_up, x_dn, z_up, z_dn):
        greet(barrier, device)
    for i in range(8):
        for device in ((dp, i, ep // 2), (i, dp, ep // 2)):

            @pl.when(jnp.logical_not(is_me(device)))
            def _():
                greet(barrier, device)

    waits = 4
    for g in range(4):
        for h in range(2):
            for device in send_to(g, h):
                waits = waits + jnp.where(is_me(device), 0, 1)
    pl.semaphore_wait(barrier, waits)

    x4 = lambda i: (i // 4, i % 4)
    z4 = lambda i: (i,)
    one = lambda i: ()

    def x_first(ref, result, slots_x, slots_z, up, sems):
        direction = 1 if up else -1
        ring_x = Ring(4, x, direction, lambda t: ref.at[:, t], slots_x, x_up if up else x_dn, sems[0], sems[1], x4)
        ring_z = Ring(8, z, direction, lambda t: result.at[t // 4, t % 4], slots_z, z_up if up else z_dn, sems[2], sems[3], one)
        return ring_x, ring_z

    def z_first(ref, result, slots_z, slots_x, up, sems):
        direction = 1 if up else -1
        ring_z = Ring(8, z, direction, lambda t: ref.at[t // 4, :, t % 4], slots_z, z_up if up else z_dn, sems[0], sems[1], z4)
        ring_x = Ring(4, x, direction, lambda t: result.at[t], slots_x, x_up if up else x_dn, sems[2], sems[3], one)
        return ring_z, ring_x

    def settle(ring, result):
        last = ring.n - 2
        ring.copy(last).wait_recv()
        own = ring.own(ring.pos)

        def each(i, carry):
            index = ring.rows(i)
            result[index] = (ring.slots.at[last][index].astype(F32) + own[index].astype(F32)).astype(BF16)
            return carry

        lax.fori_loop(0, ring.count(), each, 0)

    def finish(ring):
        last = ring.n - 2
        ring.copy(last).wait_recv()
        return ring.slots[last].astype(F32) + ring.own(ring.pos)[...].astype(F32)

    a, b, dn = [], [], []
    for i in range(2):
        a.append(x_first(gw_ref.at[i], ra.at[i], xa.at[i], za.at[i], i == 0, (xas.at[i], xar.at[i], zas.at[i], zar.at[i])))
        b.append(z_first(gw_ref.at[2 + i], rb.at[i], zb.at[i], xb.at[i], i == 0, (zbs.at[i], zbr.at[i], xbs.at[i], xbr.at[i])))
        half = dense_ref.at[:, :, :, pl.ds(16 * i, 16)]
        dn.append(x_first(half, rd.at[i], xd.at[i], zd.at[i], i == 0, (xds.at[i], xdr.at[i], zds.at[i], zdr.at[i])))

    def both(rings, which, s):
        for i in range(2):
            rings[i][which].step(s)

    both(dn, 0, 0)
    both(a, 0, 0)
    both(b, 0, 0)
    both(dn, 0, 1)
    both(dn, 0, 2)
    both(b, 0, 1)
    for i in range(2):
        settle(dn[i][0], rd.at[i])
    both(dn, 1, 0)
    both(a, 0, 1)
    both(b, 0, 2)
    both(dn, 1, 1)
    both(b, 0, 3)
    both(dn, 1, 2)
    both(a, 0, 2)
    both(dn, 1, 3)
    both(b, 0, 4)
    both(dn, 1, 4)
    both(b, 0, 5)
    both(dn, 1, 5)
    both(b, 0, 6)
    both(dn, 1, 6)

    for i in range(2):
        done = finish(dn[i][1])
        fin[2 * i] = done[0:8]
        fin[2 * i + 1] = done[8:16]

    def piece(g, h, kind, device):
        index = g * 2 + h
        if kind == 0:
            return remote(fin.at[g, :, pl.ds(0, 384)], rq.at[ep], fsend.at[index], frecv.at[ep], device)
        return remote(fin.at[g, :, pl.ds(384, 128)], rp.at[dp], hsend.at[index], hrecv.at[dp], device)

    def each_piece(act, own):
        for g in range(4):
            for h in range(2):
                for kind in (0, 1):
                    device = send_to(g, h)[kind]

                    @pl.when(jnp.logical_not(is_me(device)))
                    def _():
                        act(piece(g, h, kind, device))

                    if own:

                        @pl.when(is_me(device))
                        def _():
                            if kind == 0:
                                rq[ep] = fin[g, :, 0:384]
                            else:
                                rp[dp] = fin[g, :, 384:512]

    each_piece(lambda c: c.start(), True)

    for i in range(2):
        settle(a[i][0], ra.at[i])
    both(a, 1, 0)
    for i in range(2):
        settle(b[i][0], rb.at[i])
    both(b, 1, 0)
    both(a, 1, 1)
    both(b, 1, 1)
    both(a, 1, 2)
    both(b, 1, 2)
    both(a, 1, 3)
    for i in range(2):
        done = finish(b[i][1])
        gin_ref[2 + i] = done[0:32]
        gout_ref[2 + i] = done[32:48]
    both(a, 1, 4)
    both(a, 1, 5)
    both(a, 1, 6)

    for i in range(8):
        for kind, device in enumerate(((dp, i, ep // 2), (i, dp, ep // 2))):

            @pl.when(jnp.logical_not(is_me(device)))
            def _():
                if kind == 0:
                    src, dst, sems = fin.at[0, :, pl.ds(0, 384)], rq.at[i], (fsend.at[0], frecv.at[i])
                else:
                    src, dst, sems = fin.at[0, :, pl.ds(384, 128)], rp.at[i], (hsend.at[0], hrecv.at[i])
                remote(src, dst, sems[0], sems[1], device).wait_recv()

    odd = ctx % 2 == 1

    def mine(v):
        return jnp.where(odd, v[4:8], v[0:4])

    gq_ref[...] = mine(jnp.concatenate([rq[i, :, 0:128] for i in range(8)], axis=1))
    gk_ref[...] = mine(jnp.concatenate([rq[i, :, 128:192] for i in range(8)], axis=1))
    gv_ref[...] = mine(jnp.concatenate([rq[i, :, 192:256] for i in range(8)], axis=1))
    side = rq[0, :, 256:384]
    for i in range(1, 8):
        side = side + rq[i, :, 256:384]
    gside_ref[...] = mine(side)
    gproj_ref[...] = mine(jnp.concatenate([rp[i] for i in range(8)], axis=1))

    for i in range(2):
        done = finish(a[i][1])
        gin_ref[i] = done[0:32]
        gout_ref[i] = done[32:48]
    for i in range(2):
        for rings in (a, b, dn):
            rings[i][0].sent()
            rings[i][1].sent()
    each_piece(lambda c: c.wait_send(), False)


def call(kernel, outs, scratch, args, name, collective=None, **more):
    params = dict(vmem_limit_bytes=VMEM_LIMIT)
    if collective is not None:
        params.update(collective_id=collective, has_side_effects=True)
    space = pl.BlockSpec(memory_space=pltpu.VMEM)
    return pl.pallas_call(
        kernel,
        out_shape=[jax.ShapeDtypeStruct(shape, kind) for shape, kind in outs],
        in_specs=more.pop("in_specs", [space] * len(args)),
        out_specs=more.pop("out_specs", [space] * len(outs)),
        scratch_shapes=scratch,
        compiler_params=pltpu.CompilerParams(**params),
        name=name,
        **more,
    )(*args)


def sems(*sizes):
    return [pltpu.SemaphoreType.DMA(s if isinstance(s, tuple) else (s,)) for s in sizes]


def body(
    layer_input, gain_attn, w_query, w_key, w_value, w_proj, gain_ffn, w_router,
    w_expert_in, w_expert_out, segment_ids, expert_ids, slot_order, out_grad,
):
    ep = lax.axis_index("ep")
    gain_one, gain_two = gain_attn.reshape(1, 1024), gain_ffn.reshape(1, 1024)
    tables = [jnp.asarray(t) for t in rope_tables()]
    w_own = jnp.concatenate(
        [
            lax.dynamic_slice_in_dim(w_query, ep * 128, 128, 1),
            lax.dynamic_slice_in_dim(w_key, ep * 64, 64, 1),
            lax.dynamic_slice_in_dim(w_value, ep * 64, 64, 1),
        ],
        axis=1,
    )
    wr_rows = jnp.pad(w_router.T.reshape(8, 4, 1024), ((0, 0), (0, 4), (0, 0))).reshape(64, 1024)
    w_proj_own = lax.dynamic_slice_in_dim(w_proj, ep * 128, 128, 0)
    order = slot_order.reshape(TOK, 8)
    docs = segment_ids.reshape(32, 128)

    normed_all, query, kv, grad_all, slots, chosen, starts = call(
        first_kernel,
        [
            ((8, TOK, 1024), BF16), ((8, TOK, 128), BF16), ((8, 4, TOK, 128), BF16), ((8, TOK, 1024), BF16),
            ((8, 8, TOK), F32), ((64, TOK), F32), ((32, 128), F32),
        ],
        [pltpu.VMEM((8, 8, TOK), F32)] + sems(13, 13, 13, 13, 8, 8, 24, 24),
        [layer_input, gain_one, out_grad, w_own, *tables, expert_ids, expert_ids.T, order, order.T, docs],
        "first", 1,
    )
    kv_rows = kv.reshape(4096, 128)
    ctx = lax.axis_index("ctx")
    first = lax.dynamic_slice_in_dim(starts.reshape(8, 4, 128), ctx, 1, 1)[:, 0, 0].astype(jnp.int32) // CHUNK

    vm, sm = pl.BlockSpec(memory_space=pltpu.VMEM), pl.BlockSpec(memory_space=pltpu.SMEM)
    attended, attended_tall, log_sums = call(
        attend_kernel,
        [((8, TOK, 128), BF16), ((8, 128, TOK), F32), ((8, 8, 256), F32)],
        [pltpu.VMEM((128, 4096), BF16)],
        [first, query, kv_rows, starts],
        "attend", in_specs=[sm, vm, vm, vm],
    )
    residual, ffn_all, gates_in, gates = call(
        middle_kernel,
        [((TOK, 1024), F32), ((8, TOK, 1024), BF16), ((8, 8, TOK), F32), ((64, TOK), F32)],
        [pltpu.VMEM((8, TOK, 128), BF16), pltpu.VMEM((8, 8, TOK), F32)] + sems(8, 8, 13, 13, 8, 8),
        [attended, layer_input, gain_two, w_proj, wr_rows, chosen],
        "middle", 2,
    )
    whole = lambda *shape: pl.BlockSpec(shape, lambda j: (0,) * len(shape))
    sums, back, grad_gates, grad_experts = call(
        expert_kernel,
        [((8, TOK, 1024), BF16), ((8, TOK, 1024), BF16), ((8, 8, TOK), F32), ((4, 32, 48, 1024), BF16)],
        [pltpu.VMEM((4, 8 * CAP, 1024), F32), pltpu.VMEM((4, 8 * CAP, 1024), F32)],
        [ffn_all, grad_all, slots, gates_in, w_expert_in, w_expert_out],
        "experts", grid=(4,),
        in_specs=[
            whole(8, TOK, 1024), whole(8, TOK, 1024), whole(8, 8, TOK), whole(8, 8, TOK),
            pl.BlockSpec((1, 1024, 1024), lambda j: (j, 0, 0)), pl.BlockSpec((1, 512, 1024), lambda j: (j, 0, 0)),
        ],
        out_specs=[
            whole(8, TOK, 1024), whole(8, TOK, 1024), whole(8, 8, TOK),
            pl.BlockSpec((1, 32, 48, 1024), lambda j: (j, 0, 0, 0)),
        ],
    )
    own_ffn = lax.dynamic_index_in_dim(ffn_all, ep, 0, False)
    grad_mixed, grad_res, grad_router, grad_gain_two = call(
        turn_kernel,
        [((8, TOK, 1024), BF16), ((TOK, 1024), F32), ((64, 1024), F32), ((8, 1024), F32)],
        [pltpu.VMEM((8, 8, TOK), F32)] + scatter_sum_scratch() + sems(8, 8, 13, 13),
        [back, grad_gates, gates, residual, own_ffn, out_grad, gain_two, wr_rows],
        "turn", 3,
    )
    grad_q, grad_kv, grad_proj = call(
        attend_back_kernel,
        [((8, TOK, 128), BF16), ((4096, 128), BF16), ((128, 1024), F32)],
        [pltpu.VMEM((HD, 4096), BF16), pltpu.VMEM((4096, 128), F32)],
        [first, query, kv_rows, starts, attended_tall, log_sums, grad_mixed, w_proj_own, *tables],
        "attend_back", in_specs=[sm] + [vm] * 11,
    )
    layer_output, input_grad, dense = call(
        final_kernel,
        [((TOK, 1024), BF16), ((TOK, 1024), BF16), ((32, 32, 512), BF16)],
        [pltpu.VMEM((2, 4, 8, TOK, 128), BF16), pltpu.VMEM((8, TOK, 256), BF16), pltpu.VMEM((8, TOK, 256), BF16)]
        + scatter_sum_scratch() + sems(16, 16, 8, 8),
        [
            grad_q, grad_kv.reshape(8, 4, TOK, 128), sums, residual, layer_input, gain_one, normed_all,
            w_query, w_key, w_value, grad_res, *tables, grad_router, grad_gain_two, grad_proj,
        ],
        "final", 4,
    )
    grad_in, grad_out, out_q, out_k, out_v, side, out_proj = call(
        sums_kernel,
        [
            ((4, 32, 1024), F32), ((4, 16, 1024), F32), ((4, 1024), F32), ((4, 512), F32), ((4, 512), F32),
            ((4, 128), F32), ((4, 1024), F32),
        ],
        [
            pltpu.VMEM((2, 3, 2, 4, 48, 1024), BF16), pltpu.VMEM((2, 7, 48, 1024), BF16),
            pltpu.VMEM((2, 7, 4, 48, 1024), BF16), pltpu.VMEM((2, 3, 48, 1024), BF16),
            pltpu.VMEM((2, 3, 2, 4, 16, 512), BF16), pltpu.VMEM((2, 7, 16, 512), BF16),
            pltpu.VMEM((2, 2, 4, 48, 1024), BF16), pltpu.VMEM((2, 4, 48, 1024), BF16),
            pltpu.VMEM((2, 2, 4, 16, 512), BF16),
            pltpu.VMEM((4, 8, 512), F32), pltpu.VMEM((8, 8, 384), F32), pltpu.VMEM((8, 8, 128), F32),
        ]
        + sems((2, 3), (2, 3), (2, 7), (2, 7), (2, 7), (2, 7), (2, 3), (2, 3), (2, 3), (2, 3), (2, 7), (2, 7), 8, 8, 8, 8),
        [grad_experts.reshape(4, 2, 4, 4, 48, 1024), dense.reshape(2, 4, 4, 32, 512)],
        "sums", 5,
    )
    router = side[:, :64].reshape(4, 8, 8)[:, :, :4].reshape(4, 32)
    return (
        layer_output, input_grad, side[:, 64], out_q, out_k, out_v, out_proj, side[:, 72], router, grad_in, grad_out,
    )


def solution(mesh):
    tokens = P(("dp", "ep", "ctx"), None)
    in_specs = (
        tokens, P(), P(), P(), P(), P(), P(), P(),
        P("ep", None, None), P("ep", None, None), P("dp", None), tokens, tokens, tokens,
    )
    out_specs = (
        tokens, tokens, P(("dp", "ep", "ctx")), tokens, tokens, tokens, tokens, P(("dp", "ep", "ctx")), tokens,
        P("ep", ("dp", "ctx"), None), P("ep", ("dp", "ctx"), None),
    )
    return jax.shard_map(body, mesh=mesh, in_specs=in_specs, out_specs=out_specs, check_vma=False)
```

```python
from functools import partial

import jax
import jax.numpy as jnp
import numpy as np
from jax import lax
from jax.experimental import pallas as pl
from jax.experimental.pallas import tpu as pltpu
from jax.sharding import PartitionSpec as P

HD = 64
EPSILON = 1e-06
MASKED = -1e30
CAP = 40
TOK = 128
BIG = 4096.0
MESH = pl.DeviceIdType.MESH
F32 = jnp.float32
BF16 = jnp.bfloat16
VMEM_LIMIT = 60 * 1024 * 1024

NT = (((1,), (1,)), ((), ()))
NN = (((1,), (0,)), ((), ()))
TN = (((0,), (0,)), ((), ()))


def mm(a, b, dims=NN):
    return lax.dot_general(a, b, dims, preferred_element_type=F32)


def mm3(a, b, dims=NN):
    high = a.astype(BF16)
    low = (a - high.astype(F32)).astype(BF16)
    return mm(high, b, dims) + mm(low, b, dims)


def where_am_i():
    dp, ep, ctx = lax.axis_index("dp"), lax.axis_index("ep"), lax.axis_index("ctx")
    return dp, ep, ctx


def remote(src, dst, send, recv, device):
    return pltpu.make_async_remote_copy(
        src_ref=src, dst_ref=dst, send_sem=send, recv_sem=recv, device_id=device, device_id_type=MESH
    )


def greet(barrier, device):
    pl.semaphore_signal(barrier, inc=1, device_id=device, device_id_type=MESH)


def rotate_half(values):
    lane = lax.broadcasted_iota(jnp.int32, values.shape, 1)
    return jnp.where(lane % HD < HD // 2, pltpu.roll(values, 96, 1), pltpu.roll(values, 32, 1))


def rope_block(block, ca_ref, sa_ref, cb_ref, sb_ref):
    ca, sa = ca_ref[pl.ds(block, 1), :], sa_ref[pl.ds(block, 1), :]
    cb, sb = cb_ref[...], sb_ref[...]
    cosine = ca * cb - sa * sb
    sine = sa * cb + ca * sb
    lane = lax.broadcasted_iota(jnp.int32, cosine.shape, 1)
    return cosine, jnp.where(lane % HD < HD // 2, -sine, sine)


def rope_tables():
    frequency = 10000.0 ** (-np.arange(HD // 2, dtype=np.float64) * 2.0 / HD)
    frequency = np.tile(frequency.astype(np.float32).astype(np.float64), 4)
    blocks = np.arange(32, dtype=np.float64)[:, None] * 128.0 * frequency[None, :]
    rows = np.arange(128, dtype=np.float64)[:, None] * frequency[None, :]
    return [t.astype(np.float32) for t in (np.cos(blocks), np.sin(blocks), np.cos(rows), np.sin(rows))]


class EpGather:
    COUNT = 13

    def __init__(self, ref, send, recv, place):
        self.ref, self.send, self.recv = ref, send, recv
        dp, ep, ctx = place
        y, k = ep // 2, ep % 2
        self.up = (dp, ((y + 1) % 4) * 2 + k, ctx)
        self.dn = (dp, ((y + 3) % 4) * 2 + k, ctx)
        self.sib = (dp, y * 2 + 1 - k, ctx)

        def at(dy, other):
            return ((y + dy) % 4) * 2 + ((1 - k) if other else k)

        u, s, d = self.up, self.sib, self.dn
        self.sends = [
            (at(0, 0), None, s), (at(0, 0), 0, u), (at(0, 0), 1, u), (at(0, 0), 1, d), (at(0, 0), 0, d),
            (at(3, 0), 0, u), (at(3, 0), 0, s), (at(1, 0), 1, d), (at(1, 0), 1, s),
            (at(3, 0), 1, s), (at(1, 0), 0, s), (at(2, 0), 0, s), (at(2, 0), 1, s),
        ]
        self.gets = [
            (at(0, 1), None), (at(3, 0), 0), (at(3, 0), 1), (at(1, 0), 1), (at(1, 0), 0),
            (at(2, 0), 0), (at(3, 1), 0), (at(2, 0), 1), (at(1, 1), 1),
            (at(3, 1), 1), (at(1, 1), 0), (at(2, 1), 0), (at(2, 1), 1),
        ]

    def view(self, block, half):
        if half is None:
            return self.ref.at[block]
        rows = self.ref.shape[1] // 2
        return self.ref.at[block, pl.ds(half * rows, rows)]

    def go(self, *which):
        for i in which:
            block, half, device = self.sends[i]
            v = self.view(block, half)
            remote(v, v, self.send.at[i], self.recv.at[i], device).start()

    def got(self, *which):
        for i in which:
            v = self.view(*self.gets[i])
            remote(v, v, self.send.at[i], self.recv.at[i], self.sends[i][2]).wait_recv()

    def sent(self):
        for i in range(self.COUNT):
            block, half, device = self.sends[i]
            v = self.view(block, half)
            remote(v, v, self.send.at[i], self.recv.at[i], device).wait_send()

    def whole(self):
        self.got(1)
        self.go(5, 6)
        self.got(3)
        self.go(7, 8)
        self.got(2)
        self.go(9)
        self.got(4)
        self.go(10)
        self.got(5)
        self.go(11)
        self.got(7)
        self.go(12)
        self.got(0, 6, 8, 9, 10, 11, 12)


class EpScatterSum:
    COUNT = 8

    def __init__(self, part, cbuf, fbuf, gbuf, send, recv, place):
        self.part, self.cbuf, self.fbuf, self.gbuf = part, cbuf, fbuf, gbuf
        self.send, self.recv = send, recv
        dp, ep, ctx = place
        self.y, self.k = ep // 2, ep % 2
        y, k = self.y, self.k
        self.up = (dp, ((y + 1) % 4) * 2 + k, ctx)
        self.dn = (dp, ((y + 3) % 4) * 2 + k, ctx)
        self.sib = (dp, y * 2 + 1 - k, ctx)

    def block(self, dy, other=False):
        return ((self.y + dy) % 4) * 2 + ((1 - self.k) if other else self.k)

    def copy(self, i):
        half = self.cbuf.shape[1] // 2
        lo, hi = pl.ds(0, half), pl.ds(half, half)
        s, r = self.send, self.recv
        if i < 4:
            away = self.block((2, 1, 3, 0)[i], True)
            return remote(self.part.at[away], self.cbuf.at[i], s.at[i], r.at[i], self.sib)
        src, dst, device = (
            (self.cbuf.at[0, lo], self.fbuf.at[0], self.up),
            (self.cbuf.at[0, hi], self.fbuf.at[1], self.dn),
            (self.cbuf.at[1], self.gbuf.at[0], self.up),
            (self.cbuf.at[2], self.gbuf.at[1], self.dn),
        )[i - 4]
        return remote(src, dst, s.at[i], r.at[i], device)

    def start(self):
        for i in range(4):
            self.copy(i).start()

    def far(self):
        self.copy(0).wait_recv()
        self.cbuf[0] = (self.cbuf[0].astype(F32) + self.part[self.block(2)].astype(F32)).astype(BF16)
        self.copy(4).start()
        self.copy(5).start()

    def near(self):
        half = self.cbuf.shape[1] // 2
        for slot, dy, far, rows, rest in ((1, 1, 0, pl.ds(0, half), pl.ds(half, half)), (2, 3, 1, pl.ds(half, half), pl.ds(0, half))):
            b = self.block(dy)
            self.copy(slot).wait_recv()
            self.copy(4 + far).wait_recv()
            self.cbuf[slot, rows] = (
                self.cbuf[slot, rows].astype(F32) + self.part[b, rows].astype(F32) + self.fbuf[far].astype(F32)
            ).astype(BF16)
            self.cbuf[slot, rest] = (self.cbuf[slot, rest].astype(F32) + self.part[b, rest].astype(F32)).astype(BF16)
            self.copy(6 + far).start()

    def last(self):
        for i in (3, 6, 7):
            self.copy(i).wait_recv()
        return (
            self.part[self.block(0)].astype(F32) + self.cbuf[3].astype(F32)
            + self.gbuf[0].astype(F32) + self.gbuf[1].astype(F32)
        )

    def sent(self):
        for i in range(self.COUNT):
            self.copy(i).wait_send()


def scatter_sum_scratch():
    return [
        pltpu.VMEM((4, TOK, 1024), BF16),
        pltpu.VMEM((2, TOK // 2, 1024), BF16),
        pltpu.VMEM((2, TOK, 1024), BF16),
        pltpu.SemaphoreType.DMA((8,)),
        pltpu.SemaphoreType.DMA((8,)),
    ]


def exchange(src, dst, send, recv, place, wait):
    dp, ep, ctx = place
    for r in range(1, 8):
        to, source = (ep + r) % 8, (ep + 8 - r) % 8
        if not wait:
            remote(src.at[to], dst.at[ep], send.at[r], recv.at[r], (dp, to, ctx)).start()
        else:
            remote(src.at[to], dst.at[source], send.at[r], recv.at[r], (dp, to, ctx)).wait_recv()


def exchange_sent(src, dst, send, recv, place):
    dp, ep, ctx = place
    for r in range(1, 8):
        to = (ep + r) % 8
        remote(src.at[to], dst.at[ep], send.at[r], recv.at[r], (dp, to, ctx)).wait_send()


def starts_of(docs):
    rows = lax.broadcasted_iota(jnp.int32, docs.shape, 0)
    lane = lax.broadcasted_iota(jnp.int32, docs.shape, 1)
    docs = docs.astype(F32)
    turned = pltpu.roll(docs, 1, 1)
    before = jnp.where(lane == 0, pltpu.roll(turned, 1, 0), turned)
    place = rows * 128 + lane
    fresh = (docs != before) | (place == 0)
    value = jnp.where(fresh, place.astype(F32), 0.0)
    for shift in (1, 2, 4, 8, 16, 32, 64):
        value = jnp.maximum(value, jnp.where(lane >= shift, pltpu.roll(value, shift, 1), 0.0))
    carry = jnp.broadcast_to(jnp.max(value, axis=1, keepdims=True), value.shape)
    for shift in (1, 2, 4, 8, 16):
        carry = jnp.maximum(carry, jnp.where(rows >= shift, pltpu.roll(carry, shift, 0), 0.0))
    above = jnp.where(rows >= 1, pltpu.roll(carry, 1, 0), 0.0)
    return jnp.maximum(value, above)


def slots_of(eid_ref, eidT_ref, so_ref, soT_ref, slot_scr, sel_ref):
    def expert(index):
        return jnp.where(index % 8 < 4, (index // 8) * 4 + index % 8, -1)

    row_expert = expert(lax.broadcasted_iota(jnp.int32, (64, TOK), 0))
    lane_expert = expert(lax.broadcasted_iota(jnp.int32, (TOK, 64), 1))
    by_row = jnp.full((64, TOK), BIG, F32)
    by_lane = jnp.full((TOK, 64), BIG, F32)
    for k in range(8):
        by_row = jnp.where(eidT_ref[k : k + 1, :] == row_expert, soT_ref[k : k + 1, :].astype(F32), by_row)
        by_lane = jnp.where(eid_ref[:, k : k + 1] == lane_expert, so_ref[:, k : k + 1].astype(F32), by_lane)
    sel_ref[...] = jnp.where(by_row < BIG, 1.0, 0.0)
    for g in range(8):
        for j in range(4):
            r = 8 * g + j
            row = by_row[r : r + 1, :]
            less = jnp.where(by_lane[:, r : r + 1] < row, 1.0, 0.0)
            rank = jnp.sum(less, axis=0, keepdims=True)
            slot_scr[g, j : j + 1, :] = jnp.where((row < BIG) & (rank < CAP), rank, -1.0)
        slot_scr[g, 4:8, :] = jnp.full((4, TOK), -1.0, F32)


def first_kernel(
    x_ref, gain_ref, og_ref, w_ref, ca_ref, sa_ref, cb_ref, sb_ref, eid_ref, eidT_ref, so_ref, soT_ref, doc_ref,
    nall_ref, q_ref, kv_ref, ogall_ref, slot_ref, sel_ref, start_ref,
    slot_scr, nsend, nrecv, osend, orecv, ssend, srecv, ksend, krecv,
):
    place = where_am_i()
    dp, ep, ctx = place
    y = ep // 2
    barrier = pltpu.get_barrier_semaphore()
    for r in range(1, 8):
        greet(barrier, (dp, (ep + r) % 8, ctx))

    @pl.when(ctx > 0)
    def _():
        greet(barrier, (dp, ep, ctx - 1))

    @pl.when(ctx < 3)
    def _():
        greet(barrier, (dp, ep, ctx + 1))

    x = x_ref[...].astype(F32)
    normed = x * lax.rsqrt(jnp.mean(x * x, axis=-1, keepdims=True) + EPSILON) * gain_ref[...]
    nall_ref[ep] = normed.astype(BF16)
    ogall_ref[ep] = og_ref[...]
    edges = jnp.where(ctx > 0, 1, 0) + jnp.where(ctx < 3, 1, 0)
    pl.semaphore_wait(barrier, 7 + edges)

    gather = EpGather(nall_ref, nsend, nrecv, place)
    grads = EpGather(ogall_ref, osend, orecv, place)
    gather.go(0, 1, 3, 2, 4)

    start_ref[...] = starts_of(doc_ref[...])
    slots_of(eid_ref, eidT_ref, so_ref, soT_ref, slot_scr, sel_ref)
    slot_ref[ep] = slot_scr[ep]
    exchange(slot_scr, slot_ref, ssend, srecv, place, False)

    lane = lax.broadcasted_iota(jnp.int32, (TOK, 128), 1)

    def project(dy):
        chip = (y + dy) % 4
        rows = jnp.concatenate([nall_ref[2 * chip], nall_ref[2 * chip + 1]], axis=0)
        out = mm(rows, w_ref[...])
        for i in range(2):
            b = 2 * chip + i
            cosine, sine = rope_block(4 * b + ctx, ca_ref, sa_ref, cb_ref, sb_ref)
            q = out[i * TOK : (i + 1) * TOK, :128]
            kv = out[i * TOK : (i + 1) * TOK, 128:]
            q_rot = (q * cosine + rotate_half(q) * sine).astype(BF16)
            q_ref[b] = (q_rot.astype(F32) * (HD**-0.5)).astype(BF16)
            cosine = jnp.where(lane < HD, cosine, 1.0)
            sine = jnp.where(lane < HD, sine, 0.0)
            kv_ref[b, ctx] = (kv * cosine + rotate_half(kv) * sine).astype(BF16)

    offsets = (0, 3, 1, 2)

    def hop(direction, h, g, action):
        chip = (y + offsets[g]) % 4
        back = h - 1
        own = ctx - back if direction == 0 else ctx + back
        come = ctx - h if direction == 0 else ctx + h
        to = ctx + 1 if direction == 0 else ctx - 1
        index = (direction * 3 + back) * 4 + g
        send, recv = ksend.at[index], krecv.at[index]
        if action == "recv":
            ok = come >= 0 if direction == 0 else come <= 3

            @pl.when(ok)
            def _():
                v = kv_ref.at[pl.ds(2 * chip, 2), come]
                remote(v, v, send, recv, (dp, ep, ctx)).wait_recv()

        else:
            ok = (own >= 0) & (ctx < 3) if direction == 0 else (own <= 3) & (ctx > 0)

            @pl.when(ok)
            def _():
                v = kv_ref.at[pl.ds(2 * chip, 2), own]
                c = remote(v, v, send, recv, (dp, ep, to))
                c.start() if action == "send" else c.wait_send()

    def hops(h, g):
        for direction in (0, 1):
            if h > 1:
                hop(direction, h - 1, g, "recv")
            hop(direction, h, g, "send")

    gather.got(0)
    project(0)
    hops(1, 0)
    gather.got(1)
    gather.go(5, 6)
    gather.got(3)
    gather.go(7, 8)
    gather.got(2)
    gather.go(9)
    gather.got(4)
    gather.go(10)
    grads.go(0, 1, 3, 2, 4)
    gather.got(6, 9)
    project(3)
    hops(1, 1)
    hops(2, 0)
    gather.got(8, 10)
    project(1)
    hops(1, 2)
    hops(2, 1)
    hops(3, 0)
    gather.got(5)
    gather.go(11)
    gather.got(7)
    gather.go(12)
    gather.got(11, 12)
    project(2)
    hops(1, 3)
    hops(2, 2)
    hops(3, 1)
    hops(2, 3)
    hops(3, 2)
    grads.whole()
    hops(3, 3)
    for g in range(4):
        for direction in (0, 1):
            hop(direction, 3, g, "recv")
    exchange(slot_scr, slot_ref, ssend, srecv, place, True)
    gather.sent()
    grads.sent()
    exchange_sent(slot_scr, slot_ref, ssend, srecv, place)
    for g in range(4):
        for h in (1, 2, 3):
            for direction in (0, 1):
                hop(direction, h, g, "sent")


CHUNK = 512


def key_mask(chunk, start_row, place_row):
    keys = (lax.broadcasted_iota(jnp.int32, (CHUNK, 256), 0) + chunk * CHUNK).astype(F32)
    return (keys >= start_row) & (keys <= place_row)


def query_rows(j, ctx, start_ref):
    block = 4 * j + ctx
    start = start_ref[pl.ds(block, 1), :]
    places = (lax.broadcasted_iota(jnp.int32, (1, 128), 1) + block * 128).astype(F32)
    return jnp.concatenate([start, start], axis=1), jnp.concatenate([places, places], axis=1)


def turned(block):
    return block.astype(F32).T.astype(BF16)


def heads_wide(tall):
    return jnp.concatenate([tall[:HD], tall[HD:]], axis=1)


def attend_kernel(first_ref, q_ref, kv_ref, start_ref, att_ref, attT_ref, lse_ref, kvT):
    ctx = lax.axis_index("ctx")

    for chunk in range(8):
        part = kv_ref[chunk * CHUNK : (chunk + 1) * CHUNK, :].astype(F32).T
        row = lax.broadcasted_iota(jnp.int32, part.shape, 0)
        kvT[:, chunk * CHUNK : (chunk + 1) * CHUNK] = jnp.where(row < HD, 1.0, part).astype(BF16)

    for j in range(8):
        start_row, place_row = query_rows(j, ctx, start_ref)
        wide = heads_wide(turned(q_ref[j]))
        q_pad = jnp.concatenate([wide, jnp.zeros_like(wide)], axis=0)

        def step(chunk, carry):
            top, total = carry
            rows = pl.ds(pl.multiple_of(chunk * CHUNK, CHUNK), CHUNK)
            scores = mm(kv_ref[rows, :], q_pad)
            scores = jnp.where(key_mask(chunk, start_row, place_row), scores, MASKED)
            new_top = jnp.maximum(top, jnp.max(scores, axis=0, keepdims=True))
            probs = jnp.exp(scores - new_top).astype(BF16)
            total = total * jnp.exp(top - new_top) + mm(kvT[:, rows], probs)
            return new_top, total

        top, total = lax.fori_loop(
            first_ref[j], j + 1, step, (jnp.full((1, 256), MASKED, F32), jnp.zeros((128, 256), F32))
        )
        norm = total[0:1]
        out = total[HD:] / norm
        tall = jnp.concatenate([out[:, :128], out[:, 128:]], axis=0)
        attT_ref[j] = tall
        att_ref[j] = tall.T.astype(BF16)
        lse_ref[j] = jnp.broadcast_to(top + jnp.log(norm), (8, 256))


def attend_back_kernel(
    first_ref, q_ref, kv_ref, start_ref, attT_ref, lse_ref, gm_ref, w_ref, ca_ref, sa_ref, cb_ref, sb_ref,
    dq_ref, dkv_ref, gproj_ref, kT, acc,
):
    ctx = lax.axis_index("ctx")
    for chunk in range(8):
        part = kv_ref[chunk * CHUNK : (chunk + 1) * CHUNK, :].astype(F32).T
        kT[:, chunk * CHUNK : (chunk + 1) * CHUNK] = part[:HD].astype(BF16)
        acc[chunk * CHUNK : (chunk + 1) * CHUNK, :] = jnp.zeros((CHUNK, 128), F32)
    gproj = jnp.zeros((128, 1024), F32)
    for j in range(8):
        gproj = gproj + mm(attT_ref[j].astype(BF16), gm_ref[j])
    gproj_ref[...] = gproj
    zero = jnp.zeros((HD, 256), BF16)
    lane = lax.broadcasted_iota(jnp.int32, (256, 128), 1)
    for j in range(8):
        start_row, place_row = query_rows(j, ctx, start_ref)
        grad_tall = mm(w_ref[...], gm_ref[j], NT).astype(BF16)
        delta = jnp.sum(
            heads_wide(grad_tall.astype(F32)) * heads_wide(attT_ref[j]), axis=0, keepdims=True
        )
        q_blk = q_ref[j]
        q_pad = jnp.concatenate([heads_wide(turned(q_blk)), zero], axis=0)
        g_pad = jnp.concatenate([zero, heads_wide(grad_tall)], axis=0)
        both = jnp.concatenate([q_pad, g_pad], axis=1)
        g_blk = turned(grad_tall)
        q_f, g_f = q_blk.astype(F32), g_blk.astype(F32)
        q_rows = jnp.concatenate([q_f, pltpu.roll(q_f, HD, 1)], axis=0)
        g_rows = jnp.concatenate([pltpu.roll(g_f, HD, 1), g_f], axis=0)
        stack = jnp.concatenate(
            [jnp.where(lane < HD, q_rows, 0.0), jnp.where(lane < HD, 0.0, g_rows)], axis=0
        ).astype(BF16)
        lse = lse_ref[j, 0:1, :]

        def step(chunk, dq):
            rows = pl.ds(pl.multiple_of(chunk * CHUNK, CHUNK), CHUNK)
            pair = mm(kv_ref[rows, :], both)
            scores = jnp.where(key_mask(chunk, start_row, place_row), pair[:, :256], MASKED)
            probs = jnp.exp(scores - lse)
            grad = (probs * (pair[:, 256:] - delta)).astype(BF16)
            acc[rows, :] += mm(jnp.concatenate([grad, probs.astype(BF16)], axis=1), stack)
            return dq + mm(kT[:, rows], grad)

        dq = lax.fori_loop(first_ref[j], j + 1, step, jnp.zeros((HD, 256), F32)) * (HD**-0.5)
        dq = jnp.concatenate([dq[:, :128], dq[:, 128:]], axis=0).T
        cosine, sine = rope_block(4 * j + ctx, ca_ref, sa_ref, cb_ref, sb_ref)
        dq_ref[j] = (dq * cosine - rotate_half(dq) * sine).astype(BF16)
    for chunk in range(8):
        rows = slice(chunk * CHUNK, (chunk + 1) * CHUNK)
        dkv_ref[rows, :] = acc[rows, :].astype(BF16)


def middle_kernel(
    att_ref, x_ref, gain_ref, w_ref, wr_ref, sel_ref,
    res_ref, nf_ref, gin_ref, gates_ref,
    abuf, gscr, asend, arecv, nsend, nrecv, gsend, grecv,
):
    place = where_am_i()
    dp, ep, ctx = place
    barrier = pltpu.get_barrier_semaphore()
    for r in range(1, 8):
        greet(barrier, (dp, (ep + r) % 8, ctx))
    pl.semaphore_wait(barrier, 7)
    exchange(att_ref, abuf, asend, arecv, place, False)
    abuf[ep] = att_ref[ep]
    exchange(att_ref, abuf, asend, arecv, place, True)
    attended = jnp.concatenate([abuf[p] for p in range(8)], axis=1)
    res = x_ref[...].astype(F32) + mm(attended, w_ref[...])
    res_ref[...] = res
    normed = res * lax.rsqrt(jnp.mean(res * res, axis=-1, keepdims=True) + EPSILON) * gain_ref[...]
    normed = normed.astype(BF16)
    nf_ref[ep] = normed
    gather = EpGather(nf_ref, nsend, nrecv, place)
    gather.go(0, 1, 3, 2, 4)
    logits = mm(wr_ref[...], normed, NT)
    chosen = sel_ref[...] > 0.5
    top = jnp.max(jnp.where(chosen, logits, MASKED), axis=0, keepdims=True)
    weight = jnp.where(chosen, jnp.exp(jnp.where(chosen, logits, MASKED) - top), 0.0)
    gates = weight / jnp.sum(weight, axis=0, keepdims=True)
    gates_ref[...] = gates
    for g in range(8):
        gscr[g] = gates[8 * g : 8 * g + 8, :]
    gin_ref[ep] = gscr[ep]
    exchange(gscr, gin_ref, gsend, grecv, place, False)
    gather.whole()
    exchange(gscr, gin_ref, gsend, grecv, place, True)
    gather.sent()
    exchange_sent(gscr, gin_ref, gsend, grecv, place)
    exchange_sent(att_ref, abuf, asend, arecv, place)


def expert_kernel(
    nf_ref, og_ref, slot_ref, gate_ref, win_ref, wout_ref,
    y_ref, d_ref, dg_ref, gw_ref,
    rows_scr, grad_scr,
):
    j = pl.program_id(0)
    slot = lax.broadcasted_iota(jnp.int32, (CAP, TOK), 0).astype(F32)

    def picks(s, e):
        return slot == slot_ref[s, pl.ds(e, 1), :]

    @pl.when(j == 0)
    def _():
        def load(s, carry):
            pick = jnp.concatenate([jnp.where(picks(s, e), 1.0, 0.0) for e in range(4)], axis=0).astype(BF16)
            got = mm(pick, nf_ref[s])
            grad = mm(pick, og_ref[s])
            for e in range(4):
                rows = pl.ds(pl.multiple_of(s * CAP, 8), CAP)
                rows_scr[e, rows, :] = got[e * CAP : (e + 1) * CAP]
                grad_scr[e, rows, :] = grad[e * CAP : (e + 1) * CAP]
            return carry

        lax.fori_loop(0, 8, load, 0)

    gates = jnp.concatenate(
        [jnp.sum(jnp.where(picks(s, j), gate_ref[s, pl.ds(j, 1), :], 0.0), axis=1, keepdims=True) for s in range(8)],
        axis=0,
    )
    received = rows_scr[j].astype(BF16)
    grad_tok = grad_scr[j]
    gate_up = mm(received, win_ref[0])
    gating, up = gate_up[:, :512], gate_up[:, 512:]
    sig = 1.0 / (1.0 + jnp.exp(-gating))
    silu = gating * sig
    act = (silu * up).astype(BF16)
    result = mm(act, wout_ref[0]).astype(BF16).astype(F32)
    dots = jnp.sum(grad_tok * result, axis=1, keepdims=True)
    grad_res = (grad_tok * gates).astype(BF16)
    grad_scr[j] = result * gates
    for s in range(8):
        dg_ref[s, pl.ds(j, 1), :] = jnp.sum(
            jnp.where(picks(s, j), dots[s * CAP : (s + 1) * CAP], 0.0), axis=0, keepdims=True
        )
    gw_ref[2] = mm(act, grad_res, TN).astype(BF16).reshape(32, 16, 1024)
    grad_act = mm(grad_res, wout_ref[0], NT)
    grad_up = (grad_act * silu).astype(BF16)
    grad_gate = (grad_act * up * sig * (1.0 + gating * (1.0 - sig))).astype(BF16)
    grad_gu = jnp.concatenate([grad_gate, grad_up], axis=1)
    grad_in = mm(received, grad_gu, TN).astype(BF16).reshape(32, 32, 1024)
    gw_ref[0] = grad_in[:, 0:16]
    gw_ref[1] = grad_in[:, 16:32]
    rows_scr[j] = mm(grad_gu, win_ref[0], NT)

    @pl.when(j == 3)
    def _():
        def store(s, carry):
            pick = jnp.concatenate([jnp.where(picks(s, e), 1.0, 0.0) for e in range(4)], axis=0).astype(BF16)
            rows = pl.ds(pl.multiple_of(s * CAP, 8), CAP)
            weighted = jnp.concatenate([grad_scr[e, rows, :] for e in range(4)], axis=0).astype(BF16)
            y_ref[s] = mm(pick, weighted, TN).astype(BF16)
            back = jnp.concatenate([rows_scr[e, rows, :] for e in range(4)], axis=0).astype(BF16)
            d_ref[s] = mm(pick, back, TN).astype(BF16)
            dg_ref[s, 4:8, :] = jnp.zeros((4, TOK), F32)
            return carry

        lax.fori_loop(0, 8, store, 0)


def each_slab(lead, work):
    count = 1
    for size in lead:
        count *= size

    def each(i, carry):
        work((i,) if len(lead) == 1 else (i // lead[1], i % lead[1]))
        return carry

    lax.fori_loop(0, count, each, 0)


class Arc:
    def __init__(self, n, pos, own, half, slots, devices, send, recv):
        self.n, self.pos, self.own, self.half, self.slots = n, pos, own, half, slots
        self.devices, self.send, self.recv = devices, send, recv
        self.steps = n // 2

    def chunk(self, way, s):
        reach = self.steps - s + 1
        return (self.pos + reach) % self.n if way == 0 else (self.pos + self.n - reach) % self.n

    def copy(self, way, s):
        dst = self.slots.at[way, s - 1]
        src = self.own(self.chunk(way, s)) if s == 1 else self.slots.at[way, s - 2]
        if s == 1:
            src, dst = self.half(src, way), self.half(dst, way)
        return remote(src, dst, self.send.at[way, s - 1], self.recv.at[way, s - 1], self.devices[way])

    def start(self):
        for way in (0, 1):
            self.copy(way, 1).start()

    def slabs(self, work):
        each_slab(self.slots.shape[2:-2], work)

    def advance(self, s):
        for way in (0, 1):
            self.copy(way, s - 1).wait_recv()
            held, own = self.slots.at[way, s - 2], self.own(self.chunk(way, s))
            if s == 2:
                self.merge(way, held, own)
            else:

                def add(index):
                    held[index] = (held[index].astype(F32) + own[index].astype(F32)).astype(BF16)

                self.slabs(add)
            self.copy(way, s).start()

    def merge(self, way, held, own):
        mine, its = self.half(held, way), self.half(own, way)
        other, from_own = self.half(held, 1 - way), self.half(own, 1 - way)

        def add(index):
            mine[index] = (mine[index].astype(F32) + its[index].astype(F32)).astype(BF16)

        def take(index):
            other[index] = from_own[index]

        each_slab(mine.shape[:-2], add)
        each_slab(other.shape[:-2], take)

    def finish(self, put):
        for way in (0, 1):
            self.copy(way, self.steps).wait_recv()
        own, up, down = self.own(self.pos), self.slots.at[0, self.steps - 1], self.slots.at[1, self.steps - 1]

        def add(index):
            put(index, own[index].astype(F32) + up[index].astype(F32) + down[index].astype(F32))

        self.slabs(add)

    def sent(self):
        for way in (0, 1):
            for s in range(1, self.steps + 1):
                self.copy(way, s).wait_send()


class Torus:
    def __init__(self, place):
        self.dp, self.ep, self.ctx = place
        self.zh, self.x = self.dp // 4, self.dp % 4
        self.z = self.zh * 4 + self.ctx

    def at_x(self, v):
        return (self.zh * 4 + v % 4, self.ep, self.ctx)

    def at_z(self, v):
        v = v % 8
        return ((v // 4) * 4 + self.x, self.ep, v % 4)

    def x_ways(self):
        return self.at_x(self.x + 1), self.at_x(self.x + 3)

    def z_ways(self):
        return self.at_z(self.z + 1), self.at_z(self.z + 7)

    def x_arc(self, own, half, slots, send, recv):
        return Arc(4, self.x, own, half, slots, self.x_ways(), send, recv)

    def z_arc(self, own, half, slots, send, recv):
        return Arc(8, self.z, own, half, slots, self.z_ways(), send, recv)


def first_or_last(sizes):
    def half(view, h):
        return view.at[pl.ds(0, sizes[0])] if h == 0 else view.at[pl.ds(sizes[0], sizes[1])]

    return half


X_TURN, Z_TURN, X_FINAL, Z_FINAL = (0, 1, 2, 3), (9, 10, 11), (4, 5, 6, 7), (8,)


def unit_arcs(torus, own, x_units, z_units, x_slots, z_slots, xs, xr, zs, zr):
    xa = [
        torus.x_arc(
            lambda t, i=i: own.at[i, :, t], first_or_last((1, 1)), x_slots.at[i], xs.at[i], xr.at[i]
        )
        for i in range(len(x_units))
    ]
    za = [
        torus.z_arc(
            lambda t, i=i: own.at[len(x_units) + i, t // 4, :, t % 4], first_or_last((2, 2)), z_slots.at[i], zs.at[i], zr.at[i]
        )
        for i in range(len(z_units))
    ]
    return xa, za


def fetch_units(gw_ref, own, sem, units):
    return [pltpu.make_async_copy(gw_ref.at[u], own.at[i], sem.at[i]) for i, u in enumerate(units)]


def turn_kernel(
    part_ref, dg_ref, gates_ref, res_ref, nf_ref, og_ref, gain_ref, wr_ref, gw_ref,
    gm_ref, gres_ref, grouter_ref, ggain_ref, rx_ref, rz_ref,
    dbuf, cbuf, fbuf, gbuf, csend, crecv, dsend, drecv, gsend, grecv,
    own, x_slots, z_slots, usem, xs, xr, zs, zr,
):
    place = where_am_i()
    dp, ep, ctx = place
    torus = Torus(place)
    fetches = fetch_units(gw_ref, own, usem, X_TURN + Z_TURN)
    for f in fetches:
        f.start()
    barrier = pltpu.get_barrier_semaphore()
    for r in range(1, 8):
        greet(barrier, (dp, (ep + r) % 8, ctx))
    for device in torus.x_ways() + torus.z_ways():
        greet(barrier, device)
    pl.semaphore_wait(barrier, 11)
    total = EpScatterSum(part_ref, cbuf, fbuf, gbuf, csend, crecv, place)
    total.start()
    exchange(dg_ref, dbuf, dsend, drecv, place, False)
    dbuf[ep] = dg_ref[ep]
    xa, za = unit_arcs(torus, own, X_TURN, Z_TURN, x_slots, z_slots, xs, xr, zs, zr)
    for i in range(4):
        fetches[i].wait()
        xa[i].start()
        if i < 3:
            fetches[4 + i].wait()
            za[i].start()
    total.far()
    za[0].advance(2)
    xa[0].advance(2)
    za[1].advance(2)
    total.near()
    xa[1].advance(2)
    za[2].advance(2)
    exchange(dg_ref, dbuf, dsend, drecv, place, True)
    gates = gates_ref[...]
    grad_gates = jnp.concatenate([dbuf[p] for p in range(8)], axis=0)
    grad_logits = gates * (grad_gates - jnp.sum(gates * grad_gates, axis=0, keepdims=True))
    high = grad_logits.astype(BF16)
    low = (grad_logits - high.astype(F32)).astype(BF16)
    to = lax.broadcasted_iota(jnp.int32, (32, 64), 0)
    source = lax.broadcasted_iota(jnp.int32, (32, 64), 1)
    squeeze = jnp.where(source == (to // 4) * 8 + to % 4, 1.0, 0.0).astype(BF16)
    grouter_ref[...] = mm(mm(squeeze, high).astype(BF16), nf_ref[...]) + mm(mm(squeeze, low).astype(BF16), nf_ref[...])
    from_router = mm(high, wr_ref[...], TN) + mm(low, wr_ref[...], TN)
    res = res_ref[...]
    scale = lax.rsqrt(jnp.mean(res * res, axis=-1, keepdims=True) + EPSILON)
    scaled = res * scale
    za[0].advance(3)
    xa[2].advance(2)
    za[1].advance(3)
    grad_normed = total.last() + from_router
    ggain_ref[...] = jnp.broadcast_to(jnp.sum(grad_normed * scaled, axis=0, keepdims=True), (8, 1024))
    grad_normed = grad_normed * gain_ref[...]
    mean = jnp.mean(grad_normed * scaled, axis=-1, keepdims=True)
    gres = og_ref[...].astype(F32) + scale * (grad_normed - scaled * mean)
    gm_ref[ep] = gres.astype(BF16)
    gather = EpGather(gm_ref, gsend, grecv, place)
    gather.go(0, 1, 3, 2, 4)
    gres_ref[...] = gres
    xa[3].advance(2)
    za[2].advance(3)
    gather.got(1)
    gather.go(5, 6)
    gather.got(3)
    gather.go(7, 8)
    za[0].advance(4)
    gather.got(2)
    gather.go(9)
    gather.got(4)
    gather.go(10)
    za[1].advance(4)
    gather.got(5)
    gather.go(11)
    gather.got(7)
    gather.go(12)
    za[2].advance(4)
    gather.got(0, 6, 8, 9, 10, 11, 12)

    for i in range(4):

        def put_x(index, value, i=i):
            rx_ref[index[0] * 4 + index[1], i] = value.astype(BF16)

        xa[i].finish(put_x)
        if i < 3:

            def put_z(index, value, i=i):
                rz_ref[index[0], i] = value.astype(BF16)

            za[i].finish(put_z)
    gather.sent()
    exchange_sent(dg_ref, dbuf, dsend, drecv, place)
    total.sent()
    for arc in xa + za:
        arc.sent()


class Direct:
    def __init__(self, torus, part, x_slots, result, z_slots, send, recv):
        self.t, self.part, self.x_slots, self.result, self.z_slots = torus, part, x_slots, result, z_slots
        self.send, self.recv = send, recv

    def x_copy(self, r):
        to = (self.t.x + r) % 4
        return remote(
            self.part.at[:, to], self.x_slots.at[r - 1], self.send.at[r], self.recv.at[r], self.t.at_x(to)
        )

    def z_copy(self, r):
        to = (self.t.z + r) % 8
        return remote(
            self.result.at[to], self.z_slots.at[r - 1], self.send.at[3 + r], self.recv.at[3 + r], self.t.at_z(to)
        )

    def start(self):
        for r in (2, 1, 3):
            self.x_copy(r).start()

    def turn(self):
        for r in (1, 2, 3):
            self.x_copy(r).wait_recv()

        def add(i, carry):
            h, l = i // 4, i % 4
            value = self.part[h, self.t.x, l].astype(F32)
            for r in range(3):
                value = value + self.x_slots[r, h, l].astype(F32)
            self.result[i] = value.astype(BF16)
            return carry

        lax.fori_loop(0, 8, add, 0)
        for r in (4, 3, 5, 2, 6, 1, 7):
            self.z_copy(r).start()

    def finish(self):
        for r in range(1, 8):
            self.z_copy(r).wait_recv()
        value = self.result[self.t.z].astype(F32)
        for r in range(7):
            value = value + self.z_slots[r].astype(F32)
        return value

    def sent(self):
        for r in (1, 2, 3):
            self.x_copy(r).wait_send()
        for r in range(1, 8):
            self.z_copy(r).wait_send()


def final_kernel(
    dq_ref, dkv_ref, x_ref, gain_ref, ca_ref, sa_ref, cb_ref, sb_ref, grouter_ref, ggain_ref, gproj_ref, rx_ref, rz_ref,
    part_hbm, res_hbm, nall_hbm, wq_hbm, wk_hbm, wv_hbm, gres_hbm, gw_ref,
    out_ref, ing_ref, gin_ref, gout_ref, gq_ref, gk_ref, gv_ref, gside_ref, gproj_out, gains_ref,
    part, res, nall, wq, wk, wv, gres,
    kbuf, dkvb, qpieces, kpieces, cbuf, fbuf, gbuf,
    own, x_slots, z_slots, g0_slots, g1_slots, h0_slots, h1_slots, rx1, rz1,
    early, late, e_x, e_res, e_z, l_x, l_res, l_z, gain_own, gain_e, gain_x, gain_z, fin, rq, rp,
    fsem, csend, crecv, ksend, krecv, qsend, qrecv, psend, precv, usem, xs, xr, zs, zr,
    g0s, g0r, g1s, g1r, h0s, h0r, h1s, h1r, es, er, ls, lr, gs, gr, fsend, frecv, hsend, hrecv,
):
    place = where_am_i()
    dp, ep, ctx = place
    torus = Torus(place)
    loads = [
        pltpu.make_async_copy(src, dst, fsem.at[i])
        for i, (src, dst) in enumerate(
            ((part_hbm, part), (nall_hbm, nall), (wq_hbm, wq), (wk_hbm, wk), (wv_hbm, wv), (res_hbm, res), (gres_hbm, gres))
        )
    ]
    fetches = fetch_units(gw_ref, own, usem, X_FINAL + Z_FINAL)
    loads[0].start()
    for f in fetches:
        f.start()
    for f in loads[1:]:
        f.start()

    def send_to(g, h):
        return (dp, 2 * ctx + g // 2, 2 * (g % 2) + h), (ep, 2 * ctx + g // 2, 2 * (g % 2) + h)

    def is_me(device):
        return (device[0] == dp) & (device[1] == ep) & (device[2] == ctx)

    barrier = pltpu.get_barrier_semaphore()
    for r in range(1, 8):
        greet(barrier, (dp, (ep + r) % 8, ctx))
        greet(barrier, torus.at_z(torus.z + r))
    for r in range(1, 4):
        greet(barrier, torus.at_x(torus.x + r))
    for i in range(8):
        for device in ((dp, i, ep // 2), (i, dp, ep // 2)):

            @pl.when(jnp.logical_not(is_me(device)))
            def _():
                greet(barrier, device)

    waits = 17
    for g in range(4):
        for h in range(2):
            for device in send_to(g, h):
                waits = waits + jnp.where(is_me(device), 0, 1)
    pl.semaphore_wait(barrier, waits)

    total = EpScatterSum(part, cbuf, fbuf, gbuf, csend, crecv, place)

    def link(direction, shard, half, action):
        blocks = pl.ds(half * 4, 4)
        index = (direction * 4 + shard) * 2 + half
        send, recv = ksend.at[index], krecv.at[index]
        to = ctx + 1 if direction == 0 else ctx - 1
        first = ctx == (0 if direction == 0 else 3)
        if direction == 0:
            passes, middle, here = ctx < shard, (ctx < shard) & (ctx > 0), (ctx == shard) & (ctx > 0)
        else:
            passes, middle, here = ctx > shard, (ctx > shard) & (ctx < 3), (ctx == shard) & (ctx < 3)
        slot = kbuf.at[direction, shard, blocks]
        mine = dkv_ref.at[blocks, shard]

        def copy(src):
            return remote(src, slot, send, recv, (dp, ep, to))

        if action == "send":

            @pl.when(passes & first)
            def _():
                copy(mine).start()

            @pl.when(middle)
            def _():
                copy(slot).wait_recv()

                def add(b, carry):
                    b = b + half * 4
                    kbuf[direction, shard, b] = (
                        kbuf[direction, shard, b].astype(F32) + dkv_ref[b, shard].astype(F32)
                    ).astype(BF16)
                    return carry

                lax.fori_loop(0, 4, add, 0)
                copy(slot).start()

        elif action == "recv":

            @pl.when(here)
            def _():
                copy(slot).wait_recv()

        else:

            @pl.when(passes)
            def _():
                copy(slot).wait_send()

    def links(right, left, action):
        for half in (0, 1):
            link(0, right, half, action)
            link(1, left, half, action)

    xa, za = unit_arcs(torus, own, X_FINAL, Z_FINAL, x_slots, z_slots, xs, xr, zs, zr)
    g0 = torus.z_arc(lambda t: rx_ref.at[t], first_or_last((2, 2)), g0_slots, g0s, g0r)
    g1 = torus.z_arc(lambda t: rx1.at[t], first_or_last((2, 2)), g1_slots, g1s, g1r)
    h0 = torus.x_arc(lambda t: rz_ref.at[t], first_or_last((1, 2)), h0_slots, h0s, h0r)
    h1 = torus.x_arc(lambda t: rz1.at[t], first_or_last((1, 1)), h1_slots, h1s, h1r)

    links(3, 0, "send")
    exchange(dq_ref, qpieces, qsend, qrecv, place, False)
    qpieces[ep] = dq_ref[ep]
    loads[0].wait()
    total.start()
    for i in range(4):
        fetches[i].wait()
        xa[i].start()
    links(2, 1, "send")

    gproj = gproj_ref[...].astype(BF16)
    for d in range(8):
        for c in range(4):
            early[d // 4, d % 4, c, :, 0:128] = gproj[32 * c : 32 * c + 32, 128 * d : 128 * d + 128]
    side = jnp.concatenate([grouter_ref[...], jnp.zeros((96, 1024), F32)], axis=0)
    for d in range(8):
        tile = side[:, d * 128 : (d + 1) * 128].T.astype(BF16)
        for c in range(4):
            early[d // 4, d % 4, c, :, 128:256] = tile[32 * c : 32 * c + 32]
    total.far()
    links(1, 2, "send")
    h0.start()
    xa[0].advance(2)
    total.near()
    xa[1].advance(2)
    sums_early = Direct(torus, early, e_x, e_res, e_z, es, er)
    sums_late = Direct(torus, late, l_x, l_res, l_z, ls, lr)
    loads[1].wait()
    exchange(dq_ref, qpieces, qsend, qrecv, place, True)

    def weights(grad, column):
        out = mm(nall[...].reshape(1024, 1024), grad.reshape(1024, 128), TN).astype(BF16)
        for d in range(8):
            for c in range(4):
                rows = d * 128 + c * 32
                late[d // 4, d % 4, c, :, column : column + 128] = out[rows : rows + 32]

    weights(dq_ref[...], 0)
    loads[2].wait()
    grad_q = jnp.concatenate([qpieces[p] for p in range(8)], axis=1)
    grad_normed = mm(grad_q, wq[...], NT)
    xa[2].advance(2)
    h0.advance(2)
    for shard in range(4):
        for half in (0, 1):
            link(0, shard, half, "recv")
            link(1, shard, half, "recv")

    lane = lax.broadcasted_iota(jnp.int32, (TOK, 128), 1)

    @pl.when(ctx == 0)
    def _():
        kbuf[0, 0] = jnp.zeros((8, TOK, 128), BF16)

    @pl.when(ctx == 3)
    def _():
        kbuf[1, 3] = jnp.zeros((8, TOK, 128), BF16)

    def own_block(b, carry):
        grad = dkv_ref[b, ctx].astype(F32) + kbuf[0, ctx, b].astype(F32) + kbuf[1, ctx, b].astype(F32)
        cosine, sine = rope_block(4 * b + ctx, ca_ref, sa_ref, cb_ref, sb_ref)
        cosine = jnp.where(lane < HD, cosine, 1.0)
        sine = jnp.where(lane < HD, sine, 0.0)
        dkvb[b] = (grad * cosine - rotate_half(grad) * sine).astype(BF16)
        return carry

    lax.fori_loop(0, 8, own_block, 0)
    exchange(dkvb, kpieces, psend, precv, place, False)
    kpieces[ep] = dkvb[ep]
    fetches[4].wait()
    za[0].start()
    g0.start()
    weights(dkvb[...], 128)
    sums_late.start()
    sums_early.start()
    xa[3].advance(2)
    loads[5].wait()
    out_ref[...] = (res[...] + total.last()).astype(BF16)
    for f in (loads[3], loads[4], loads[6]):
        f.wait()
    exchange(dkvb, kpieces, psend, precv, place, True)
    grad_k = jnp.concatenate([kpieces[p, :, 0:HD] for p in range(8)], axis=1)
    grad_v = jnp.concatenate([kpieces[p, :, HD:128] for p in range(8)], axis=1)
    grad_normed = grad_normed + mm(grad_k, wk[...], NT) + mm(grad_v, wv[...], NT)
    x = x_ref[...].astype(F32)
    scale = lax.rsqrt(jnp.mean(x * x, axis=-1, keepdims=True) + EPSILON)
    scaled = x * scale
    ggain = jnp.sum(grad_normed * scaled, axis=0, keepdims=True)
    for t in range(8):
        gain_own[0, t : t + 1, :] = ggain[:, 128 * t : 128 * t + 128]
        gain_own[0, 8 + t : 9 + t, :] = ggain_ref[0:1, 128 * t : 128 * t + 128]

    def gain_copy(stage, r):
        src = gain_own.at[stage]
        if stage == 0:
            dst, device, base = gain_e.at[r - 1], (dp, (ep + r) % 8, ctx), 0
        elif stage == 1:
            dst, device, base = gain_x.at[r - 1], torus.at_x(torus.x + r), 7
        else:
            dst, device, base = gain_z.at[r - 1], torus.at_z(torus.z + r), 10
        return remote(src, dst, gs.at[base + r], gr.at[base + r], device)

    def gain_stage(stage, count):
        if stage > 0:
            last, slots = ((7, gain_e), (3, gain_x), (7, gain_z))[stage - 1]
            value = gain_own[stage - 1]
            for r in range(1, last + 1):
                gain_copy(stage - 1, r).wait_recv()
                value = value + slots[r - 1]
            gain_own[stage] = value
        for r in range(1, count + 1):
            gain_copy(stage, r).start()

    gain_stage(0, 7)
    grad_normed = grad_normed * gain_ref[...]
    mean = jnp.mean(grad_normed * scaled, axis=-1, keepdims=True)
    ing_ref[...] = (gres[...] + scale * (grad_normed - scaled * mean)).astype(BF16)

    za[0].advance(2)
    g0.advance(2)
    sums_late.turn()
    gain_stage(1, 3)
    sums_early.turn()
    za[0].advance(3)
    g0.advance(3)

    def put_rx(index, value, i):
        rx1[index[0] * 4 + index[1], i] = value.astype(BF16)

    for i in range(4):
        xa[i].finish(partial(put_rx, i=i))
    g1.start()
    gain_stage(2, 7)
    za[0].advance(4)
    g0.advance(4)

    def piece(g, h, kind, device):
        index = g * 2 + h
        if kind == 0:
            return remote(fin.at[g, :, pl.ds(0, 384)], rq.at[ep], fsend.at[index], frecv.at[ep], device)
        return remote(fin.at[g, :, pl.ds(384, 128)], rp.at[dp], hsend.at[index], hrecv.at[dp], device)

    def each_piece(act, local):
        for g in range(4):
            for h in range(2):
                for kind in (0, 1):
                    device = send_to(g, h)[kind]

                    @pl.when(jnp.logical_not(is_me(device)))
                    def _():
                        act(piece(g, h, kind, device))

                    if local:

                        @pl.when(is_me(device))
                        def _():
                            if kind == 0:
                                rq[ep] = fin[g, :, 0:384]
                            else:
                                rp[dp] = fin[g, :, 384:512]

    done_late, done_early = sums_late.finish(), sums_early.finish()
    for g in range(4):
        rows = slice(8 * g, 8 * g + 8)
        fin[g, :, 0:256] = done_late[rows]
        fin[g, :, 256:384] = done_early[rows, 128:256]
        fin[g, :, 384:512] = done_early[rows, 0:128]
    each_piece(lambda c: c.start(), True)

    g1.advance(2)

    def put_unit(units):
        def put(unit, value):
            j, u = unit // 3, unit % 3
            if u < 2:
                gin_ref[j, 16 * u : 16 * u + 16, :] = value
            else:
                gout_ref[j] = value

        return put

    def finish_units(arc, units):
        for way in (0, 1):
            arc.copy(way, arc.steps).wait_recv()
        mine = arc.own(arc.pos)
        up, down = arc.slots.at[0, arc.steps - 1], arc.slots.at[1, arc.steps - 1]
        put = put_unit(units)
        for i, unit in enumerate(units):
            put(unit, mine[i].astype(F32) + up[i].astype(F32) + down[i].astype(F32))

    finish_units(h0, Z_TURN)

    def put_rz(index, value):
        for h in (0, 1):
            rz1[index[0], h] = value[:, 512 * h : 512 * h + 512].astype(BF16)

    za[0].finish(put_rz)
    h1.start()
    g1.advance(3)
    h1.advance(2)
    finish_units(g0, X_TURN)
    gain_stage_last = gain_own[2]
    for r in range(1, 8):
        gain_copy(2, r).wait_recv()
        gain_stage_last = gain_stage_last + gain_z[r - 1]
    gain_own[3] = gain_stage_last
    g1.advance(4)

    for i in range(8):
        for kind, device in enumerate(((dp, i, ep // 2), (i, dp, ep // 2))):

            @pl.when(jnp.logical_not(is_me(device)))
            def _():
                if kind == 0:
                    src, dst, pair = fin.at[0, :, pl.ds(0, 384)], rq.at[i], (fsend.at[0], frecv.at[i])
                else:
                    src, dst, pair = fin.at[0, :, pl.ds(384, 128)], rp.at[i], (hsend.at[0], hrecv.at[i])
                remote(src, dst, pair[0], pair[1], device).wait_recv()

    odd = ctx % 2 == 1

    def mine(v):
        return jnp.where(odd, v[4:8], v[0:4])

    gq_ref[...] = mine(jnp.concatenate([rq[i, :, 0:128] for i in range(8)], axis=1))
    gk_ref[...] = mine(jnp.concatenate([rq[i, :, 128:192] for i in range(8)], axis=1))
    gv_ref[...] = mine(jnp.concatenate([rq[i, :, 192:256] for i in range(8)], axis=1))
    side = rq[0, :, 256:384]
    for i in range(1, 8):
        side = side + rq[i, :, 256:384]
    gside_ref[...] = mine(side)
    gproj_out[...] = mine(jnp.concatenate([rp[i] for i in range(8)], axis=1))
    for which in (0, 1):
        row = jnp.broadcast_to(gain_own[3, pl.ds(8 * which + dp, 1), :], (8, 128))
        gains_ref[8 * which : 8 * which + 8, :] = pltpu.roll(row, (128 - 16 * ep - 4 * ctx) % 128, 1)

    for way in (0, 1):
        h1.copy(way, 2).wait_recv()
    for h in (0, 1):
        value = rz1[torus.x, h].astype(F32) + h1_slots[0, 1, h].astype(F32) + h1_slots[1, 1, h].astype(F32)
        gout_ref[2, :, 512 * h : 512 * h + 512] = value
    finish_units(g1, X_FINAL)

    total.sent()
    exchange_sent(dq_ref, qpieces, qsend, qrecv, place)
    exchange_sent(dkvb, kpieces, psend, precv, place)
    for shard in range(4):
        for half in (0, 1):
            for direction in (0, 1):
                link(direction, shard, half, "sent")
    for arc in xa + za + [g0, g1, h0, h1]:
        arc.sent()
    sums_early.sent()
    sums_late.sent()
    for stage, count in ((0, 7), (1, 3), (2, 7)):
        for r in range(1, count + 1):
            gain_copy(stage, r).wait_send()
    each_piece(lambda c: c.wait_send(), False)


def pack_kernel(*refs):
    count = len(refs) // 2
    for src, dst in zip(refs[:count], refs[count:]):
        dst[...] = src[...]


def call(kernel, outs, scratch, args, name, collective=None, **more):
    params = dict(vmem_limit_bytes=VMEM_LIMIT)
    if collective is not None:
        params.update(collective_id=collective, has_side_effects=True)
    space = pl.BlockSpec(memory_space=pltpu.VMEM)
    return pl.pallas_call(
        kernel,
        out_shape=[jax.ShapeDtypeStruct(shape, kind) for shape, kind in outs],
        in_specs=more.pop("in_specs", [space] * len(args)),
        out_specs=more.pop("out_specs", [space] * len(outs)),
        scratch_shapes=scratch,
        compiler_params=pltpu.CompilerParams(**params),
        name=name,
        **more,
    )(*args)


def sems(*sizes):
    return [pltpu.SemaphoreType.DMA(s if isinstance(s, tuple) else (s,)) for s in sizes]


def body(
    layer_input, gain_attn, w_query, w_key, w_value, w_proj, gain_ffn, w_router,
    w_expert_in, w_expert_out, segment_ids, expert_ids, slot_order, out_grad,
):
    ep = lax.axis_index("ep")
    gain_one, gain_two = gain_attn.reshape(1, 1024), gain_ffn.reshape(1, 1024)
    tables = [jnp.asarray(t) for t in rope_tables()]
    w_own = jnp.concatenate(
        [
            lax.dynamic_slice_in_dim(w_query, ep * 128, 128, 1),
            lax.dynamic_slice_in_dim(w_key, ep * 64, 64, 1),
            lax.dynamic_slice_in_dim(w_value, ep * 64, 64, 1),
        ],
        axis=1,
    )
    wr_rows = jnp.pad(w_router.T.reshape(8, 4, 1024), ((0, 0), (0, 4), (0, 0))).reshape(64, 1024)
    w_proj_own = lax.dynamic_slice_in_dim(w_proj, ep * 128, 128, 0)
    order = slot_order.reshape(TOK, 8)
    docs = segment_ids.reshape(32, 128)

    normed_all, query, kv, grad_all, slots, chosen, starts = call(
        first_kernel,
        [
            ((8, TOK, 1024), BF16), ((8, TOK, 128), BF16), ((8, 4, TOK, 128), BF16), ((8, TOK, 1024), BF16),
            ((8, 8, TOK), F32), ((64, TOK), F32), ((32, 128), F32),
        ],
        [pltpu.VMEM((8, 8, TOK), F32)] + sems(13, 13, 13, 13, 8, 8, 24, 24),
        [layer_input, gain_one, out_grad, w_own, *tables, expert_ids, expert_ids.T, order, order.T, docs],
        "first", 1,
    )
    kv_rows = kv.reshape(4096, 128)
    ctx = lax.axis_index("ctx")
    first = lax.dynamic_slice_in_dim(starts.reshape(8, 4, 128), ctx, 1, 1)[:, 0, 0].astype(jnp.int32) // CHUNK

    vm, sm = pl.BlockSpec(memory_space=pltpu.VMEM), pl.BlockSpec(memory_space=pltpu.SMEM)
    attended, attended_tall, log_sums = call(
        attend_kernel,
        [((8, TOK, 128), BF16), ((8, 128, TOK), F32), ((8, 8, 256), F32)],
        [pltpu.VMEM((128, 4096), BF16)],
        [first, query, kv_rows, starts],
        "attend", in_specs=[sm, vm, vm, vm],
    )
    residual, ffn_all, gates_in, gates = call(
        middle_kernel,
        [((TOK, 1024), F32), ((8, TOK, 1024), BF16), ((8, 8, TOK), F32), ((64, TOK), F32)],
        [pltpu.VMEM((8, TOK, 128), BF16), pltpu.VMEM((8, 8, TOK), F32)] + sems(8, 8, 13, 13, 8, 8),
        [attended, layer_input, gain_two, w_proj, wr_rows, chosen],
        "middle", 2,
    )
    whole = lambda *shape: pl.BlockSpec(shape, lambda j: (0,) * len(shape))
    sums, back, grad_gates, grad_experts = call(
        expert_kernel,
        [((8, TOK, 1024), BF16), ((8, TOK, 1024), BF16), ((8, 8, TOK), F32), ((12, 32, 16, 1024), BF16)],
        [pltpu.VMEM((4, 8 * CAP, 1024), F32), pltpu.VMEM((4, 8 * CAP, 1024), F32)],
        [ffn_all, grad_all, slots, gates_in, w_expert_in, w_expert_out],
        "experts", grid=(4,),
        in_specs=[
            whole(8, TOK, 1024), whole(8, TOK, 1024), whole(8, 8, TOK), whole(8, 8, TOK),
            pl.BlockSpec((1, 1024, 1024), lambda j: (j, 0, 0)), pl.BlockSpec((1, 512, 1024), lambda j: (j, 0, 0)),
        ],
        out_specs=[
            whole(8, TOK, 1024), whole(8, TOK, 1024), whole(8, 8, TOK),
            pl.BlockSpec((3, 32, 16, 1024), lambda j: (j, 0, 0, 0)),
        ],
    )
    units = grad_experts.reshape(12, 2, 4, 4, 16, 1024)
    own_ffn = lax.dynamic_index_in_dim(ffn_all, ep, 0, False)
    hbm = pl.BlockSpec(memory_space=pl.ANY)
    nx, nz = len(X_TURN), len(Z_TURN)
    grad_mixed, grad_res, grad_router, grad_gain_two, sums_x, sums_z = call(
        turn_kernel,
        [
            ((8, TOK, 1024), BF16), ((TOK, 1024), F32), ((32, 1024), F32), ((8, 1024), F32),
            ((8, nx, 16, 1024), BF16), ((4, nz, 16, 1024), BF16),
        ],
        [pltpu.VMEM((8, 8, TOK), F32)] + scatter_sum_scratch() + sems(8, 8, 13, 13)
        + [
            pltpu.VMEM((nx + nz, 2, 4, 4, 16, 1024), BF16),
            pltpu.VMEM((nx, 2, 2, 2, 4, 16, 1024), BF16), pltpu.VMEM((nz, 2, 4, 4, 16, 1024), BF16),
        ]
        + sems(nx + nz, (nx, 2, 2), (nx, 2, 2), (nz, 2, 4), (nz, 2, 4)),
        [back, grad_gates, gates, residual, own_ffn, out_grad, gain_two, wr_rows, units],
        "turn", 3, in_specs=[vm] * 8 + [hbm],
    )
    grad_q, grad_kv, grad_proj = call(
        attend_back_kernel,
        [((8, TOK, 128), BF16), ((4096, 128), BF16), ((128, 1024), F32)],
        [pltpu.VMEM((HD, 4096), BF16), pltpu.VMEM((4096, 128), F32)],
        [first, query, kv_rows, starts, attended_tall, log_sums, grad_mixed, w_proj_own, *tables],
        "attend_back", in_specs=[sm] + [vm] * 11,
    )
    fx, fz = len(X_FINAL), len(Z_FINAL)
    results = call(
        final_kernel,
        [
            ((TOK, 1024), BF16), ((TOK, 1024), BF16), ((4, 32, 1024), F32), ((4, 16, 1024), F32), ((4, 1024), F32),
            ((4, 512), F32), ((4, 512), F32), ((4, 128), F32), ((4, 1024), F32), ((16, 128), F32),
        ],
        [
            pltpu.VMEM((8, TOK, 1024), BF16), pltpu.VMEM((TOK, 1024), F32), pltpu.VMEM((8, TOK, 1024), BF16),
            pltpu.VMEM((1024, 1024), BF16), pltpu.VMEM((1024, 512), BF16), pltpu.VMEM((1024, 512), BF16),
            pltpu.VMEM((TOK, 1024), F32),
            pltpu.VMEM((2, 4, 8, TOK, 128), BF16), pltpu.VMEM((8, TOK, 128), BF16), pltpu.VMEM((8, TOK, 128), BF16),
            pltpu.VMEM((8, TOK, 128), BF16),
        ]
        + scatter_sum_scratch()[:3]
        + [
            pltpu.VMEM((fx + fz, 2, 4, 4, 16, 1024), BF16),
            pltpu.VMEM((fx, 2, 2, 2, 4, 16, 1024), BF16), pltpu.VMEM((fz, 2, 4, 4, 16, 1024), BF16),
            pltpu.VMEM((2, 4, nx, 16, 1024), BF16), pltpu.VMEM((2, 4, fx, 16, 1024), BF16),
            pltpu.VMEM((2, 2, nz, 16, 1024), BF16), pltpu.VMEM((2, 2, 2, 16, 512), BF16),
            pltpu.VMEM((8, fx, 16, 1024), BF16), pltpu.VMEM((4, 2, 16, 512), BF16),
        ]
        + [pltpu.VMEM((2, 4, 4, 32, 256), BF16)] * 2
        + [pltpu.VMEM((3, 2, 4, 32, 256), BF16), pltpu.VMEM((8, 32, 256), BF16), pltpu.VMEM((7, 32, 256), BF16)] * 2
        + [
            pltpu.VMEM((4, 16, 128), F32), pltpu.VMEM((7, 16, 128), F32), pltpu.VMEM((3, 16, 128), F32),
            pltpu.VMEM((7, 16, 128), F32),
            pltpu.VMEM((4, 8, 512), F32), pltpu.VMEM((8, 8, 384), F32), pltpu.VMEM((8, 8, 128), F32),
        ]
        + sems(
            7, 8, 8, 16, 16, 8, 8, 8, 8, fx + fz, (fx, 2, 2), (fx, 2, 2), (fz, 2, 4), (fz, 2, 4),
            (2, 4), (2, 4), (2, 4), (2, 4), (2, 2), (2, 2), (2, 2), (2, 2), 11, 11, 11, 11, 18, 18, 8, 8, 8, 8,
        ),
        [
            grad_q, grad_kv.reshape(8, 4, TOK, 128), layer_input, gain_one, *tables, grad_router, grad_gain_two,
            grad_proj, sums_x, sums_z,
            sums, residual, normed_all, w_query, w_key, w_value, grad_res, units,
        ],
        "final", 4, in_specs=[vm] * 13 + [hbm] * 8,
    )
    layer_output, input_grad, grad_in, grad_out, out_q, out_k, out_v, side, out_proj, gains = call(
        pack_kernel, [(r.shape, r.dtype) for r in results], [], results, "pack"
    )
    return (
        layer_output, input_grad, gains[0, :4], out_q, out_k, out_v, out_proj, gains[8, :4], side[:, :32], grad_in, grad_out,
    )


def solution(mesh):
    tokens = P(("dp", "ep", "ctx"), None)
    in_specs = (
        tokens, P(), P(), P(), P(), P(), P(), P(),
        P("ep", None, None), P("ep", None, None), P("dp", None), tokens, tokens, tokens,
    )
    out_specs = (
        tokens, tokens, P(("dp", "ep", "ctx")), tokens, tokens, tokens, tokens, P(("dp", "ep", "ctx")), tokens,
        P("ep", ("dp", "ctx"), None), P("ep", ("dp", "ctx"), None),
    )
    return jax.shard_map(body, mesh=mesh, in_specs=in_specs, out_specs=out_specs, check_vma=False)
```

```python
from functools import partial

import jax
import jax.numpy as jnp
import numpy as np
from jax import lax
from jax.experimental import pallas as pl
from jax.experimental.pallas import tpu as pltpu
from jax.sharding import PartitionSpec as P

HD = 64
EPSILON = 1e-06
MASKED = -1e30
CAP = 40
TOK = 128
BIG = 4096.0
MESH = pl.DeviceIdType.MESH
F32 = jnp.float32
BF16 = jnp.bfloat16
VMEM_LIMIT = 60 * 1024 * 1024

NT = (((1,), (1,)), ((), ()))
NN = (((1,), (0,)), ((), ()))
TN = (((0,), (0,)), ((), ()))


def mm(a, b, dims=NN):
    return lax.dot_general(a, b, dims, preferred_element_type=F32)


def mm3(a, b, dims=NN):
    high = a.astype(BF16)
    low = (a - high.astype(F32)).astype(BF16)
    return mm(high, b, dims) + mm(low, b, dims)


def where_am_i():
    dp, ep, ctx = lax.axis_index("dp"), lax.axis_index("ep"), lax.axis_index("ctx")
    return dp, ep, ctx


def remote(src, dst, send, recv, device):
    return pltpu.make_async_remote_copy(
        src_ref=src, dst_ref=dst, send_sem=send, recv_sem=recv, device_id=device, device_id_type=MESH
    )


def greet(barrier, device):
    pl.semaphore_signal(barrier, inc=1, device_id=device, device_id_type=MESH)


def rotate_half(values):
    lane = lax.broadcasted_iota(jnp.int32, values.shape, 1)
    return jnp.where(lane % HD < HD // 2, pltpu.roll(values, 96, 1), pltpu.roll(values, 32, 1))


def rope_block(block, ca_ref, sa_ref, cb_ref, sb_ref):
    ca, sa = ca_ref[pl.ds(block, 1), :], sa_ref[pl.ds(block, 1), :]
    cb, sb = cb_ref[...], sb_ref[...]
    cosine = ca * cb - sa * sb
    sine = sa * cb + ca * sb
    lane = lax.broadcasted_iota(jnp.int32, cosine.shape, 1)
    return cosine, jnp.where(lane % HD < HD // 2, -sine, sine)


def rope_tables():
    frequency = 10000.0 ** (-np.arange(HD // 2, dtype=np.float64) * 2.0 / HD)
    frequency = np.tile(frequency.astype(np.float32).astype(np.float64), 4)
    blocks = np.arange(32, dtype=np.float64)[:, None] * 128.0 * frequency[None, :]
    rows = np.arange(128, dtype=np.float64)[:, None] * frequency[None, :]
    return [t.astype(np.float32) for t in (np.cos(blocks), np.sin(blocks), np.cos(rows), np.sin(rows))]


class EpGather:
    COUNT = 13

    def __init__(self, ref, send, recv, place):
        self.ref, self.send, self.recv = ref, send, recv
        dp, ep, ctx = place
        y, k = ep // 2, ep % 2
        self.up = (dp, ((y + 1) % 4) * 2 + k, ctx)
        self.dn = (dp, ((y + 3) % 4) * 2 + k, ctx)
        self.sib = (dp, y * 2 + 1 - k, ctx)

        def at(dy, other):
            return ((y + dy) % 4) * 2 + ((1 - k) if other else k)

        u, s, d = self.up, self.sib, self.dn
        self.sends = [
            (at(0, 0), None, s), (at(0, 0), 0, u), (at(0, 0), 1, u), (at(0, 0), 1, d), (at(0, 0), 0, d),
            (at(3, 0), 0, u), (at(3, 0), 0, s), (at(1, 0), 1, d), (at(1, 0), 1, s),
            (at(3, 0), 1, s), (at(1, 0), 0, s), (at(2, 0), 0, s), (at(2, 0), 1, s),
        ]
        self.gets = [
            (at(0, 1), None), (at(3, 0), 0), (at(3, 0), 1), (at(1, 0), 1), (at(1, 0), 0),
            (at(2, 0), 0), (at(3, 1), 0), (at(2, 0), 1), (at(1, 1), 1),
            (at(3, 1), 1), (at(1, 1), 0), (at(2, 1), 0), (at(2, 1), 1),
        ]

    def view(self, block, half):
        if half is None:
            return self.ref.at[block]
        rows = self.ref.shape[1] // 2
        return self.ref.at[block, pl.ds(half * rows, rows)]

    def go(self, *which):
        for i in which:
            block, half, device = self.sends[i]
            v = self.view(block, half)
            remote(v, v, self.send.at[i], self.recv.at[i], device).start()

    def got(self, *which):
        for i in which:
            v = self.view(*self.gets[i])
            remote(v, v, self.send.at[i], self.recv.at[i], self.sends[i][2]).wait_recv()

    def sent(self):
        for i in range(self.COUNT):
            block, half, device = self.sends[i]
            v = self.view(block, half)
            remote(v, v, self.send.at[i], self.recv.at[i], device).wait_send()

    def whole(self):
        self.got(1)
        self.go(5, 6)
        self.got(3)
        self.go(7, 8)
        self.got(2)
        self.go(9)
        self.got(4)
        self.go(10)
        self.got(5)
        self.go(11)
        self.got(7)
        self.go(12)
        self.got(0, 6, 8, 9, 10, 11, 12)


class EpScatterSum:
    COUNT = 8

    def __init__(self, part, cbuf, fbuf, gbuf, send, recv, place):
        self.part, self.cbuf, self.fbuf, self.gbuf = part, cbuf, fbuf, gbuf
        self.send, self.recv = send, recv
        dp, ep, ctx = place
        self.y, self.k = ep // 2, ep % 2
        y, k = self.y, self.k
        self.up = (dp, ((y + 1) % 4) * 2 + k, ctx)
        self.dn = (dp, ((y + 3) % 4) * 2 + k, ctx)
        self.sib = (dp, y * 2 + 1 - k, ctx)

    def block(self, dy, other=False):
        return ((self.y + dy) % 4) * 2 + ((1 - self.k) if other else self.k)

    def copy(self, i):
        half = self.cbuf.shape[1] // 2
        lo, hi = pl.ds(0, half), pl.ds(half, half)
        s, r = self.send, self.recv
        if i < 4:
            away = self.block((2, 1, 3, 0)[i], True)
            return remote(self.part.at[away], self.cbuf.at[i], s.at[i], r.at[i], self.sib)
        src, dst, device = (
            (self.cbuf.at[0, lo], self.fbuf.at[0], self.up),
            (self.cbuf.at[0, hi], self.fbuf.at[1], self.dn),
            (self.cbuf.at[1], self.gbuf.at[0], self.up),
            (self.cbuf.at[2], self.gbuf.at[1], self.dn),
        )[i - 4]
        return remote(src, dst, s.at[i], r.at[i], device)

    def start(self):
        for i in range(4):
            self.copy(i).start()

    def far(self):
        self.copy(0).wait_recv()
        self.cbuf[0] = (self.cbuf[0].astype(F32) + self.part[self.block(2)].astype(F32)).astype(BF16)
        self.copy(4).start()
        self.copy(5).start()

    def near(self):
        half = self.cbuf.shape[1] // 2
        for slot, dy, far, rows, rest in ((1, 1, 0, pl.ds(0, half), pl.ds(half, half)), (2, 3, 1, pl.ds(half, half), pl.ds(0, half))):
            b = self.block(dy)
            self.copy(slot).wait_recv()
            self.copy(4 + far).wait_recv()
            self.cbuf[slot, rows] = (
                self.cbuf[slot, rows].astype(F32) + self.part[b, rows].astype(F32) + self.fbuf[far].astype(F32)
            ).astype(BF16)
            self.cbuf[slot, rest] = (self.cbuf[slot, rest].astype(F32) + self.part[b, rest].astype(F32)).astype(BF16)
            self.copy(6 + far).start()

    def last(self):
        for i in (3, 6, 7):
            self.copy(i).wait_recv()
        return (
            self.part[self.block(0)].astype(F32) + self.cbuf[3].astype(F32)
            + self.gbuf[0].astype(F32) + self.gbuf[1].astype(F32)
        )

    def sent(self):
        for i in range(self.COUNT):
            self.copy(i).wait_send()


def scatter_sum_scratch():
    return [
        pltpu.VMEM((4, TOK, 1024), BF16),
        pltpu.VMEM((2, TOK // 2, 1024), BF16),
        pltpu.VMEM((2, TOK, 1024), BF16),
        pltpu.SemaphoreType.DMA((8,)),
        pltpu.SemaphoreType.DMA((8,)),
    ]


def exchange(src, dst, send, recv, place, wait):
    dp, ep, ctx = place
    for r in range(1, 8):
        to, source = (ep + r) % 8, (ep + 8 - r) % 8
        if not wait:
            remote(src.at[to], dst.at[ep], send.at[r], recv.at[r], (dp, to, ctx)).start()
        else:
            remote(src.at[to], dst.at[source], send.at[r], recv.at[r], (dp, to, ctx)).wait_recv()


def exchange_sent(src, dst, send, recv, place):
    dp, ep, ctx = place
    for r in range(1, 8):
        to = (ep + r) % 8
        remote(src.at[to], dst.at[ep], send.at[r], recv.at[r], (dp, to, ctx)).wait_send()


def starts_of(docs):
    rows = lax.broadcasted_iota(jnp.int32, docs.shape, 0)
    lane = lax.broadcasted_iota(jnp.int32, docs.shape, 1)
    docs = docs.astype(F32)
    turned = pltpu.roll(docs, 1, 1)
    before = jnp.where(lane == 0, pltpu.roll(turned, 1, 0), turned)
    place = rows * 128 + lane
    fresh = (docs != before) | (place == 0)
    value = jnp.where(fresh, place.astype(F32), 0.0)
    for shift in (1, 2, 4, 8, 16, 32, 64):
        value = jnp.maximum(value, jnp.where(lane >= shift, pltpu.roll(value, shift, 1), 0.0))
    carry = jnp.broadcast_to(jnp.max(value, axis=1, keepdims=True), value.shape)
    for shift in (1, 2, 4, 8, 16):
        carry = jnp.maximum(carry, jnp.where(rows >= shift, pltpu.roll(carry, shift, 0), 0.0))
    above = jnp.where(rows >= 1, pltpu.roll(carry, 1, 0), 0.0)
    return jnp.maximum(value, above)


def slots_of(eid_ref, eidT_ref, so_ref, soT_ref, slot_scr, sel_ref):
    def expert(index):
        return jnp.where(index % 8 < 4, (index // 8) * 4 + index % 8, -1)

    row_expert = expert(lax.broadcasted_iota(jnp.int32, (64, TOK), 0))
    lane_expert = expert(lax.broadcasted_iota(jnp.int32, (TOK, 64), 1))
    by_row = jnp.full((64, TOK), BIG, F32)
    by_lane = jnp.full((TOK, 64), BIG, F32)
    for k in range(8):
        by_row = jnp.where(eidT_ref[k : k + 1, :] == row_expert, soT_ref[k : k + 1, :].astype(F32), by_row)
        by_lane = jnp.where(eid_ref[:, k : k + 1] == lane_expert, so_ref[:, k : k + 1].astype(F32), by_lane)
    sel_ref[...] = jnp.where(by_row < BIG, 1.0, 0.0)
    for g in range(8):
        for j in range(4):
            r = 8 * g + j
            row = by_row[r : r + 1, :]
            less = jnp.where(by_lane[:, r : r + 1] < row, 1.0, 0.0)
            rank = jnp.sum(less, axis=0, keepdims=True)
            slot_scr[g, j : j + 1, :] = jnp.where((row < BIG) & (rank < CAP), rank, -1.0)
        slot_scr[g, 4:8, :] = jnp.full((4, TOK), -1.0, F32)


def first_kernel(
    x_ref, gain_ref, og_ref, w_ref, ca_ref, sa_ref, cb_ref, sb_ref, eid_ref, eidT_ref, so_ref, soT_ref, doc_ref,
    nall_ref, q_ref, kv_ref, ogall_ref, slot_ref, sel_ref, start_ref,
    slot_scr, nsend, nrecv, osend, orecv, ssend, srecv, ksend, krecv,
):
    place = where_am_i()
    dp, ep, ctx = place
    y = ep // 2
    barrier = pltpu.get_barrier_semaphore()
    for r in range(1, 8):
        greet(barrier, (dp, (ep + r) % 8, ctx))

    @pl.when(ctx > 0)
    def _():
        greet(barrier, (dp, ep, ctx - 1))

    @pl.when(ctx < 3)
    def _():
        greet(barrier, (dp, ep, ctx + 1))

    x = x_ref[...].astype(F32)
    normed = x * lax.rsqrt(jnp.mean(x * x, axis=-1, keepdims=True) + EPSILON) * gain_ref[...]
    nall_ref[ep] = normed.astype(BF16)
    ogall_ref[ep] = og_ref[...]
    edges = jnp.where(ctx > 0, 1, 0) + jnp.where(ctx < 3, 1, 0)
    pl.semaphore_wait(barrier, 7 + edges)

    gather = EpGather(nall_ref, nsend, nrecv, place)
    grads = EpGather(ogall_ref, osend, orecv, place)
    gather.go(0, 1, 3, 2, 4)

    start_ref[...] = starts_of(doc_ref[...])
    slots_of(eid_ref, eidT_ref, so_ref, soT_ref, slot_scr, sel_ref)
    slot_ref[ep] = slot_scr[ep]
    exchange(slot_scr, slot_ref, ssend, srecv, place, False)

    lane = lax.broadcasted_iota(jnp.int32, (TOK, 128), 1)

    def project(dy):
        chip = (y + dy) % 4
        rows = jnp.concatenate([nall_ref[2 * chip], nall_ref[2 * chip + 1]], axis=0)
        out = mm(rows, w_ref[...])
        for i in range(2):
            b = 2 * chip + i
            cosine, sine = rope_block(4 * b + ctx, ca_ref, sa_ref, cb_ref, sb_ref)
            q = out[i * TOK : (i + 1) * TOK, :128]
            kv = out[i * TOK : (i + 1) * TOK, 128:]
            q_rot = (q * cosine + rotate_half(q) * sine).astype(BF16)
            q_ref[b] = (q_rot.astype(F32) * (HD**-0.5)).astype(BF16)
            cosine = jnp.where(lane < HD, cosine, 1.0)
            sine = jnp.where(lane < HD, sine, 0.0)
            kv_ref[b, ctx] = (kv * cosine + rotate_half(kv) * sine).astype(BF16)

    offsets = (0, 3, 1, 2)

    def hop(direction, h, g, action):
        chip = (y + offsets[g]) % 4
        back = h - 1
        own = ctx - back if direction == 0 else ctx + back
        come = ctx - h if direction == 0 else ctx + h
        to = ctx + 1 if direction == 0 else ctx - 1
        index = (direction * 3 + back) * 4 + g
        send, recv = ksend.at[index], krecv.at[index]
        if action == "recv":
            ok = come >= 0 if direction == 0 else come <= 3

            @pl.when(ok)
            def _():
                v = kv_ref.at[pl.ds(2 * chip, 2), come]
                remote(v, v, send, recv, (dp, ep, ctx)).wait_recv()

        else:
            ok = (own >= 0) & (ctx < 3) if direction == 0 else (own <= 3) & (ctx > 0)

            @pl.when(ok)
            def _():
                v = kv_ref.at[pl.ds(2 * chip, 2), own]
                c = remote(v, v, send, recv, (dp, ep, to))
                c.start() if action == "send" else c.wait_send()

    def hops(h, g):
        for direction in (0, 1):
            if h > 1:
                hop(direction, h - 1, g, "recv")
            hop(direction, h, g, "send")

    gather.got(0)
    project(0)
    hops(1, 0)
    gather.got(1)
    gather.go(5, 6)
    gather.got(3)
    gather.go(7, 8)
    gather.got(2)
    gather.go(9)
    gather.got(4)
    gather.go(10)
    grads.go(0, 1, 3, 2, 4)
    gather.got(6, 9)
    project(3)
    hops(1, 1)
    hops(2, 0)
    gather.got(8, 10)
    project(1)
    hops(1, 2)
    hops(2, 1)
    hops(3, 0)
    gather.got(5)
    gather.go(11)
    gather.got(7)
    gather.go(12)
    gather.got(11, 12)
    project(2)
    hops(1, 3)
    hops(2, 2)
    hops(3, 1)
    hops(2, 3)
    hops(3, 2)
    grads.whole()
    hops(3, 3)
    for g in range(4):
        for direction in (0, 1):
            hop(direction, 3, g, "recv")
    exchange(slot_scr, slot_ref, ssend, srecv, place, True)
    gather.sent()
    grads.sent()
    exchange_sent(slot_scr, slot_ref, ssend, srecv, place)
    for g in range(4):
        for h in (1, 2, 3):
            for direction in (0, 1):
                hop(direction, h, g, "sent")


CHUNK = 512


def key_mask(chunk, start_row, place_row):
    keys = (lax.broadcasted_iota(jnp.int32, (CHUNK, 256), 0) + chunk * CHUNK).astype(F32)
    return (keys >= start_row) & (keys <= place_row)


def query_rows(j, ctx, start_ref):
    block = 4 * j + ctx
    start = start_ref[pl.ds(block, 1), :]
    places = (lax.broadcasted_iota(jnp.int32, (1, 128), 1) + block * 128).astype(F32)
    return jnp.concatenate([start, start], axis=1), jnp.concatenate([places, places], axis=1)


def turned(block):
    return block.astype(F32).T.astype(BF16)


def heads_wide(tall):
    return jnp.concatenate([tall[:HD], tall[HD:]], axis=1)


def attend_kernel(first_ref, q_ref, kv_ref, start_ref, att_ref, attT_ref, lse_ref, kvT):
    ctx = lax.axis_index("ctx")

    for chunk in range(8):
        part = kv_ref[chunk * CHUNK : (chunk + 1) * CHUNK, :].astype(F32).T
        row = lax.broadcasted_iota(jnp.int32, part.shape, 0)
        kvT[:, chunk * CHUNK : (chunk + 1) * CHUNK] = jnp.where(row < HD, 1.0, part).astype(BF16)

    for j in range(8):
        start_row, place_row = query_rows(j, ctx, start_ref)
        wide = heads_wide(turned(q_ref[j]))
        q_pad = jnp.concatenate([wide, jnp.zeros_like(wide)], axis=0)

        def step(chunk, carry):
            top, total = carry
            rows = pl.ds(pl.multiple_of(chunk * CHUNK, CHUNK), CHUNK)
            scores = mm(kv_ref[rows, :], q_pad)
            scores = jnp.where(key_mask(chunk, start_row, place_row), scores, MASKED)
            new_top = jnp.maximum(top, jnp.max(scores, axis=0, keepdims=True))
            probs = jnp.exp(scores - new_top).astype(BF16)
            total = total * jnp.exp(top - new_top) + mm(kvT[:, rows], probs)
            return new_top, total

        top, total = lax.fori_loop(
            first_ref[j], j + 1, step, (jnp.full((1, 256), MASKED, F32), jnp.zeros((128, 256), F32))
        )
        norm = total[0:1]
        out = total[HD:] / norm
        tall = jnp.concatenate([out[:, :128], out[:, 128:]], axis=0)
        attT_ref[j] = tall
        att_ref[j] = tall.T.astype(BF16)
        lse_ref[j] = jnp.broadcast_to(top + jnp.log(norm), (8, 256))


def middle_kernel(
    att_ref, x_ref, gain_ref, w_ref, wr_ref, sel_ref,
    res_ref, nf_ref, gin_ref, gates_ref,
    abuf, gscr, asend, arecv, nsend, nrecv, gsend, grecv,
):
    place = where_am_i()
    dp, ep, ctx = place
    barrier = pltpu.get_barrier_semaphore()
    for r in range(1, 8):
        greet(barrier, (dp, (ep + r) % 8, ctx))
    pl.semaphore_wait(barrier, 7)
    exchange(att_ref, abuf, asend, arecv, place, False)
    abuf[ep] = att_ref[ep]
    exchange(att_ref, abuf, asend, arecv, place, True)
    attended = jnp.concatenate([abuf[p] for p in range(8)], axis=1)
    res = x_ref[...].astype(F32) + mm(attended, w_ref[...])
    res_ref[...] = res
    normed = res * lax.rsqrt(jnp.mean(res * res, axis=-1, keepdims=True) + EPSILON) * gain_ref[...]
    normed = normed.astype(BF16)
    nf_ref[ep] = normed
    gather = EpGather(nf_ref, nsend, nrecv, place)
    gather.go(0, 1, 3, 2, 4)
    logits = mm(wr_ref[...], normed, NT)
    chosen = sel_ref[...] > 0.5
    top = jnp.max(jnp.where(chosen, logits, MASKED), axis=0, keepdims=True)
    weight = jnp.where(chosen, jnp.exp(jnp.where(chosen, logits, MASKED) - top), 0.0)
    gates = weight / jnp.sum(weight, axis=0, keepdims=True)
    gates_ref[...] = gates
    for g in range(8):
        gscr[g] = gates[8 * g : 8 * g + 8, :]
    gin_ref[ep] = gscr[ep]
    exchange(gscr, gin_ref, gsend, grecv, place, False)
    gather.whole()
    exchange(gscr, gin_ref, gsend, grecv, place, True)
    gather.sent()
    exchange_sent(gscr, gin_ref, gsend, grecv, place)
    exchange_sent(att_ref, abuf, asend, arecv, place)


def expert_kernel(
    nf_ref, og_ref, slot_ref, gate_ref, win_ref, wout_ref,
    y_ref, d_ref, dg_ref, gw_ref,
    rows_scr, grad_scr,
):
    j = pl.program_id(0)
    slot = lax.broadcasted_iota(jnp.int32, (CAP, TOK), 0).astype(F32)

    def picks(s, e):
        return slot == slot_ref[s, pl.ds(e, 1), :]

    @pl.when(j == 0)
    def _():
        def load(s, carry):
            pick = jnp.concatenate([jnp.where(picks(s, e), 1.0, 0.0) for e in range(4)], axis=0).astype(BF16)
            got = mm(pick, nf_ref[s])
            grad = mm(pick, og_ref[s])
            for e in range(4):
                rows = pl.ds(pl.multiple_of(s * CAP, 8), CAP)
                rows_scr[e, rows, :] = got[e * CAP : (e + 1) * CAP]
                grad_scr[e, rows, :] = grad[e * CAP : (e + 1) * CAP]
            return carry

        lax.fori_loop(0, 8, load, 0)

    gates = jnp.concatenate(
        [jnp.sum(jnp.where(picks(s, j), gate_ref[s, pl.ds(j, 1), :], 0.0), axis=1, keepdims=True) for s in range(8)],
        axis=0,
    )
    received = rows_scr[j].astype(BF16)
    grad_tok = grad_scr[j]
    gate_up = mm(received, win_ref[0])
    gating, up = gate_up[:, :512], gate_up[:, 512:]
    sig = 1.0 / (1.0 + jnp.exp(-gating))
    silu = gating * sig
    act = (silu * up).astype(BF16)
    result = mm(act, wout_ref[0]).astype(BF16).astype(F32)
    dots = jnp.sum(grad_tok * result, axis=1, keepdims=True)
    grad_res = (grad_tok * gates).astype(BF16)
    grad_scr[j] = result * gates
    for s in range(8):
        dg_ref[s, pl.ds(j, 1), :] = jnp.sum(
            jnp.where(picks(s, j), dots[s * CAP : (s + 1) * CAP], 0.0), axis=0, keepdims=True
        )
    gw_ref[2] = mm(act, grad_res, TN).astype(BF16).reshape(32, 16, 1024)
    grad_act = mm(grad_res, wout_ref[0], NT)
    grad_up = (grad_act * silu).astype(BF16)
    grad_gate = (grad_act * up * sig * (1.0 + gating * (1.0 - sig))).astype(BF16)
    grad_gu = jnp.concatenate([grad_gate, grad_up], axis=1)
    grad_in = mm(received, grad_gu, TN).astype(BF16).reshape(32, 32, 1024)
    gw_ref[0] = grad_in[:, 0:16]
    gw_ref[1] = grad_in[:, 16:32]
    rows_scr[j] = mm(grad_gu, win_ref[0], NT)

    @pl.when(j == 3)
    def _():
        def store(s, carry):
            pick = jnp.concatenate([jnp.where(picks(s, e), 1.0, 0.0) for e in range(4)], axis=0).astype(BF16)
            rows = pl.ds(pl.multiple_of(s * CAP, 8), CAP)
            weighted = jnp.concatenate([grad_scr[e, rows, :] for e in range(4)], axis=0).astype(BF16)
            y_ref[s] = mm(pick, weighted, TN).astype(BF16)
            back = jnp.concatenate([rows_scr[e, rows, :] for e in range(4)], axis=0).astype(BF16)
            d_ref[s] = mm(pick, back, TN).astype(BF16)
            dg_ref[s, 4:8, :] = jnp.zeros((4, TOK), F32)
            return carry

        lax.fori_loop(0, 8, store, 0)


def each_slab(lead, work):
    count = 1
    for size in lead:
        count *= size

    def each(i, carry):
        work((i,) if len(lead) == 1 else (i // lead[1], i % lead[1]))
        return carry

    lax.fori_loop(0, count, each, 0)


class Arc:
    def __init__(self, n, pos, own, half, slots, devices, send, recv):
        self.n, self.pos, self.own, self.half, self.slots = n, pos, own, half, slots
        self.devices, self.send, self.recv = devices, send, recv
        self.steps = n // 2

    def chunk(self, way, s):
        reach = self.steps - s + 1
        return (self.pos + reach) % self.n if way == 0 else (self.pos + self.n - reach) % self.n

    def copy(self, way, s):
        dst = self.slots.at[way, s - 1]
        src = self.own(self.chunk(way, s)) if s == 1 else self.slots.at[way, s - 2]
        if s == 1:
            src, dst = self.half(src, way), self.half(dst, way)
        return remote(src, dst, self.send.at[way, s - 1], self.recv.at[way, s - 1], self.devices[way])

    def start(self):
        for way in (0, 1):
            self.copy(way, 1).start()

    def slabs(self, work):
        each_slab(self.slots.shape[2:-2], work)

    def advance(self, s):
        for way in (0, 1):
            self.copy(way, s - 1).wait_recv()
            held, own = self.slots.at[way, s - 2], self.own(self.chunk(way, s))
            if s == 2:
                self.merge(way, held, own)
            else:

                def add(index):
                    held[index] = (held[index].astype(F32) + own[index].astype(F32)).astype(BF16)

                self.slabs(add)
            self.copy(way, s).start()

    def merge(self, way, held, own):
        mine, its = self.half(held, way), self.half(own, way)
        other, from_own = self.half(held, 1 - way), self.half(own, 1 - way)

        def add(index):
            mine[index] = (mine[index].astype(F32) + its[index].astype(F32)).astype(BF16)

        def take(index):
            other[index] = from_own[index]

        each_slab(mine.shape[:-2], add)
        each_slab(other.shape[:-2], take)

    def finish(self, put):
        for way in (0, 1):
            self.copy(way, self.steps).wait_recv()
        own, up, down = self.own(self.pos), self.slots.at[0, self.steps - 1], self.slots.at[1, self.steps - 1]

        def add(index):
            put(index, own[index].astype(F32) + up[index].astype(F32) + down[index].astype(F32))

        self.slabs(add)

    def sent(self):
        for way in (0, 1):
            for s in range(1, self.steps + 1):
                self.copy(way, s).wait_send()


class Torus:
    def __init__(self, place):
        self.dp, self.ep, self.ctx = place
        self.zh, self.x = self.dp // 4, self.dp % 4
        self.z = self.zh * 4 + self.ctx

    def at_x(self, v):
        return (self.zh * 4 + v % 4, self.ep, self.ctx)

    def at_z(self, v):
        v = v % 8
        return ((v // 4) * 4 + self.x, self.ep, v % 4)

    def x_ways(self):
        return self.at_x(self.x + 1), self.at_x(self.x + 3)

    def z_ways(self):
        return self.at_z(self.z + 1), self.at_z(self.z + 7)

    def x_arc(self, own, half, slots, send, recv):
        return Arc(4, self.x, own, half, slots, self.x_ways(), send, recv)

    def z_arc(self, own, half, slots, send, recv):
        return Arc(8, self.z, own, half, slots, self.z_ways(), send, recv)


def first_or_last(sizes):
    def half(view, h):
        return view.at[pl.ds(0, sizes[0])] if h == 0 else view.at[pl.ds(sizes[0], sizes[1])]

    return half


X_UNITS, Z_UNITS = (0, 1, 2, 3, 4, 5, 6, 7), (9, 10, 11, 8)


def unit_arcs(torus, own, x_units, z_units, x_slots, z_slots, xs, xr, zs, zr):
    xa = [
        torus.x_arc(
            lambda t, i=i: own.at[i, :, t], first_or_last((1, 1)), x_slots.at[i], xs.at[i], xr.at[i]
        )
        for i in range(len(x_units))
    ]
    za = [
        torus.z_arc(
            lambda t, i=i: own.at[len(x_units) + i, t // 4, :, t % 4], first_or_last((2, 2)), z_slots.at[i], zs.at[i], zr.at[i]
        )
        for i in range(len(z_units))
    ]
    return xa, za


class Direct:
    def __init__(self, torus, part, x_slots, result, z_slots, send, recv):
        self.t, self.part, self.x_slots, self.result, self.z_slots = torus, part, x_slots, result, z_slots
        self.send, self.recv = send, recv

    def x_copy(self, r):
        to = (self.t.x + r) % 4
        return remote(
            self.part.at[:, to], self.x_slots.at[r - 1], self.send.at[r], self.recv.at[r], self.t.at_x(to)
        )

    def z_copy(self, r):
        to = (self.t.z + r) % 8
        return remote(
            self.result.at[to], self.z_slots.at[r - 1], self.send.at[3 + r], self.recv.at[3 + r], self.t.at_z(to)
        )

    def start(self):
        for r in (2, 1, 3):
            self.x_copy(r).start()

    def turn(self):
        for r in (1, 2, 3):
            self.x_copy(r).wait_recv()

        def add(i, carry):
            h, l = i // 4, i % 4
            value = self.part[h, self.t.x, l].astype(F32)
            for r in range(3):
                value = value + self.x_slots[r, h, l].astype(F32)
            self.result[i] = value.astype(BF16)
            return carry

        lax.fori_loop(0, 8, add, 0)
        for r in (4, 3, 5, 2, 6, 1, 7):
            self.z_copy(r).start()

    def finish(self):
        for r in range(1, 8):
            self.z_copy(r).wait_recv()
        value = self.result[self.t.z].astype(F32)
        for r in range(7):
            value = value + self.z_slots[r].astype(F32)
        return value

    def sent(self):
        for r in (1, 2, 3):
            self.x_copy(r).wait_send()
        for r in range(1, 8):
            self.z_copy(r).wait_send()


def prepare_queries(j, ctx, start_ref, q_ref, lse_ref, both, stack, rows):
    lane = lax.broadcasted_iota(jnp.int32, (256, 128), 1)
    start_row, place_row = query_rows(j, ctx, start_ref)
    q_blk = q_ref[j]
    zero = jnp.zeros((HD, 256), BF16)
    both[j, 0:HD, 0:256] = heads_wide(turned(q_blk))
    both[j, HD:128, 0:256] = zero
    both[j, 0:HD, 256:512] = zero
    q_f = q_blk.astype(F32)
    q_rows = jnp.concatenate([q_f, pltpu.roll(q_f, HD, 1)], axis=0)
    stack[j, 0:256] = jnp.where(lane < HD, q_rows, 0.0).astype(BF16)
    rows[j, 0:1, :] = lse_ref[j, 0:1, :]
    rows[j, 2:3, :] = start_row
    rows[j, 3:4, :] = place_row


def prepare_grads(j, attT_ref, gm_ref, w_ref, both, stack, rows):
    lane = lax.broadcasted_iota(jnp.int32, (256, 128), 1)
    tall = mm(w_ref[...], gm_ref[j], NT).astype(BF16).astype(F32)
    rows[j, 1:2, :] = jnp.sum(heads_wide(tall) * heads_wide(attT_ref[j]), axis=0, keepdims=True)
    both[j, HD:128, 256:512] = heads_wide(tall).astype(BF16)
    g_f = tall.T
    g_rows = jnp.concatenate([pltpu.roll(g_f, HD, 1), g_f], axis=0)
    stack[j, 256:512] = jnp.where(lane < HD, 0.0, g_rows).astype(BF16)


def attend_pair(m, j, kv, kT, both, stack, rows):
    row = rows[j]
    chunk = slice(m * CHUNK, (m + 1) * CHUNK)
    pair = mm(kv[chunk, :], both[j])
    keys = (lax.broadcasted_iota(jnp.int32, (CHUNK, 256), 0) + m * CHUNK).astype(F32)
    allowed = keys >= row[2:3]
    if j == m:
        allowed = allowed & (keys <= row[3:4])
    probs = jnp.exp(jnp.where(allowed, pair[:, :256], MASKED) - row[0:1])
    grad = (probs * (pair[:, 256:] - row[1:2])).astype(BF16)
    return mm(jnp.concatenate([grad, probs.astype(BF16)], axis=1), stack[j]), mm(kT[:, chunk], grad)


def tail_kernel(
    dg_ref, gates_ref, gain_two_ref, wr_ref, x_ref, gain_one_ref, ca_ref, sa_ref, cb_ref, sb_ref, start_ref, lse_ref,
    back_hbm, nf_hbm, res_hbm, og_hbm, q_hbm, kv_hbm, attT_hbm, wp_hbm, y_hbm, nall_hbm, wq_hbm, wk_hbm, wv_hbm, gw_hbm,
    out_ref, ing_ref, gin_ref, gout_ref, gq_ref, gk_ref, gv_ref, gside_ref, gproj_out, gains_ref,
    back, nf, res, og, q_ref, kv, attT, wp, y_part, wq, wk, wv, own,
    dbuf, cbuf, fbuf, gbuf, cbuf2, fbuf2, gbuf2, gm, gres,
    kT, both, stack, rows, dqs, dkv, dqb, dkvb, kbuf, qpieces, kpieces,
    x_slots, z_slots, g0_slots, g1_slots, h0_slots, h1_slots, rx0, rx1, rz0, rz1,
    early, late_q, late_k, e_x, e_res, e_z, q_x, q_res, q_z, k_x, k_res, k_z,
    gain_own, gain_e, gain_x, gain_z, fin, rq, rp,
    fsem, usem, csend, crecv, c2send, c2recv, dsend, drecv, msend, mrecv, ksend, krecv, qsend, qrecv, psend, precv,
    xs, xr, zs, zr, g0s, g0r, g1s, g1r, h0s, h0r, h1s, h1r, es, er, lqs, lqr, lks, lkr, gs, gr,
    fsend, frecv, hsend, hrecv,
):
    place = where_am_i()
    dp, ep, ctx = place
    torus = Torus(place)
    nall = back
    sources = dict(
        back=(back_hbm, back), nf=(nf_hbm.at[ep], nf), res=(res_hbm, res), og=(og_hbm, og), q=(q_hbm, q_ref),
        kv=(kv_hbm, kv), attT=(attT_hbm, attT), wp=(wp_hbm.at[pl.ds(pl.multiple_of(ep * 128, 128), 128)], wp), y=(y_hbm, y_part),
        nall=(nall_hbm, nall), wq=(wq_hbm, wq), wk=(wk_hbm, wk), wv=(wv_hbm, wv),
    )
    loads = {
        name: pltpu.make_async_copy(src, dst, fsem.at[i]) for i, (name, (src, dst)) in enumerate(sources.items())
    }
    units = {u: pltpu.make_async_copy(gw_hbm.at[u], own.at[i], usem.at[i]) for i, u in enumerate(X_UNITS + Z_UNITS)}
    loads["back"].start()
    for u in (0, 9, 1, 10, 2, 11, 3):
        units[u].start()
    for name in ("nf", "res", "og", "kv", "q", "attT", "wp"):
        loads[name].start()
    for u in (4, 5, 6, 7, 8):
        units[u].start()
    for name in ("y", "wq", "wk", "wv"):
        loads[name].start()

    def send_to(g, h):
        return (dp, 2 * ctx + g // 2, 2 * (g % 2) + h), (ep, 2 * ctx + g // 2, 2 * (g % 2) + h)

    def is_me(device):
        return (device[0] == dp) & (device[1] == ep) & (device[2] == ctx)

    barrier = pltpu.get_barrier_semaphore()
    for r in range(1, 8):
        greet(barrier, (dp, (ep + r) % 8, ctx))
        greet(barrier, torus.at_z(torus.z + r))
    for r in range(1, 4):
        greet(barrier, torus.at_x(torus.x + r))
    for i in range(8):
        for device in ((dp, i, ep // 2), (i, dp, ep // 2)):

            @pl.when(jnp.logical_not(is_me(device)))
            def _():
                greet(barrier, device)

    waits = 17
    for g in range(4):
        for h in range(2):
            for device in send_to(g, h):
                waits = waits + jnp.where(is_me(device), 0, 1)
    pl.semaphore_wait(barrier, waits)

    xa, za = unit_arcs(torus, own, X_UNITS, Z_UNITS, x_slots, z_slots, xs, xr, zs, zr)
    g0 = torus.z_arc(lambda t: rx0.at[t], first_or_last((2, 2)), g0_slots, g0s, g0r)
    g1 = torus.z_arc(lambda t: rx1.at[t], first_or_last((2, 2)), g1_slots, g1s, g1r)
    h0 = torus.x_arc(lambda t: rz0.at[t], first_or_last((1, 2)), h0_slots, h0s, h0r)
    h1 = torus.x_arc(lambda t: rz1.at[t], first_or_last((1, 1)), h1_slots, h1s, h1r)

    def finish_x(i):
        target = rx0 if i < 4 else rx1

        def put(index, value):
            target[index[0] * 4 + index[1], i % 4] = value.astype(BF16)

        xa[i].finish(put)

    def finish_z(i):
        def put(index, value):
            if i < 3:
                rz0[index[0], i] = value.astype(BF16)
            else:
                for h in (0, 1):
                    rz1[index[0], h] = value[:, 512 * h : 512 * h + 512].astype(BF16)

        za[i].finish(put)

    total = EpScatterSum(back, cbuf, fbuf, gbuf, csend, crecv, place)
    loads["back"].wait()
    total.start()
    exchange(dg_ref, dbuf, dsend, drecv, place, False)
    dbuf[ep] = dg_ref[ep]
    for i in range(4):
        units[X_UNITS[i]].wait()
        xa[i].start()
        if i < 3:
            units[Z_UNITS[i]].wait()
            za[i].start()
    total.far()
    za[0].advance(2)
    xa[0].advance(2)
    za[1].advance(2)
    total.near()
    xa[1].advance(2)
    za[2].advance(2)
    exchange(dg_ref, dbuf, dsend, drecv, place, True)
    for name in ("nf", "res", "og"):
        loads[name].wait()
    gates = gates_ref[...]
    grad_gates = jnp.concatenate([dbuf[p] for p in range(8)], axis=0)
    grad_logits = gates * (grad_gates - jnp.sum(gates * grad_gates, axis=0, keepdims=True))
    high = grad_logits.astype(BF16)
    low = (grad_logits - high.astype(F32)).astype(BF16)
    from_router = mm(high, wr_ref[...], TN) + mm(low, wr_ref[...], TN)
    resid = res[...]
    scale = lax.rsqrt(jnp.mean(resid * resid, axis=-1, keepdims=True) + EPSILON)
    scaled = resid * scale
    za[0].advance(3)
    xa[2].advance(2)
    za[1].advance(3)
    grad_normed = total.last() + from_router
    gain_two = jnp.sum(grad_normed * scaled, axis=0, keepdims=True)
    grad_normed = grad_normed * gain_two_ref[...]
    mean = jnp.mean(grad_normed * scaled, axis=-1, keepdims=True)
    grad_res = og[...].astype(F32) + scale * (grad_normed - scaled * mean)
    gm[ep] = grad_res.astype(BF16)
    gather = EpGather(gm, msend, mrecv, place)
    gather.go(0, 1, 3, 2, 4)
    gres[...] = grad_res
    for t in range(8):
        gain_own[0, 8 + t : 9 + t, :] = gain_two[:, 128 * t : 128 * t + 128]
    xa[3].advance(2)
    za[2].advance(3)

    for name in ("kv", "q"):
        loads[name].wait()
    for chunk in range(4):
        part = kv[chunk * CHUNK : (chunk + 1) * CHUNK, :].astype(F32).T
        kT[:, chunk * CHUNK : (chunk + 1) * CHUNK] = part[:HD].astype(BF16)
    gather.got(1)
    gather.go(5, 6)
    gather.got(3)
    gather.go(7, 8)
    za[0].advance(4)
    for chunk in range(4, 8):
        part = kv[chunk * CHUNK : (chunk + 1) * CHUNK, :].astype(F32).T
        kT[:, chunk * CHUNK : (chunk + 1) * CHUNK] = part[:HD].astype(BF16)
    gather.got(2)
    gather.go(9)
    gather.got(4)
    gather.go(10)
    za[1].advance(4)
    for j in range(8):
        prepare_queries(j, ctx, start_ref, q_ref, lse_ref, both, stack, rows)
    gather.got(5)
    gather.go(11)
    gather.got(7)
    gather.go(12)
    za[2].advance(4)
    to = lax.broadcasted_iota(jnp.int32, (32, 64), 0)
    source = lax.broadcasted_iota(jnp.int32, (32, 64), 1)
    squeeze = jnp.where(source == (to // 4) * 8 + to % 4, 1.0, 0.0).astype(BF16)
    grad_router = mm(mm(squeeze, high).astype(BF16), nf[...]) + mm(mm(squeeze, low).astype(BF16), nf[...])
    side = jnp.concatenate([grad_router, jnp.zeros((96, 1024), F32)], axis=0)
    for d in range(8):
        tile = side[:, d * 128 : (d + 1) * 128].T.astype(BF16)
        for c in range(4):
            early[d // 4, d % 4, c, :, 128:256] = tile[32 * c : 32 * c + 32]
    for i in range(4, 8):
        units[X_UNITS[i]].wait()
        xa[i].start()
    for name in ("attT", "wp"):
        loads[name].wait()
    gather.got(0, 6, 8, 9, 10, 11, 12)

    total.sent()
    loads["nall"].start()
    results = EpScatterSum(y_part, cbuf2, fbuf2, gbuf2, c2send, c2recv, place)
    loads["y"].wait()
    results.start()
    for j in range(8):
        prepare_grads(j, attT, gm, wp, both, stack, rows)
    grad_proj = mm(attT[0].astype(BF16), gm[0])
    for j in range(1, 8):
        grad_proj = grad_proj + mm(attT[j].astype(BF16), gm[j])
    grad_proj = grad_proj.astype(BF16)
    for d in range(8):
        for c in range(4):
            early[d // 4, d % 4, c, :, 0:128] = grad_proj[32 * c : 32 * c + 32, 128 * d : 128 * d + 128]
    sums_early = Direct(torus, early, e_x, e_res, e_z, es, er)
    sums_q = Direct(torus, late_q, q_x, q_res, q_z, lqs, lqr)
    sums_k = Direct(torus, late_k, k_x, k_res, k_z, lks, lkr)
    sums_early.start()

    lane = lax.broadcasted_iota(jnp.int32, (TOK, 128), 1)

    @pl.when(ctx == 0)
    def _():
        kbuf[0, :, 0] = jnp.zeros((8, TOK, 128), BF16)

    @pl.when(ctx == 3)
    def _():
        kbuf[1, :, 3] = jnp.zeros((8, TOK, 128), BF16)

    def sum_copy(way, c, m):
        shards = pl.ds(c + 1, 3 - c) if way == 0 else pl.ds(0, c)
        edge = c == (0 if way == 0 else 3)
        src = dkv.at[m, shards] if edge else kbuf.at[way, m, shards]
        to = (dp, ep, c + 1 if way == 0 else c - 1)
        return remote(src, kbuf.at[way, m, shards], ksend.at[way, m], krecv.at[way, m], to)

    def sum_got(way, c, m):
        shards = pl.ds(c, 4 - c) if way == 0 else pl.ds(0, c + 1)
        v = kbuf.at[way, m, shards]
        remote(v, v, ksend.at[way, m], krecv.at[way, m], (dp, ep, c)).wait_recv()

    def pass_on(way, c, m):
        sum_got(way, c, m)
        for shard in range(c + 1, 4) if way == 0 else range(c):
            kbuf[way, m, shard] = (kbuf[way, m, shard].astype(F32) + dkv[m, shard].astype(F32)).astype(BF16)
        sum_copy(way, c, m).start()

    def hop_one(m):
        @pl.when(ctx == 0)
        def _():
            sum_copy(0, 0, m).start()

        @pl.when(ctx == 3)
        def _():
            sum_copy(1, 3, m).start()

    def hop_two(m):
        @pl.when(ctx == 1)
        def _():
            pass_on(0, 1, m)

        @pl.when(ctx == 2)
        def _():
            pass_on(1, 2, m)

    def hop_three(m):
        @pl.when(ctx == 2)
        def _():
            pass_on(0, 2, m)

        @pl.when(ctx == 1)
        def _():
            pass_on(1, 1, m)

    def piece_copy(src, dst, send, recv, m):
        return remote(src.at[m], dst.at[ep], send.at[m], recv.at[ep], (dp, m, ctx))

    def piece_go(src, dst, send, recv, m):
        @pl.when(ep != m)
        def _():
            piece_copy(src, dst, send, recv, m).start()

        @pl.when(ep == m)
        def _():
            dst[ep] = src[m]

    def pieces_got(src, dst, send, recv):
        for p in range(8):

            @pl.when(ep != p)
            def _():
                remote(src.at[p], dst.at[p], send.at[p], recv.at[p], (dp, p, ctx)).wait_recv()

    def pieces_sent(src, dst, send, recv):
        for p in range(8):

            @pl.when(ep != p)
            def _():
                piece_copy(src, dst, send, recv, p).wait_send()

    def hop_four(m):
        @pl.when(ctx == 3)
        def _():
            sum_got(0, 3, m)

        @pl.when(ctx == 0)
        def _():
            sum_got(1, 0, m)

        grad = dkv[m, ctx].astype(F32) + kbuf[0, m, ctx].astype(F32) + kbuf[1, m, ctx].astype(F32)
        cosine, sine = rope_block(4 * m + ctx, ca_ref, sa_ref, cb_ref, sb_ref)
        cosine = jnp.where(lane < HD, cosine, 1.0)
        sine = jnp.where(lane < HD, sine, 0.0)
        dkvb[m] = (grad * cosine - rotate_half(grad) * sine).astype(BF16)
        piece_go(dkvb, kpieces, psend, precv, m)

    def progress(m):
        if m == 0:
            finish_x(0)
            finish_z(0)
            results.far()
        elif m == 1:
            xa[4].advance(2)
            finish_z(1)
            finish_z(2)
            results.near()
        elif m == 2:
            xa[5].advance(2)
            finish_x(1)
            h0.start()
        elif m == 3:
            xa[6].advance(2)
            finish_x(2)
            finish_x(3)
            sums_early.turn()
        elif m == 4:
            xa[7].advance(2)
            h0.advance(2)
            out_ref[...] = (res[...] + results.last()).astype(BF16)

    for m in range(8):
        keys_grad = None
        for j in range(m, 8):
            both_grads, query_grad = attend_pair(m, j, kv, kT, both, stack, rows)
            keys_grad = both_grads if keys_grad is None else keys_grad + both_grads
            dqs[j] = query_grad if m == 0 else dqs[j] + query_grad
        dkv[m] = keys_grad.astype(BF16).reshape(4, TOK, 128)
        hop_one(m)
        dq = dqs[m] * (HD**-0.5)
        dq = jnp.concatenate([dq[:, :128], dq[:, 128:]], axis=0).T
        cosine, sine = rope_block(4 * m + ctx, ca_ref, sa_ref, cb_ref, sb_ref)
        dqb[m] = (dq * cosine - rotate_half(dq) * sine).astype(BF16)
        piece_go(dqb, qpieces, qsend, qrecv, m)
        if m >= 1:
            hop_two(m - 1)
        if m >= 2:
            hop_three(m - 2)
        if m >= 3:
            hop_four(m - 3)
        progress(m)

    hop_two(7)
    hop_three(6)
    hop_four(5)
    g0.start()
    units[8].wait()
    za[3].start()
    for name in ("nall", "wq"):
        loads[name].wait()

    def weights(grad, late):
        out = mm(nall[...].reshape(1024, 1024), grad.reshape(1024, 128), TN).astype(BF16)
        for d in range(8):
            for c in range(4):
                at = d * 128 + c * 32
                late[d // 4, d % 4, c] = out[at : at + 32]

    weights(dqb[...], late_q)
    sums_q.start()
    hop_three(7)
    hop_four(6)
    pieces_got(dqb, qpieces, qsend, qrecv)
    grad_q = jnp.concatenate([qpieces[p] for p in range(8)], axis=1)
    grad_normed = mm(grad_q, wq[...], NT)
    g0.advance(2)
    za[3].advance(2)
    hop_four(7)
    weights(dkvb[...], late_k)
    sums_k.start()
    g0.advance(3)
    za[3].advance(3)
    for name in ("wk", "wv"):
        loads[name].wait()
    pieces_got(dkvb, kpieces, psend, precv)
    grad_k = jnp.concatenate([kpieces[p, :, 0:HD] for p in range(8)], axis=1)
    grad_v = jnp.concatenate([kpieces[p, :, HD:128] for p in range(8)], axis=1)
    grad_normed = grad_normed + mm(grad_k, wk[...], NT) + mm(grad_v, wv[...], NT)
    x = x_ref[...].astype(F32)
    scale = lax.rsqrt(jnp.mean(x * x, axis=-1, keepdims=True) + EPSILON)
    scaled = x * scale
    gain_one = jnp.sum(grad_normed * scaled, axis=0, keepdims=True)
    for t in range(8):
        gain_own[0, t : t + 1, :] = gain_one[:, 128 * t : 128 * t + 128]

    def gain_copy(stage, r):
        src = gain_own.at[stage]
        if stage == 0:
            dst, device, base = gain_e.at[r - 1], (dp, (ep + r) % 8, ctx), 0
        elif stage == 1:
            dst, device, base = gain_x.at[r - 1], torus.at_x(torus.x + r), 7
        else:
            dst, device, base = gain_z.at[r - 1], torus.at_z(torus.z + r), 10
        return remote(src, dst, gs.at[base + r], gr.at[base + r], device)

    def gain_stage(stage, count):
        if stage > 0:
            last, slots = ((7, gain_e), (3, gain_x), (7, gain_z))[stage - 1]
            value = gain_own[stage - 1]
            for r in range(1, last + 1):
                gain_copy(stage - 1, r).wait_recv()
                value = value + slots[r - 1]
            gain_own[stage] = value
        for r in range(1, count + 1):
            gain_copy(stage, r).start()

    gain_stage(0, 7)
    grad_normed = grad_normed * gain_one_ref[...]
    mean = jnp.mean(grad_normed * scaled, axis=-1, keepdims=True)
    ing_ref[...] = (gres[...] + scale * (grad_normed - scaled * mean)).astype(BF16)

    sums_q.turn()
    gain_stage(1, 3)
    sums_k.turn()
    g0.advance(4)
    za[3].advance(4)
    for i in range(4, 8):
        finish_x(i)
    g1.start()
    gain_stage(2, 7)

    def piece(g, h, kind, device):
        index = g * 2 + h
        if kind == 0:
            return remote(fin.at[g, :, pl.ds(0, 384)], rq.at[ep], fsend.at[index], frecv.at[ep], device)
        return remote(fin.at[g, :, pl.ds(384, 128)], rp.at[dp], hsend.at[index], hrecv.at[dp], device)

    def each_piece(act, local):
        for g in range(4):
            for h in range(2):
                for kind in (0, 1):
                    device = send_to(g, h)[kind]

                    @pl.when(jnp.logical_not(is_me(device)))
                    def _():
                        act(piece(g, h, kind, device))

                    if local:

                        @pl.when(is_me(device))
                        def _():
                            if kind == 0:
                                rq[ep] = fin[g, :, 0:384]
                            else:
                                rp[dp] = fin[g, :, 384:512]

    done_early, done_q, done_k = sums_early.finish(), sums_q.finish(), sums_k.finish()
    for g in range(4):
        at = slice(8 * g, 8 * g + 8)
        fin[g, :, 0:128] = done_q[at]
        fin[g, :, 128:256] = done_k[at]
        fin[g, :, 256:384] = done_early[at, 128:256]
        fin[g, :, 384:512] = done_early[at, 0:128]
    each_piece(lambda c: c.start(), True)

    g1.advance(2)

    def put_unit(unit, value):
        j, u = unit // 3, unit % 3
        if u < 2:
            gin_ref[j, 16 * u : 16 * u + 16, :] = value
        else:
            gout_ref[j] = value

    def finish_units(arc, units):
        for way in (0, 1):
            arc.copy(way, arc.steps).wait_recv()
        mine = arc.own(arc.pos)
        up, down = arc.slots.at[0, arc.steps - 1], arc.slots.at[1, arc.steps - 1]
        for i, unit in enumerate(units):
            put_unit(unit, mine[i].astype(F32) + up[i].astype(F32) + down[i].astype(F32))

    finish_units(h0, Z_UNITS[:3])
    finish_z(3)
    h1.start()
    g1.advance(3)
    finish_units(g0, X_UNITS[:4])
    h1.advance(2)
    g1.advance(4)
    last = gain_own[2]
    for r in range(1, 8):
        gain_copy(2, r).wait_recv()
        last = last + gain_z[r - 1]
    gain_own[3] = last

    for i in range(8):
        for kind, device in enumerate(((dp, i, ep // 2), (i, dp, ep // 2))):

            @pl.when(jnp.logical_not(is_me(device)))
            def _():
                if kind == 0:
                    src, dst, pair = fin.at[0, :, pl.ds(0, 384)], rq.at[i], (fsend.at[0], frecv.at[i])
                else:
                    src, dst, pair = fin.at[0, :, pl.ds(384, 128)], rp.at[i], (hsend.at[0], hrecv.at[i])
                remote(src, dst, pair[0], pair[1], device).wait_recv()

    odd = ctx % 2 == 1

    def mine(v):
        return jnp.where(odd, v[4:8], v[0:4])

    gq_ref[...] = mine(jnp.concatenate([rq[i, :, 0:128] for i in range(8)], axis=1))
    gk_ref[...] = mine(jnp.concatenate([rq[i, :, 128:192] for i in range(8)], axis=1))
    gv_ref[...] = mine(jnp.concatenate([rq[i, :, 192:256] for i in range(8)], axis=1))
    side = rq[0, :, 256:384]
    for i in range(1, 8):
        side = side + rq[i, :, 256:384]
    gside_ref[...] = mine(side)
    gproj_out[...] = mine(jnp.concatenate([rp[i] for i in range(8)], axis=1))
    for which in (0, 1):
        row = jnp.broadcast_to(gain_own[3, pl.ds(8 * which + dp, 1), :], (8, 128))
        gains_ref[8 * which : 8 * which + 8, :] = pltpu.roll(row, (128 - 16 * ep - 4 * ctx) % 128, 1)

    for way in (0, 1):
        h1.copy(way, 2).wait_recv()
    for h in (0, 1):
        value = rz1[torus.x, h].astype(F32) + h1_slots[0, 1, h].astype(F32) + h1_slots[1, 1, h].astype(F32)
        gout_ref[2, :, 512 * h : 512 * h + 512] = value
    finish_units(g1, X_UNITS[4:])

    results.sent()
    gather.sent()
    exchange_sent(dg_ref, dbuf, dsend, drecv, place)
    pieces_sent(dqb, qpieces, qsend, qrecv)
    pieces_sent(dkvb, kpieces, psend, precv)
    for c in range(4):

        @pl.when(ctx == c)
        def _():
            for m in range(8):
                for way in (0, 1):
                    if (way == 0 and c < 3) or (way == 1 and c > 0):
                        sum_copy(way, c, m).wait_send()

    for arc in xa + za + [g0, g1, h0, h1]:
        arc.sent()
    for sums in (sums_early, sums_q, sums_k):
        sums.sent()
    for stage, count in ((0, 7), (1, 3), (2, 7)):
        for r in range(1, count + 1):
            gain_copy(stage, r).wait_send()
    each_piece(lambda c: c.wait_send(), False)


def pack_kernel(*refs):
    count = len(refs) // 2
    for src, dst in zip(refs[:count], refs[count:]):
        dst[...] = src[...]


def call(kernel, outs, scratch, args, name, collective=None, **more):
    params = dict(vmem_limit_bytes=VMEM_LIMIT)
    if collective is not None:
        params.update(collective_id=collective, has_side_effects=True)
    space = pl.BlockSpec(memory_space=pltpu.VMEM)
    return pl.pallas_call(
        kernel,
        out_shape=[jax.ShapeDtypeStruct(shape, kind) for shape, kind in outs],
        in_specs=more.pop("in_specs", [space] * len(args)),
        out_specs=more.pop("out_specs", [space] * len(outs)),
        scratch_shapes=scratch,
        compiler_params=pltpu.CompilerParams(**params),
        name=name,
        **more,
    )(*args)


def sems(*sizes):
    return [pltpu.SemaphoreType.DMA(s if isinstance(s, tuple) else (s,)) for s in sizes]


def body(
    layer_input, gain_attn, w_query, w_key, w_value, w_proj, gain_ffn, w_router,
    w_expert_in, w_expert_out, segment_ids, expert_ids, slot_order, out_grad,
):
    ep = lax.axis_index("ep")
    gain_one, gain_two = gain_attn.reshape(1, 1024), gain_ffn.reshape(1, 1024)
    tables = [jnp.asarray(t) for t in rope_tables()]
    w_own = jnp.concatenate(
        [
            lax.dynamic_slice_in_dim(w_query, ep * 128, 128, 1),
            lax.dynamic_slice_in_dim(w_key, ep * 64, 64, 1),
            lax.dynamic_slice_in_dim(w_value, ep * 64, 64, 1),
        ],
        axis=1,
    )
    wr_rows = jnp.pad(w_router.T.reshape(8, 4, 1024), ((0, 0), (0, 4), (0, 0))).reshape(64, 1024)
    order = slot_order.reshape(TOK, 8)
    docs = segment_ids.reshape(32, 128)

    normed_all, query, kv, grad_all, slots, chosen, starts = call(
        first_kernel,
        [
            ((8, TOK, 1024), BF16), ((8, TOK, 128), BF16), ((8, 4, TOK, 128), BF16), ((8, TOK, 1024), BF16),
            ((8, 8, TOK), F32), ((64, TOK), F32), ((32, 128), F32),
        ],
        [pltpu.VMEM((8, 8, TOK), F32)] + sems(13, 13, 13, 13, 8, 8, 24, 24),
        [layer_input, gain_one, out_grad, w_own, *tables, expert_ids, expert_ids.T, order, order.T, docs],
        "first", 1,
    )
    kv_rows = kv.reshape(4096, 128)
    ctx = lax.axis_index("ctx")
    first = lax.dynamic_slice_in_dim(starts.reshape(8, 4, 128), ctx, 1, 1)[:, 0, 0].astype(jnp.int32) // CHUNK

    vm, sm = pl.BlockSpec(memory_space=pltpu.VMEM), pl.BlockSpec(memory_space=pltpu.SMEM)
    attended, attended_tall, log_sums = call(
        attend_kernel,
        [((8, TOK, 128), BF16), ((8, 128, TOK), F32), ((8, 8, 256), F32)],
        [pltpu.VMEM((128, 4096), BF16)],
        [first, query, kv_rows, starts],
        "attend", in_specs=[sm, vm, vm, vm],
    )
    residual, ffn_all, gates_in, gates = call(
        middle_kernel,
        [((TOK, 1024), F32), ((8, TOK, 1024), BF16), ((8, 8, TOK), F32), ((64, TOK), F32)],
        [pltpu.VMEM((8, TOK, 128), BF16), pltpu.VMEM((8, 8, TOK), F32)] + sems(8, 8, 13, 13, 8, 8),
        [attended, layer_input, gain_two, w_proj, wr_rows, chosen],
        "middle", 2,
    )
    whole = lambda *shape: pl.BlockSpec(shape, lambda j: (0,) * len(shape))
    sums, back, grad_gates, grad_experts = call(
        expert_kernel,
        [((8, TOK, 1024), BF16), ((8, TOK, 1024), BF16), ((8, 8, TOK), F32), ((12, 32, 16, 1024), BF16)],
        [pltpu.VMEM((4, 8 * CAP, 1024), F32), pltpu.VMEM((4, 8 * CAP, 1024), F32)],
        [ffn_all, grad_all, slots, gates_in, w_expert_in, w_expert_out],
        "experts", grid=(4,),
        in_specs=[
            whole(8, TOK, 1024), whole(8, TOK, 1024), whole(8, 8, TOK), whole(8, 8, TOK),
            pl.BlockSpec((1, 1024, 1024), lambda j: (j, 0, 0)), pl.BlockSpec((1, 512, 1024), lambda j: (j, 0, 0)),
        ],
        out_specs=[
            whole(8, TOK, 1024), whole(8, TOK, 1024), whole(8, 8, TOK),
            pl.BlockSpec((3, 32, 16, 1024), lambda j: (j, 0, 0, 0)),
        ],
    )
    units = grad_experts.reshape(12, 2, 4, 4, 16, 1024)
    hbm = pl.BlockSpec(memory_space=pl.ANY)
    nx, nz = len(X_UNITS), len(Z_UNITS)
    block = pltpu.VMEM((8, TOK, 128), BF16)
    wide = pltpu.VMEM((8, TOK, 1024), BF16)

    def direct(lanes):
        return [
            pltpu.VMEM((3, 2, 4, 32, lanes), BF16), pltpu.VMEM((8, 32, lanes), BF16), pltpu.VMEM((7, 32, lanes), BF16)
        ]

    results = call(
        tail_kernel,
        [
            ((TOK, 1024), BF16), ((TOK, 1024), BF16), ((4, 32, 1024), F32), ((4, 16, 1024), F32), ((4, 1024), F32),
            ((4, 512), F32), ((4, 512), F32), ((4, 128), F32), ((4, 1024), F32), ((16, 128), F32),
        ],
        [
            wide, pltpu.VMEM((TOK, 1024), BF16), pltpu.VMEM((TOK, 1024), F32), pltpu.VMEM((TOK, 1024), BF16), block,
            pltpu.VMEM((4096, 128), BF16), pltpu.VMEM((8, 128, TOK), F32), pltpu.VMEM((128, 1024), BF16), wide,
            pltpu.VMEM((1024, 1024), BF16), pltpu.VMEM((1024, 512), BF16), pltpu.VMEM((1024, 512), BF16),
            pltpu.VMEM((nx + nz, 2, 4, 4, 16, 1024), BF16),
            pltpu.VMEM((8, 8, TOK), F32),
        ]
        + scatter_sum_scratch()[:3] * 2
        + [
            wide, pltpu.VMEM((TOK, 1024), F32),
            pltpu.VMEM((HD, 4096), BF16), pltpu.VMEM((8, 128, 512), BF16), pltpu.VMEM((8, 512, 128), BF16),
            pltpu.VMEM((8, 8, 256), F32), pltpu.VMEM((8, HD, 256), F32), pltpu.VMEM((8, 4, TOK, 128), BF16),
            block, block, pltpu.VMEM((2, 8, 4, TOK, 128), BF16), block, block,
            pltpu.VMEM((nx, 2, 2, 2, 4, 16, 1024), BF16), pltpu.VMEM((nz, 2, 4, 4, 16, 1024), BF16),
            pltpu.VMEM((2, 4, 4, 16, 1024), BF16), pltpu.VMEM((2, 4, 4, 16, 1024), BF16),
            pltpu.VMEM((2, 2, 3, 16, 1024), BF16), pltpu.VMEM((2, 2, 2, 16, 512), BF16),
            pltpu.VMEM((8, 4, 16, 1024), BF16), pltpu.VMEM((8, 4, 16, 1024), BF16),
            pltpu.VMEM((4, 3, 16, 1024), BF16), pltpu.VMEM((4, 2, 16, 512), BF16),
            pltpu.VMEM((2, 4, 4, 32, 256), BF16), pltpu.VMEM((2, 4, 4, 32, 128), BF16), pltpu.VMEM((2, 4, 4, 32, 128), BF16),
        ]
        + direct(256) + direct(128) + direct(128)
        + [
            pltpu.VMEM((4, 16, 128), F32), pltpu.VMEM((7, 16, 128), F32), pltpu.VMEM((3, 16, 128), F32),
            pltpu.VMEM((7, 16, 128), F32),
            pltpu.VMEM((4, 8, 512), F32), pltpu.VMEM((8, 8, 384), F32), pltpu.VMEM((8, 8, 128), F32),
        ]
        + sems(
            13, nx + nz, 8, 8, 8, 8, 8, 8, 13, 13, (2, 8), (2, 8), 8, 8, 8, 8,
            (nx, 2, 2), (nx, 2, 2), (nz, 2, 4), (nz, 2, 4),
            (2, 4), (2, 4), (2, 4), (2, 4), (2, 2), (2, 2), (2, 2), (2, 2), 11, 11, 11, 11, 11, 11, 18, 18, 8, 8, 8, 8,
        ),
        [
            grad_gates, gates, gain_two, wr_rows, layer_input, gain_one, *tables, starts, log_sums,
            back, ffn_all, residual, out_grad, query, kv_rows, attended_tall, w_proj, sums, normed_all,
            w_query, w_key, w_value, units,
        ],
        "tail", 3, in_specs=[vm] * 12 + [hbm] * 14,
    )
    layer_output, input_grad, grad_in, grad_out, out_q, out_k, out_v, side, out_proj, gains = call(
        pack_kernel, [(r.shape, r.dtype) for r in results], [], results, "pack"
    )
    return (
        layer_output, input_grad, gains[0, :4], out_q, out_k, out_v, out_proj, gains[8, :4], side[:, :32], grad_in, grad_out,
    )


def solution(mesh):
    tokens = P(("dp", "ep", "ctx"), None)
    in_specs = (
        tokens, P(), P(), P(), P(), P(), P(), P(),
        P("ep", None, None), P("ep", None, None), P("dp", None), tokens, tokens, tokens,
    )
    out_specs = (
        tokens, tokens, P(("dp", "ep", "ctx")), tokens, tokens, tokens, tokens, P(("dp", "ep", "ctx")), tokens,
        P("ep", ("dp", "ctx"), None), P("ep", ("dp", "ctx"), None),
    )
    return jax.shard_map(body, mesh=mesh, in_specs=in_specs, out_specs=out_specs, check_vma=False)
```

```python
from functools import partial

import jax
import jax.numpy as jnp
import numpy as np
from jax import lax
from jax.experimental import pallas as pl
from jax.experimental.pallas import tpu as pltpu
from jax.sharding import PartitionSpec as P

HD = 64
EPSILON = 1e-06
MASKED = -1e30
CAP = 40
TOK = 128
BIG = 4096.0
MESH = pl.DeviceIdType.MESH
F32 = jnp.float32
BF16 = jnp.bfloat16
VMEM_LIMIT = 60 * 1024 * 1024

NT = (((1,), (1,)), ((), ()))
NN = (((1,), (0,)), ((), ()))
TN = (((0,), (0,)), ((), ()))


def mm(a, b, dims=NN):
    return lax.dot_general(a, b, dims, preferred_element_type=F32)


def mm3(a, b, dims=NN):
    high = a.astype(BF16)
    low = (a - high.astype(F32)).astype(BF16)
    return mm(high, b, dims) + mm(low, b, dims)


def where_am_i():
    dp, ep, ctx = lax.axis_index("dp"), lax.axis_index("ep"), lax.axis_index("ctx")
    return dp, ep, ctx


def remote(src, dst, send, recv, device):
    return pltpu.make_async_remote_copy(
        src_ref=src, dst_ref=dst, send_sem=send, recv_sem=recv, device_id=device, device_id_type=MESH
    )


def greet(barrier, device):
    pl.semaphore_signal(barrier, inc=1, device_id=device, device_id_type=MESH)


def rotate_half(values):
    lane = lax.broadcasted_iota(jnp.int32, values.shape, 1)
    return jnp.where(lane % HD < HD // 2, pltpu.roll(values, 96, 1), pltpu.roll(values, 32, 1))


def rope_block(block, ca_ref, sa_ref, cb_ref, sb_ref):
    ca, sa = ca_ref[pl.ds(block, 1), :], sa_ref[pl.ds(block, 1), :]
    cb, sb = cb_ref[...], sb_ref[...]
    cosine = ca * cb - sa * sb
    sine = sa * cb + ca * sb
    lane = lax.broadcasted_iota(jnp.int32, cosine.shape, 1)
    return cosine, jnp.where(lane % HD < HD // 2, -sine, sine)


def rope_tables():
    frequency = 10000.0 ** (-np.arange(HD // 2, dtype=np.float64) * 2.0 / HD)
    frequency = np.tile(frequency.astype(np.float32).astype(np.float64), 4)
    blocks = np.arange(32, dtype=np.float64)[:, None] * 128.0 * frequency[None, :]
    rows = np.arange(128, dtype=np.float64)[:, None] * frequency[None, :]
    return [t.astype(np.float32) for t in (np.cos(blocks), np.sin(blocks), np.cos(rows), np.sin(rows))]


class EpGather:
    COUNT = 13

    def __init__(self, ref, send, recv, place):
        self.ref, self.send, self.recv = ref, send, recv
        dp, ep, ctx = place
        y, k = ep // 2, ep % 2
        self.up = (dp, ((y + 1) % 4) * 2 + k, ctx)
        self.dn = (dp, ((y + 3) % 4) * 2 + k, ctx)
        self.sib = (dp, y * 2 + 1 - k, ctx)

        def at(dy, other):
            return ((y + dy) % 4) * 2 + ((1 - k) if other else k)

        u, s, d = self.up, self.sib, self.dn
        self.sends = [
            (at(0, 0), None, s), (at(0, 0), 0, u), (at(0, 0), 1, u), (at(0, 0), 1, d), (at(0, 0), 0, d),
            (at(3, 0), 0, u), (at(3, 0), 0, s), (at(1, 0), 1, d), (at(1, 0), 1, s),
            (at(3, 0), 1, s), (at(1, 0), 0, s), (at(2, 0), 0, s), (at(2, 0), 1, s),
        ]
        self.gets = [
            (at(0, 1), None), (at(3, 0), 0), (at(3, 0), 1), (at(1, 0), 1), (at(1, 0), 0),
            (at(2, 0), 0), (at(3, 1), 0), (at(2, 0), 1), (at(1, 1), 1),
            (at(3, 1), 1), (at(1, 1), 0), (at(2, 1), 0), (at(2, 1), 1),
        ]

    def view(self, block, half):
        if half is None:
            return self.ref.at[block]
        rows = self.ref.shape[1] // 2
        return self.ref.at[block, pl.ds(half * rows, rows)]

    def go(self, *which):
        for i in which:
            block, half, device = self.sends[i]
            v = self.view(block, half)
            remote(v, v, self.send.at[i], self.recv.at[i], device).start()

    def got(self, *which):
        for i in which:
            v = self.view(*self.gets[i])
            remote(v, v, self.send.at[i], self.recv.at[i], self.sends[i][2]).wait_recv()

    def sent(self):
        for i in range(self.COUNT):
            block, half, device = self.sends[i]
            v = self.view(block, half)
            remote(v, v, self.send.at[i], self.recv.at[i], device).wait_send()

    def whole(self):
        self.got(1)
        self.go(5, 6)
        self.got(3)
        self.go(7, 8)
        self.got(2)
        self.go(9)
        self.got(4)
        self.go(10)
        self.got(5)
        self.go(11)
        self.got(7)
        self.go(12)
        self.got(0, 6, 8, 9, 10, 11, 12)


class EpScatterSum:
    COUNT = 8

    def __init__(self, part, cbuf, fbuf, gbuf, send, recv, place):
        self.part, self.cbuf, self.fbuf, self.gbuf = part, cbuf, fbuf, gbuf
        self.send, self.recv = send, recv
        dp, ep, ctx = place
        self.y, self.k = ep // 2, ep % 2
        y, k = self.y, self.k
        self.up = (dp, ((y + 1) % 4) * 2 + k, ctx)
        self.dn = (dp, ((y + 3) % 4) * 2 + k, ctx)
        self.sib = (dp, y * 2 + 1 - k, ctx)

    def block(self, dy, other=False):
        return ((self.y + dy) % 4) * 2 + ((1 - self.k) if other else self.k)

    def copy(self, i):
        half = self.cbuf.shape[1] // 2
        lo, hi = pl.ds(0, half), pl.ds(half, half)
        s, r = self.send, self.recv
        if i < 4:
            away = self.block((2, 1, 3, 0)[i], True)
            return remote(self.part.at[away], self.cbuf.at[i], s.at[i], r.at[i], self.sib)
        src, dst, device = (
            (self.cbuf.at[0, lo], self.fbuf.at[0], self.up),
            (self.cbuf.at[0, hi], self.fbuf.at[1], self.dn),
            (self.cbuf.at[1], self.gbuf.at[0], self.up),
            (self.cbuf.at[2], self.gbuf.at[1], self.dn),
        )[i - 4]
        return remote(src, dst, s.at[i], r.at[i], device)

    def start(self):
        for i in range(4):
            self.copy(i).start()

    def far(self):
        self.copy(0).wait_recv()
        self.cbuf[0] = (self.cbuf[0].astype(F32) + self.part[self.block(2)].astype(F32)).astype(BF16)
        self.copy(4).start()
        self.copy(5).start()

    def near(self):
        half = self.cbuf.shape[1] // 2
        for slot, dy, far, rows, rest in ((1, 1, 0, pl.ds(0, half), pl.ds(half, half)), (2, 3, 1, pl.ds(half, half), pl.ds(0, half))):
            b = self.block(dy)
            self.copy(slot).wait_recv()
            self.copy(4 + far).wait_recv()
            self.cbuf[slot, rows] = (
                self.cbuf[slot, rows].astype(F32) + self.part[b, rows].astype(F32) + self.fbuf[far].astype(F32)
            ).astype(BF16)
            self.cbuf[slot, rest] = (self.cbuf[slot, rest].astype(F32) + self.part[b, rest].astype(F32)).astype(BF16)
            self.copy(6 + far).start()

    def last(self):
        for i in (3, 6, 7):
            self.copy(i).wait_recv()
        return (
            self.part[self.block(0)].astype(F32) + self.cbuf[3].astype(F32)
            + self.gbuf[0].astype(F32) + self.gbuf[1].astype(F32)
        )

    def sent(self):
        for i in range(self.COUNT):
            self.copy(i).wait_send()


def scatter_sum_scratch():
    return [
        pltpu.VMEM((4, TOK, 1024), BF16),
        pltpu.VMEM((2, TOK // 2, 1024), BF16),
        pltpu.VMEM((2, TOK, 1024), BF16),
        pltpu.SemaphoreType.DMA((8,)),
        pltpu.SemaphoreType.DMA((8,)),
    ]


def repeat(first, last, work):
    def each(i, carry):
        work(i)
        return carry

    lax.fori_loop(first, last, each, 0)


def exchange(src, dst, send, recv, place, wait):
    dp, ep, ctx = place

    def one(r):
        to, source = (ep + r) % 8, (ep + 8 - r) % 8
        if not wait:
            remote(src.at[to], dst.at[ep], send.at[r], recv.at[r], (dp, to, ctx)).start()
        else:
            remote(src.at[to], dst.at[source], send.at[r], recv.at[r], (dp, to, ctx)).wait_recv()

    repeat(1, 8, one)


def exchange_sent(src, dst, send, recv, place):
    dp, ep, ctx = place

    def one(r):
        to = (ep + r) % 8
        remote(src.at[to], dst.at[ep], send.at[r], recv.at[r], (dp, to, ctx)).wait_send()

    repeat(1, 8, one)


def starts_of(docs):
    rows = lax.broadcasted_iota(jnp.int32, docs.shape, 0)
    lane = lax.broadcasted_iota(jnp.int32, docs.shape, 1)
    docs = docs.astype(F32)
    turned = pltpu.roll(docs, 1, 1)
    before = jnp.where(lane == 0, pltpu.roll(turned, 1, 0), turned)
    place = rows * 128 + lane
    fresh = (docs != before) | (place == 0)
    value = jnp.where(fresh, place.astype(F32), 0.0)
    for shift in (1, 2, 4, 8, 16, 32, 64):
        value = jnp.maximum(value, jnp.where(lane >= shift, pltpu.roll(value, shift, 1), 0.0))
    carry = jnp.broadcast_to(jnp.max(value, axis=1, keepdims=True), value.shape)
    for shift in (1, 2, 4, 8, 16):
        carry = jnp.maximum(carry, jnp.where(rows >= shift, pltpu.roll(carry, shift, 0), 0.0))
    above = jnp.where(rows >= 1, pltpu.roll(carry, 1, 0), 0.0)
    return jnp.maximum(value, above)


def slots_of(eid_ref, eidT_ref, so_ref, soT_ref, slot_scr, sel_ref):
    def expert(index):
        return jnp.where(index % 8 < 4, (index // 8) * 4 + index % 8, -1)

    row_expert = expert(lax.broadcasted_iota(jnp.int32, (64, TOK), 0))
    lane_expert = expert(lax.broadcasted_iota(jnp.int32, (TOK, 64), 1))
    by_row = jnp.full((64, TOK), BIG, F32)
    by_lane = jnp.full((TOK, 64), BIG, F32)
    for k in range(8):
        by_row = jnp.where(eidT_ref[k : k + 1, :] == row_expert, soT_ref[k : k + 1, :].astype(F32), by_row)
        by_lane = jnp.where(eid_ref[:, k : k + 1] == lane_expert, so_ref[:, k : k + 1].astype(F32), by_lane)
    sel_ref[...] = jnp.where(by_row < BIG, 1.0, 0.0)
    for g in range(8):
        for j in range(4):
            r = 8 * g + j
            row = by_row[r : r + 1, :]
            less = jnp.where(by_lane[:, r : r + 1] < row, 1.0, 0.0)
            rank = jnp.sum(less, axis=0, keepdims=True)
            slot_scr[g, j : j + 1, :] = jnp.where((row < BIG) & (rank < CAP), rank, -1.0)
        slot_scr[g, 4:8, :] = jnp.full((4, TOK), -1.0, F32)


def first_kernel(
    x_ref, gain_ref, og_ref, w_ref, ca_ref, sa_ref, cb_ref, sb_ref, eid_ref, eidT_ref, so_ref, soT_ref, doc_ref,
    nall_ref, q_ref, kv_ref, ogall_ref, slot_ref, sel_ref, start_ref,
    slot_scr, nsend, nrecv, osend, orecv, ssend, srecv, ksend, krecv,
):
    place = where_am_i()
    dp, ep, ctx = place
    y = ep // 2
    barrier = pltpu.get_barrier_semaphore()
    for r in range(1, 8):
        greet(barrier, (dp, (ep + r) % 8, ctx))

    @pl.when(ctx > 0)
    def _():
        greet(barrier, (dp, ep, ctx - 1))

    @pl.when(ctx < 3)
    def _():
        greet(barrier, (dp, ep, ctx + 1))

    x = x_ref[...].astype(F32)
    normed = x * lax.rsqrt(jnp.mean(x * x, axis=-1, keepdims=True) + EPSILON) * gain_ref[...]
    nall_ref[ep] = normed.astype(BF16)
    ogall_ref[ep] = og_ref[...]
    edges = jnp.where(ctx > 0, 1, 0) + jnp.where(ctx < 3, 1, 0)
    pl.semaphore_wait(barrier, 7 + edges)

    gather = EpGather(nall_ref, nsend, nrecv, place)
    grads = EpGather(ogall_ref, osend, orecv, place)
    gather.go(0, 1, 3, 2, 4)

    start_ref[...] = starts_of(doc_ref[...])
    slots_of(eid_ref, eidT_ref, so_ref, soT_ref, slot_scr, sel_ref)
    slot_ref[ep] = slot_scr[ep]
    exchange(slot_scr, slot_ref, ssend, srecv, place, False)

    lane = lax.broadcasted_iota(jnp.int32, (TOK, 128), 1)

    def project(dy):
        chip = (y + dy) % 4
        rows = jnp.concatenate([nall_ref[2 * chip], nall_ref[2 * chip + 1]], axis=0)
        out = mm(rows, w_ref[...])
        for i in range(2):
            b = 2 * chip + i
            cosine, sine = rope_block(4 * b + ctx, ca_ref, sa_ref, cb_ref, sb_ref)
            q = out[i * TOK : (i + 1) * TOK, :128]
            kv = out[i * TOK : (i + 1) * TOK, 128:]
            q_rot = (q * cosine + rotate_half(q) * sine).astype(BF16)
            q_ref[b] = (q_rot.astype(F32) * (HD**-0.5)).astype(BF16)
            cosine = jnp.where(lane < HD, cosine, 1.0)
            sine = jnp.where(lane < HD, sine, 0.0)
            kv_ref[b, ctx] = (kv * cosine + rotate_half(kv) * sine).astype(BF16)

    offsets = (0, 3, 1, 2)

    def hop(direction, h, g, action):
        chip = (y + offsets[g]) % 4
        back = h - 1
        own = ctx - back if direction == 0 else ctx + back
        come = ctx - h if direction == 0 else ctx + h
        to = ctx + 1 if direction == 0 else ctx - 1
        index = (direction * 3 + back) * 4 + g
        send, recv = ksend.at[index], krecv.at[index]
        if action == "recv":
            ok = come >= 0 if direction == 0 else come <= 3

            @pl.when(ok)
            def _():
                v = kv_ref.at[pl.ds(2 * chip, 2), come]
                remote(v, v, send, recv, (dp, ep, ctx)).wait_recv()

        else:
            ok = (own >= 0) & (ctx < 3) if direction == 0 else (own <= 3) & (ctx > 0)

            @pl.when(ok)
            def _():
                v = kv_ref.at[pl.ds(2 * chip, 2), own]
                c = remote(v, v, send, recv, (dp, ep, to))
                c.start() if action == "send" else c.wait_send()

    def hops(h, g):
        for direction in (0, 1):
            if h > 1:
                hop(direction, h - 1, g, "recv")
            hop(direction, h, g, "send")

    gather.got(0)
    project(0)
    hops(1, 0)
    gather.got(1)
    gather.go(5, 6)
    gather.got(3)
    gather.go(7, 8)
    gather.got(2)
    gather.go(9)
    gather.got(4)
    gather.go(10)
    grads.go(0, 1, 3, 2, 4)
    gather.got(6, 9)
    project(3)
    hops(1, 1)
    hops(2, 0)
    gather.got(8, 10)
    project(1)
    hops(1, 2)
    hops(2, 1)
    hops(3, 0)
    gather.got(5)
    gather.go(11)
    gather.got(7)
    gather.go(12)
    gather.got(11, 12)
    project(2)
    hops(1, 3)
    hops(2, 2)
    hops(3, 1)
    hops(2, 3)
    hops(3, 2)
    grads.whole()
    hops(3, 3)
    for g in range(4):
        for direction in (0, 1):
            hop(direction, 3, g, "recv")
    exchange(slot_scr, slot_ref, ssend, srecv, place, True)
    gather.sent()
    grads.sent()
    exchange_sent(slot_scr, slot_ref, ssend, srecv, place)
    for g in range(4):
        for h in (1, 2, 3):
            for direction in (0, 1):
                hop(direction, h, g, "sent")


CHUNK = 512


def key_mask(chunk, start_row, place_row):
    keys = (lax.broadcasted_iota(jnp.int32, (CHUNK, 256), 0) + chunk * CHUNK).astype(F32)
    return (keys >= start_row) & (keys <= place_row)


def query_rows(j, ctx, start_ref):
    block = 4 * j + ctx
    start = start_ref[pl.ds(block, 1), :]
    places = (lax.broadcasted_iota(jnp.int32, (1, 128), 1) + block * 128).astype(F32)
    return jnp.concatenate([start, start], axis=1), jnp.concatenate([places, places], axis=1)


def turned(block):
    return block.astype(F32).T.astype(BF16)


def heads_wide(tall):
    return jnp.concatenate([tall[:HD], tall[HD:]], axis=1)


def attend_kernel(first_ref, q_ref, kv_ref, start_ref, att_ref, attT_ref, lse_ref, kvT):
    ctx = lax.axis_index("ctx")

    for chunk in range(8):
        part = kv_ref[chunk * CHUNK : (chunk + 1) * CHUNK, :].astype(F32).T
        row = lax.broadcasted_iota(jnp.int32, part.shape, 0)
        kvT[:, chunk * CHUNK : (chunk + 1) * CHUNK] = jnp.where(row < HD, 1.0, part).astype(BF16)

    for j in range(8):
        start_row, place_row = query_rows(j, ctx, start_ref)
        wide = heads_wide(turned(q_ref[j]))
        q_pad = jnp.concatenate([wide, jnp.zeros_like(wide)], axis=0)

        def step(chunk, carry):
            top, total = carry
            rows = pl.ds(pl.multiple_of(chunk * CHUNK, CHUNK), CHUNK)
            scores = mm(kv_ref[rows, :], q_pad)
            scores = jnp.where(key_mask(chunk, start_row, place_row), scores, MASKED)
            new_top = jnp.maximum(top, jnp.max(scores, axis=0, keepdims=True))
            probs = jnp.exp(scores - new_top).astype(BF16)
            total = total * jnp.exp(top - new_top) + mm(kvT[:, rows], probs)
            return new_top, total

        top, total = lax.fori_loop(
            first_ref[j], j + 1, step, (jnp.full((1, 256), MASKED, F32), jnp.zeros((128, 256), F32))
        )
        norm = total[0:1]
        out = total[HD:] / norm
        tall = jnp.concatenate([out[:, :128], out[:, 128:]], axis=0)
        attT_ref[j] = tall
        att_ref[j] = tall.T.astype(BF16)
        lse_ref[j] = jnp.broadcast_to(top + jnp.log(norm), (8, 256))


def middle_kernel(
    att_ref, x_ref, gain_ref, w_ref, wr_ref, sel_ref,
    res_ref, nf_ref, gin_ref, gates_ref,
    abuf, gscr, asend, arecv, nsend, nrecv, gsend, grecv,
):
    place = where_am_i()
    dp, ep, ctx = place
    barrier = pltpu.get_barrier_semaphore()
    for r in range(1, 8):
        greet(barrier, (dp, (ep + r) % 8, ctx))
    pl.semaphore_wait(barrier, 7)
    exchange(att_ref, abuf, asend, arecv, place, False)
    abuf[ep] = att_ref[ep]
    exchange(att_ref, abuf, asend, arecv, place, True)
    attended = jnp.concatenate([abuf[p] for p in range(8)], axis=1)
    res = x_ref[...].astype(F32) + mm(attended, w_ref[...])
    res_ref[...] = res
    normed = res * lax.rsqrt(jnp.mean(res * res, axis=-1, keepdims=True) + EPSILON) * gain_ref[...]
    normed = normed.astype(BF16)
    nf_ref[ep] = normed
    gather = EpGather(nf_ref, nsend, nrecv, place)
    gather.go(0, 1, 3, 2, 4)
    logits = mm(wr_ref[...], normed, NT)
    chosen = sel_ref[...] > 0.5
    top = jnp.max(jnp.where(chosen, logits, MASKED), axis=0, keepdims=True)
    weight = jnp.where(chosen, jnp.exp(jnp.where(chosen, logits, MASKED) - top), 0.0)
    gates = weight / jnp.sum(weight, axis=0, keepdims=True)
    gates_ref[...] = gates
    for g in range(8):
        gscr[g] = gates[8 * g : 8 * g + 8, :]
    gin_ref[ep] = gscr[ep]
    exchange(gscr, gin_ref, gsend, grecv, place, False)
    gather.whole()
    exchange(gscr, gin_ref, gsend, grecv, place, True)
    gather.sent()
    exchange_sent(gscr, gin_ref, gsend, grecv, place)
    exchange_sent(att_ref, abuf, asend, arecv, place)


def each_slab(lead, work):
    count = 1
    for size in lead:
        count *= size

    def each(i, carry):
        work((i,) if len(lead) == 1 else (i // lead[1], i % lead[1]))
        return carry

    lax.fori_loop(0, count, each, 0)


class Arc:
    def __init__(self, n, pos, own, half, slots, devices, send, recv):
        self.n, self.pos, self.own, self.half, self.slots = n, pos, own, half, slots
        self.devices, self.send, self.recv = devices, send, recv
        self.steps = n // 2

    def chunk(self, way, s):
        reach = self.steps - s + 1
        return (self.pos + reach) % self.n if way == 0 else (self.pos + self.n - reach) % self.n

    def copy(self, way, s):
        dst = self.slots.at[way, s - 1]
        src = self.own(self.chunk(way, s)) if s == 1 else self.slots.at[way, s - 2]
        if s == 1:
            src, dst = self.half(src, way), self.half(dst, way)
        return remote(src, dst, self.send.at[way, s - 1], self.recv.at[way, s - 1], self.devices[way])

    def start(self):
        for way in (0, 1):
            self.copy(way, 1).start()

    def slabs(self, work):
        each_slab(self.slots.shape[2:-2], work)

    def advance(self, s):
        for way in (0, 1):
            self.copy(way, s - 1).wait_recv()
            held, own = self.slots.at[way, s - 2], self.own(self.chunk(way, s))
            if s == 2:
                self.merge(way, held, own)
            else:

                def add(index):
                    held[index] = (held[index].astype(F32) + own[index].astype(F32)).astype(BF16)

                self.slabs(add)
            self.copy(way, s).start()

    def merge(self, way, held, own):
        mine, its = self.half(held, way), self.half(own, way)
        other, from_own = self.half(held, 1 - way), self.half(own, 1 - way)

        def add(index):
            mine[index] = (mine[index].astype(F32) + its[index].astype(F32)).astype(BF16)

        def take(index):
            other[index] = from_own[index]

        each_slab(mine.shape[:-2], add)
        each_slab(other.shape[:-2], take)

    def finish(self, put):
        for way in (0, 1):
            self.copy(way, self.steps).wait_recv()
        own, up, down = self.own(self.pos), self.slots.at[0, self.steps - 1], self.slots.at[1, self.steps - 1]

        def add(index):
            put(index, own[index].astype(F32) + up[index].astype(F32) + down[index].astype(F32))

        self.slabs(add)

    def sent(self):
        for way in (0, 1):
            for s in range(1, self.steps + 1):
                self.copy(way, s).wait_send()


class Torus:
    def __init__(self, place):
        self.dp, self.ep, self.ctx = place
        self.zh, self.x = self.dp // 4, self.dp % 4
        self.z = self.zh * 4 + self.ctx

    def at_x(self, v):
        return (self.zh * 4 + v % 4, self.ep, self.ctx)

    def at_z(self, v):
        v = v % 8
        return ((v // 4) * 4 + self.x, self.ep, v % 4)

    def x_ways(self):
        return self.at_x(self.x + 1), self.at_x(self.x + 3)

    def z_ways(self):
        return self.at_z(self.z + 1), self.at_z(self.z + 7)

    def x_arc(self, own, half, slots, send, recv):
        return Arc(4, self.x, own, half, slots, self.x_ways(), send, recv)

    def z_arc(self, own, half, slots, send, recv):
        return Arc(8, self.z, own, half, slots, self.z_ways(), send, recv)


def first_or_last(sizes):
    def half(view, h):
        return view.at[pl.ds(0, sizes[0])] if h == 0 else view.at[pl.ds(sizes[0], sizes[1])]

    return half


X_FIRST, Z_FIRST = (0, 1), (2,)
KEPT = 3
X_UNITS, Z_UNITS = (3, 4, 5, 6, 7, 8, 9), (10, 11)


def unit_arcs(torus, own, x_units, z_units, x_slots, z_slots, xs, xr, zs, zr):
    xa = [
        torus.x_arc(
            lambda t, i=i: own.at[i, :, t], first_or_last((1, 1)), x_slots.at[i], xs.at[i], xr.at[i]
        )
        for i in range(len(x_units))
    ]
    za = [
        torus.z_arc(
            lambda t, i=i: own.at[len(x_units) + i, t // 4, :, t % 4], first_or_last((2, 2)), z_slots.at[i], zs.at[i], zr.at[i]
        )
        for i in range(len(z_units))
    ]
    return xa, za


def expert_kernel(
    slot_ref, gate_ref, nf_hbm, og_hbm, win_hbm, wout_hbm,
    y_ref, d_ref, dg_ref, rx_ref, rz_ref, gw_hbm,
    nf, og, win, wout, rows_scr, grad_scr, units, x_slots, z_slots,
    fsem, wsem, gsem, xs, xr, zs, zr,
):
    torus = Torus(where_am_i())
    loads = [pltpu.make_async_copy(nf_hbm, nf, fsem.at[0]), pltpu.make_async_copy(og_hbm, og, fsem.at[1])]

    def weights(j):
        return (
            pltpu.make_async_copy(win_hbm.at[j], win.at[j % 2], wsem.at[j, 0]),
            pltpu.make_async_copy(wout_hbm.at[j], wout.at[j % 2], wsem.at[j, 1]),
        )

    for f in loads + list(weights(0)) + list(weights(1)):
        f.start()
    barrier = pltpu.get_barrier_semaphore()
    for device in torus.x_ways() + torus.z_ways():
        greet(barrier, device)
    slot = lax.broadcasted_iota(jnp.int32, (CAP, TOK), 0).astype(F32)

    def picks(s, e):
        return slot == slot_ref[s, pl.ds(e, 1), :]

    for f in loads:
        f.wait()

    def load(s, carry):
        pick = jnp.concatenate([jnp.where(picks(s, e), 1.0, 0.0) for e in range(4)], axis=0).astype(BF16)
        got = mm(pick, nf[s])
        grad = mm(pick, og[s])
        for e in range(4):
            rows = pl.ds(pl.multiple_of(s * CAP, 8), CAP)
            rows_scr[e, rows, :] = got[e * CAP : (e + 1) * CAP]
            grad_scr[e, rows, :] = grad[e * CAP : (e + 1) * CAP]
        return carry

    lax.fori_loop(0, 8, load, 0)

    xa, za = unit_arcs(torus, units, X_FIRST, Z_FIRST, x_slots, z_slots, xs, xr, zs, zr)
    views = (2, 4, 4, 16, 1024)

    def back_weights(j, received, grad_gu):
        grad_in = mm(received, grad_gu, TN).astype(BF16).reshape(32, 32, 1024)
        units[3 * j] = grad_in[:, 0:16].reshape(views)
        units[3 * j + 1] = grad_in[:, 16:32].reshape(views)

    def expert(j, carry):
        gates = jnp.concatenate(
            [
                jnp.sum(jnp.where(picks(s, j), gate_ref[s, pl.ds(j, 1), :], 0.0), axis=1, keepdims=True)
                for s in range(8)
            ],
            axis=0,
        )
        for f in weights(j):
            f.wait()
        w_in, w_out = win[j % 2], wout[j % 2]
        received = rows_scr[j].astype(BF16)
        grad_tok = grad_scr[j]
        gate_up = mm(received, w_in)
        gating, up = gate_up[:, :512], gate_up[:, 512:]
        sig = 1.0 / (1.0 + jnp.exp(-gating))
        silu = gating * sig
        act = (silu * up).astype(BF16)
        result = mm(act, w_out).astype(BF16).astype(F32)
        dots = jnp.sum(grad_tok * result, axis=1, keepdims=True)
        grad_res = (grad_tok * gates).astype(BF16)
        grad_scr[j] = result * gates
        for s in range(8):
            dg_ref[s, pl.ds(j, 1), :] = jnp.sum(
                jnp.where(picks(s, j), dots[s * CAP : (s + 1) * CAP], 0.0), axis=0, keepdims=True
            )
        units[3 * j + 2] = mm(act, grad_res, TN).astype(BF16).reshape(views)
        grad_act = mm(grad_res, w_out, NT)
        grad_up = (grad_act * silu).astype(BF16)
        grad_gate = (grad_act * up * sig * (1.0 + gating * (1.0 - sig))).astype(BF16)
        grad_gu = jnp.concatenate([grad_gate, grad_up], axis=1)
        between(j)
        back_weights(j, received, grad_gu)
        rows_scr[j] = mm(grad_gu, w_in, NT)
        after(j)
        return carry

    def keep(first, last):
        return [pltpu.make_async_copy(units.at[u], gw_hbm.at[u - KEPT], gsem.at[u - KEPT]) for u in range(first, last)]

    def between(j):
        @pl.when(j == 1)
        def _():
            za[0].advance(2)
            xa[0].advance(2)

        @pl.when(j == 2)
        def _():
            za[0].advance(3)

        @pl.when(j == 3)
        def _():
            za[0].advance(4)

    def after(j):
        @pl.when(j < 2)
        def _():
            for f in weights(j + 2):
                f.start()

        @pl.when(j == 0)
        def _():
            for arc in za + xa:
                arc.start()

        @pl.when(j == 1)
        def _():
            xa[1].advance(2)
            for f in keep(KEPT, 6):
                f.start()

        @pl.when(j == 2)
        def _():
            for f in keep(6, 9):
                f.start()

    pl.semaphore_wait(barrier, 4)
    lax.fori_loop(0, 4, expert, 0)
    for f in keep(9, 12):
        f.start()

    def store(s, carry):
        pick = jnp.concatenate([jnp.where(picks(s, e), 1.0, 0.0) for e in range(4)], axis=0).astype(BF16)
        rows = pl.ds(pl.multiple_of(s * CAP, 8), CAP)
        weighted = jnp.concatenate([grad_scr[e, rows, :] for e in range(4)], axis=0).astype(BF16)
        y_ref[s] = mm(pick, weighted, TN).astype(BF16)
        back = jnp.concatenate([rows_scr[e, rows, :] for e in range(4)], axis=0).astype(BF16)
        d_ref[s] = mm(pick, back, TN).astype(BF16)
        dg_ref[s, 4:8, :] = jnp.zeros((4, TOK), F32)
        return carry

    lax.fori_loop(0, 8, store, 0)

    def put_z(index, value):
        for h in (0, 1):
            rz_ref[index[0], h] = value[:, 512 * h : 512 * h + 512].astype(BF16)

    za[0].finish(put_z)
    for i, arc in enumerate(xa):

        def put_x(index, value, i=i):
            rx_ref[index[0] * 4 + index[1], i] = value.astype(BF16)

        arc.finish(put_x)
    for f in keep(KEPT, 12):
        f.wait()
    for arc in xa + za:
        arc.sent()


class Direct:
    def __init__(self, torus, part, x_slots, result, z_slots, send, recv):
        self.t, self.part, self.x_slots, self.result, self.z_slots = torus, part, x_slots, result, z_slots
        self.send, self.recv = send, recv

    def x_copy(self, r):
        to = (self.t.x + r) % 4
        return remote(
            self.part.at[:, to], self.x_slots.at[r - 1], self.send.at[r], self.recv.at[r], self.t.at_x(to)
        )

    def z_copy(self, r):
        to = (self.t.z + r) % 8
        return remote(
            self.result.at[to], self.z_slots.at[r - 1], self.send.at[3 + r], self.recv.at[3 + r], self.t.at_z(to)
        )

    def start(self):
        for r in (2, 1, 3):
            self.x_copy(r).start()

    def turn(self):
        for r in (1, 2, 3):
            self.x_copy(r).wait_recv()

        def add(i, carry):
            h, l = i // 4, i % 4
            value = self.part[h, self.t.x, l].astype(F32)
            for r in range(3):
                value = value + self.x_slots[r, h, l].astype(F32)
            self.result[i] = value.astype(BF16)
            return carry

        lax.fori_loop(0, 8, add, 0)
        repeat(0, 7, lambda i: self.z_copy(4 + (2 * (i % 2) - 1) * ((i + 1) // 2)).start())

    def finish(self):
        repeat(1, 8, lambda r: self.z_copy(r).wait_recv())
        value = self.result[self.t.z].astype(F32)
        for r in range(7):
            value = value + self.z_slots[r].astype(F32)
        return value

    def sent(self):
        repeat(1, 4, lambda r: self.x_copy(r).wait_send())
        repeat(1, 8, lambda r: self.z_copy(r).wait_send())


def prepare_queries(j, ctx, start_ref, q_ref, lse_ref, both, stack, rows):
    lane = lax.broadcasted_iota(jnp.int32, (256, 128), 1)
    start_row, place_row = query_rows(j, ctx, start_ref)
    q_blk = q_ref[j]
    zero = jnp.zeros((HD, 256), BF16)
    both[j, 0:HD, 0:256] = heads_wide(turned(q_blk))
    both[j, HD:128, 0:256] = zero
    both[j, 0:HD, 256:512] = zero
    q_f = q_blk.astype(F32)
    q_rows = jnp.concatenate([q_f, pltpu.roll(q_f, HD, 1)], axis=0)
    stack[j, 0:256] = jnp.where(lane < HD, q_rows, 0.0).astype(BF16)
    rows[j, 0:1, :] = lse_ref[j, 0:1, :]
    rows[j, 2:3, :] = start_row
    rows[j, 3:4, :] = place_row


def prepare_grads(j, attT_ref, gm_ref, w_ref, both, stack, rows):
    lane = lax.broadcasted_iota(jnp.int32, (256, 128), 1)
    tall = mm(w_ref[...], gm_ref[j], NT).astype(BF16).astype(F32)
    rows[j, 1:2, :] = jnp.sum(heads_wide(tall) * heads_wide(attT_ref[j]), axis=0, keepdims=True)
    both[j, HD:128, 256:512] = heads_wide(tall).astype(BF16)
    g_f = tall.T
    g_rows = jnp.concatenate([pltpu.roll(g_f, HD, 1), g_f], axis=0)
    stack[j, 256:512] = jnp.where(lane < HD, 0.0, g_rows).astype(BF16)


def attend_pair(m, j, kv, kT, both, stack, rows):
    row = rows[j]
    chunk = pl.ds(pl.multiple_of(m * CHUNK, CHUNK), CHUNK)
    pair = mm(kv[chunk, :], both[j])
    keys = (lax.broadcasted_iota(jnp.int32, (CHUNK, 256), 0) + m * CHUNK).astype(F32)
    allowed = (keys >= row[2:3]) & (keys <= row[3:4])
    probs = jnp.exp(jnp.where(allowed, pair[:, :256], MASKED) - row[0:1])
    grad = (probs * (pair[:, 256:] - row[1:2])).astype(BF16)
    return mm(jnp.concatenate([grad, probs.astype(BF16)], axis=1), stack[j]), mm(kT[:, chunk], grad)


def tail_kernel(
    dg_ref, gates_ref, gain_two_ref, wr_ref, x_ref, gain_one_ref, ca_ref, sa_ref, cb_ref, sb_ref, start_ref, lse_ref,
    rx0, rz0,
    back_hbm, nf_hbm, res_hbm, og_hbm, q_hbm, kv_hbm, attT_hbm, wp_hbm, y_hbm, nall_hbm, wq_hbm, wk_hbm, wv_hbm, gw_hbm,
    out_ref, ing_ref, gin_ref, gout_ref, gq_ref, gk_ref, gv_ref, gside_ref, gproj_out, gains_ref,
    back, nf, res, og, q_ref, kv, attT, wp, y_part, wq, wk, wv, own,
    dbuf, cbuf, fbuf, gbuf, cbuf2, fbuf2, gbuf2, gm, gres,
    kT, both, stack, rows, dqs, acc, dkv, dqb, dkvb, kbuf, qpieces, kpieces,
    x_slots, z_slots, g0_slots, g1_slots, g2_slots, h0_slots, h1_slots, rx1, rx2, rz1,
    early, late_q, late_k, e_x, e_res, e_z, q_x, q_res, q_z, k_x, k_res, k_z,
    gain_own, gain_e, gain_x, gain_z, fin, fin_late, rs, rp, rq,
    fsem, usem, csend, crecv, c2send, c2recv, dsend, drecv, msend, mrecv, ksend, krecv, qsend, qrecv, psend, precv,
    xs, xr, zs, zr, g0s, g0r, g1s, g1r, g2s, g2r, h0s, h0r, h1s, h1r, es, er, lqs, lqr, lks, lkr, gs, gr,
    fsend, frecv,
):
    place = where_am_i()
    dp, ep, ctx = place
    torus = Torus(place)
    nall = back
    sources = dict(
        back=(back_hbm, back), nf=(nf_hbm.at[ep], nf), res=(res_hbm, res), og=(og_hbm, og), q=(q_hbm, q_ref),
        kv=(kv_hbm, kv), attT=(attT_hbm, attT), wp=(wp_hbm.at[pl.ds(pl.multiple_of(ep * 128, 128), 128)], wp), y=(y_hbm, y_part),
        nall=(nall_hbm, nall), wq=(wq_hbm, wq), wk=(wk_hbm, wk), wv=(wv_hbm, wv),
    )
    loads = {
        name: pltpu.make_async_copy(src, dst, fsem.at[i]) for i, (name, (src, dst)) in enumerate(sources.items())
    }
    units = {u: pltpu.make_async_copy(gw_hbm.at[u - KEPT], own.at[i], usem.at[i]) for i, u in enumerate(X_UNITS + Z_UNITS)}
    loads["back"].start()
    for u in (3, 10, 4, 11, 5, 6, 7, 8, 9):
        units[u].start()
    for name in ("nf", "res", "og", "kv", "q", "attT", "wp"):
        loads[name].start()
    for name in ("y", "wq", "wk", "wv"):
        loads[name].start()

    def send_to(g, h):
        return (dp, 2 * ctx + g // 2, 2 * (g % 2) + h), (ep, 2 * ctx + g // 2, 2 * (g % 2) + h)

    def is_me(device):
        return (device[0] == dp) & (device[1] == ep) & (device[2] == ctx)

    barrier = pltpu.get_barrier_semaphore()

    def greet_peers(r):
        greet(barrier, (dp, (ep + r) % 8, ctx))
        greet(barrier, torus.at_z(torus.z + r))

    repeat(1, 8, greet_peers)
    repeat(1, 4, lambda r: greet(barrier, torus.at_x(torus.x + r)))

    def greet_senders(i):
        for device in ((dp, i, ep // 2), (i, dp, ep // 2)):

            @pl.when(jnp.logical_not(is_me(device)))
            def _():
                greet(barrier, device)

    repeat(0, 8, greet_senders)
    waits = 17
    for g in range(4):
        for h in range(2):
            for device in send_to(g, h):
                waits = waits + jnp.where(is_me(device), 0, 1)
    pl.semaphore_wait(barrier, waits)

    xa, za = unit_arcs(torus, own, X_UNITS, Z_UNITS, x_slots, z_slots, xs, xr, zs, zr)
    g0 = torus.z_arc(lambda t: rx0.at[t], first_or_last((1, 1)), g0_slots, g0s, g0r)
    g1 = torus.z_arc(lambda t: rx1.at[t], first_or_last((2, 2)), g1_slots, g1s, g1r)
    g2 = torus.z_arc(lambda t: rx2.at[t], first_or_last((1, 2)), g2_slots, g2s, g2r)
    h0 = torus.x_arc(lambda t: rz0.at[t], first_or_last((1, 1)), h0_slots, h0s, h0r)
    h1 = torus.x_arc(lambda t: rz1.at[t], first_or_last((1, 1)), h1_slots, h1s, h1r)

    def finish_x(i):
        target = rx1 if i < 4 else rx2

        def put(index, value):
            target[index[0] * 4 + index[1], i % 4] = value.astype(BF16)

        xa[i].finish(put)

    def finish_z(i):
        def put(index, value):
            rz1[index[0], i] = value.astype(BF16)

        za[i].finish(put)

    total = EpScatterSum(back, cbuf, fbuf, gbuf, csend, crecv, place)
    loads["back"].wait()
    total.start()
    exchange(dg_ref, dbuf, dsend, drecv, place, False)
    dbuf[ep] = dg_ref[ep]
    h0.start()
    for i in range(4):
        units[X_UNITS[i]].wait()
        xa[i].start()
        if i < 2:
            units[Z_UNITS[i]].wait()
            za[i].start()
    g0.start()
    total.far()
    za[0].advance(2)
    xa[0].advance(2)
    za[1].advance(2)
    total.near()
    h0.advance(2)
    xa[1].advance(2)
    g0.advance(2)
    exchange(dg_ref, dbuf, dsend, drecv, place, True)
    for name in ("nf", "res", "og"):
        loads[name].wait()
    gates = gates_ref[...]
    grad_gates = jnp.concatenate([dbuf[p] for p in range(8)], axis=0)
    grad_logits = gates * (grad_gates - jnp.sum(gates * grad_gates, axis=0, keepdims=True))
    high = grad_logits.astype(BF16)
    low = (grad_logits - high.astype(F32)).astype(BF16)
    from_router = mm(high, wr_ref[...], TN) + mm(low, wr_ref[...], TN)
    resid = res[...]
    scale = lax.rsqrt(jnp.mean(resid * resid, axis=-1, keepdims=True) + EPSILON)
    scaled = resid * scale
    za[0].advance(3)
    xa[2].advance(2)
    za[1].advance(3)
    grad_normed = total.last() + from_router
    gain_two = jnp.sum(grad_normed * scaled, axis=0, keepdims=True)
    grad_normed = grad_normed * gain_two_ref[...]
    mean = jnp.mean(grad_normed * scaled, axis=-1, keepdims=True)
    grad_res = og[...].astype(F32) + scale * (grad_normed - scaled * mean)
    gm[ep] = grad_res.astype(BF16)
    gather = EpGather(gm, msend, mrecv, place)
    gather.go(0, 1, 3, 2, 4)
    gres[...] = grad_res
    for t in range(8):
        gain_own[0, 8 + t : 9 + t, :] = gain_two[:, 128 * t : 128 * t + 128]
    xa[3].advance(2)
    g0.advance(3)

    for name in ("kv", "q"):
        loads[name].wait()
    for chunk in range(4):
        part = kv[chunk * CHUNK : (chunk + 1) * CHUNK, :].astype(F32).T
        kT[:, chunk * CHUNK : (chunk + 1) * CHUNK] = part[:HD].astype(BF16)
    gather.got(1)
    gather.go(5, 6)
    gather.got(3)
    gather.go(7, 8)
    za[0].advance(4)
    for chunk in range(4, 8):
        part = kv[chunk * CHUNK : (chunk + 1) * CHUNK, :].astype(F32).T
        kT[:, chunk * CHUNK : (chunk + 1) * CHUNK] = part[:HD].astype(BF16)
    gather.got(2)
    gather.go(9)
    gather.got(4)
    gather.go(10)
    za[1].advance(4)
    repeat(0, 8, lambda j: prepare_queries(j, ctx, start_ref, q_ref, lse_ref, both, stack, rows))
    gather.got(5)
    gather.go(11)
    gather.got(7)
    gather.go(12)
    g0.advance(4)
    to = lax.broadcasted_iota(jnp.int32, (32, 64), 0)
    source = lax.broadcasted_iota(jnp.int32, (32, 64), 1)
    squeeze = jnp.where(source == (to // 4) * 8 + to % 4, 1.0, 0.0).astype(BF16)
    grad_router = mm(mm(squeeze, high).astype(BF16), nf[...]) + mm(mm(squeeze, low).astype(BF16), nf[...])
    side = jnp.concatenate([grad_router, jnp.zeros((96, 1024), F32)], axis=0)
    for d in range(8):
        tile = side[:, d * 128 : (d + 1) * 128].T.astype(BF16)
        for c in range(4):
            early[d // 4, d % 4, c, :, 128:256] = tile[32 * c : 32 * c + 32]
    for i in (4, 5, 6):
        units[X_UNITS[i]].wait()
        xa[i].start()
    for name in ("attT", "wp"):
        loads[name].wait()
    gather.got(0, 6, 8, 9, 10, 11, 12)

    total.sent()
    loads["nall"].start()
    results = EpScatterSum(y_part, cbuf2, fbuf2, gbuf2, c2send, c2recv, place)
    loads["y"].wait()
    results.start()
    repeat(0, 8, lambda j: prepare_grads(j, attT, gm, wp, both, stack, rows))
    grad_proj = mm(attT[0].astype(BF16), gm[0])
    for j in range(1, 8):
        grad_proj = grad_proj + mm(attT[j].astype(BF16), gm[j])
    grad_proj = grad_proj.astype(BF16)
    for d in range(8):
        for c in range(4):
            early[d // 4, d % 4, c, :, 0:128] = grad_proj[32 * c : 32 * c + 32, 128 * d : 128 * d + 128]
    sums_early = Direct(torus, early, e_x, e_res, e_z, es, er)
    sums_q = Direct(torus, late_q, q_x, q_res, q_z, lqs, lqr)
    sums_k = Direct(torus, late_k, k_x, k_res, k_z, lks, lkr)
    sums_early.start()

    lane = lax.broadcasted_iota(jnp.int32, (TOK, 128), 1)

    def chunk_copy(r, m):
        shard = (ctx + r) % 4
        return remote(dkv.at[m, shard], kbuf.at[m, ctx], ksend.at[m, r], krecv.at[m, r], (dp, ep, shard))

    def chunk_go(m):
        for r in (2, 1, 3):
            chunk_copy(r, m).start()
        kbuf[m, ctx] = dkv[m, ctx]

    def piece_copy(src, dst, send, recv, m):
        return remote(src.at[m], dst.at[ep], send.at[m], recv.at[ep], (dp, m, ctx))

    def piece_go(src, dst, send, recv, m):
        @pl.when(ep != m)
        def _():
            piece_copy(src, dst, send, recv, m).start()

        @pl.when(ep == m)
        def _():
            dst[ep] = src[m]

    def pieces_got(src, dst, send, recv):
        def one(r):
            p = (ep + r) % 8
            remote(src.at[p], dst.at[p], send.at[p], recv.at[p], (dp, p, ctx)).wait_recv()

        repeat(1, 8, one)

    def pieces_sent(src, dst, send, recv):
        repeat(1, 8, lambda r: piece_copy(src, dst, send, recv, (ep + r) % 8).wait_send())

    def chunk_done(m):
        for r in (1, 2, 3):
            v = kbuf.at[m, (ctx + 4 - r) % 4]
            remote(v, v, ksend.at[m, r], krecv.at[m, r], (dp, ep, (ctx + r) % 4)).wait_recv()
        grad = kbuf[m, 0].astype(F32) + kbuf[m, 1].astype(F32) + kbuf[m, 2].astype(F32) + kbuf[m, 3].astype(F32)
        cosine, sine = rope_block(4 * m + ctx, ca_ref, sa_ref, cb_ref, sb_ref)
        cosine = jnp.where(lane < HD, cosine, 1.0)
        sine = jnp.where(lane < HD, sine, 0.0)
        dkvb[m] = (grad * cosine - rotate_half(grad) * sine).astype(BF16)
        piece_go(dkvb, kpieces, psend, precv, m)

    def progress(m):
        @pl.when(m == 0)
        def _():
            finish_x(0)
            finish_z(0)
            results.far()

        @pl.when(m == 1)
        def _():
            finish_x(1)
            finish_z(1)
            results.near()

        @pl.when(m == 2)
        def _():
            finish_x(2)
            xa[4].advance(2)
            h1.start()

        @pl.when(m == 3)
        def _():
            finish_x(3)
            g1.start()
            xa[5].advance(2)
            sums_early.turn()

        @pl.when(m == 4)
        def _():
            h1.advance(2)
            xa[6].advance(2)
            out_ref[...] = (res[...] + results.last()).astype(BF16)

        @pl.when(m == 6)
        def _():
            g1.advance(2)

    dqs[...] = jnp.zeros((8, HD, 256), F32)

    def key_chunk(m):
        acc[...] = jnp.zeros((CHUNK, 128), F32)

        def pair(j):
            both_grads, query_grad = attend_pair(m, j, kv, kT, both, stack, rows)
            acc[...] += both_grads
            dqs[j] += query_grad

        repeat(m, 8, pair)
        dkv[m] = acc[...].astype(BF16).reshape(4, TOK, 128)
        chunk_go(m)
        dq = dqs[m] * (HD**-0.5)
        dq = jnp.concatenate([dq[:, :128], dq[:, 128:]], axis=0).T
        cosine, sine = rope_block(4 * m + ctx, ca_ref, sa_ref, cb_ref, sb_ref)
        dqb[m] = (dq * cosine - rotate_half(dq) * sine).astype(BF16)
        piece_go(dqb, qpieces, qsend, qrecv, m)

        @pl.when(m >= 2)
        def _():
            chunk_done(m - 2)

        progress(m)

    repeat(0, 8, key_chunk)
    chunk_done(6)
    for name in ("nall", "wq"):
        loads[name].wait()

    def weights(grad, late):
        out = mm(nall[...].reshape(1024, 1024), grad.reshape(1024, 128), TN).astype(BF16)
        for d in range(8):
            for c in range(4):
                at = d * 128 + c * 32
                late[d // 4, d % 4, c] = out[at : at + 32]

    weights(dqb[...], late_q)
    sums_q.start()
    chunk_done(7)
    weights(dkvb[...], late_k)
    sums_k.start()
    pieces_got(dqb, qpieces, qsend, qrecv)
    grad_q = jnp.concatenate([qpieces[p] for p in range(8)], axis=1)
    grad_normed = mm(grad_q, wq[...], NT)

    def piece(g, h, kind, device):
        index = (kind * 4 + g) * 2 + h
        src = (fin.at[g, :, pl.ds(128, 128)], fin.at[g, :, pl.ds(0, 128)], fin_late.at[g])[kind]
        mine = dp if kind == 1 else ep
        return remote(src, (rs, rp, rq)[kind].at[mine], fsend.at[index], frecv.at[kind, mine], device)

    def each_piece(kinds, act, local):
        def one(i):
            g, h = i // 2, i % 2
            for kind in kinds:
                device = send_to(g, h)[kind % 2]

                @pl.when(jnp.logical_not(is_me(device)))
                def _():
                    act(piece(g, h, kind, device))

                if local:

                    @pl.when(is_me(device))
                    def _():
                        if kind == 0:
                            rs[ep] = fin[g, :, 128:256]
                        elif kind == 1:
                            rp[dp] = fin[g, :, 0:128]
                        else:
                            rq[ep] = fin_late[g]

        repeat(0, 8, one)

    def pieces_in(kind):
        def one(i):
            device = (i, dp, ep // 2) if kind == 1 else (dp, i, ep // 2)

            @pl.when(jnp.logical_not(is_me(device)))
            def _():
                dst = (rs, rp, rq)[kind].at[i]
                remote(dst, dst, fsend.at[kind * 8], frecv.at[kind, i], device).wait_recv()

        repeat(0, 8, one)

    done_early = sums_early.finish()
    for g in range(4):
        fin[g] = done_early[8 * g : 8 * g + 8]
    each_piece((0, 1), lambda c: c.start(), True)
    g1.advance(3)
    for name in ("wk", "wv"):
        loads[name].wait()
    pieces_got(dkvb, kpieces, psend, precv)
    grad_k = jnp.concatenate([kpieces[p, :, 0:HD] for p in range(8)], axis=1)
    grad_v = jnp.concatenate([kpieces[p, :, HD:128] for p in range(8)], axis=1)
    grad_normed = grad_normed + mm(grad_k, wk[...], NT) + mm(grad_v, wv[...], NT)
    x = x_ref[...].astype(F32)
    scale = lax.rsqrt(jnp.mean(x * x, axis=-1, keepdims=True) + EPSILON)
    scaled = x * scale
    gain_one = jnp.sum(grad_normed * scaled, axis=0, keepdims=True)
    for t in range(8):
        gain_own[0, t : t + 1, :] = gain_one[:, 128 * t : 128 * t + 128]

    def gain_copy(stage, r):
        src = gain_own.at[stage]
        if stage == 0:
            dst, device, base = gain_e.at[r - 1], (dp, (ep + r) % 8, ctx), 0
        elif stage == 1:
            dst, device, base = gain_x.at[r - 1], torus.at_x(torus.x + r), 7
        else:
            dst, device, base = gain_z.at[r - 1], torus.at_z(torus.z + r), 10
        return remote(src, dst, gs.at[base + r], gr.at[base + r], device)

    def gain_stage(stage, count):
        if stage > 0:
            last, slots = ((7, gain_e), (3, gain_x), (7, gain_z))[stage - 1]
            repeat(1, last + 1, lambda r: gain_copy(stage - 1, r).wait_recv())
            value = gain_own[stage - 1]
            for r in range(1, last + 1):
                value = value + slots[r - 1]
            gain_own[stage] = value
        repeat(1, count + 1, lambda r: gain_copy(stage, r).start())

    gain_stage(0, 7)
    grad_normed = grad_normed * gain_one_ref[...]
    mean = jnp.mean(grad_normed * scaled, axis=-1, keepdims=True)
    ing_ref[...] = (gres[...] + scale * (grad_normed - scaled * mean)).astype(BF16)

    sums_q.turn()
    gain_stage(1, 3)
    sums_k.turn()
    for i in (4, 5, 6):
        finish_x(i)
    g2.start()
    gain_stage(2, 7)

    done_q, done_k = sums_q.finish(), sums_k.finish()
    for g in range(4):
        at = slice(8 * g, 8 * g + 8)
        fin_late[g, :, 0:128] = done_q[at]
        fin_late[g, :, 128:256] = done_k[at]
    each_piece((2,), lambda c: c.start(), True)

    g1.advance(4)
    g2.advance(2)

    def put_unit(unit, value):
        j, u = unit // 3, unit % 3
        if u < 2:
            gin_ref[j, 16 * u : 16 * u + 16, :] = value
        else:
            gout_ref[j] = value

    def finish_units(arc, units):
        for way in (0, 1):
            arc.copy(way, arc.steps).wait_recv()
        mine = arc.own(arc.pos)
        up, down = arc.slots.at[0, arc.steps - 1], arc.slots.at[1, arc.steps - 1]
        for i, unit in enumerate(units):
            put_unit(unit, mine[i].astype(F32) + up[i].astype(F32) + down[i].astype(F32))

    for way in (0, 1):
        h0.copy(way, 2).wait_recv()
    for h in (0, 1):
        value = rz0[torus.x, h].astype(F32) + h0_slots[0, 1, h].astype(F32) + h0_slots[1, 1, h].astype(F32)
        gout_ref[0, :, 512 * h : 512 * h + 512] = value
    finish_units(h1, Z_UNITS)
    finish_units(g0, X_FIRST)
    g2.advance(3)
    finish_units(g1, X_UNITS[:4])
    pieces_in(0)
    pieces_in(1)
    last = gain_own[2]
    repeat(1, 8, lambda r: gain_copy(2, r).wait_recv())
    for r in range(7):
        last = last + gain_z[r]
    gain_own[3] = last

    g2.advance(4)
    pieces_in(2)
    odd = ctx % 2 == 1

    def mine(v):
        return jnp.where(odd, v[4:8], v[0:4])

    gq_ref[...] = mine(jnp.concatenate([rq[i, :, 0:128] for i in range(8)], axis=1))
    gk_ref[...] = mine(jnp.concatenate([rq[i, :, 128:192] for i in range(8)], axis=1))
    gv_ref[...] = mine(jnp.concatenate([rq[i, :, 192:256] for i in range(8)], axis=1))
    side = rs[0]
    for i in range(1, 8):
        side = side + rs[i]
    gside_ref[...] = mine(side)
    gproj_out[...] = mine(jnp.concatenate([rp[i] for i in range(8)], axis=1))
    for which in (0, 1):
        row = jnp.broadcast_to(gain_own[3, pl.ds(8 * which + dp, 1), :], (8, 128))
        gains_ref[8 * which : 8 * which + 8, :] = pltpu.roll(row, (128 - 16 * ep - 4 * ctx) % 128, 1)

    finish_units(g2, X_UNITS[4:])

    results.sent()
    gather.sent()
    exchange_sent(dg_ref, dbuf, dsend, drecv, place)
    pieces_sent(dqb, qpieces, qsend, qrecv)
    pieces_sent(dkvb, kpieces, psend, precv)

    def chunk_sent(m):
        for r in (1, 2, 3):
            chunk_copy(r, m).wait_send()

    repeat(0, 8, chunk_sent)
    for arc in xa + za + [g0, g1, g2, h0, h1]:
        arc.sent()
    for sums in (sums_early, sums_q, sums_k):
        sums.sent()
    for stage, count in ((0, 7), (1, 3), (2, 7)):
        repeat(1, count + 1, lambda r: gain_copy(stage, r).wait_send())
    each_piece((0, 1, 2), lambda c: c.wait_send(), False)


def pack_kernel(*refs):
    count = len(refs) // 2
    for src, dst in zip(refs[:count], refs[count:]):
        dst[...] = src[...]


def call(kernel, outs, scratch, args, name, collective=None, **more):
    params = dict(vmem_limit_bytes=VMEM_LIMIT)
    if collective is not None:
        params.update(collective_id=collective, has_side_effects=True)
    space = pl.BlockSpec(memory_space=pltpu.VMEM)
    return pl.pallas_call(
        kernel,
        out_shape=[jax.ShapeDtypeStruct(shape, kind) for shape, kind in outs],
        in_specs=more.pop("in_specs", [space] * len(args)),
        out_specs=more.pop("out_specs", [space] * len(outs)),
        scratch_shapes=scratch,
        compiler_params=pltpu.CompilerParams(**params),
        name=name,
        **more,
    )(*args)


def sems(*sizes):
    return [pltpu.SemaphoreType.DMA(s if isinstance(s, tuple) else (s,)) for s in sizes]


def body(
    layer_input, gain_attn, w_query, w_key, w_value, w_proj, gain_ffn, w_router,
    w_expert_in, w_expert_out, segment_ids, expert_ids, slot_order, out_grad,
):
    ep = lax.axis_index("ep")
    gain_one, gain_two = gain_attn.reshape(1, 1024), gain_ffn.reshape(1, 1024)
    tables = [jnp.asarray(t) for t in rope_tables()]
    w_own = jnp.concatenate(
        [
            lax.dynamic_slice_in_dim(w_query, ep * 128, 128, 1),
            lax.dynamic_slice_in_dim(w_key, ep * 64, 64, 1),
            lax.dynamic_slice_in_dim(w_value, ep * 64, 64, 1),
        ],
        axis=1,
    )
    wr_rows = jnp.pad(w_router.T.reshape(8, 4, 1024), ((0, 0), (0, 4), (0, 0))).reshape(64, 1024)
    order = slot_order.reshape(TOK, 8)
    docs = segment_ids.reshape(32, 128)

    normed_all, query, kv, grad_all, slots, chosen, starts = call(
        first_kernel,
        [
            ((8, TOK, 1024), BF16), ((8, TOK, 128), BF16), ((8, 4, TOK, 128), BF16), ((8, TOK, 1024), BF16),
            ((8, 8, TOK), F32), ((64, TOK), F32), ((32, 128), F32),
        ],
        [pltpu.VMEM((8, 8, TOK), F32)] + sems(13, 13, 13, 13, 8, 8, 24, 24),
        [layer_input, gain_one, out_grad, w_own, *tables, expert_ids, expert_ids.T, order, order.T, docs],
        "first", 1,
    )
    kv_rows = kv.reshape(4096, 128)
    ctx = lax.axis_index("ctx")
    first = lax.dynamic_slice_in_dim(starts.reshape(8, 4, 128), ctx, 1, 1)[:, 0, 0].astype(jnp.int32) // CHUNK

    vm, sm = pl.BlockSpec(memory_space=pltpu.VMEM), pl.BlockSpec(memory_space=pltpu.SMEM)
    attended, attended_tall, log_sums = call(
        attend_kernel,
        [((8, TOK, 128), BF16), ((8, 128, TOK), F32), ((8, 8, 256), F32)],
        [pltpu.VMEM((128, 4096), BF16)],
        [first, query, kv_rows, starts],
        "attend", in_specs=[sm, vm, vm, vm],
    )
    residual, ffn_all, gates_in, gates = call(
        middle_kernel,
        [((TOK, 1024), F32), ((8, TOK, 1024), BF16), ((8, 8, TOK), F32), ((64, TOK), F32)],
        [pltpu.VMEM((8, TOK, 128), BF16), pltpu.VMEM((8, 8, TOK), F32)] + sems(8, 8, 13, 13, 8, 8),
        [attended, layer_input, gain_two, w_proj, wr_rows, chosen],
        "middle", 2,
    )
    hbm = pl.BlockSpec(memory_space=pl.ANY)
    wide = pltpu.VMEM((8, TOK, 1024), BF16)
    ex, ez = len(X_FIRST), len(Z_FIRST)
    sums, back, grad_gates, sums_x, sums_z, units = call(
        expert_kernel,
        [
            ((8, TOK, 1024), BF16), ((8, TOK, 1024), BF16), ((8, 8, TOK), F32), ((8, ex, 16, 1024), BF16),
            ((4, 2, 16, 512), BF16), ((12 - KEPT, 2, 4, 4, 16, 1024), BF16),
        ],
        [
            wide, wide, pltpu.VMEM((2, 1024, 1024), BF16), pltpu.VMEM((2, 512, 1024), BF16),
            pltpu.VMEM((4, 8 * CAP, 1024), F32), pltpu.VMEM((4, 8 * CAP, 1024), F32),
            pltpu.VMEM((12, 2, 4, 4, 16, 1024), BF16),
            pltpu.VMEM((ex, 2, 2, 2, 4, 16, 1024), BF16), pltpu.VMEM((ez, 2, 4, 4, 16, 1024), BF16),
        ]
        + sems(2, (4, 2), 12 - KEPT, (ex, 2, 2), (ex, 2, 2), (ez, 2, 4), (ez, 2, 4)),
        [slots, gates_in, ffn_all, grad_all, w_expert_in, w_expert_out],
        "experts", 4, in_specs=[vm, vm] + [hbm] * 4, out_specs=[vm] * 5 + [hbm],
    )
    nx, nz = len(X_UNITS), len(Z_UNITS)
    block = pltpu.VMEM((8, TOK, 128), BF16)

    def direct(lanes):
        return [
            pltpu.VMEM((3, 2, 4, 32, lanes), BF16), pltpu.VMEM((8, 32, lanes), BF16), pltpu.VMEM((7, 32, lanes), BF16)
        ]

    results = call(
        tail_kernel,
        [
            ((TOK, 1024), BF16), ((TOK, 1024), BF16), ((4, 32, 1024), F32), ((4, 16, 1024), F32), ((4, 1024), F32),
            ((4, 512), F32), ((4, 512), F32), ((4, 128), F32), ((4, 1024), F32), ((16, 128), F32),
        ],
        [
            wide, pltpu.VMEM((TOK, 1024), BF16), pltpu.VMEM((TOK, 1024), F32), pltpu.VMEM((TOK, 1024), BF16), block,
            pltpu.VMEM((4096, 128), BF16), pltpu.VMEM((8, 128, TOK), F32), pltpu.VMEM((128, 1024), BF16), wide,
            pltpu.VMEM((1024, 1024), BF16), pltpu.VMEM((1024, 512), BF16), pltpu.VMEM((1024, 512), BF16),
            pltpu.VMEM((nx + nz, 2, 4, 4, 16, 1024), BF16),
            pltpu.VMEM((8, 8, TOK), F32),
        ]
        + scatter_sum_scratch()[:3] * 2
        + [
            wide, pltpu.VMEM((TOK, 1024), F32),
            pltpu.VMEM((HD, 4096), BF16), pltpu.VMEM((8, 128, 512), BF16), pltpu.VMEM((8, 512, 128), BF16),
            pltpu.VMEM((8, 8, 256), F32), pltpu.VMEM((8, HD, 256), F32), pltpu.VMEM((CHUNK, 128), F32),
            pltpu.VMEM((8, 4, TOK, 128), BF16),
            block, block, pltpu.VMEM((8, 4, TOK, 128), BF16), block, block,
            pltpu.VMEM((nx, 2, 2, 2, 4, 16, 1024), BF16), pltpu.VMEM((nz, 2, 4, 4, 16, 1024), BF16),
            pltpu.VMEM((2, 4, ex, 16, 1024), BF16), pltpu.VMEM((2, 4, 4, 16, 1024), BF16), pltpu.VMEM((2, 4, 3, 16, 1024), BF16),
            pltpu.VMEM((2, 2, 2, 16, 512), BF16), pltpu.VMEM((2, 2, nz, 16, 1024), BF16),
            pltpu.VMEM((8, 4, 16, 1024), BF16), pltpu.VMEM((8, 3, 16, 1024), BF16), pltpu.VMEM((4, nz, 16, 1024), BF16),
            pltpu.VMEM((2, 4, 4, 32, 256), BF16), pltpu.VMEM((2, 4, 4, 32, 128), BF16), pltpu.VMEM((2, 4, 4, 32, 128), BF16),
        ]
        + direct(256) + direct(128) + direct(128)
        + [
            pltpu.VMEM((4, 16, 128), F32), pltpu.VMEM((7, 16, 128), F32), pltpu.VMEM((3, 16, 128), F32),
            pltpu.VMEM((7, 16, 128), F32),
            pltpu.VMEM((4, 8, 256), F32), pltpu.VMEM((4, 8, 256), F32), pltpu.VMEM((8, 8, 128), F32),
            pltpu.VMEM((8, 8, 128), F32), pltpu.VMEM((8, 8, 256), F32),
        ]
        + sems(
            13, nx + nz, 8, 8, 8, 8, 8, 8, 13, 13, (8, 4), (8, 4), 8, 8, 8, 8,
            (nx, 2, 2), (nx, 2, 2), (nz, 2, 4), (nz, 2, 4),
            (2, 4), (2, 4), (2, 4), (2, 4), (2, 4), (2, 4), (2, 2), (2, 2), (2, 2), (2, 2), 11, 11, 11, 11, 11, 11, 18, 18,
            24, (3, 8),
        ),
        [
            grad_gates, gates, gain_two, wr_rows, layer_input, gain_one, *tables, starts, log_sums,
            sums_x, sums_z, back, ffn_all, residual, out_grad, query, kv_rows, attended_tall, w_proj, sums, normed_all,
            w_query, w_key, w_value, units,
        ],
        "tail", 3, in_specs=[vm] * 14 + [hbm] * 14,
    )
    layer_output, input_grad, grad_in, grad_out, out_q, out_k, out_v, side, out_proj, gains = call(
        pack_kernel, [(r.shape, r.dtype) for r in results], [], results, "pack"
    )
    return (
        layer_output, input_grad, gains[0, :4], out_q, out_k, out_v, out_proj, gains[8, :4], side[:, :32], grad_in, grad_out,
    )


def solution(mesh):
    tokens = P(("dp", "ep", "ctx"), None)
    in_specs = (
        tokens, P(), P(), P(), P(), P(), P(), P(),
        P("ep", None, None), P("ep", None, None), P("dp", None), tokens, tokens, tokens,
    )
    out_specs = (
        tokens, tokens, P(("dp", "ep", "ctx")), tokens, tokens, tokens, tokens, P(("dp", "ep", "ctx")), tokens,
        P("ep", ("dp", "ctx"), None), P("ep", ("dp", "ctx"), None),
    )
    return jax.shard_map(body, mesh=mesh, in_specs=in_specs, out_specs=out_specs, check_vma=False)
```

```python
from functools import partial

import jax
import jax.numpy as jnp
import numpy as np
from jax import lax
from jax.experimental import pallas as pl
from jax.experimental.pallas import tpu as pltpu
from jax.sharding import PartitionSpec as P

HD = 64
EPSILON = 1e-06
MASKED = -1e30
CAP = 40
TOK = 128
BIG = 4096.0
MESH = pl.DeviceIdType.MESH
F32 = jnp.float32
BF16 = jnp.bfloat16
VMEM_LIMIT = 60 * 1024 * 1024

NT = (((1,), (1,)), ((), ()))
NN = (((1,), (0,)), ((), ()))
TN = (((0,), (0,)), ((), ()))


def mm(a, b, dims=NN):
    return lax.dot_general(a, b, dims, preferred_element_type=F32)


def mm3(a, b, dims=NN):
    high = a.astype(BF16)
    low = (a - high.astype(F32)).astype(BF16)
    return mm(high, b, dims) + mm(low, b, dims)


def where_am_i():
    dp, ep, ctx = lax.axis_index("dp"), lax.axis_index("ep"), lax.axis_index("ctx")
    return dp, ep, ctx


def remote(src, dst, send, recv, device):
    return pltpu.make_async_remote_copy(
        src_ref=src, dst_ref=dst, send_sem=send, recv_sem=recv, device_id=device, device_id_type=MESH
    )


def greet(barrier, device):
    pl.semaphore_signal(barrier, inc=1, device_id=device, device_id_type=MESH)


def rotate_half(values):
    lane = lax.broadcasted_iota(jnp.int32, values.shape, 1)
    return jnp.where(lane % HD < HD // 2, pltpu.roll(values, 96, 1), pltpu.roll(values, 32, 1))


def rope_block(block, ca_ref, sa_ref, cb_ref, sb_ref):
    ca, sa = ca_ref[pl.ds(block, 1), :], sa_ref[pl.ds(block, 1), :]
    cb, sb = cb_ref[...], sb_ref[...]
    cosine = ca * cb - sa * sb
    sine = sa * cb + ca * sb
    lane = lax.broadcasted_iota(jnp.int32, cosine.shape, 1)
    return cosine, jnp.where(lane % HD < HD // 2, -sine, sine)


def rope_tables():
    frequency = 10000.0 ** (-np.arange(HD // 2, dtype=np.float64) * 2.0 / HD)
    frequency = np.tile(frequency.astype(np.float32).astype(np.float64), 4)
    blocks = np.arange(32, dtype=np.float64)[:, None] * 128.0 * frequency[None, :]
    rows = np.arange(128, dtype=np.float64)[:, None] * frequency[None, :]
    return [t.astype(np.float32) for t in (np.cos(blocks), np.sin(blocks), np.cos(rows), np.sin(rows))]


class EpGather:
    COUNT = 13

    def __init__(self, ref, send, recv, place):
        self.ref, self.send, self.recv = ref, send, recv
        dp, ep, ctx = place
        y, k = ep // 2, ep % 2
        self.up = (dp, ((y + 1) % 4) * 2 + k, ctx)
        self.dn = (dp, ((y + 3) % 4) * 2 + k, ctx)
        self.sib = (dp, y * 2 + 1 - k, ctx)

        def at(dy, other):
            return ((y + dy) % 4) * 2 + ((1 - k) if other else k)

        u, s, d = self.up, self.sib, self.dn
        self.sends = [
            (at(0, 0), None, s), (at(0, 0), 0, u), (at(0, 0), 1, u), (at(0, 0), 1, d), (at(0, 0), 0, d),
            (at(3, 0), 0, u), (at(3, 0), 0, s), (at(1, 0), 1, d), (at(1, 0), 1, s),
            (at(3, 0), 1, s), (at(1, 0), 0, s), (at(2, 0), 0, s), (at(2, 0), 1, s),
        ]
        self.gets = [
            (at(0, 1), None), (at(3, 0), 0), (at(3, 0), 1), (at(1, 0), 1), (at(1, 0), 0),
            (at(2, 0), 0), (at(3, 1), 0), (at(2, 0), 1), (at(1, 1), 1),
            (at(3, 1), 1), (at(1, 1), 0), (at(2, 1), 0), (at(2, 1), 1),
        ]

    def view(self, block, half):
        if half is None:
            return self.ref.at[block]
        rows = self.ref.shape[1] // 2
        return self.ref.at[block, pl.ds(half * rows, rows)]

    def go(self, *which):
        for i in which:
            block, half, device = self.sends[i]
            v = self.view(block, half)
            remote(v, v, self.send.at[i], self.recv.at[i], device).start()

    def got(self, *which):
        for i in which:
            v = self.view(*self.gets[i])
            remote(v, v, self.send.at[i], self.recv.at[i], self.sends[i][2]).wait_recv()

    def sent(self):
        for i in range(self.COUNT):
            block, half, device = self.sends[i]
            v = self.view(block, half)
            remote(v, v, self.send.at[i], self.recv.at[i], device).wait_send()

    def whole(self):
        self.got(1)
        self.go(5, 6)
        self.got(3)
        self.go(7, 8)
        self.got(2)
        self.go(9)
        self.got(4)
        self.go(10)
        self.got(5)
        self.go(11)
        self.got(7)
        self.go(12)
        self.got(0, 6, 8, 9, 10, 11, 12)


class EpScatterSum:
    COUNT = 8

    def __init__(self, part, cbuf, fbuf, gbuf, send, recv, place):
        self.part, self.cbuf, self.fbuf, self.gbuf = part, cbuf, fbuf, gbuf
        self.send, self.recv = send, recv
        dp, ep, ctx = place
        self.y, self.k = ep // 2, ep % 2
        y, k = self.y, self.k
        self.up = (dp, ((y + 1) % 4) * 2 + k, ctx)
        self.dn = (dp, ((y + 3) % 4) * 2 + k, ctx)
        self.sib = (dp, y * 2 + 1 - k, ctx)

    def block(self, dy, other=False):
        return ((self.y + dy) % 4) * 2 + ((1 - self.k) if other else self.k)

    def copy(self, i):
        half = self.cbuf.shape[1] // 2
        lo, hi = pl.ds(0, half), pl.ds(half, half)
        s, r = self.send, self.recv
        if i < 4:
            away = self.block((2, 1, 3, 0)[i], True)
            return remote(self.part.at[away], self.cbuf.at[i], s.at[i], r.at[i], self.sib)
        src, dst, device = (
            (self.cbuf.at[0, lo], self.fbuf.at[0], self.up),
            (self.cbuf.at[0, hi], self.fbuf.at[1], self.dn),
            (self.cbuf.at[1], self.gbuf.at[0], self.up),
            (self.cbuf.at[2], self.gbuf.at[1], self.dn),
        )[i - 4]
        return remote(src, dst, s.at[i], r.at[i], device)

    def start(self):
        for i in range(4):
            self.copy(i).start()

    def far(self):
        self.copy(0).wait_recv()
        self.cbuf[0] = (self.cbuf[0].astype(F32) + self.part[self.block(2)].astype(F32)).astype(BF16)
        self.copy(4).start()
        self.copy(5).start()

    def near(self):
        half = self.cbuf.shape[1] // 2
        for slot, dy, far, rows, rest in ((1, 1, 0, pl.ds(0, half), pl.ds(half, half)), (2, 3, 1, pl.ds(half, half), pl.ds(0, half))):
            b = self.block(dy)
            self.copy(slot).wait_recv()
            self.copy(4 + far).wait_recv()
            self.cbuf[slot, rows] = (
                self.cbuf[slot, rows].astype(F32) + self.part[b, rows].astype(F32) + self.fbuf[far].astype(F32)
            ).astype(BF16)
            self.cbuf[slot, rest] = (self.cbuf[slot, rest].astype(F32) + self.part[b, rest].astype(F32)).astype(BF16)
            self.copy(6 + far).start()

    def last(self):
        for i in (3, 6, 7):
            self.copy(i).wait_recv()
        return (
            self.part[self.block(0)].astype(F32) + self.cbuf[3].astype(F32)
            + self.gbuf[0].astype(F32) + self.gbuf[1].astype(F32)
        )

    def sent(self):
        for i in range(self.COUNT):
            self.copy(i).wait_send()


def scatter_sum_scratch():
    return [
        pltpu.VMEM((4, TOK, 1024), BF16),
        pltpu.VMEM((2, TOK // 2, 1024), BF16),
        pltpu.VMEM((2, TOK, 1024), BF16),
        pltpu.SemaphoreType.DMA((8,)),
        pltpu.SemaphoreType.DMA((8,)),
    ]


def repeat(first, last, work):
    def each(i, carry):
        work(i)
        return carry

    lax.fori_loop(first, last, each, 0)


def exchange(src, dst, send, recv, place, wait):
    dp, ep, ctx = place

    def one(r):
        to, source = (ep + r) % 8, (ep + 8 - r) % 8
        if not wait:
            remote(src.at[to], dst.at[ep], send.at[r], recv.at[r], (dp, to, ctx)).start()
        else:
            remote(src.at[to], dst.at[source], send.at[r], recv.at[r], (dp, to, ctx)).wait_recv()

    repeat(1, 8, one)


def exchange_sent(src, dst, send, recv, place):
    dp, ep, ctx = place

    def one(r):
        to = (ep + r) % 8
        remote(src.at[to], dst.at[ep], send.at[r], recv.at[r], (dp, to, ctx)).wait_send()

    repeat(1, 8, one)


def starts_of(docs):
    rows = lax.broadcasted_iota(jnp.int32, docs.shape, 0)
    lane = lax.broadcasted_iota(jnp.int32, docs.shape, 1)
    docs = docs.astype(F32)
    turned = pltpu.roll(docs, 1, 1)
    before = jnp.where(lane == 0, pltpu.roll(turned, 1, 0), turned)
    place = rows * 128 + lane
    fresh = (docs != before) | (place == 0)
    value = jnp.where(fresh, place.astype(F32), 0.0)
    for shift in (1, 2, 4, 8, 16, 32, 64):
        value = jnp.maximum(value, jnp.where(lane >= shift, pltpu.roll(value, shift, 1), 0.0))
    carry = jnp.broadcast_to(jnp.max(value, axis=1, keepdims=True), value.shape)
    for shift in (1, 2, 4, 8, 16):
        carry = jnp.maximum(carry, jnp.where(rows >= shift, pltpu.roll(carry, shift, 0), 0.0))
    above = jnp.where(rows >= 1, pltpu.roll(carry, 1, 0), 0.0)
    return jnp.maximum(value, above)


def slots_of(eidT_ref, soT_ref, slot_scr, sel_ref):
    def expert(index):
        return jnp.where(index % 8 < 4, (index // 8) * 4 + index % 8, -1)

    row_expert = expert(lax.broadcasted_iota(jnp.int32, (64, TOK), 0))
    by_row = jnp.full((64, TOK), BIG, F32)
    for k in range(8):
        by_row = jnp.where(eidT_ref[k : k + 1, :] == row_expert, soT_ref[k : k + 1, :].astype(F32), by_row)
    by_lane = by_row.T
    sel_ref[...] = jnp.where(by_row < BIG, 1.0, 0.0)
    for g in range(8):
        for j in range(4):
            r = 8 * g + j
            row = by_row[r : r + 1, :]
            less = jnp.where(by_lane[:, r : r + 1] < row, 1.0, 0.0)
            rank = jnp.sum(less, axis=0, keepdims=True)
            slot_scr[g, j : j + 1, :] = jnp.where((row < BIG) & (rank < CAP), rank, -1.0)
        slot_scr[g, 4:8, :] = jnp.full((4, TOK), -1.0, F32)


CHUNK = 512


def key_mask(chunk, start_row, place_row):
    keys = (lax.broadcasted_iota(jnp.int32, (CHUNK, 256), 0) + chunk * CHUNK).astype(F32)
    return (keys >= start_row) & (keys <= place_row)


def query_rows(j, ctx, start_ref):
    block = 4 * j + ctx
    start = start_ref[pl.ds(block, 1), :]
    places = (lax.broadcasted_iota(jnp.int32, (1, 128), 1) + block * 128).astype(F32)
    return jnp.concatenate([start, start], axis=1), jnp.concatenate([places, places], axis=1)


def turned(block):
    return block.astype(F32).T.astype(BF16)


def heads_wide(tall):
    return jnp.concatenate([tall[:HD], tall[HD:]], axis=1)


def head_kernel(
    x_ref, gain_one_ref, gain_two_ref, og_ref, ca_ref, sa_ref, cb_ref, sb_ref, eidT_ref, soT_ref, doc_ref, wr_ref,
    wq_hbm, wk_hbm, wv_hbm, wp_hbm,
    nall_ref, ogall_ref, q_ref, kv_ref, slot_ref, start_ref, attT_ref, lse_ref, res_ref, nf_ref, gin_ref, gates_ref,
    wq, wk, wv, w_own, wp, slot_scr, sel, att, abuf, kv_rows, kvT, gscr,
    wsem, nsend, nrecv, osend, orecv, ssend, srecv, ksend, krecv, asend, arecv, fsend, frecv, gsend, grecv,
):
    place = where_am_i()
    dp, ep, ctx = place
    y = ep // 2
    pair = pl.ds(pl.multiple_of(y * 128, 128), 128)
    loads = [
        pltpu.make_async_copy(src, dst, wsem.at[i])
        for i, (src, dst) in enumerate(
            (
                (wq_hbm.at[:, pl.ds(pl.multiple_of(ep * 128, 128), 128)], wq),
                (wk_hbm.at[:, pair], wk),
                (wv_hbm.at[:, pair], wv),
                (wp_hbm, wp),
            )
        )
    ]
    for f in loads:
        f.start()
    barrier = pltpu.get_barrier_semaphore()
    repeat(1, 8, lambda r: greet(barrier, (dp, (ep + r) % 8, ctx)))

    @pl.when(ctx > 0)
    def _():
        greet(barrier, (dp, ep, ctx - 1))

    @pl.when(ctx < 3)
    def _():
        greet(barrier, (dp, ep, ctx + 1))

    x = x_ref[...].astype(F32)
    normed = x * lax.rsqrt(jnp.mean(x * x, axis=-1, keepdims=True) + EPSILON) * gain_one_ref[...]
    nall_ref[ep] = normed.astype(BF16)
    ogall_ref[ep] = og_ref[...]
    edges = jnp.where(ctx > 0, 1, 0) + jnp.where(ctx < 3, 1, 0)
    pl.semaphore_wait(barrier, 7 + edges)

    gather = EpGather(nall_ref, nsend, nrecv, place)
    grads = EpGather(ogall_ref, osend, orecv, place)
    gather.go(0, 1, 3, 2, 4)
    for f in loads[:3]:
        f.wait()
    lane = lax.broadcasted_iota(jnp.int32, (1024, 128), 1)
    even = ep % 2 == 0
    k_pair, v_pair = wk[...].astype(F32), wv[...].astype(F32)
    k_half = jnp.where(even, k_pair, pltpu.roll(k_pair, HD, 1))
    v_half = jnp.where(even, pltpu.roll(v_pair, HD, 1), v_pair)
    w_own[:, 0:128] = wq[...]
    w_own[:, 128:256] = jnp.where(lane < HD, k_half, v_half).astype(BF16)
    lane = lax.broadcasted_iota(jnp.int32, (TOK, 128), 1)

    def project(dy):
        chip = (y + dy) % 4
        rows = jnp.concatenate([nall_ref[2 * chip], nall_ref[2 * chip + 1]], axis=0)
        out = mm(rows, w_own[...])
        for i in range(2):
            b = 2 * chip + i
            cosine, sine = rope_block(4 * b + ctx, ca_ref, sa_ref, cb_ref, sb_ref)
            q = out[i * TOK : (i + 1) * TOK, :128]
            kv = out[i * TOK : (i + 1) * TOK, 128:]
            q_rot = (q * cosine + rotate_half(q) * sine).astype(BF16)
            q_ref[b] = (q_rot.astype(F32) * (HD**-0.5)).astype(BF16)
            cosine = jnp.where(lane < HD, cosine, 1.0)
            sine = jnp.where(lane < HD, sine, 0.0)
            kv_ref[b, ctx] = (kv * cosine + rotate_half(kv) * sine).astype(BF16)

    offsets = (0, 3, 1, 2)

    def hop(direction, h, g, action):
        chip = (y + offsets[g]) % 4
        back = h - 1
        own = ctx - back if direction == 0 else ctx + back
        come = ctx - h if direction == 0 else ctx + h
        to = ctx + 1 if direction == 0 else ctx - 1
        index = (direction * 3 + back) * 4 + g
        send, recv = ksend.at[index], krecv.at[index]
        if action == "recv":
            ok = come >= 0 if direction == 0 else come <= 3

            @pl.when(ok)
            def _():
                v = kv_ref.at[pl.ds(2 * chip, 2), come]
                remote(v, v, send, recv, (dp, ep, ctx)).wait_recv()

        else:
            ok = (own >= 0) & (ctx < 3) if direction == 0 else (own <= 3) & (ctx > 0)

            @pl.when(ok)
            def _():
                v = kv_ref.at[pl.ds(2 * chip, 2), own]
                c = remote(v, v, send, recv, (dp, ep, to))
                c.start() if action == "send" else c.wait_send()

    def hops(h, g):
        for direction in (0, 1):
            if h > 1:
                hop(direction, h - 1, g, "recv")
            hop(direction, h, g, "send")

    gather.got(0)
    project(0)
    hops(1, 0)
    start_ref[...] = starts_of(doc_ref[...])
    slots_of(eidT_ref, soT_ref, slot_scr, sel)
    gather.got(1)
    gather.go(5, 6)
    gather.got(3)
    gather.go(7, 8)
    gather.got(2)
    gather.go(9)
    gather.got(4)
    gather.go(10)
    slot_ref[ep] = slot_scr[ep]
    exchange(slot_scr, slot_ref, ssend, srecv, place, False)
    hops(2, 0)
    gather.got(6, 9)
    project(3)
    hops(1, 1)
    gather.got(8, 10)
    project(1)
    hops(1, 2)
    hops(3, 0)
    hops(2, 1)
    gather.got(5)
    gather.go(11)
    gather.got(7)
    gather.go(12)
    grads.go(0, 1, 3, 2, 4)
    gather.got(11, 12)
    project(2)
    hops(1, 3)
    hops(2, 2)
    hops(3, 1)
    hops(2, 3)
    hops(3, 2)
    hops(3, 3)
    grads.got(1)
    grads.go(5, 6)
    grads.got(3)
    grads.go(7, 8)
    for g in range(4):
        for direction in (0, 1):
            hop(direction, 3, g, "recv")

    def turn_keys(chunk):
        rows = kv_ref[chunk].reshape(CHUNK, 128)
        at = pl.ds(pl.multiple_of(chunk * CHUNK, CHUNK), CHUNK)
        kv_rows[at, :] = rows
        part = rows.astype(F32).T
        row = lax.broadcasted_iota(jnp.int32, part.shape, 0)
        kvT[:, at] = jnp.where(row < HD, 1.0, part).astype(BF16)

    repeat(0, 8, turn_keys)

    def piece_copy(m):
        return remote(att.at[m], abuf.at[ep], asend.at[m], arecv.at[ep], (dp, m, ctx))

    def block(j):
        start_row, place_row = query_rows(j, ctx, start_ref)
        wide = heads_wide(turned(q_ref[j]))
        q_pad = jnp.concatenate([wide, jnp.zeros_like(wide)], axis=0)

        def step(chunk, carry):
            top, total = carry
            rows = pl.ds(pl.multiple_of(chunk * CHUNK, CHUNK), CHUNK)
            scores = mm(kv_rows[rows, :], q_pad)
            scores = jnp.where(key_mask(chunk, start_row, place_row), scores, MASKED)
            new_top = jnp.maximum(top, jnp.max(scores, axis=0, keepdims=True))
            probs = jnp.exp(scores - new_top).astype(BF16)
            total = total * jnp.exp(top - new_top) + mm(kvT[:, rows], probs)
            return new_top, total

        top, total = lax.fori_loop(0, j + 1, step, (jnp.full((1, 256), MASKED, F32), jnp.zeros((128, 256), F32)))
        norm = total[0:1]
        out = total[HD:] / norm
        tall = jnp.concatenate([out[:, :128], out[:, 128:]], axis=0)
        attT_ref[j] = tall
        att[j] = tall.T.astype(BF16)
        lse_ref[j] = jnp.broadcast_to(top + jnp.log(norm), (8, 256))

        @pl.when(ep != j)
        def _():
            piece_copy(j).start()

        @pl.when(ep == j)
        def _():
            abuf[ep] = att[j]

    repeat(0, 6, block)
    grads.got(2)
    grads.go(9)
    grads.got(4)
    grads.go(10)
    grads.got(5)
    grads.go(11)
    grads.got(7)
    grads.go(12)
    repeat(6, 8, block)

    loads[3].wait()

    def piece_got(r):
        p = (ep + r) % 8
        remote(att.at[p], abuf.at[p], asend.at[p], arecv.at[p], (dp, p, ctx)).wait_recv()

    repeat(1, 8, piece_got)
    attended = jnp.concatenate([abuf[p] for p in range(8)], axis=1)
    res = x_ref[...].astype(F32) + mm(attended, wp[...])
    res_ref[...] = res
    normed = res * lax.rsqrt(jnp.mean(res * res, axis=-1, keepdims=True) + EPSILON) * gain_two_ref[...]
    normed = normed.astype(BF16)
    nf_ref[ep] = normed
    rows = EpGather(nf_ref, fsend, frecv, place)
    rows.go(0, 1, 3, 2, 4)
    logits = mm(wr_ref[...], normed, NT)
    chosen = sel[...] > 0.5
    top = jnp.max(jnp.where(chosen, logits, MASKED), axis=0, keepdims=True)
    weight = jnp.where(chosen, jnp.exp(jnp.where(chosen, logits, MASKED) - top), 0.0)
    gates = weight / jnp.sum(weight, axis=0, keepdims=True)
    gates_ref[...] = gates
    for g in range(8):
        gscr[g] = gates[8 * g : 8 * g + 8, :]
    gin_ref[ep] = gscr[ep]
    exchange(gscr, gin_ref, gsend, grecv, place, False)
    exchange(slot_scr, slot_ref, ssend, srecv, place, True)
    grads.got(0, 6, 8, 9, 10, 11, 12)
    rows.whole()
    exchange(gscr, gin_ref, gsend, grecv, place, True)
    for g in (gather, grads, rows):
        g.sent()
    exchange_sent(slot_scr, slot_ref, ssend, srecv, place)
    exchange_sent(gscr, gin_ref, gsend, grecv, place)
    repeat(1, 8, lambda r: piece_copy((ep + r) % 8).wait_send())
    for g in range(4):
        for h in (1, 2, 3):
            for direction in (0, 1):
                hop(direction, h, g, "sent")


def each_slab(lead, work):
    count = 1
    for size in lead:
        count *= size

    def each(i, carry):
        work((i,) if len(lead) == 1 else (i // lead[1], i % lead[1]))
        return carry

    lax.fori_loop(0, count, each, 0)


class Arc:
    def __init__(self, n, pos, own, half, slots, devices, send, recv):
        self.n, self.pos, self.own, self.half, self.slots = n, pos, own, half, slots
        self.devices, self.send, self.recv = devices, send, recv
        self.steps = n // 2

    def chunk(self, way, s):
        reach = self.steps - s + 1
        return (self.pos + reach) % self.n if way == 0 else (self.pos + self.n - reach) % self.n

    def copy(self, way, s):
        dst = self.slots.at[way, s - 1]
        src = self.own(self.chunk(way, s)) if s == 1 else self.slots.at[way, s - 2]
        if s == 1:
            src, dst = self.half(src, way), self.half(dst, way)
        return remote(src, dst, self.send.at[way, s - 1], self.recv.at[way, s - 1], self.devices[way])

    def start(self):
        for way in (0, 1):
            self.copy(way, 1).start()

    def slabs(self, work):
        each_slab(self.slots.shape[2:-2], work)

    def advance(self, s):
        for way in (0, 1):
            self.copy(way, s - 1).wait_recv()
            held, own = self.slots.at[way, s - 2], self.own(self.chunk(way, s))
            if s == 2:
                self.merge(way, held, own)
            else:

                def add(index):
                    held[index] = (held[index].astype(F32) + own[index].astype(F32)).astype(BF16)

                self.slabs(add)
            self.copy(way, s).start()

    def merge(self, way, held, own):
        mine, its = self.half(held, way), self.half(own, way)
        other, from_own = self.half(held, 1 - way), self.half(own, 1 - way)

        def add(index):
            mine[index] = (mine[index].astype(F32) + its[index].astype(F32)).astype(BF16)

        def take(index):
            other[index] = from_own[index]

        each_slab(mine.shape[:-2], add)
        each_slab(other.shape[:-2], take)

    def finish(self, put):
        for way in (0, 1):
            self.copy(way, self.steps).wait_recv()
        own, up, down = self.own(self.pos), self.slots.at[0, self.steps - 1], self.slots.at[1, self.steps - 1]

        def add(index):
            put(index, own[index].astype(F32) + up[index].astype(F32) + down[index].astype(F32))

        self.slabs(add)

    def sent(self):
        for way in (0, 1):
            for s in range(1, self.steps + 1):
                self.copy(way, s).wait_send()


class Torus:
    def __init__(self, place):
        self.dp, self.ep, self.ctx = place
        self.zh, self.x = self.dp // 4, self.dp % 4
        self.z = self.zh * 4 + self.ctx

    def at_x(self, v):
        return (self.zh * 4 + v % 4, self.ep, self.ctx)

    def at_z(self, v):
        v = v % 8
        return ((v // 4) * 4 + self.x, self.ep, v % 4)

    def x_ways(self):
        return self.at_x(self.x + 1), self.at_x(self.x + 3)

    def z_ways(self):
        return self.at_z(self.z + 1), self.at_z(self.z + 7)

    def x_arc(self, own, half, slots, send, recv):
        return Arc(4, self.x, own, half, slots, self.x_ways(), send, recv)

    def z_arc(self, own, half, slots, send, recv):
        return Arc(8, self.z, own, half, slots, self.z_ways(), send, recv)


def first_or_last(sizes):
    def half(view, h):
        return view.at[pl.ds(0, sizes[0])] if h == 0 else view.at[pl.ds(sizes[0], sizes[1])]

    return half


X_FIRST, Z_FIRST = (0, 1), (2,)
KEPT = 3
X_UNITS, Z_UNITS = (3, 4, 5, 6, 7, 8, 9), (10, 11)


def unit_arcs(torus, own, x_units, z_units, x_slots, z_slots, xs, xr, zs, zr):
    xa = [
        torus.x_arc(
            lambda t, i=i: own.at[i, :, t], first_or_last((1, 1)), x_slots.at[i], xs.at[i], xr.at[i]
        )
        for i in range(len(x_units))
    ]
    za = [
        torus.z_arc(
            lambda t, i=i: own.at[len(x_units) + i, t // 4, :, t % 4], first_or_last((2, 2)), z_slots.at[i], zs.at[i], zr.at[i]
        )
        for i in range(len(z_units))
    ]
    return xa, za


def expert_kernel(
    slot_ref, gate_ref, nf_hbm, og_hbm, win_hbm, wout_hbm,
    y_ref, d_ref, dg_ref, rx_ref, rz_ref, gw_hbm,
    nf, og, win, wout, rows_scr, grad_scr, units, x_slots, z_slots,
    fsem, wsem, gsem, xs, xr, zs, zr,
):
    torus = Torus(where_am_i())
    loads = [pltpu.make_async_copy(nf_hbm, nf, fsem.at[0]), pltpu.make_async_copy(og_hbm, og, fsem.at[1])]

    def weights(j):
        return (
            pltpu.make_async_copy(win_hbm.at[j], win.at[j % 2], wsem.at[j, 0]),
            pltpu.make_async_copy(wout_hbm.at[j], wout.at[j % 2], wsem.at[j, 1]),
        )

    for f in loads + list(weights(0)) + list(weights(1)):
        f.start()
    barrier = pltpu.get_barrier_semaphore()
    for device in torus.x_ways() + torus.z_ways():
        greet(barrier, device)
    slot = lax.broadcasted_iota(jnp.int32, (CAP, TOK), 0).astype(F32)

    def picks(s, e):
        return slot == slot_ref[s, pl.ds(e, 1), :]

    for f in loads:
        f.wait()

    def load(s, carry):
        pick = jnp.concatenate([jnp.where(picks(s, e), 1.0, 0.0) for e in range(4)], axis=0).astype(BF16)
        got = mm(pick, nf[s])
        grad = mm(pick, og[s])
        for e in range(4):
            rows = pl.ds(pl.multiple_of(s * CAP, 8), CAP)
            rows_scr[e, rows, :] = got[e * CAP : (e + 1) * CAP]
            grad_scr[e, rows, :] = grad[e * CAP : (e + 1) * CAP]
        return carry

    lax.fori_loop(0, 8, load, 0)

    xa, za = unit_arcs(torus, units, X_FIRST, Z_FIRST, x_slots, z_slots, xs, xr, zs, zr)
    views = (2, 4, 4, 16, 1024)

    def back_weights(j, received, grad_gu):
        grad_in = mm(received, grad_gu, TN).astype(BF16).reshape(32, 32, 1024)
        units[3 * j] = grad_in[:, 0:16].reshape(views)
        units[3 * j + 1] = grad_in[:, 16:32].reshape(views)

    def expert(j, carry):
        gates = jnp.concatenate(
            [
                jnp.sum(jnp.where(picks(s, j), gate_ref[s, pl.ds(j, 1), :], 0.0), axis=1, keepdims=True)
                for s in range(8)
            ],
            axis=0,
        )
        for f in weights(j):
            f.wait()
        w_in, w_out = win[j % 2], wout[j % 2]
        received = rows_scr[j].astype(BF16)
        grad_tok = grad_scr[j]
        gate_up = mm(received, w_in)
        gating, up = gate_up[:, :512], gate_up[:, 512:]
        sig = 1.0 / (1.0 + jnp.exp(-gating))
        silu = gating * sig
        act = (silu * up).astype(BF16)
        result = mm(act, w_out).astype(BF16).astype(F32)
        dots = jnp.sum(grad_tok * result, axis=1, keepdims=True)
        grad_res = (grad_tok * gates).astype(BF16)
        grad_scr[j] = result * gates
        for s in range(8):
            dg_ref[s, pl.ds(j, 1), :] = jnp.sum(
                jnp.where(picks(s, j), dots[s * CAP : (s + 1) * CAP], 0.0), axis=0, keepdims=True
            )
        units[3 * j + 2] = mm(act, grad_res, TN).astype(BF16).reshape(views)
        grad_act = mm(grad_res, w_out, NT)
        grad_up = (grad_act * silu).astype(BF16)
        grad_gate = (grad_act * up * sig * (1.0 + gating * (1.0 - sig))).astype(BF16)
        grad_gu = jnp.concatenate([grad_gate, grad_up], axis=1)
        between(j)
        back_weights(j, received, grad_gu)
        rows_scr[j] = mm(grad_gu, w_in, NT)
        after(j)
        return carry

    def keep(first, last):
        return [pltpu.make_async_copy(units.at[u], gw_hbm.at[u - KEPT], gsem.at[u - KEPT]) for u in range(first, last)]

    def between(j):
        @pl.when(j == 1)
        def _():
            za[0].advance(2)
            xa[0].advance(2)

        @pl.when(j == 2)
        def _():
            za[0].advance(3)

        @pl.when(j == 3)
        def _():
            za[0].advance(4)

    def after(j):
        @pl.when(j < 2)
        def _():
            for f in weights(j + 2):
                f.start()

        @pl.when(j == 0)
        def _():
            for arc in za + xa:
                arc.start()

        @pl.when(j == 1)
        def _():
            xa[1].advance(2)
            for f in keep(KEPT, 6):
                f.start()

        @pl.when(j == 2)
        def _():
            for f in keep(6, 9):
                f.start()

    pl.semaphore_wait(barrier, 4)
    lax.fori_loop(0, 4, expert, 0)
    for f in keep(9, 12):
        f.start()

    def store(s, carry):
        pick = jnp.concatenate([jnp.where(picks(s, e), 1.0, 0.0) for e in range(4)], axis=0).astype(BF16)
        rows = pl.ds(pl.multiple_of(s * CAP, 8), CAP)
        weighted = jnp.concatenate([grad_scr[e, rows, :] for e in range(4)], axis=0).astype(BF16)
        y_ref[s] = mm(pick, weighted, TN).astype(BF16)
        back = jnp.concatenate([rows_scr[e, rows, :] for e in range(4)], axis=0).astype(BF16)
        d_ref[s] = mm(pick, back, TN).astype(BF16)
        dg_ref[s, 4:8, :] = jnp.zeros((4, TOK), F32)
        return carry

    lax.fori_loop(0, 8, store, 0)

    def put_z(index, value):
        for h in (0, 1):
            rz_ref[index[0], h] = value[:, 512 * h : 512 * h + 512].astype(BF16)

    za[0].finish(put_z)
    for i, arc in enumerate(xa):

        def put_x(index, value, i=i):
            rx_ref[index[0] * 4 + index[1], i] = value.astype(BF16)

        arc.finish(put_x)
    for f in keep(KEPT, 12):
        f.wait()
    for arc in xa + za:
        arc.sent()


class Direct:
    def __init__(self, torus, part, x_slots, result, z_slots, send, recv):
        self.t, self.part, self.x_slots, self.result, self.z_slots = torus, part, x_slots, result, z_slots
        self.send, self.recv = send, recv

    def x_copy(self, r):
        to = (self.t.x + r) % 4
        return remote(
            self.part.at[:, to], self.x_slots.at[r - 1], self.send.at[r], self.recv.at[r], self.t.at_x(to)
        )

    def z_copy(self, r):
        to = (self.t.z + r) % 8
        return remote(
            self.result.at[to], self.z_slots.at[r - 1], self.send.at[3 + r], self.recv.at[3 + r], self.t.at_z(to)
        )

    def start(self):
        for r in (2, 1, 3):
            self.x_copy(r).start()

    def turn(self):
        for r in (1, 2, 3):
            self.x_copy(r).wait_recv()

        def add(i, carry):
            h, l = i // 4, i % 4
            value = self.part[h, self.t.x, l].astype(F32)
            for r in range(3):
                value = value + self.x_slots[r, h, l].astype(F32)
            self.result[i] = value.astype(BF16)
            return carry

        lax.fori_loop(0, 8, add, 0)
        repeat(0, 7, lambda i: self.z_copy(4 + (2 * (i % 2) - 1) * ((i + 1) // 2)).start())

    def finish(self):
        repeat(1, 8, lambda r: self.z_copy(r).wait_recv())
        value = self.result[self.t.z].astype(F32)
        for r in range(7):
            value = value + self.z_slots[r].astype(F32)
        return value

    def sent(self):
        repeat(1, 4, lambda r: self.x_copy(r).wait_send())
        repeat(1, 8, lambda r: self.z_copy(r).wait_send())


def prepare_queries(j, ctx, start_ref, q_ref, lse_ref, both, stack, rows):
    lane = lax.broadcasted_iota(jnp.int32, (256, 128), 1)
    start_row, place_row = query_rows(j, ctx, start_ref)
    q_blk = q_ref[j]
    zero = jnp.zeros((HD, 256), BF16)
    both[j, 0:HD, 0:256] = heads_wide(turned(q_blk))
    both[j, HD:128, 0:256] = zero
    both[j, 0:HD, 256:512] = zero
    q_f = q_blk.astype(F32)
    q_rows = jnp.concatenate([q_f, pltpu.roll(q_f, HD, 1)], axis=0)
    stack[j, 0:256] = jnp.where(lane < HD, q_rows, 0.0).astype(BF16)
    rows[j, 0:1, :] = lse_ref[j, 0:1, :]
    rows[j, 2:3, :] = start_row
    rows[j, 3:4, :] = place_row


def prepare_grads(j, attT_ref, gm_ref, w_ref, both, stack, rows):
    lane = lax.broadcasted_iota(jnp.int32, (256, 128), 1)
    tall = mm(w_ref[...], gm_ref[j], NT).astype(BF16).astype(F32)
    rows[j, 1:2, :] = jnp.sum(heads_wide(tall) * heads_wide(attT_ref[j]), axis=0, keepdims=True)
    both[j, HD:128, 256:512] = heads_wide(tall).astype(BF16)
    g_f = tall.T
    g_rows = jnp.concatenate([pltpu.roll(g_f, HD, 1), g_f], axis=0)
    stack[j, 256:512] = jnp.where(lane < HD, 0.0, g_rows).astype(BF16)


def attend_pair(m, j, kv, kT, both, stack, rows):
    row = rows[j]
    chunk = pl.ds(pl.multiple_of(m * CHUNK, CHUNK), CHUNK)
    pair = mm(kv[chunk, :], both[j])
    keys = (lax.broadcasted_iota(jnp.int32, (CHUNK, 256), 0) + m * CHUNK).astype(F32)
    allowed = (keys >= row[2:3]) & (keys <= row[3:4])
    probs = jnp.exp(jnp.where(allowed, pair[:, :256], MASKED) - row[0:1])
    grad = (probs * (pair[:, 256:] - row[1:2])).astype(BF16)
    return mm(jnp.concatenate([grad, probs.astype(BF16)], axis=1), stack[j]), mm(kT[:, chunk], grad)


def tail_kernel(
    dg_ref, gates_ref, gain_two_ref, wr_ref, x_ref, gain_one_ref, ca_ref, sa_ref, cb_ref, sb_ref, start_ref, lse_ref,
    rx0, rz0,
    back_hbm, nf_hbm, res_hbm, og_hbm, q_hbm, kv_hbm, attT_hbm, wp_hbm, y_hbm, nall_hbm, wq_hbm, wk_hbm, wv_hbm, gw_hbm,
    out_ref, ing_ref, gin_ref, gout_ref, gq_ref, gk_ref, gv_ref, gside_ref, gproj_out, gains_ref,
    back, nf, res, og, q_ref, kv, attT, wp, y_part, wq, wk, wv, own,
    dbuf, cbuf, fbuf, gbuf, cbuf2, fbuf2, gbuf2, gm, gres,
    kT, both, stack, rows, dqs, acc, dkv, dqb, dkvb, kbuf, qpieces, kpieces,
    x_slots, z_slots, g0_slots, g1_slots, g2_slots, h0_slots, h1_slots, rx1, rx2, rz1,
    early, late_q, late_k, e_x, e_res, e_z, q_x, q_res, q_z, k_x, k_res, k_z,
    gain_own, gain_e, gain_x, gain_z, fin, fin_late, rs, rp, rq,
    fsem, usem, csend, crecv, c2send, c2recv, dsend, drecv, msend, mrecv, ksend, krecv, qsend, qrecv, psend, precv,
    xs, xr, zs, zr, g0s, g0r, g1s, g1r, g2s, g2r, h0s, h0r, h1s, h1r, es, er, lqs, lqr, lks, lkr, gs, gr,
    fsend, frecv,
):
    place = where_am_i()
    dp, ep, ctx = place
    torus = Torus(place)
    nall = back
    sources = dict(
        back=(back_hbm, back), nf=(nf_hbm.at[ep], nf), res=(res_hbm, res), og=(og_hbm, og), q=(q_hbm, q_ref),
        kv=(kv_hbm, kv), attT=(attT_hbm, attT), wp=(wp_hbm.at[pl.ds(pl.multiple_of(ep * 128, 128), 128)], wp), y=(y_hbm, y_part),
        nall=(nall_hbm, nall), wq=(wq_hbm, wq), wk=(wk_hbm, wk), wv=(wv_hbm, wv),
    )
    loads = {
        name: pltpu.make_async_copy(src, dst, fsem.at[i]) for i, (name, (src, dst)) in enumerate(sources.items())
    }
    units = {u: pltpu.make_async_copy(gw_hbm.at[u - KEPT], own.at[i], usem.at[i]) for i, u in enumerate(X_UNITS + Z_UNITS)}
    loads["back"].start()
    for u in (3, 10, 4, 11, 5, 6, 7, 8, 9):
        units[u].start()
    for name in ("nf", "res", "og", "kv", "q", "attT", "wp"):
        loads[name].start()
    for name in ("y", "wq", "wk", "wv"):
        loads[name].start()

    def send_to(g, h):
        return (dp, 2 * ctx + g // 2, 2 * (g % 2) + h), (ep, 2 * ctx + g // 2, 2 * (g % 2) + h)

    def is_me(device):
        return (device[0] == dp) & (device[1] == ep) & (device[2] == ctx)

    barrier = pltpu.get_barrier_semaphore()

    def greet_peers(r):
        greet(barrier, (dp, (ep + r) % 8, ctx))
        greet(barrier, torus.at_z(torus.z + r))

    repeat(1, 8, greet_peers)
    repeat(1, 4, lambda r: greet(barrier, torus.at_x(torus.x + r)))

    def greet_senders(i):
        for device in ((dp, i, ep // 2), (i, dp, ep // 2)):

            @pl.when(jnp.logical_not(is_me(device)))
            def _():
                greet(barrier, device)

    repeat(0, 8, greet_senders)
    waits = 17
    for g in range(4):
        for h in range(2):
            for device in send_to(g, h):
                waits = waits + jnp.where(is_me(device), 0, 1)
    pl.semaphore_wait(barrier, waits)

    xa, za = unit_arcs(torus, own, X_UNITS, Z_UNITS, x_slots, z_slots, xs, xr, zs, zr)
    g0 = torus.z_arc(lambda t: rx0.at[t], first_or_last((1, 1)), g0_slots, g0s, g0r)
    g1 = torus.z_arc(lambda t: rx1.at[t], first_or_last((2, 2)), g1_slots, g1s, g1r)
    g2 = torus.z_arc(lambda t: rx2.at[t], first_or_last((1, 2)), g2_slots, g2s, g2r)
    h0 = torus.x_arc(lambda t: rz0.at[t], first_or_last((1, 1)), h0_slots, h0s, h0r)
    h1 = torus.x_arc(lambda t: rz1.at[t], first_or_last((1, 1)), h1_slots, h1s, h1r)

    def finish_x(i):
        target = rx1 if i < 4 else rx2

        def put(index, value):
            target[index[0] * 4 + index[1], i % 4] = value.astype(BF16)

        xa[i].finish(put)

    def finish_z(i):
        def put(index, value):
            rz1[index[0], i] = value.astype(BF16)

        za[i].finish(put)

    total = EpScatterSum(back, cbuf, fbuf, gbuf, csend, crecv, place)
    loads["back"].wait()
    total.start()
    exchange(dg_ref, dbuf, dsend, drecv, place, False)
    dbuf[ep] = dg_ref[ep]
    h0.start()
    for i in range(4):
        units[X_UNITS[i]].wait()
        xa[i].start()
        if i < 2:
            units[Z_UNITS[i]].wait()
            za[i].start()
    g0.start()
    total.far()
    za[0].advance(2)
    xa[0].advance(2)
    za[1].advance(2)
    total.near()
    h0.advance(2)
    xa[1].advance(2)
    g0.advance(2)
    exchange(dg_ref, dbuf, dsend, drecv, place, True)
    for name in ("nf", "res", "og"):
        loads[name].wait()
    gates = gates_ref[...]
    grad_gates = jnp.concatenate([dbuf[p] for p in range(8)], axis=0)
    grad_logits = gates * (grad_gates - jnp.sum(gates * grad_gates, axis=0, keepdims=True))
    high = grad_logits.astype(BF16)
    low = (grad_logits - high.astype(F32)).astype(BF16)
    from_router = mm(high, wr_ref[...], TN) + mm(low, wr_ref[...], TN)
    resid = res[...]
    scale = lax.rsqrt(jnp.mean(resid * resid, axis=-1, keepdims=True) + EPSILON)
    scaled = resid * scale
    za[0].advance(3)
    xa[2].advance(2)
    za[1].advance(3)
    grad_normed = total.last() + from_router
    gain_two = jnp.sum(grad_normed * scaled, axis=0, keepdims=True)
    grad_normed = grad_normed * gain_two_ref[...]
    mean = jnp.mean(grad_normed * scaled, axis=-1, keepdims=True)
    grad_res = og[...].astype(F32) + scale * (grad_normed - scaled * mean)
    gm[ep] = grad_res.astype(BF16)
    gather = EpGather(gm, msend, mrecv, place)
    gather.go(0, 1, 3, 2, 4)
    gres[...] = grad_res
    for t in range(8):
        gain_own[0, 8 + t : 9 + t, :] = gain_two[:, 128 * t : 128 * t + 128]
    xa[3].advance(2)
    g0.advance(3)

    for name in ("kv", "q"):
        loads[name].wait()
    for chunk in range(4):
        part = kv[chunk * CHUNK : (chunk + 1) * CHUNK, :].astype(F32).T
        kT[:, chunk * CHUNK : (chunk + 1) * CHUNK] = part[:HD].astype(BF16)
    gather.got(1)
    gather.go(5, 6)
    gather.got(3)
    gather.go(7, 8)
    za[0].advance(4)
    for chunk in range(4, 8):
        part = kv[chunk * CHUNK : (chunk + 1) * CHUNK, :].astype(F32).T
        kT[:, chunk * CHUNK : (chunk + 1) * CHUNK] = part[:HD].astype(BF16)
    gather.got(2)
    gather.go(9)
    gather.got(4)
    gather.go(10)
    za[1].advance(4)
    repeat(0, 8, lambda j: prepare_queries(j, ctx, start_ref, q_ref, lse_ref, both, stack, rows))
    gather.got(5)
    gather.go(11)
    gather.got(7)
    gather.go(12)
    g0.advance(4)
    to = lax.broadcasted_iota(jnp.int32, (32, 64), 0)
    source = lax.broadcasted_iota(jnp.int32, (32, 64), 1)
    squeeze = jnp.where(source == (to // 4) * 8 + to % 4, 1.0, 0.0).astype(BF16)
    grad_router = mm(mm(squeeze, high).astype(BF16), nf[...]) + mm(mm(squeeze, low).astype(BF16), nf[...])
    side = jnp.concatenate([grad_router, jnp.zeros((96, 1024), F32)], axis=0)
    for d in range(8):
        tile = side[:, d * 128 : (d + 1) * 128].T.astype(BF16)
        for c in range(4):
            early[d // 4, d % 4, c, :, 128:256] = tile[32 * c : 32 * c + 32]
    for i in (4, 5, 6):
        units[X_UNITS[i]].wait()
        xa[i].start()
    for name in ("attT", "wp"):
        loads[name].wait()
    gather.got(0, 6, 8, 9, 10, 11, 12)

    total.sent()
    loads["nall"].start()
    results = EpScatterSum(y_part, cbuf2, fbuf2, gbuf2, c2send, c2recv, place)
    loads["y"].wait()
    results.start()
    repeat(0, 8, lambda j: prepare_grads(j, attT, gm, wp, both, stack, rows))
    grad_proj = mm(attT[0].astype(BF16), gm[0])
    for j in range(1, 8):
        grad_proj = grad_proj + mm(attT[j].astype(BF16), gm[j])
    grad_proj = grad_proj.astype(BF16)
    for d in range(8):
        for c in range(4):
            early[d // 4, d % 4, c, :, 0:128] = grad_proj[32 * c : 32 * c + 32, 128 * d : 128 * d + 128]
    sums_early = Direct(torus, early, e_x, e_res, e_z, es, er)
    sums_q = Direct(torus, late_q, q_x, q_res, q_z, lqs, lqr)
    sums_k = Direct(torus, late_k, k_x, k_res, k_z, lks, lkr)
    sums_early.start()

    lane = lax.broadcasted_iota(jnp.int32, (TOK, 128), 1)

    def chunk_copy(r, m):
        shard = (ctx + r) % 4
        return remote(dkv.at[m, shard], kbuf.at[m, ctx], ksend.at[m, r], krecv.at[m, r], (dp, ep, shard))

    def chunk_go(m):
        for r in (2, 1, 3):
            chunk_copy(r, m).start()
        kbuf[m, ctx] = dkv[m, ctx]

    def piece_copy(src, dst, send, recv, m):
        return remote(src.at[m], dst.at[ep], send.at[m], recv.at[ep], (dp, m, ctx))

    def piece_go(src, dst, send, recv, m):
        @pl.when(ep != m)
        def _():
            piece_copy(src, dst, send, recv, m).start()

        @pl.when(ep == m)
        def _():
            dst[ep] = src[m]

    def pieces_got(src, dst, send, recv):
        def one(r):
            p = (ep + r) % 8
            remote(src.at[p], dst.at[p], send.at[p], recv.at[p], (dp, p, ctx)).wait_recv()

        repeat(1, 8, one)

    def pieces_sent(src, dst, send, recv):
        repeat(1, 8, lambda r: piece_copy(src, dst, send, recv, (ep + r) % 8).wait_send())

    def chunk_done(m):
        for r in (1, 2, 3):
            v = kbuf.at[m, (ctx + 4 - r) % 4]
            remote(v, v, ksend.at[m, r], krecv.at[m, r], (dp, ep, (ctx + r) % 4)).wait_recv()
        grad = kbuf[m, 0].astype(F32) + kbuf[m, 1].astype(F32) + kbuf[m, 2].astype(F32) + kbuf[m, 3].astype(F32)
        cosine, sine = rope_block(4 * m + ctx, ca_ref, sa_ref, cb_ref, sb_ref)
        cosine = jnp.where(lane < HD, cosine, 1.0)
        sine = jnp.where(lane < HD, sine, 0.0)
        dkvb[m] = (grad * cosine - rotate_half(grad) * sine).astype(BF16)
        piece_go(dkvb, kpieces, psend, precv, m)

    def progress(m):
        @pl.when(m == 0)
        def _():
            finish_x(0)
            finish_z(0)
            results.far()

        @pl.when(m == 1)
        def _():
            finish_x(1)
            finish_z(1)
            results.near()

        @pl.when(m == 2)
        def _():
            finish_x(2)
            xa[4].advance(2)
            h1.start()

        @pl.when(m == 3)
        def _():
            finish_x(3)
            g1.start()
            xa[5].advance(2)
            sums_early.turn()

        @pl.when(m == 4)
        def _():
            h1.advance(2)
            xa[6].advance(2)
            out_ref[...] = (res[...] + results.last()).astype(BF16)

        @pl.when(m == 6)
        def _():
            g1.advance(2)

    dqs[...] = jnp.zeros((8, HD, 256), F32)

    def key_chunk(m):
        acc[...] = jnp.zeros((CHUNK, 128), F32)

        def pair(j):
            both_grads, query_grad = attend_pair(m, j, kv, kT, both, stack, rows)
            acc[...] += both_grads
            dqs[j] += query_grad

        repeat(m, 8, pair)
        dkv[m] = acc[...].astype(BF16).reshape(4, TOK, 128)
        chunk_go(m)
        dq = dqs[m] * (HD**-0.5)
        dq = jnp.concatenate([dq[:, :128], dq[:, 128:]], axis=0).T
        cosine, sine = rope_block(4 * m + ctx, ca_ref, sa_ref, cb_ref, sb_ref)
        dqb[m] = (dq * cosine - rotate_half(dq) * sine).astype(BF16)
        piece_go(dqb, qpieces, qsend, qrecv, m)

        @pl.when(m >= 2)
        def _():
            chunk_done(m - 2)

        progress(m)

    repeat(0, 8, key_chunk)
    chunk_done(6)
    for name in ("nall", "wq"):
        loads[name].wait()

    def weights(grad, late):
        out = mm(nall[...].reshape(1024, 1024), grad.reshape(1024, 128), TN).astype(BF16)
        for d in range(8):
            for c in range(4):
                at = d * 128 + c * 32
                late[d // 4, d % 4, c] = out[at : at + 32]

    weights(dqb[...], late_q)
    sums_q.start()
    chunk_done(7)
    weights(dkvb[...], late_k)
    sums_k.start()
    pieces_got(dqb, qpieces, qsend, qrecv)
    grad_q = jnp.concatenate([qpieces[p] for p in range(8)], axis=1)
    grad_normed = mm(grad_q, wq[...], NT)

    def piece(g, h, kind, device):
        index = (kind * 4 + g) * 2 + h
        src = (fin.at[g, :, pl.ds(128, 128)], fin.at[g, :, pl.ds(0, 128)], fin_late.at[g])[kind]
        mine = dp if kind == 1 else ep
        return remote(src, (rs, rp, rq)[kind].at[mine], fsend.at[index], frecv.at[kind, mine], device)

    def each_piece(kinds, act, local):
        def one(i):
            g, h = i // 2, i % 2
            for kind in kinds:
                device = send_to(g, h)[kind % 2]

                @pl.when(jnp.logical_not(is_me(device)))
                def _():
                    act(piece(g, h, kind, device))

                if local:

                    @pl.when(is_me(device))
                    def _():
                        if kind == 0:
                            rs[ep] = fin[g, :, 128:256]
                        elif kind == 1:
                            rp[dp] = fin[g, :, 0:128]
                        else:
                            rq[ep] = fin_late[g]

        repeat(0, 8, one)

    def pieces_in(kind):
        def one(i):
            device = (i, dp, ep // 2) if kind == 1 else (dp, i, ep // 2)

            @pl.when(jnp.logical_not(is_me(device)))
            def _():
                dst = (rs, rp, rq)[kind].at[i]
                remote(dst, dst, fsend.at[kind * 8], frecv.at[kind, i], device).wait_recv()

        repeat(0, 8, one)

    done_early = sums_early.finish()
    for g in range(4):
        fin[g] = done_early[8 * g : 8 * g + 8]
    each_piece((0, 1), lambda c: c.start(), True)
    g1.advance(3)
    for name in ("wk", "wv"):
        loads[name].wait()
    pieces_got(dkvb, kpieces, psend, precv)
    grad_k = jnp.concatenate([kpieces[p, :, 0:HD] for p in range(8)], axis=1)
    grad_v = jnp.concatenate([kpieces[p, :, HD:128] for p in range(8)], axis=1)
    grad_normed = grad_normed + mm(grad_k, wk[...], NT) + mm(grad_v, wv[...], NT)
    x = x_ref[...].astype(F32)
    scale = lax.rsqrt(jnp.mean(x * x, axis=-1, keepdims=True) + EPSILON)
    scaled = x * scale
    gain_one = jnp.sum(grad_normed * scaled, axis=0, keepdims=True)
    for t in range(8):
        gain_own[0, t : t + 1, :] = gain_one[:, 128 * t : 128 * t + 128]

    def gain_copy(stage, r):
        src = gain_own.at[stage]
        if stage == 0:
            dst, device, base = gain_e.at[r - 1], (dp, (ep + r) % 8, ctx), 0
        elif stage == 1:
            dst, device, base = gain_x.at[r - 1], torus.at_x(torus.x + r), 7
        else:
            dst, device, base = gain_z.at[r - 1], torus.at_z(torus.z + r), 10
        return remote(src, dst, gs.at[base + r], gr.at[base + r], device)

    def gain_stage(stage, count):
        if stage > 0:
            last, slots = ((7, gain_e), (3, gain_x), (7, gain_z))[stage - 1]
            repeat(1, last + 1, lambda r: gain_copy(stage - 1, r).wait_recv())
            value = gain_own[stage - 1]
            for r in range(1, last + 1):
                value = value + slots[r - 1]
            gain_own[stage] = value
        repeat(1, count + 1, lambda r: gain_copy(stage, r).start())

    gain_stage(0, 7)
    grad_normed = grad_normed * gain_one_ref[...]
    mean = jnp.mean(grad_normed * scaled, axis=-1, keepdims=True)
    ing_ref[...] = (gres[...] + scale * (grad_normed - scaled * mean)).astype(BF16)

    sums_q.turn()
    gain_stage(1, 3)
    sums_k.turn()
    for i in (4, 5, 6):
        finish_x(i)
    g2.start()
    gain_stage(2, 7)

    done_q, done_k = sums_q.finish(), sums_k.finish()
    for g in range(4):
        at = slice(8 * g, 8 * g + 8)
        fin_late[g, :, 0:128] = done_q[at]
        fin_late[g, :, 128:256] = done_k[at]
    each_piece((2,), lambda c: c.start(), True)

    g1.advance(4)
    g2.advance(2)

    def put_unit(unit, value):
        j, u = unit // 3, unit % 3
        if u < 2:
            gin_ref[j, 16 * u : 16 * u + 16, :] = value
        else:
            gout_ref[j] = value

    def finish_units(arc, units):
        for way in (0, 1):
            arc.copy(way, arc.steps).wait_recv()
        mine = arc.own(arc.pos)
        up, down = arc.slots.at[0, arc.steps - 1], arc.slots.at[1, arc.steps - 1]
        for i, unit in enumerate(units):
            put_unit(unit, mine[i].astype(F32) + up[i].astype(F32) + down[i].astype(F32))

    for way in (0, 1):
        h0.copy(way, 2).wait_recv()
    for h in (0, 1):
        value = rz0[torus.x, h].astype(F32) + h0_slots[0, 1, h].astype(F32) + h0_slots[1, 1, h].astype(F32)
        gout_ref[0, :, 512 * h : 512 * h + 512] = value
    finish_units(h1, Z_UNITS)
    finish_units(g0, X_FIRST)
    g2.advance(3)
    finish_units(g1, X_UNITS[:4])
    pieces_in(0)
    pieces_in(1)
    last = gain_own[2]
    repeat(1, 8, lambda r: gain_copy(2, r).wait_recv())
    for r in range(7):
        last = last + gain_z[r]
    gain_own[3] = last

    g2.advance(4)
    pieces_in(2)
    odd = ctx % 2 == 1

    def mine(v):
        return jnp.where(odd, v[4:8], v[0:4])

    gq_ref[...] = mine(jnp.concatenate([rq[i, :, 0:128] for i in range(8)], axis=1))
    gk_ref[...] = mine(jnp.concatenate([rq[i, :, 128:192] for i in range(8)], axis=1))
    gv_ref[...] = mine(jnp.concatenate([rq[i, :, 192:256] for i in range(8)], axis=1))
    side = rs[0]
    for i in range(1, 8):
        side = side + rs[i]
    gside_ref[...] = mine(side)
    gproj_out[...] = mine(jnp.concatenate([rp[i] for i in range(8)], axis=1))
    for which in (0, 1):
        row = jnp.broadcast_to(gain_own[3, pl.ds(8 * which + dp, 1), :], (8, 128))
        gains_ref[8 * which : 8 * which + 8, :] = pltpu.roll(row, (128 - 16 * ep - 4 * ctx) % 128, 1)

    finish_units(g2, X_UNITS[4:])

    results.sent()
    gather.sent()
    exchange_sent(dg_ref, dbuf, dsend, drecv, place)
    pieces_sent(dqb, qpieces, qsend, qrecv)
    pieces_sent(dkvb, kpieces, psend, precv)

    def chunk_sent(m):
        for r in (1, 2, 3):
            chunk_copy(r, m).wait_send()

    repeat(0, 8, chunk_sent)
    for arc in xa + za + [g0, g1, g2, h0, h1]:
        arc.sent()
    for sums in (sums_early, sums_q, sums_k):
        sums.sent()
    for stage, count in ((0, 7), (1, 3), (2, 7)):
        repeat(1, count + 1, lambda r: gain_copy(stage, r).wait_send())
    each_piece((0, 1, 2), lambda c: c.wait_send(), False)


def pack_kernel(*refs):
    count = len(refs) // 2
    for src, dst in zip(refs[:count], refs[count:]):
        dst[...] = src[...]


def call(kernel, outs, scratch, args, name, collective=None, **more):
    params = dict(vmem_limit_bytes=VMEM_LIMIT)
    if collective is not None:
        params.update(collective_id=collective, has_side_effects=True)
    space = pl.BlockSpec(memory_space=pltpu.VMEM)
    return pl.pallas_call(
        kernel,
        out_shape=[jax.ShapeDtypeStruct(shape, kind) for shape, kind in outs],
        in_specs=more.pop("in_specs", [space] * len(args)),
        out_specs=more.pop("out_specs", [space] * len(outs)),
        scratch_shapes=scratch,
        compiler_params=pltpu.CompilerParams(**params),
        name=name,
        **more,
    )(*args)


def sems(*sizes):
    return [pltpu.SemaphoreType.DMA(s if isinstance(s, tuple) else (s,)) for s in sizes]


def body(
    layer_input, gain_attn, w_query, w_key, w_value, w_proj, gain_ffn, w_router,
    w_expert_in, w_expert_out, segment_ids, expert_ids, slot_order, out_grad,
):
    gain_one, gain_two = gain_attn.reshape(1, 1024), gain_ffn.reshape(1, 1024)
    tables = [jnp.asarray(t) for t in rope_tables()]
    wr_rows = jnp.pad(w_router.T.reshape(8, 4, 1024), ((0, 0), (0, 4), (0, 0))).reshape(64, 1024)
    order = slot_order.reshape(TOK, 8)
    docs = segment_ids.reshape(32, 128)

    vm, hbm = pl.BlockSpec(memory_space=pltpu.VMEM), pl.BlockSpec(memory_space=pl.ANY)
    wide, block = pltpu.VMEM((8, TOK, 1024), BF16), pltpu.VMEM((8, TOK, 128), BF16)
    (
        normed_all, grad_all, query, kv, slots, starts, attended_tall, log_sums, residual, ffn_all, gates_in, gates,
    ) = call(
        head_kernel,
        [
            ((8, TOK, 1024), BF16), ((8, TOK, 1024), BF16), ((8, TOK, 128), BF16), ((8, 4, TOK, 128), BF16),
            ((8, 8, TOK), F32), ((32, 128), F32), ((8, 128, TOK), F32), ((8, 8, 256), F32),
            ((TOK, 1024), F32), ((8, TOK, 1024), BF16), ((8, 8, TOK), F32), ((64, TOK), F32),
        ],
        [
            pltpu.VMEM((1024, 128), BF16), pltpu.VMEM((1024, 128), BF16), pltpu.VMEM((1024, 128), BF16),
            pltpu.VMEM((1024, 256), BF16), pltpu.VMEM((1024, 1024), BF16), pltpu.VMEM((8, 8, TOK), F32),
            pltpu.VMEM((64, TOK), F32), block, block, pltpu.VMEM((4096, 128), BF16), pltpu.VMEM((128, 4096), BF16),
            pltpu.VMEM((8, 8, TOK), F32),
        ]
        + sems(4, 13, 13, 13, 13, 8, 8, 24, 24, 8, 8, 13, 13, 8, 8),
        [
            layer_input, gain_one, gain_two, out_grad, *tables, expert_ids.T, order.T, docs, wr_rows,
            w_query, w_key, w_value, w_proj,
        ],
        "head", 1, in_specs=[vm] * 12 + [hbm] * 4,
    )
    kv_rows = kv.reshape(4096, 128)
    ex, ez = len(X_FIRST), len(Z_FIRST)
    sums, back, grad_gates, sums_x, sums_z, units = call(
        expert_kernel,
        [
            ((8, TOK, 1024), BF16), ((8, TOK, 1024), BF16), ((8, 8, TOK), F32), ((8, ex, 16, 1024), BF16),
            ((4, 2, 16, 512), BF16), ((12 - KEPT, 2, 4, 4, 16, 1024), BF16),
        ],
        [
            wide, wide, pltpu.VMEM((2, 1024, 1024), BF16), pltpu.VMEM((2, 512, 1024), BF16),
            pltpu.VMEM((4, 8 * CAP, 1024), F32), pltpu.VMEM((4, 8 * CAP, 1024), F32),
            pltpu.VMEM((12, 2, 4, 4, 16, 1024), BF16),
            pltpu.VMEM((ex, 2, 2, 2, 4, 16, 1024), BF16), pltpu.VMEM((ez, 2, 4, 4, 16, 1024), BF16),
        ]
        + sems(2, (4, 2), 12 - KEPT, (ex, 2, 2), (ex, 2, 2), (ez, 2, 4), (ez, 2, 4)),
        [slots, gates_in, ffn_all, grad_all, w_expert_in, w_expert_out],
        "experts", 4, in_specs=[vm, vm] + [hbm] * 4, out_specs=[vm] * 5 + [hbm],
    )
    nx, nz = len(X_UNITS), len(Z_UNITS)

    def direct(lanes):
        return [
            pltpu.VMEM((3, 2, 4, 32, lanes), BF16), pltpu.VMEM((8, 32, lanes), BF16), pltpu.VMEM((7, 32, lanes), BF16)
        ]

    results = call(
        tail_kernel,
        [
            ((TOK, 1024), BF16), ((TOK, 1024), BF16), ((4, 32, 1024), F32), ((4, 16, 1024), F32), ((4, 1024), F32),
            ((4, 512), F32), ((4, 512), F32), ((4, 128), F32), ((4, 1024), F32), ((16, 128), F32),
        ],
        [
            wide, pltpu.VMEM((TOK, 1024), BF16), pltpu.VMEM((TOK, 1024), F32), pltpu.VMEM((TOK, 1024), BF16), block,
            pltpu.VMEM((4096, 128), BF16), pltpu.VMEM((8, 128, TOK), F32), pltpu.VMEM((128, 1024), BF16), wide,
            pltpu.VMEM((1024, 1024), BF16), pltpu.VMEM((1024, 512), BF16), pltpu.VMEM((1024, 512), BF16),
            pltpu.VMEM((nx + nz, 2, 4, 4, 16, 1024), BF16),
            pltpu.VMEM((8, 8, TOK), F32),
        ]
        + scatter_sum_scratch()[:3] * 2
        + [
            wide, pltpu.VMEM((TOK, 1024), F32),
            pltpu.VMEM((HD, 4096), BF16), pltpu.VMEM((8, 128, 512), BF16), pltpu.VMEM((8, 512, 128), BF16),
            pltpu.VMEM((8, 8, 256), F32), pltpu.VMEM((8, HD, 256), F32), pltpu.VMEM((CHUNK, 128), F32),
            pltpu.VMEM((8, 4, TOK, 128), BF16),
            block, block, pltpu.VMEM((8, 4, TOK, 128), BF16), block, block,
            pltpu.VMEM((nx, 2, 2, 2, 4, 16, 1024), BF16), pltpu.VMEM((nz, 2, 4, 4, 16, 1024), BF16),
            pltpu.VMEM((2, 4, ex, 16, 1024), BF16), pltpu.VMEM((2, 4, 4, 16, 1024), BF16), pltpu.VMEM((2, 4, 3, 16, 1024), BF16),
            pltpu.VMEM((2, 2, 2, 16, 512), BF16), pltpu.VMEM((2, 2, nz, 16, 1024), BF16),
            pltpu.VMEM((8, 4, 16, 1024), BF16), pltpu.VMEM((8, 3, 16, 1024), BF16), pltpu.VMEM((4, nz, 16, 1024), BF16),
            pltpu.VMEM((2, 4, 4, 32, 256), BF16), pltpu.VMEM((2, 4, 4, 32, 128), BF16), pltpu.VMEM((2, 4, 4, 32, 128), BF16),
        ]
        + direct(256) + direct(128) + direct(128)
        + [
            pltpu.VMEM((4, 16, 128), F32), pltpu.VMEM((7, 16, 128), F32), pltpu.VMEM((3, 16, 128), F32),
            pltpu.VMEM((7, 16, 128), F32),
            pltpu.VMEM((4, 8, 256), F32), pltpu.VMEM((4, 8, 256), F32), pltpu.VMEM((8, 8, 128), F32),
            pltpu.VMEM((8, 8, 128), F32), pltpu.VMEM((8, 8, 256), F32),
        ]
        + sems(
            13, nx + nz, 8, 8, 8, 8, 8, 8, 13, 13, (8, 4), (8, 4), 8, 8, 8, 8,
            (nx, 2, 2), (nx, 2, 2), (nz, 2, 4), (nz, 2, 4),
            (2, 4), (2, 4), (2, 4), (2, 4), (2, 4), (2, 4), (2, 2), (2, 2), (2, 2), (2, 2), 11, 11, 11, 11, 11, 11, 18, 18,
            24, (3, 8),
        ),
        [
            grad_gates, gates, gain_two, wr_rows, layer_input, gain_one, *tables, starts, log_sums,
            sums_x, sums_z, back, ffn_all, residual, out_grad, query, kv_rows, attended_tall, w_proj, sums, normed_all,
            w_query, w_key, w_value, units,
        ],
        "tail", 3, in_specs=[vm] * 14 + [hbm] * 14,
    )
    layer_output, input_grad, grad_in, grad_out, out_q, out_k, out_v, side, out_proj, gains = call(
        pack_kernel, [(r.shape, r.dtype) for r in results], [], results, "pack"
    )
    return (
        layer_output, input_grad, gains[0, :4], out_q, out_k, out_v, out_proj, gains[8, :4], side[:, :32], grad_in, grad_out,
    )


def solution(mesh):
    tokens = P(("dp", "ep", "ctx"), None)
    in_specs = (
        tokens, P(), P(), P(), P(), P(), P(), P(),
        P("ep", None, None), P("ep", None, None), P("dp", None), tokens, tokens, tokens,
    )
    out_specs = (
        tokens, tokens, P(("dp", "ep", "ctx")), tokens, tokens, tokens, tokens, P(("dp", "ep", "ctx")), tokens,
        P("ep", ("dp", "ctx"), None), P("ep", ("dp", "ctx"), None),
    )
    return jax.shard_map(body, mesh=mesh, in_specs=in_specs, out_specs=out_specs, check_vma=False)
```

```python
from functools import partial

import jax
import jax.numpy as jnp
import numpy as np
from jax import lax
from jax.experimental import pallas as pl
from jax.experimental.pallas import tpu as pltpu
from jax.sharding import PartitionSpec as P

HD = 64
EPSILON = 1e-06
MASKED = -1e30
CAP = 40
TOK = 128
BIG = 4096.0
MESH = pl.DeviceIdType.MESH
F32 = jnp.float32
BF16 = jnp.bfloat16
VMEM_LIMIT = 60 * 1024 * 1024

NT = (((1,), (1,)), ((), ()))
NN = (((1,), (0,)), ((), ()))
TN = (((0,), (0,)), ((), ()))


def mm(a, b, dims=NN):
    return lax.dot_general(a, b, dims, preferred_element_type=F32)


def mm3(a, b, dims=NN):
    high = a.astype(BF16)
    low = (a - high.astype(F32)).astype(BF16)
    return mm(high, b, dims) + mm(low, b, dims)


def where_am_i():
    dp, ep, ctx = lax.axis_index("dp"), lax.axis_index("ep"), lax.axis_index("ctx")
    return dp, ep, ctx


def remote(src, dst, send, recv, device):
    return pltpu.make_async_remote_copy(
        src_ref=src, dst_ref=dst, send_sem=send, recv_sem=recv, device_id=device, device_id_type=MESH
    )


def greet(barrier, device):
    pl.semaphore_signal(barrier, inc=1, device_id=device, device_id_type=MESH)


def rotate_half(values):
    lane = lax.broadcasted_iota(jnp.int32, values.shape, 1)
    return jnp.where(lane % HD < HD // 2, pltpu.roll(values, 96, 1), pltpu.roll(values, 32, 1))


def rope_block(block, ca_ref, sa_ref, cb_ref, sb_ref):
    ca, sa = ca_ref[pl.ds(block, 1), :], sa_ref[pl.ds(block, 1), :]
    cb, sb = cb_ref[...], sb_ref[...]
    cosine = ca * cb - sa * sb
    sine = sa * cb + ca * sb
    lane = lax.broadcasted_iota(jnp.int32, cosine.shape, 1)
    return cosine, jnp.where(lane % HD < HD // 2, -sine, sine)


def rope_tables():
    frequency = 10000.0 ** (-np.arange(HD // 2, dtype=np.float64) * 2.0 / HD)
    frequency = np.tile(frequency.astype(np.float32).astype(np.float64), 4)
    blocks = np.arange(32, dtype=np.float64)[:, None] * 128.0 * frequency[None, :]
    rows = np.arange(128, dtype=np.float64)[:, None] * frequency[None, :]
    return [t.astype(np.float32) for t in (np.cos(blocks), np.sin(blocks), np.cos(rows), np.sin(rows))]


class EpGather:
    COUNT = 13

    def __init__(self, ref, send, recv, place):
        self.ref, self.send, self.recv = ref, send, recv
        dp, ep, ctx = place
        y, k = ep // 2, ep % 2
        self.up = (dp, ((y + 1) % 4) * 2 + k, ctx)
        self.dn = (dp, ((y + 3) % 4) * 2 + k, ctx)
        self.sib = (dp, y * 2 + 1 - k, ctx)

        def at(dy, other):
            return ((y + dy) % 4) * 2 + ((1 - k) if other else k)

        u, s, d = self.up, self.sib, self.dn
        self.sends = [
            (at(0, 0), None, s), (at(0, 0), 0, u), (at(0, 0), 1, u), (at(0, 0), 1, d), (at(0, 0), 0, d),
            (at(3, 0), 0, u), (at(3, 0), 0, s), (at(1, 0), 1, d), (at(1, 0), 1, s),
            (at(3, 0), 1, s), (at(1, 0), 0, s), (at(2, 0), 0, s), (at(2, 0), 1, s),
        ]
        self.gets = [
            (at(0, 1), None), (at(3, 0), 0), (at(3, 0), 1), (at(1, 0), 1), (at(1, 0), 0),
            (at(2, 0), 0), (at(3, 1), 0), (at(2, 0), 1), (at(1, 1), 1),
            (at(3, 1), 1), (at(1, 1), 0), (at(2, 1), 0), (at(2, 1), 1),
        ]

    def view(self, block, half):
        if half is None:
            return self.ref.at[block]
        rows = self.ref.shape[1] // 2
        return self.ref.at[block, pl.ds(half * rows, rows)]

    def go(self, *which):
        for i in which:
            block, half, device = self.sends[i]
            v = self.view(block, half)
            remote(v, v, self.send.at[i], self.recv.at[i], device).start()

    def got(self, *which):
        for i in which:
            v = self.view(*self.gets[i])
            remote(v, v, self.send.at[i], self.recv.at[i], self.sends[i][2]).wait_recv()

    def sent(self):
        for i in range(self.COUNT):
            block, half, device = self.sends[i]
            v = self.view(block, half)
            remote(v, v, self.send.at[i], self.recv.at[i], device).wait_send()

    def whole(self):
        self.got(1)
        self.go(5, 6)
        self.got(3)
        self.go(7, 8)
        self.got(2)
        self.go(9)
        self.got(4)
        self.go(10)
        self.got(5)
        self.go(11)
        self.got(7)
        self.go(12)
        self.got(0, 6, 8, 9, 10, 11, 12)


class EpScatterSum:
    COUNT = 8

    def __init__(self, part, cbuf, fbuf, gbuf, send, recv, place):
        self.part, self.cbuf, self.fbuf, self.gbuf = part, cbuf, fbuf, gbuf
        self.send, self.recv = send, recv
        dp, ep, ctx = place
        self.y, self.k = ep // 2, ep % 2
        y, k = self.y, self.k
        self.up = (dp, ((y + 1) % 4) * 2 + k, ctx)
        self.dn = (dp, ((y + 3) % 4) * 2 + k, ctx)
        self.sib = (dp, y * 2 + 1 - k, ctx)

    def block(self, dy, other=False):
        return ((self.y + dy) % 4) * 2 + ((1 - self.k) if other else self.k)

    def copy(self, i):
        half = self.cbuf.shape[1] // 2
        lo, hi = pl.ds(0, half), pl.ds(half, half)
        s, r = self.send, self.recv
        if i < 4:
            away = self.block((2, 1, 3, 0)[i], True)
            return remote(self.part.at[away], self.cbuf.at[i], s.at[i], r.at[i], self.sib)
        src, dst, device = (
            (self.cbuf.at[0, lo], self.fbuf.at[0], self.up),
            (self.cbuf.at[0, hi], self.fbuf.at[1], self.dn),
            (self.cbuf.at[1], self.gbuf.at[0], self.up),
            (self.cbuf.at[2], self.gbuf.at[1], self.dn),
        )[i - 4]
        return remote(src, dst, s.at[i], r.at[i], device)

    def start(self):
        for i in range(4):
            self.copy(i).start()

    def far(self):
        self.copy(0).wait_recv()
        self.cbuf[0] = (self.cbuf[0].astype(F32) + self.part[self.block(2)].astype(F32)).astype(BF16)
        self.copy(4).start()
        self.copy(5).start()

    def near(self):
        half = self.cbuf.shape[1] // 2
        for slot, dy, far, rows, rest in ((1, 1, 0, pl.ds(0, half), pl.ds(half, half)), (2, 3, 1, pl.ds(half, half), pl.ds(0, half))):
            b = self.block(dy)
            self.copy(slot).wait_recv()
            self.copy(4 + far).wait_recv()
            self.cbuf[slot, rows] = (
                self.cbuf[slot, rows].astype(F32) + self.part[b, rows].astype(F32) + self.fbuf[far].astype(F32)
            ).astype(BF16)
            self.cbuf[slot, rest] = (self.cbuf[slot, rest].astype(F32) + self.part[b, rest].astype(F32)).astype(BF16)
            self.copy(6 + far).start()

    def last(self):
        for i in (3, 6, 7):
            self.copy(i).wait_recv()
        return (
            self.part[self.block(0)].astype(F32) + self.cbuf[3].astype(F32)
            + self.gbuf[0].astype(F32) + self.gbuf[1].astype(F32)
        )

    def sent(self):
        for i in range(self.COUNT):
            self.copy(i).wait_send()


def scatter_sum_scratch():
    return [
        pltpu.VMEM((4, TOK, 1024), BF16),
        pltpu.VMEM((2, TOK // 2, 1024), BF16),
        pltpu.VMEM((2, TOK, 1024), BF16),
        pltpu.SemaphoreType.DMA((8,)),
        pltpu.SemaphoreType.DMA((8,)),
    ]


def repeat(first, last, work):
    def each(i, carry):
        work(i)
        return carry

    lax.fori_loop(first, last, each, 0)


def exchange(src, dst, send, recv, place, wait):
    dp, ep, ctx = place

    def one(r):
        to, source = (ep + r) % 8, (ep + 8 - r) % 8
        if not wait:
            remote(src.at[to], dst.at[ep], send.at[r], recv.at[r], (dp, to, ctx)).start()
        else:
            remote(src.at[to], dst.at[source], send.at[r], recv.at[r], (dp, to, ctx)).wait_recv()

    repeat(1, 8, one)


def exchange_sent(src, dst, send, recv, place):
    dp, ep, ctx = place

    def one(r):
        to = (ep + r) % 8
        remote(src.at[to], dst.at[ep], send.at[r], recv.at[r], (dp, to, ctx)).wait_send()

    repeat(1, 8, one)


def starts_of(docs):
    rows = lax.broadcasted_iota(jnp.int32, docs.shape, 0)
    lane = lax.broadcasted_iota(jnp.int32, docs.shape, 1)
    docs = docs.astype(F32)
    turned = pltpu.roll(docs, 1, 1)
    before = jnp.where(lane == 0, pltpu.roll(turned, 1, 0), turned)
    place = rows * 128 + lane
    fresh = (docs != before) | (place == 0)
    value = jnp.where(fresh, place.astype(F32), 0.0)
    for shift in (1, 2, 4, 8, 16, 32, 64):
        value = jnp.maximum(value, jnp.where(lane >= shift, pltpu.roll(value, shift, 1), 0.0))
    carry = jnp.broadcast_to(jnp.max(value, axis=1, keepdims=True), value.shape)
    for shift in (1, 2, 4, 8, 16):
        carry = jnp.maximum(carry, jnp.where(rows >= shift, pltpu.roll(carry, shift, 0), 0.0))
    above = jnp.where(rows >= 1, pltpu.roll(carry, 1, 0), 0.0)
    return jnp.maximum(value, above)


def priorities(order):
    def spread(part):
        return mm(part.astype(F32).astype(BF16), from_rows, TN)

    r = lax.broadcasted_iota(jnp.int32, (8, 128), 0)
    t = lax.broadcasted_iota(jnp.int32, (8, 128), 1)
    from_rows = jnp.where(t // 16 == r, 1.0, 0.0).astype(BF16)
    of_k = jnp.where(t % 8 == r, 1.0, 0.0).astype(BF16)
    l = lax.broadcasted_iota(jnp.int32, (128, 128), 0)
    t = lax.broadcasted_iota(jnp.int32, (128, 128), 1)
    meets = l // 8 == t % 16
    high = jnp.where(meets, spread(order // 32), 0.0).astype(BF16)
    low = jnp.where(meets, spread(order % 32), 0.0).astype(BF16)
    return mm(of_k, high) * 32.0 + mm(of_k, low)


def slots_of(eidT_ref, order_ref, slot_scr, sel_ref):
    def expert(index):
        return jnp.where(index % 8 < 4, (index // 8) * 4 + index % 8, -1)

    row_expert = expert(lax.broadcasted_iota(jnp.int32, (64, TOK), 0))
    by_row = jnp.full((64, TOK), BIG, F32)
    ranks = priorities(order_ref[...])
    for k in range(8):
        by_row = jnp.where(eidT_ref[k : k + 1, :] == row_expert, ranks[k : k + 1, :], by_row)
    by_lane = by_row.T
    sel_ref[...] = jnp.where(by_row < BIG, 1.0, 0.0)
    for g in range(8):
        for j in range(4):
            r = 8 * g + j
            row = by_row[r : r + 1, :]
            less = jnp.where(by_lane[:, r : r + 1] < row, 1.0, 0.0)
            rank = jnp.sum(less, axis=0, keepdims=True)
            slot_scr[g, j : j + 1, :] = jnp.where((row < BIG) & (rank < CAP), rank, -1.0)
        slot_scr[g, 4:8, :] = jnp.full((4, TOK), -1.0, F32)


CHUNK = 512


def key_mask(step, start_row, place_row):
    keys = (lax.broadcasted_iota(jnp.int32, (2 * CHUNK, 256), 0) + step * (2 * CHUNK)).astype(F32)
    return (keys >= start_row) & (keys <= place_row)


def query_rows(j, ctx, start_ref):
    block = 4 * j + ctx
    start = start_ref[pl.ds(block, 1), :]
    places = (lax.broadcasted_iota(jnp.int32, (1, 128), 1) + block * 128).astype(F32)
    return jnp.concatenate([start, start], axis=1), jnp.concatenate([places, places], axis=1)


def turned(block):
    return block.astype(F32).T.astype(BF16)


def heads_wide(tall):
    return jnp.concatenate([tall[:HD], tall[HD:]], axis=1)


def head_kernel(
    x_ref, gain_one_ref, gain_two_ref, og_ref, ca_ref, sa_ref, cb_ref, sb_ref, eidT_ref, order_ref, doc_ref, wr_ref,
    wq_hbm, wk_hbm, wv_hbm, wp_hbm,
    nall_ref, ogall_ref, q_ref, kv_ref, slot_ref, start_ref, attT_ref, lse_ref, res_ref, nf_ref, gin_ref, gates_ref,
    wq, wk, wv, w_own, wp, slot_scr, sel, att, abuf, kv_rows, kvT, gscr,
    wsem, nsend, nrecv, osend, orecv, ssend, srecv, ksend, krecv, asend, arecv, fsend, frecv, gsend, grecv,
):
    place = where_am_i()
    dp, ep, ctx = place
    y = ep // 2
    pair = pl.ds(pl.multiple_of(y * 128, 128), 128)
    loads = [
        pltpu.make_async_copy(src, dst, wsem.at[i])
        for i, (src, dst) in enumerate(
            (
                (wq_hbm.at[:, pl.ds(pl.multiple_of(ep * 128, 128), 128)], wq),
                (wk_hbm.at[:, pair], wk),
                (wv_hbm.at[:, pair], wv),
                (wp_hbm, wp),
            )
        )
    ]
    for f in loads:
        f.start()
    barrier = pltpu.get_barrier_semaphore()
    repeat(1, 8, lambda r: greet(barrier, (dp, (ep + r) % 8, ctx)))

    @pl.when(ctx > 0)
    def _():
        greet(barrier, (dp, ep, ctx - 1))

    @pl.when(ctx < 3)
    def _():
        greet(barrier, (dp, ep, ctx + 1))

    x = x_ref[...].astype(F32)
    normed = x * lax.rsqrt(jnp.mean(x * x, axis=-1, keepdims=True) + EPSILON) * gain_one_ref[...]
    nall_ref[ep] = normed.astype(BF16)
    ogall_ref[ep] = og_ref[...]
    edges = jnp.where(ctx > 0, 1, 0) + jnp.where(ctx < 3, 1, 0)
    pl.semaphore_wait(barrier, 7 + edges)

    gather = EpGather(nall_ref, nsend, nrecv, place)
    grads = EpGather(ogall_ref, osend, orecv, place)
    gather.go(0, 1, 3, 2, 4)
    for f in loads[:3]:
        f.wait()
    lane = lax.broadcasted_iota(jnp.int32, (1024, 128), 1)
    even = ep % 2 == 0
    k_pair, v_pair = wk[...].astype(F32), wv[...].astype(F32)
    k_half = jnp.where(even, k_pair, pltpu.roll(k_pair, HD, 1))
    v_half = jnp.where(even, pltpu.roll(v_pair, HD, 1), v_pair)
    w_own[:, 0:128] = wq[...]
    w_own[:, 128:256] = jnp.where(lane < HD, k_half, v_half).astype(BF16)
    lane = lax.broadcasted_iota(jnp.int32, (TOK, 128), 1)

    def project(dy):
        chip = (y + dy) % 4
        rows = jnp.concatenate([nall_ref[2 * chip], nall_ref[2 * chip + 1]], axis=0)
        out = mm(rows, w_own[...])
        for i in range(2):
            b = 2 * chip + i
            cosine, sine = rope_block(4 * b + ctx, ca_ref, sa_ref, cb_ref, sb_ref)
            q = out[i * TOK : (i + 1) * TOK, :128]
            kv = out[i * TOK : (i + 1) * TOK, 128:]
            q_rot = (q * cosine + rotate_half(q) * sine).astype(BF16)
            q_ref[b] = (q_rot.astype(F32) * (HD**-0.5)).astype(BF16)
            cosine = jnp.where(lane < HD, cosine, 1.0)
            sine = jnp.where(lane < HD, sine, 0.0)
            kv_ref[b, ctx] = (kv * cosine + rotate_half(kv) * sine).astype(BF16)

    offsets = (0, 3, 1, 2)

    def hop(direction, h, g, action):
        chip = (y + offsets[g]) % 4
        back = h - 1
        own = ctx - back if direction == 0 else ctx + back
        come = ctx - h if direction == 0 else ctx + h
        to = ctx + 1 if direction == 0 else ctx - 1
        index = (direction * 3 + back) * 4 + g
        send, recv = ksend.at[index], krecv.at[index]
        if action == "recv":
            ok = come >= 0 if direction == 0 else come <= 3

            @pl.when(ok)
            def _():
                v = kv_ref.at[pl.ds(2 * chip, 2), come]
                remote(v, v, send, recv, (dp, ep, ctx)).wait_recv()

        else:
            ok = (own >= 0) & (ctx < 3) if direction == 0 else (own <= 3) & (ctx > 0)

            @pl.when(ok)
            def _():
                v = kv_ref.at[pl.ds(2 * chip, 2), own]
                c = remote(v, v, send, recv, (dp, ep, to))
                c.start() if action == "send" else c.wait_send()

    def hops(h, g):
        for direction in (0, 1):
            if h > 1:
                hop(direction, h - 1, g, "recv")
            hop(direction, h, g, "send")

    gather.got(0)
    project(0)
    hops(1, 0)
    start_ref[...] = starts_of(doc_ref[...])
    slots_of(eidT_ref, order_ref, slot_scr, sel)
    gather.got(1)
    gather.go(5, 6)
    gather.got(3)
    gather.go(7, 8)
    gather.got(2)
    gather.go(9)
    gather.got(4)
    gather.go(10)
    slot_ref[ep] = slot_scr[ep]
    exchange(slot_scr, slot_ref, ssend, srecv, place, False)
    hops(2, 0)
    gather.got(6, 9)
    project(3)
    hops(1, 1)
    gather.got(8, 10)
    project(1)
    hops(1, 2)
    hops(3, 0)
    hops(2, 1)
    gather.got(5)
    gather.go(11)
    gather.got(7)
    gather.go(12)
    grads.go(0, 1, 3, 2, 4)
    gather.got(11, 12)
    project(2)
    hops(1, 3)
    hops(2, 2)
    hops(3, 1)
    hops(2, 3)
    hops(3, 2)
    hops(3, 3)
    grads.got(1)
    grads.go(5, 6)
    grads.got(3)
    grads.go(7, 8)
    for g in range(4):
        for direction in (0, 1):
            hop(direction, 3, g, "recv")

    def turn_keys(chunk):
        rows = kv_ref[chunk].reshape(CHUNK, 128)
        at = pl.ds(pl.multiple_of(chunk * CHUNK, CHUNK), CHUNK)
        kv_rows[at, :] = rows
        part = rows.astype(F32).T
        row = lax.broadcasted_iota(jnp.int32, part.shape, 0)
        kvT[:, at] = jnp.where(row < HD, 1.0, part).astype(BF16)

    repeat(0, 8, turn_keys)

    def piece_copy(m):
        return remote(att.at[m], abuf.at[ep], asend.at[m], arecv.at[ep], (dp, m, ctx))

    def block(j):
        start_row, place_row = query_rows(j, ctx, start_ref)
        wide = heads_wide(turned(q_ref[j]))
        q_pad = jnp.concatenate([wide, jnp.zeros_like(wide)], axis=0)

        def step(i, carry):
            top, total = carry
            rows = pl.ds(pl.multiple_of(i * (2 * CHUNK), 2 * CHUNK), 2 * CHUNK)
            scores = mm(kv_rows[rows, :], q_pad)
            scores = jnp.where(key_mask(i, start_row, place_row), scores, MASKED)
            new_top = jnp.maximum(top, jnp.max(scores, axis=0, keepdims=True))
            probs = jnp.exp(scores - new_top).astype(BF16)
            total = total * jnp.exp(top - new_top) + mm(kvT[:, rows], probs)
            return new_top, total

        top, total = lax.fori_loop(0, j // 2 + 1, step, (jnp.full((1, 256), MASKED, F32), jnp.zeros((128, 256), F32)))
        norm = total[0:1]
        out = total[HD:] / norm
        tall = jnp.concatenate([out[:, :128], out[:, 128:]], axis=0)
        attT_ref[j] = tall
        att[j] = tall.T.astype(BF16)
        lse_ref[j] = jnp.broadcast_to(top + jnp.log(norm), (8, 256))

        @pl.when(ep != j)
        def _():
            piece_copy(j).start()

        @pl.when(ep == j)
        def _():
            abuf[ep] = att[j]

    repeat(0, 6, block)
    grads.got(2)
    grads.go(9)
    grads.got(4)
    grads.go(10)
    grads.got(5)
    grads.go(11)
    grads.got(7)
    grads.go(12)
    repeat(6, 8, block)

    loads[3].wait()

    def piece_got(r):
        p = (ep + r) % 8
        remote(att.at[p], abuf.at[p], asend.at[p], arecv.at[p], (dp, p, ctx)).wait_recv()

    repeat(1, 8, piece_got)
    attended = jnp.concatenate([abuf[p] for p in range(8)], axis=1)
    res = x_ref[...].astype(F32) + mm(attended, wp[...])
    res_ref[...] = res
    normed = res * lax.rsqrt(jnp.mean(res * res, axis=-1, keepdims=True) + EPSILON) * gain_two_ref[...]
    normed = normed.astype(BF16)
    nf_ref[ep] = normed
    rows = EpGather(nf_ref, fsend, frecv, place)
    rows.go(0, 1, 3, 2, 4)
    to = lax.broadcasted_iota(jnp.int32, (64, 32), 0)
    source = lax.broadcasted_iota(jnp.int32, (64, 32), 1)
    spread = jnp.where((to % 8 < 4) & (source == (to // 8) * 4 + to % 8), 1.0, 0.0).astype(BF16)
    logits = mm(mm(spread, wr_ref[...]).astype(BF16), normed, NT)
    chosen = sel[...] > 0.5
    top = jnp.max(jnp.where(chosen, logits, MASKED), axis=0, keepdims=True)
    weight = jnp.where(chosen, jnp.exp(jnp.where(chosen, logits, MASKED) - top), 0.0)
    gates = weight / jnp.sum(weight, axis=0, keepdims=True)
    gates_ref[...] = gates
    for g in range(8):
        gscr[g] = gates[8 * g : 8 * g + 8, :]
    gin_ref[ep] = gscr[ep]
    exchange(gscr, gin_ref, gsend, grecv, place, False)
    exchange(slot_scr, slot_ref, ssend, srecv, place, True)
    grads.got(0, 6, 8, 9, 10, 11, 12)
    rows.whole()
    exchange(gscr, gin_ref, gsend, grecv, place, True)
    for g in (gather, grads, rows):
        g.sent()
    exchange_sent(slot_scr, slot_ref, ssend, srecv, place)
    exchange_sent(gscr, gin_ref, gsend, grecv, place)
    repeat(1, 8, lambda r: piece_copy((ep + r) % 8).wait_send())
    for g in range(4):
        for h in (1, 2, 3):
            for direction in (0, 1):
                hop(direction, h, g, "sent")


def each_slab(lead, work):
    count = 1
    for size in lead:
        count *= size

    def each(i, carry):
        work((i,) if len(lead) == 1 else (i // lead[1], i % lead[1]))
        return carry

    lax.fori_loop(0, count, each, 0)


class Arc:
    def __init__(self, n, pos, own, half, slots, devices, send, recv):
        self.n, self.pos, self.own, self.half, self.slots = n, pos, own, half, slots
        self.devices, self.send, self.recv = devices, send, recv
        self.steps = n // 2

    def chunk(self, way, s):
        reach = self.steps - s + 1
        return (self.pos + reach) % self.n if way == 0 else (self.pos + self.n - reach) % self.n

    def copy(self, way, s):
        dst = self.slots.at[way, s - 1]
        src = self.own(self.chunk(way, s)) if s == 1 else self.slots.at[way, s - 2]
        if s == 1:
            src, dst = self.half(src, way), self.half(dst, way)
        return remote(src, dst, self.send.at[way, s - 1], self.recv.at[way, s - 1], self.devices[way])

    def start(self):
        for way in (0, 1):
            self.copy(way, 1).start()

    def slabs(self, work):
        each_slab(self.slots.shape[2:-2], work)

    def advance(self, s):
        for way in (0, 1):
            self.copy(way, s - 1).wait_recv()
            held, own = self.slots.at[way, s - 2], self.own(self.chunk(way, s))
            if s == 2:
                self.merge(way, held, own)
            else:

                def add(index):
                    held[index] = (held[index].astype(F32) + own[index].astype(F32)).astype(BF16)

                self.slabs(add)
            self.copy(way, s).start()

    def merge(self, way, held, own):
        mine, its = self.half(held, way), self.half(own, way)
        other, from_own = self.half(held, 1 - way), self.half(own, 1 - way)

        def add(index):
            mine[index] = (mine[index].astype(F32) + its[index].astype(F32)).astype(BF16)

        def take(index):
            other[index] = from_own[index]

        each_slab(mine.shape[:-2], add)
        each_slab(other.shape[:-2], take)

    def finish(self, put):
        for way in (0, 1):
            self.copy(way, self.steps).wait_recv()
        own, up, down = self.own(self.pos), self.slots.at[0, self.steps - 1], self.slots.at[1, self.steps - 1]

        def add(index):
            put(index, own[index].astype(F32) + up[index].astype(F32) + down[index].astype(F32))

        self.slabs(add)

    def sent(self):
        for way in (0, 1):
            for s in range(1, self.steps + 1):
                self.copy(way, s).wait_send()


class Torus:
    def __init__(self, place):
        self.dp, self.ep, self.ctx = place
        self.zh, self.x = self.dp // 4, self.dp % 4
        self.z = self.zh * 4 + self.ctx

    def at_x(self, v):
        return (self.zh * 4 + v % 4, self.ep, self.ctx)

    def at_z(self, v):
        v = v % 8
        return ((v // 4) * 4 + self.x, self.ep, v % 4)

    def x_ways(self):
        return self.at_x(self.x + 1), self.at_x(self.x + 3)

    def z_ways(self):
        return self.at_z(self.z + 1), self.at_z(self.z + 7)

    def x_arc(self, own, half, slots, send, recv):
        return Arc(4, self.x, own, half, slots, self.x_ways(), send, recv)

    def z_arc(self, own, half, slots, send, recv):
        return Arc(8, self.z, own, half, slots, self.z_ways(), send, recv)


def first_or_last(sizes):
    def half(view, h):
        return view.at[pl.ds(0, sizes[0])] if h == 0 else view.at[pl.ds(sizes[0], sizes[1])]

    return half


X_FIRST, Z_FIRST = (0, 1), (2,)
KEPT = 3
X_UNITS, Z_UNITS = (3, 4, 5, 6, 7, 8, 9), (10, 11)


def unit_arcs(torus, own, x_units, z_units, x_slots, z_slots, xs, xr, zs, zr):
    xa = [
        torus.x_arc(
            lambda t, i=i: own.at[i, :, t], first_or_last((1, 1)), x_slots.at[i], xs.at[i], xr.at[i]
        )
        for i in range(len(x_units))
    ]
    za = [
        torus.z_arc(
            lambda t, i=i: own.at[len(x_units) + i, t // 4, :, t % 4], first_or_last((2, 2)), z_slots.at[i], zs.at[i], zr.at[i]
        )
        for i in range(len(z_units))
    ]
    return xa, za


def expert_kernel(
    slot_ref, gate_ref, nf_hbm, og_hbm, win_hbm, wout_hbm,
    y_ref, d_ref, dg_ref, rx_ref, rz_ref, gw_hbm,
    nf, og, win, wout, rows_scr, grad_scr, units, x_slots, z_slots,
    fsem, wsem, gsem, xs, xr, zs, zr,
):
    torus = Torus(where_am_i())
    loads = [pltpu.make_async_copy(nf_hbm, nf, fsem.at[0]), pltpu.make_async_copy(og_hbm, og, fsem.at[1])]

    def weights(j):
        return (
            pltpu.make_async_copy(win_hbm.at[j], win.at[j % 2], wsem.at[j, 0]),
            pltpu.make_async_copy(wout_hbm.at[j], wout.at[j % 2], wsem.at[j, 1]),
        )

    for f in loads + list(weights(0)) + list(weights(1)):
        f.start()
    barrier = pltpu.get_barrier_semaphore()
    for device in torus.x_ways() + torus.z_ways():
        greet(barrier, device)
    slot = lax.broadcasted_iota(jnp.int32, (CAP, TOK), 0).astype(F32)

    def picks(s, e):
        return slot == slot_ref[s, pl.ds(e, 1), :]

    for f in loads:
        f.wait()

    def load(s, carry):
        pick = jnp.concatenate([jnp.where(picks(s, e), 1.0, 0.0) for e in range(4)], axis=0).astype(BF16)
        got = mm(pick, nf[s])
        grad = mm(pick, og[s])
        for e in range(4):
            rows = pl.ds(pl.multiple_of(s * CAP, 8), CAP)
            rows_scr[e, rows, :] = got[e * CAP : (e + 1) * CAP]
            grad_scr[e, rows, :] = grad[e * CAP : (e + 1) * CAP]
        return carry

    lax.fori_loop(0, 8, load, 0)

    xa, za = unit_arcs(torus, units, X_FIRST, Z_FIRST, x_slots, z_slots, xs, xr, zs, zr)
    views = (2, 4, 4, 16, 1024)

    def back_weights(j, received, grad_gu):
        grad_in = mm(received, grad_gu, TN).astype(BF16).reshape(32, 32, 1024)
        units[3 * j] = grad_in[:, 0:16].reshape(views)
        units[3 * j + 1] = grad_in[:, 16:32].reshape(views)

    def expert(j, carry):
        gates = jnp.concatenate(
            [
                jnp.sum(jnp.where(picks(s, j), gate_ref[s, pl.ds(j, 1), :], 0.0), axis=1, keepdims=True)
                for s in range(8)
            ],
            axis=0,
        )
        for f in weights(j):
            f.wait()
        w_in, w_out = win[j % 2], wout[j % 2]
        received = rows_scr[j].astype(BF16)
        grad_tok = grad_scr[j]
        gate_up = mm(received, w_in)
        gating, up = gate_up[:, :512], gate_up[:, 512:]
        sig = 1.0 / (1.0 + jnp.exp(-gating))
        silu = gating * sig
        act = (silu * up).astype(BF16)
        result = mm(act, w_out).astype(BF16).astype(F32)
        dots = jnp.sum(grad_tok * result, axis=1, keepdims=True)
        grad_res = (grad_tok * gates).astype(BF16)
        grad_scr[j] = result * gates
        for s in range(8):
            dg_ref[s, pl.ds(j, 1), :] = jnp.sum(
                jnp.where(picks(s, j), dots[s * CAP : (s + 1) * CAP], 0.0), axis=0, keepdims=True
            )
        units[3 * j + 2] = mm(act, grad_res, TN).astype(BF16).reshape(views)
        grad_act = mm(grad_res, w_out, NT)
        grad_up = (grad_act * silu).astype(BF16)
        grad_gate = (grad_act * up * sig * (1.0 + gating * (1.0 - sig))).astype(BF16)
        grad_gu = jnp.concatenate([grad_gate, grad_up], axis=1)
        between(j)
        back_weights(j, received, grad_gu)
        rows_scr[j] = mm(grad_gu, w_in, NT)
        after(j)
        return carry

    def keep(first, last):
        return [pltpu.make_async_copy(units.at[u], gw_hbm.at[u - KEPT], gsem.at[u - KEPT]) for u in range(first, last)]

    def between(j):
        @pl.when(j == 1)
        def _():
            za[0].advance(2)
            xa[0].advance(2)

        @pl.when(j == 2)
        def _():
            za[0].advance(3)

        @pl.when(j == 3)
        def _():
            za[0].advance(4)

    def after(j):
        @pl.when(j < 2)
        def _():
            for f in weights(j + 2):
                f.start()

        @pl.when(j == 0)
        def _():
            for arc in za + xa:
                arc.start()

        @pl.when(j == 1)
        def _():
            xa[1].advance(2)
            for f in keep(KEPT, 6):
                f.start()

        @pl.when(j == 2)
        def _():
            for f in keep(6, 9):
                f.start()

    pl.semaphore_wait(barrier, 4)
    lax.fori_loop(0, 4, expert, 0)
    for f in keep(9, 12):
        f.start()

    def store(s, carry):
        pick = jnp.concatenate([jnp.where(picks(s, e), 1.0, 0.0) for e in range(4)], axis=0).astype(BF16)
        rows = pl.ds(pl.multiple_of(s * CAP, 8), CAP)
        weighted = jnp.concatenate([grad_scr[e, rows, :] for e in range(4)], axis=0).astype(BF16)
        y_ref[s] = mm(pick, weighted, TN).astype(BF16)
        back = jnp.concatenate([rows_scr[e, rows, :] for e in range(4)], axis=0).astype(BF16)
        d_ref[s] = mm(pick, back, TN).astype(BF16)
        dg_ref[s, 4:8, :] = jnp.zeros((4, TOK), F32)
        return carry

    lax.fori_loop(0, 8, store, 0)

    def put_z(index, value):
        for h in (0, 1):
            rz_ref[index[0], h] = value[:, 512 * h : 512 * h + 512].astype(BF16)

    za[0].finish(put_z)
    for i, arc in enumerate(xa):

        def put_x(index, value, i=i):
            rx_ref[index[0] * 4 + index[1], i] = value.astype(BF16)

        arc.finish(put_x)
    for f in keep(KEPT, 12):
        f.wait()
    for arc in xa + za:
        arc.sent()


class Direct:
    def __init__(self, torus, part, x_slots, result, z_slots, send, recv):
        self.t, self.part, self.x_slots, self.result, self.z_slots = torus, part, x_slots, result, z_slots
        self.send, self.recv = send, recv

    def x_copy(self, r):
        to = (self.t.x + r) % 4
        return remote(
            self.part.at[:, to], self.x_slots.at[r - 1], self.send.at[r], self.recv.at[r], self.t.at_x(to)
        )

    def z_copy(self, r):
        to = (self.t.z + r) % 8
        return remote(
            self.result.at[to], self.z_slots.at[r - 1], self.send.at[3 + r], self.recv.at[3 + r], self.t.at_z(to)
        )

    def start(self):
        for r in (2, 1, 3):
            self.x_copy(r).start()

    def turn(self):
        for r in (1, 2, 3):
            self.x_copy(r).wait_recv()

        def add(i, carry):
            h, l = i // 4, i % 4
            value = self.part[h, self.t.x, l].astype(F32)
            for r in range(3):
                value = value + self.x_slots[r, h, l].astype(F32)
            self.result[i] = value.astype(BF16)
            return carry

        lax.fori_loop(0, 8, add, 0)
        repeat(0, 7, lambda i: self.z_copy(4 + (2 * (i % 2) - 1) * ((i + 1) // 2)).start())

    def finish(self):
        repeat(1, 8, lambda r: self.z_copy(r).wait_recv())
        value = self.result[self.t.z].astype(F32)
        for r in range(7):
            value = value + self.z_slots[r].astype(F32)
        return value

    def sent(self):
        repeat(1, 4, lambda r: self.x_copy(r).wait_send())
        repeat(1, 8, lambda r: self.z_copy(r).wait_send())


def prepare_queries(j, ctx, start_ref, q_ref, lse_ref, both, stack, rows):
    lane = lax.broadcasted_iota(jnp.int32, (256, 128), 1)
    start_row, place_row = query_rows(j, ctx, start_ref)
    q_blk = q_ref[j]
    zero = jnp.zeros((HD, 256), BF16)
    both[j, 0:HD, 0:256] = heads_wide(turned(q_blk))
    both[j, HD:128, 0:256] = zero
    both[j, 0:HD, 256:512] = zero
    q_f = q_blk.astype(F32)
    q_rows = jnp.concatenate([q_f, pltpu.roll(q_f, HD, 1)], axis=0)
    stack[j, 0:256] = jnp.where(lane < HD, q_rows, 0.0).astype(BF16)
    rows[j, 0:1, :] = lse_ref[j, 0:1, :]
    rows[j, 2:3, :] = start_row
    rows[j, 3:4, :] = place_row


def prepare_grads(j, attT_ref, gm_ref, w_ref, both, stack, rows):
    lane = lax.broadcasted_iota(jnp.int32, (256, 128), 1)
    tall = mm(w_ref[...], gm_ref[j], NT).astype(BF16).astype(F32)
    rows[j, 1:2, :] = jnp.sum(heads_wide(tall) * heads_wide(attT_ref[j]), axis=0, keepdims=True)
    both[j, HD:128, 256:512] = heads_wide(tall).astype(BF16)
    g_f = tall.T
    g_rows = jnp.concatenate([pltpu.roll(g_f, HD, 1), g_f], axis=0)
    stack[j, 256:512] = jnp.where(lane < HD, 0.0, g_rows).astype(BF16)


def attend_pair(m, j, kv, kT, both, stack, rows):
    row = rows[j]
    chunk = pl.ds(pl.multiple_of(m * CHUNK, CHUNK), CHUNK)
    pair = mm(kv[chunk, :], both[j])
    keys = (lax.broadcasted_iota(jnp.int32, (CHUNK, 256), 0) + m * CHUNK).astype(F32)
    allowed = (keys >= row[2:3]) & (keys <= row[3:4])
    probs = jnp.exp(jnp.where(allowed, pair[:, :256], MASKED) - row[0:1])
    grad = (probs * (pair[:, 256:] - row[1:2])).astype(BF16)
    return mm(jnp.concatenate([grad, probs.astype(BF16)], axis=1), stack[j]), mm(kT[:, chunk], grad)


def tail_kernel(
    dg_ref, gates_ref, gain_two_ref, wr_ref, x_ref, gain_one_ref, ca_ref, sa_ref, cb_ref, sb_ref, start_ref, lse_ref,
    rx0, rz0,
    back_hbm, nf_hbm, res_hbm, og_hbm, q_hbm, kv_hbm, attT_hbm, wp_hbm, y_hbm, nall_hbm, wq_hbm, wk_hbm, wv_hbm, gw_hbm,
    out_ref, ing_ref, gin_ref, gout_ref, gq_ref, gk_ref, gv_ref, gproj_out, gside_ref, gains_ref,
    back, nf, res, og, q_ref, kv, attT, wp, y_part, wq, wk, wv, own,
    dbuf, cbuf, fbuf, gbuf, cbuf2, fbuf2, gbuf2, gm, gres,
    kT, both, stack, rows, dqs, acc, dkv, dqb, dkvb, kbuf, qpieces, kpieces,
    x_slots, z_slots, g0_slots, g1_slots, g2_slots, h0_slots, h1_slots, rx1, rx2, rz1,
    early, late_q, late_k, e_x, e_res, e_z, q_x, q_res, q_z, k_x, k_res, k_z,
    gain_own, gain_e, gain_x, gain_z, fin, fin_late, rs, rp, rq,
    fsem, usem, csend, crecv, c2send, c2recv, dsend, drecv, msend, mrecv, ksend, krecv, qsend, qrecv, psend, precv,
    xs, xr, zs, zr, g0s, g0r, g1s, g1r, g2s, g2r, h0s, h0r, h1s, h1r, es, er, lqs, lqr, lks, lkr, gs, gr,
    fsend, frecv,
):
    place = where_am_i()
    dp, ep, ctx = place
    torus = Torus(place)
    nall = back
    sources = dict(
        back=(back_hbm, back), nf=(nf_hbm.at[ep], nf), res=(res_hbm, res), og=(og_hbm, og), q=(q_hbm, q_ref),
        kv=(kv_hbm, kv), attT=(attT_hbm, attT), wp=(wp_hbm.at[pl.ds(pl.multiple_of(ep * 128, 128), 128)], wp), y=(y_hbm, y_part),
        nall=(nall_hbm, nall), wq=(wq_hbm, wq), wk=(wk_hbm, wk), wv=(wv_hbm, wv),
    )
    loads = {
        name: pltpu.make_async_copy(src, dst, fsem.at[i]) for i, (name, (src, dst)) in enumerate(sources.items())
    }
    units = {u: pltpu.make_async_copy(gw_hbm.at[u - KEPT], own.at[i], usem.at[i]) for i, u in enumerate(X_UNITS + Z_UNITS)}
    loads["back"].start()
    for u in (3, 10, 4, 11, 5, 6, 7, 8, 9):
        units[u].start()
    for name in ("nf", "res", "og", "kv", "q", "attT", "wp"):
        loads[name].start()
    for name in ("y", "wq", "wk", "wv"):
        loads[name].start()

    def send_to(g, h):
        return (dp, 2 * ctx + g // 2, 2 * (g % 2) + h), (ep, 2 * ctx + g // 2, 2 * (g % 2) + h)

    def is_me(device):
        return (device[0] == dp) & (device[1] == ep) & (device[2] == ctx)

    barrier = pltpu.get_barrier_semaphore()

    def greet_peers(r):
        greet(barrier, (dp, (ep + r) % 8, ctx))
        greet(barrier, torus.at_z(torus.z + r))

    repeat(1, 8, greet_peers)
    repeat(1, 4, lambda r: greet(barrier, torus.at_x(torus.x + r)))

    def greet_senders(i):
        for device in ((dp, i, ep // 2), (i, dp, ep // 2)):

            @pl.when(jnp.logical_not(is_me(device)))
            def _():
                greet(barrier, device)

    repeat(0, 8, greet_senders)
    waits = 17
    for g in range(4):
        for h in range(2):
            for device in send_to(g, h):
                waits = waits + jnp.where(is_me(device), 0, 1)
    pl.semaphore_wait(barrier, waits)

    xa, za = unit_arcs(torus, own, X_UNITS, Z_UNITS, x_slots, z_slots, xs, xr, zs, zr)
    g0 = torus.z_arc(lambda t: rx0.at[t], first_or_last((1, 1)), g0_slots, g0s, g0r)
    g1 = torus.z_arc(lambda t: rx1.at[t], first_or_last((2, 2)), g1_slots, g1s, g1r)
    g2 = torus.z_arc(lambda t: rx2.at[t], first_or_last((1, 2)), g2_slots, g2s, g2r)
    h0 = torus.x_arc(lambda t: rz0.at[t], first_or_last((1, 1)), h0_slots, h0s, h0r)
    h1 = torus.x_arc(lambda t: rz1.at[t], first_or_last((1, 1)), h1_slots, h1s, h1r)

    def finish_x(i):
        target = rx1 if i < 4 else rx2

        def put(index, value):
            target[index[0] * 4 + index[1], i % 4] = value.astype(BF16)

        xa[i].finish(put)

    def finish_z(i):
        def put(index, value):
            rz1[index[0], i] = value.astype(BF16)

        za[i].finish(put)

    total = EpScatterSum(back, cbuf, fbuf, gbuf, csend, crecv, place)
    loads["back"].wait()
    total.start()
    exchange(dg_ref, dbuf, dsend, drecv, place, False)
    dbuf[ep] = dg_ref[ep]
    h0.start()
    for i in range(4):
        units[X_UNITS[i]].wait()
        xa[i].start()
        if i < 2:
            units[Z_UNITS[i]].wait()
            za[i].start()
    g0.start()
    total.far()
    za[0].advance(2)
    xa[0].advance(2)
    za[1].advance(2)
    total.near()
    h0.advance(2)
    xa[1].advance(2)
    g0.advance(2)
    exchange(dg_ref, dbuf, dsend, drecv, place, True)
    for name in ("nf", "res", "og"):
        loads[name].wait()
    gates = gates_ref[...]
    grad_gates = jnp.concatenate([dbuf[p] for p in range(8)], axis=0)
    grad_logits = gates * (grad_gates - jnp.sum(gates * grad_gates, axis=0, keepdims=True))
    high = grad_logits.astype(BF16)
    low = (grad_logits - high.astype(F32)).astype(BF16)
    to = lax.broadcasted_iota(jnp.int32, (32, 64), 0)
    source = lax.broadcasted_iota(jnp.int32, (32, 64), 1)
    squeeze = jnp.where(source == (to // 4) * 8 + to % 4, 1.0, 0.0).astype(BF16)
    high, low = mm(squeeze, high).astype(BF16), mm(squeeze, low).astype(BF16)
    from_router = mm(high, wr_ref[...], TN) + mm(low, wr_ref[...], TN)
    resid = res[...]
    scale = lax.rsqrt(jnp.mean(resid * resid, axis=-1, keepdims=True) + EPSILON)
    scaled = resid * scale
    za[0].advance(3)
    xa[2].advance(2)
    za[1].advance(3)
    grad_normed = total.last() + from_router
    gain_two = jnp.sum(grad_normed * scaled, axis=0, keepdims=True)
    grad_normed = grad_normed * gain_two_ref[...]
    mean = jnp.mean(grad_normed * scaled, axis=-1, keepdims=True)
    grad_res = og[...].astype(F32) + scale * (grad_normed - scaled * mean)
    gm[ep] = grad_res.astype(BF16)
    gather = EpGather(gm, msend, mrecv, place)
    gather.go(0, 1, 3, 2, 4)
    gres[...] = grad_res
    for t in range(8):
        gain_own[0, 8 + t : 9 + t, :] = gain_two[:, 128 * t : 128 * t + 128]
    xa[3].advance(2)
    g0.advance(3)

    for name in ("kv", "q"):
        loads[name].wait()
    for chunk in range(4):
        part = kv[chunk * CHUNK : (chunk + 1) * CHUNK, :].astype(F32).T
        kT[:, chunk * CHUNK : (chunk + 1) * CHUNK] = part[:HD].astype(BF16)
    gather.got(1)
    gather.go(5, 6)
    gather.got(3)
    gather.go(7, 8)
    za[0].advance(4)
    for chunk in range(4, 8):
        part = kv[chunk * CHUNK : (chunk + 1) * CHUNK, :].astype(F32).T
        kT[:, chunk * CHUNK : (chunk + 1) * CHUNK] = part[:HD].astype(BF16)
    gather.got(2)
    gather.go(9)
    gather.got(4)
    gather.go(10)
    za[1].advance(4)
    repeat(0, 8, lambda j: prepare_queries(j, ctx, start_ref, q_ref, lse_ref, both, stack, rows))
    gather.got(5)
    gather.go(11)
    gather.got(7)
    gather.go(12)
    g0.advance(4)
    grad_router = mm(high, nf[...]) + mm(low, nf[...])
    side = jnp.concatenate([grad_router, jnp.zeros((96, 1024), F32)], axis=0)
    for d in range(8):
        tile = side[:, d * 128 : (d + 1) * 128].T.astype(BF16)
        for c in range(4):
            early[d // 4, d % 4, c, :, 128:256] = tile[32 * c : 32 * c + 32]
    for i in (4, 5, 6):
        units[X_UNITS[i]].wait()
        xa[i].start()
    for name in ("attT", "wp"):
        loads[name].wait()
    gather.got(0, 6, 8, 9, 10, 11, 12)

    total.sent()
    loads["nall"].start()
    results = EpScatterSum(y_part, cbuf2, fbuf2, gbuf2, c2send, c2recv, place)
    loads["y"].wait()
    results.start()
    repeat(0, 8, lambda j: prepare_grads(j, attT, gm, wp, both, stack, rows))
    grad_proj = mm(attT[0].astype(BF16), gm[0])
    for j in range(1, 8):
        grad_proj = grad_proj + mm(attT[j].astype(BF16), gm[j])
    grad_proj = grad_proj.astype(BF16)
    for d in range(8):
        for c in range(4):
            early[d // 4, d % 4, c, :, 0:128] = grad_proj[32 * c : 32 * c + 32, 128 * d : 128 * d + 128]
    sums_early = Direct(torus, early, e_x, e_res, e_z, es, er)
    sums_q = Direct(torus, late_q, q_x, q_res, q_z, lqs, lqr)
    sums_k = Direct(torus, late_k, k_x, k_res, k_z, lks, lkr)
    sums_early.start()

    lane = lax.broadcasted_iota(jnp.int32, (TOK, 128), 1)

    def chunk_copy(r, m):
        shard = (ctx + r) % 4
        return remote(dkv.at[m, shard], kbuf.at[m, ctx], ksend.at[m, r], krecv.at[m, r], (dp, ep, shard))

    def chunk_go(m):
        for r in (2, 1, 3):
            chunk_copy(r, m).start()
        kbuf[m, ctx] = dkv[m, ctx]

    def piece_copy(src, dst, send, recv, m):
        return remote(src.at[m], dst.at[ep], send.at[m], recv.at[ep], (dp, m, ctx))

    def piece_go(src, dst, send, recv, m):
        @pl.when(ep != m)
        def _():
            piece_copy(src, dst, send, recv, m).start()

        @pl.when(ep == m)
        def _():
            dst[ep] = src[m]

    def pieces_got(src, dst, send, recv):
        def one(r):
            p = (ep + r) % 8
            remote(src.at[p], dst.at[p], send.at[p], recv.at[p], (dp, p, ctx)).wait_recv()

        repeat(1, 8, one)

    def pieces_sent(src, dst, send, recv):
        repeat(1, 8, lambda r: piece_copy(src, dst, send, recv, (ep + r) % 8).wait_send())

    def chunk_done(m):
        for r in (1, 2, 3):
            v = kbuf.at[m, (ctx + 4 - r) % 4]
            remote(v, v, ksend.at[m, r], krecv.at[m, r], (dp, ep, (ctx + r) % 4)).wait_recv()
        grad = kbuf[m, 0].astype(F32) + kbuf[m, 1].astype(F32) + kbuf[m, 2].astype(F32) + kbuf[m, 3].astype(F32)
        cosine, sine = rope_block(4 * m + ctx, ca_ref, sa_ref, cb_ref, sb_ref)
        cosine = jnp.where(lane < HD, cosine, 1.0)
        sine = jnp.where(lane < HD, sine, 0.0)
        dkvb[m] = (grad * cosine - rotate_half(grad) * sine).astype(BF16)
        piece_go(dkvb, kpieces, psend, precv, m)

    def progress(m):
        @pl.when(m == 0)
        def _():
            finish_x(0)
            finish_z(0)
            results.far()

        @pl.when(m == 1)
        def _():
            finish_x(1)
            finish_z(1)
            results.near()

        @pl.when(m == 2)
        def _():
            finish_x(2)
            xa[4].advance(2)
            h1.start()

        @pl.when(m == 3)
        def _():
            finish_x(3)
            g1.start()
            xa[5].advance(2)
            sums_early.turn()

        @pl.when(m == 4)
        def _():
            h1.advance(2)
            xa[6].advance(2)
            out_ref[...] = (res[...] + results.last()).astype(BF16)

        @pl.when(m == 6)
        def _():
            g1.advance(2)

    dqs[...] = jnp.zeros((8, HD, 256), F32)

    def key_chunk(m):
        acc[...] = jnp.zeros((CHUNK, 128), F32)

        def pair(j):
            both_grads, query_grad = attend_pair(m, j, kv, kT, both, stack, rows)
            acc[...] += both_grads
            dqs[j] += query_grad

        repeat(m, 8, pair)
        dkv[m] = acc[...].astype(BF16).reshape(4, TOK, 128)
        chunk_go(m)
        dq = dqs[m] * (HD**-0.5)
        dq = jnp.concatenate([dq[:, :128], dq[:, 128:]], axis=0).T
        cosine, sine = rope_block(4 * m + ctx, ca_ref, sa_ref, cb_ref, sb_ref)
        dqb[m] = (dq * cosine - rotate_half(dq) * sine).astype(BF16)
        piece_go(dqb, qpieces, qsend, qrecv, m)

        @pl.when(m >= 2)
        def _():
            chunk_done(m - 2)

        progress(m)

    repeat(0, 8, key_chunk)
    chunk_done(6)
    for name in ("nall", "wq"):
        loads[name].wait()

    def weights(grad, late):
        out = mm(nall[...].reshape(1024, 1024), grad.reshape(1024, 128), TN).astype(BF16)
        for d in range(8):
            for c in range(4):
                at = d * 128 + c * 32
                late[d // 4, d % 4, c] = out[at : at + 32]

    weights(dqb[...], late_q)
    sums_q.start()
    chunk_done(7)
    weights(dkvb[...], late_k)
    sums_k.start()
    for i in (4, 5, 6):
        finish_x(i)
    g2.start()
    pieces_got(dqb, qpieces, qsend, qrecv)
    grad_q = jnp.concatenate([qpieces[p] for p in range(8)], axis=1)
    grad_normed = mm(grad_q, wq[...], NT)

    def piece(g, h, kind, device):
        index = (kind * 4 + g) * 2 + h
        src = (fin.at[g, :, pl.ds(128, 128)], fin.at[g, :, pl.ds(0, 128)], fin_late.at[g])[kind]
        mine = dp if kind == 1 else ep
        return remote(src, (rs, rp, rq)[kind].at[mine], fsend.at[index], frecv.at[kind, mine], device)

    def each_piece(kinds, act, local):
        def one(i):
            g, h = i // 2, i % 2
            for kind in kinds:
                device = send_to(g, h)[kind % 2]

                @pl.when(jnp.logical_not(is_me(device)))
                def _():
                    act(piece(g, h, kind, device))

                if local:

                    @pl.when(is_me(device))
                    def _():
                        if kind == 0:
                            rs[ep] = fin[g, :, 128:256]
                        elif kind == 1:
                            rp[dp] = fin[g, :, 0:128]
                        else:
                            rq[ep] = fin_late[g]

        repeat(0, 8, one)

    def pieces_in(kind):
        def one(i):
            device = (i, dp, ep // 2) if kind == 1 else (dp, i, ep // 2)

            @pl.when(jnp.logical_not(is_me(device)))
            def _():
                dst = (rs, rp, rq)[kind].at[i]
                remote(dst, dst, fsend.at[kind * 8], frecv.at[kind, i], device).wait_recv()

        repeat(0, 8, one)

    done_early = sums_early.finish()
    for g in range(4):
        fin[g] = done_early[8 * g : 8 * g + 8]
    each_piece((0, 1), lambda c: c.start(), True)
    g1.advance(3)
    for name in ("wk", "wv"):
        loads[name].wait()
    pieces_got(dkvb, kpieces, psend, precv)
    grad_k = jnp.concatenate([kpieces[p, :, 0:HD] for p in range(8)], axis=1)
    grad_v = jnp.concatenate([kpieces[p, :, HD:128] for p in range(8)], axis=1)
    grad_normed = grad_normed + mm(grad_k, wk[...], NT) + mm(grad_v, wv[...], NT)
    x = x_ref[...].astype(F32)
    scale = lax.rsqrt(jnp.mean(x * x, axis=-1, keepdims=True) + EPSILON)
    scaled = x * scale
    gain_one = jnp.sum(grad_normed * scaled, axis=0, keepdims=True)
    for t in range(8):
        gain_own[0, t : t + 1, :] = gain_one[:, 128 * t : 128 * t + 128]

    def gain_copy(stage, r):
        src = gain_own.at[stage]
        if stage == 0:
            dst, device, base = gain_e.at[r - 1], (dp, (ep + r) % 8, ctx), 0
        elif stage == 1:
            dst, device, base = gain_x.at[r - 1], torus.at_x(torus.x + r), 7
        else:
            dst, device, base = gain_z.at[r - 1], torus.at_z(torus.z + r), 10
        return remote(src, dst, gs.at[base + r], gr.at[base + r], device)

    def gain_stage(stage, count):
        if stage > 0:
            last, slots = ((7, gain_e), (3, gain_x), (7, gain_z))[stage - 1]
            repeat(1, last + 1, lambda r: gain_copy(stage - 1, r).wait_recv())
            value = gain_own[stage - 1]
            for r in range(1, last + 1):
                value = value + slots[r - 1]
            gain_own[stage] = value
        repeat(1, count + 1, lambda r: gain_copy(stage, r).start())

    gain_stage(0, 7)
    g2.advance(2)
    grad_normed = grad_normed * gain_one_ref[...]
    mean = jnp.mean(grad_normed * scaled, axis=-1, keepdims=True)
    ing_ref[...] = (gres[...] + scale * (grad_normed - scaled * mean)).astype(BF16)

    sums_q.turn()
    gain_stage(1, 3)
    g2.advance(3)
    sums_k.turn()
    gain_stage(2, 7)
    g1.advance(4)
    g2.advance(4)

    done_q, done_k = sums_q.finish(), sums_k.finish()
    for g in range(4):
        at = slice(8 * g, 8 * g + 8)
        fin_late[g, :, 0:128] = done_q[at]
        fin_late[g, :, 128:256] = done_k[at]
    each_piece((2,), lambda c: c.start(), True)


    def put_unit(unit, value):
        j, u = unit // 3, unit % 3
        if u < 2:
            gin_ref[j, 16 * u : 16 * u + 16, :] = value
        else:
            gout_ref[j] = value

    def finish_units(arc, units):
        for way in (0, 1):
            arc.copy(way, arc.steps).wait_recv()
        mine = arc.own(arc.pos)
        up, down = arc.slots.at[0, arc.steps - 1], arc.slots.at[1, arc.steps - 1]
        for i, unit in enumerate(units):
            put_unit(unit, mine[i].astype(F32) + up[i].astype(F32) + down[i].astype(F32))

    for way in (0, 1):
        h0.copy(way, 2).wait_recv()
    for h in (0, 1):
        value = rz0[torus.x, h].astype(F32) + h0_slots[0, 1, h].astype(F32) + h0_slots[1, 1, h].astype(F32)
        gout_ref[0, :, 512 * h : 512 * h + 512] = value
    finish_units(h1, Z_UNITS)
    finish_units(g0, X_FIRST)
    finish_units(g1, X_UNITS[:4])
    pieces_in(0)
    pieces_in(1)
    last = gain_own[2]
    repeat(1, 8, lambda r: gain_copy(2, r).wait_recv())
    for r in range(7):
        last = last + gain_z[r]
    gain_own[3] = last

    pieces_in(2)
    odd = ctx % 2 == 1

    def mine(v):
        return jnp.where(odd, v[4:8], v[0:4])

    gq_ref[...] = mine(jnp.concatenate([rq[i, :, 0:128] for i in range(8)], axis=1))
    gk_ref[...] = mine(jnp.concatenate([rq[i, :, 128:192] for i in range(8)], axis=1))
    gv_ref[...] = mine(jnp.concatenate([rq[i, :, 192:256] for i in range(8)], axis=1))
    side = rs[0]
    for i in range(1, 8):
        side = side + rs[i]
    gside_ref[...] = mine(side)
    gproj_out[...] = mine(jnp.concatenate([rp[i] for i in range(8)], axis=1))
    for which in (0, 1):
        row = jnp.broadcast_to(gain_own[3, pl.ds(8 * which + dp, 1), :], (8, 128))
        gains_ref[8 * which : 8 * which + 8, :] = pltpu.roll(row, (128 - 16 * ep - 4 * ctx) % 128, 1)

    finish_units(g2, X_UNITS[4:])

    results.sent()
    gather.sent()
    exchange_sent(dg_ref, dbuf, dsend, drecv, place)
    pieces_sent(dqb, qpieces, qsend, qrecv)
    pieces_sent(dkvb, kpieces, psend, precv)

    def chunk_sent(m):
        for r in (1, 2, 3):
            chunk_copy(r, m).wait_send()

    repeat(0, 8, chunk_sent)
    for arc in xa + za + [g0, g1, g2, h0, h1]:
        arc.sent()
    for sums in (sums_early, sums_q, sums_k):
        sums.sent()
    for stage, count in ((0, 7), (1, 3), (2, 7)):
        repeat(1, count + 1, lambda r: gain_copy(stage, r).wait_send())
    each_piece((0, 1, 2), lambda c: c.wait_send(), False)


def pack_kernel(*refs):
    count = (len(refs) - 1) // 2
    for src, dst in zip(refs[: count - 2], refs[count:]):
        dst[...] = src[...]
    side, gains = refs[count - 2 : count]
    router, one, two = refs[-3:]
    router[...] = side[:, 0:32]
    one[...] = gains[0, 0:4]
    two[...] = gains[8, 0:4]


def call(kernel, outs, scratch, args, name, collective=None, **more):
    params = dict(vmem_limit_bytes=VMEM_LIMIT)
    if collective is not None:
        params.update(collective_id=collective, has_side_effects=True)
    space = pl.BlockSpec(memory_space=pltpu.VMEM)
    return pl.pallas_call(
        kernel,
        out_shape=[jax.ShapeDtypeStruct(shape, kind) for shape, kind in outs],
        in_specs=more.pop("in_specs", [space] * len(args)),
        out_specs=more.pop("out_specs", [space] * len(outs)),
        scratch_shapes=scratch,
        compiler_params=pltpu.CompilerParams(**params),
        name=name,
        **more,
    )(*args)


def sems(*sizes):
    return [pltpu.SemaphoreType.DMA(s if isinstance(s, tuple) else (s,)) for s in sizes]


def body(
    layer_input, gain_attn, w_query, w_key, w_value, w_proj, gain_ffn, w_router,
    w_expert_in, w_expert_out, segment_ids, expert_ids, slot_order, out_grad,
):
    gain_one, gain_two = gain_attn.reshape(1, 1024), gain_ffn.reshape(1, 1024)
    tables = [jnp.asarray(t) for t in rope_tables()]
    wr_rows = w_router.T
    order = slot_order.reshape(8, 128)
    docs = segment_ids.reshape(32, 128)

    vm, hbm = pl.BlockSpec(memory_space=pltpu.VMEM), pl.BlockSpec(memory_space=pl.ANY)
    wide, block = pltpu.VMEM((8, TOK, 1024), BF16), pltpu.VMEM((8, TOK, 128), BF16)
    (
        normed_all, grad_all, query, kv, slots, starts, attended_tall, log_sums, residual, ffn_all, gates_in, gates,
    ) = call(
        head_kernel,
        [
            ((8, TOK, 1024), BF16), ((8, TOK, 1024), BF16), ((8, TOK, 128), BF16), ((8, 4, TOK, 128), BF16),
            ((8, 8, TOK), F32), ((32, 128), F32), ((8, 128, TOK), F32), ((8, 8, 256), F32),
            ((TOK, 1024), F32), ((8, TOK, 1024), BF16), ((8, 8, TOK), F32), ((64, TOK), F32),
        ],
        [
            pltpu.VMEM((1024, 128), BF16), pltpu.VMEM((1024, 128), BF16), pltpu.VMEM((1024, 128), BF16),
            pltpu.VMEM((1024, 256), BF16), pltpu.VMEM((1024, 1024), BF16), pltpu.VMEM((8, 8, TOK), F32),
            pltpu.VMEM((64, TOK), F32), block, block, pltpu.VMEM((4096, 128), BF16), pltpu.VMEM((128, 4096), BF16),
            pltpu.VMEM((8, 8, TOK), F32),
        ]
        + sems(4, 13, 13, 13, 13, 8, 8, 24, 24, 8, 8, 13, 13, 8, 8),
        [
            layer_input, gain_one, gain_two, out_grad, *tables, expert_ids.T, order, docs, wr_rows,
            w_query, w_key, w_value, w_proj,
        ],
        "head", 1, in_specs=[vm] * 12 + [hbm] * 4,
    )
    kv_rows = kv.reshape(4096, 128)
    ex, ez = len(X_FIRST), len(Z_FIRST)
    sums, back, grad_gates, sums_x, sums_z, units = call(
        expert_kernel,
        [
            ((8, TOK, 1024), BF16), ((8, TOK, 1024), BF16), ((8, 8, TOK), F32), ((8, ex, 16, 1024), BF16),
            ((4, 2, 16, 512), BF16), ((12 - KEPT, 2, 4, 4, 16, 1024), BF16),
        ],
        [
            wide, wide, pltpu.VMEM((2, 1024, 1024), BF16), pltpu.VMEM((2, 512, 1024), BF16),
            pltpu.VMEM((4, 8 * CAP, 1024), F32), pltpu.VMEM((4, 8 * CAP, 1024), F32),
            pltpu.VMEM((12, 2, 4, 4, 16, 1024), BF16),
            pltpu.VMEM((ex, 2, 2, 2, 4, 16, 1024), BF16), pltpu.VMEM((ez, 2, 4, 4, 16, 1024), BF16),
        ]
        + sems(2, (4, 2), 12 - KEPT, (ex, 2, 2), (ex, 2, 2), (ez, 2, 4), (ez, 2, 4)),
        [slots, gates_in, ffn_all, grad_all, w_expert_in, w_expert_out],
        "experts", 4, in_specs=[vm, vm] + [hbm] * 4, out_specs=[vm] * 5 + [hbm],
    )
    nx, nz = len(X_UNITS), len(Z_UNITS)

    def direct(lanes):
        return [
            pltpu.VMEM((3, 2, 4, 32, lanes), BF16), pltpu.VMEM((8, 32, lanes), BF16), pltpu.VMEM((7, 32, lanes), BF16)
        ]

    results = call(
        tail_kernel,
        [
            ((TOK, 1024), BF16), ((TOK, 1024), BF16), ((4, 32, 1024), F32), ((4, 16, 1024), F32), ((4, 1024), F32),
            ((4, 512), F32), ((4, 512), F32), ((4, 1024), F32), ((4, 128), F32), ((16, 128), F32),
        ],
        [
            wide, pltpu.VMEM((TOK, 1024), BF16), pltpu.VMEM((TOK, 1024), F32), pltpu.VMEM((TOK, 1024), BF16), block,
            pltpu.VMEM((4096, 128), BF16), pltpu.VMEM((8, 128, TOK), F32), pltpu.VMEM((128, 1024), BF16), wide,
            pltpu.VMEM((1024, 1024), BF16), pltpu.VMEM((1024, 512), BF16), pltpu.VMEM((1024, 512), BF16),
            pltpu.VMEM((nx + nz, 2, 4, 4, 16, 1024), BF16),
            pltpu.VMEM((8, 8, TOK), F32),
        ]
        + scatter_sum_scratch()[:3] * 2
        + [
            wide, pltpu.VMEM((TOK, 1024), F32),
            pltpu.VMEM((HD, 4096), BF16), pltpu.VMEM((8, 128, 512), BF16), pltpu.VMEM((8, 512, 128), BF16),
            pltpu.VMEM((8, 8, 256), F32), pltpu.VMEM((8, HD, 256), F32), pltpu.VMEM((CHUNK, 128), F32),
            pltpu.VMEM((8, 4, TOK, 128), BF16),
            block, block, pltpu.VMEM((8, 4, TOK, 128), BF16), block, block,
            pltpu.VMEM((nx, 2, 2, 2, 4, 16, 1024), BF16), pltpu.VMEM((nz, 2, 4, 4, 16, 1024), BF16),
            pltpu.VMEM((2, 4, ex, 16, 1024), BF16), pltpu.VMEM((2, 4, 4, 16, 1024), BF16), pltpu.VMEM((2, 4, 3, 16, 1024), BF16),
            pltpu.VMEM((2, 2, 2, 16, 512), BF16), pltpu.VMEM((2, 2, nz, 16, 1024), BF16),
            pltpu.VMEM((8, 4, 16, 1024), BF16), pltpu.VMEM((8, 3, 16, 1024), BF16), pltpu.VMEM((4, nz, 16, 1024), BF16),
            pltpu.VMEM((2, 4, 4, 32, 256), BF16), pltpu.VMEM((2, 4, 4, 32, 128), BF16), pltpu.VMEM((2, 4, 4, 32, 128), BF16),
        ]
        + direct(256) + direct(128) + direct(128)
        + [
            pltpu.VMEM((4, 16, 128), F32), pltpu.VMEM((7, 16, 128), F32), pltpu.VMEM((3, 16, 128), F32),
            pltpu.VMEM((7, 16, 128), F32),
            pltpu.VMEM((4, 8, 256), F32), pltpu.VMEM((4, 8, 256), F32), pltpu.VMEM((8, 8, 128), F32),
            pltpu.VMEM((8, 8, 128), F32), pltpu.VMEM((8, 8, 256), F32),
        ]
        + sems(
            13, nx + nz, 8, 8, 8, 8, 8, 8, 13, 13, (8, 4), (8, 4), 8, 8, 8, 8,
            (nx, 2, 2), (nx, 2, 2), (nz, 2, 4), (nz, 2, 4),
            (2, 4), (2, 4), (2, 4), (2, 4), (2, 4), (2, 4), (2, 2), (2, 2), (2, 2), (2, 2), 11, 11, 11, 11, 11, 11, 18, 18,
            24, (3, 8),
        ),
        [
            grad_gates, gates, gain_two, wr_rows, layer_input, gain_one, *tables, starts, log_sums,
            sums_x, sums_z, back, ffn_all, residual, out_grad, query, kv_rows, attended_tall, w_proj, sums, normed_all,
            w_query, w_key, w_value, units,
        ],
        "tail", 3, in_specs=[vm] * 14 + [hbm] * 14,
    )
    layer_output, input_grad, grad_in, grad_out, out_q, out_k, out_v, out_proj, router, gain_a, gain_b = call(
        pack_kernel,
        [(r.shape, r.dtype) for r in results[:8]] + [((4, 32), F32), ((4,), F32), ((4,), F32)], [], results, "pack",
    )
    return layer_output, input_grad, gain_a, out_q, out_k, out_v, out_proj, gain_b, router, grad_in, grad_out


def solution(mesh):
    tokens = P(("dp", "ep", "ctx"), None)
    in_specs = (
        tokens, P(), P(), P(), P(), P(), P(), P(),
        P("ep", None, None), P("ep", None, None), P("dp", None), tokens, tokens, tokens,
    )
    out_specs = (
        tokens, tokens, P(("dp", "ep", "ctx")), tokens, tokens, tokens, tokens, P(("dp", "ep", "ctx")), tokens,
        P("ep", ("dp", "ctx"), None), P("ep", ("dp", "ctx"), None),
    )
    return jax.shard_map(body, mesh=mesh, in_specs=in_specs, out_specs=out_specs, check_vma=False)
```

```python
from functools import partial

import jax
import jax.numpy as jnp
import numpy as np
from jax import lax
from jax.experimental import pallas as pl
from jax.experimental.pallas import tpu as pltpu
from jax.sharding import PartitionSpec as P

HD = 64
EPSILON = 1e-06
MASKED = -1e30
CAP = 40
TOK = 128
BIG = 4096.0
MESH = pl.DeviceIdType.MESH
F32 = jnp.float32
BF16 = jnp.bfloat16
VMEM_LIMIT = 60 * 1024 * 1024

NT = (((1,), (1,)), ((), ()))
NN = (((1,), (0,)), ((), ()))
TN = (((0,), (0,)), ((), ()))


def mm(a, b, dims=NN):
    return lax.dot_general(a, b, dims, preferred_element_type=F32)


def mm3(a, b, dims=NN):
    high = a.astype(BF16)
    low = (a - high.astype(F32)).astype(BF16)
    return mm(high, b, dims) + mm(low, b, dims)


def where_am_i():
    dp, ep, ctx = lax.axis_index("dp"), lax.axis_index("ep"), lax.axis_index("ctx")
    return dp, ep, ctx


def remote(src, dst, send, recv, device):
    return pltpu.make_async_remote_copy(
        src_ref=src, dst_ref=dst, send_sem=send, recv_sem=recv, device_id=device, device_id_type=MESH
    )


def greet(barrier, device):
    pl.semaphore_signal(barrier, inc=1, device_id=device, device_id_type=MESH)


def rotate_half(values):
    lane = lax.broadcasted_iota(jnp.int32, values.shape, 1)
    return jnp.where(lane % HD < HD // 2, pltpu.roll(values, 96, 1), pltpu.roll(values, 32, 1))


def rope_block(block, ca_ref, sa_ref, cb_ref, sb_ref):
    ca, sa = ca_ref[pl.ds(block, 1), :], sa_ref[pl.ds(block, 1), :]
    cb, sb = cb_ref[...], sb_ref[...]
    cosine = ca * cb - sa * sb
    sine = sa * cb + ca * sb
    lane = lax.broadcasted_iota(jnp.int32, cosine.shape, 1)
    return cosine, jnp.where(lane % HD < HD // 2, -sine, sine)


def rope_tables():
    frequency = 10000.0 ** (-np.arange(HD // 2, dtype=np.float64) * 2.0 / HD)
    frequency = np.tile(frequency.astype(np.float32).astype(np.float64), 4)
    blocks = np.arange(32, dtype=np.float64)[:, None] * 128.0 * frequency[None, :]
    rows = np.arange(128, dtype=np.float64)[:, None] * frequency[None, :]
    return [t.astype(np.float32) for t in (np.cos(blocks), np.sin(blocks), np.cos(rows), np.sin(rows))]


class EpGather:
    COUNT = 13

    def __init__(self, ref, send, recv, place):
        self.ref, self.send, self.recv = ref, send, recv
        dp, ep, ctx = place
        y, k = ep // 2, ep % 2
        self.up = (dp, ((y + 1) % 4) * 2 + k, ctx)
        self.dn = (dp, ((y + 3) % 4) * 2 + k, ctx)
        self.sib = (dp, y * 2 + 1 - k, ctx)

        def at(dy, other):
            return ((y + dy) % 4) * 2 + ((1 - k) if other else k)

        u, s, d = self.up, self.sib, self.dn
        self.sends = [
            (at(0, 0), None, s), (at(0, 0), 0, u), (at(0, 0), 1, u), (at(0, 0), 1, d), (at(0, 0), 0, d),
            (at(3, 0), 0, u), (at(3, 0), 0, s), (at(1, 0), 1, d), (at(1, 0), 1, s),
            (at(3, 0), 1, s), (at(1, 0), 0, s), (at(2, 0), 0, s), (at(2, 0), 1, s),
        ]
        self.gets = [
            (at(0, 1), None), (at(3, 0), 0), (at(3, 0), 1), (at(1, 0), 1), (at(1, 0), 0),
            (at(2, 0), 0), (at(3, 1), 0), (at(2, 0), 1), (at(1, 1), 1),
            (at(3, 1), 1), (at(1, 1), 0), (at(2, 1), 0), (at(2, 1), 1),
        ]

    def view(self, block, half):
        if half is None:
            return self.ref.at[block]
        rows = self.ref.shape[1] // 2
        return self.ref.at[block, pl.ds(half * rows, rows)]

    def go(self, *which):
        for i in which:
            block, half, device = self.sends[i]
            v = self.view(block, half)
            remote(v, v, self.send.at[i], self.recv.at[i], device).start()

    def got(self, *which):
        for i in which:
            v = self.view(*self.gets[i])
            remote(v, v, self.send.at[i], self.recv.at[i], self.sends[i][2]).wait_recv()

    def sent(self):
        for i in range(self.COUNT):
            block, half, device = self.sends[i]
            v = self.view(block, half)
            remote(v, v, self.send.at[i], self.recv.at[i], device).wait_send()

    def whole(self):
        self.got(1)
        self.go(5, 6)
        self.got(3)
        self.go(7, 8)
        self.got(2)
        self.go(9)
        self.got(4)
        self.go(10)
        self.got(5)
        self.go(11)
        self.got(7)
        self.go(12)
        self.got(0, 6, 8, 9, 10, 11, 12)


class EpScatterSum:
    COUNT = 8

    def __init__(self, part, cbuf, fbuf, gbuf, send, recv, place):
        self.part, self.cbuf, self.fbuf, self.gbuf = part, cbuf, fbuf, gbuf
        self.send, self.recv = send, recv
        dp, ep, ctx = place
        self.y, self.k = ep // 2, ep % 2
        y, k = self.y, self.k
        self.up = (dp, ((y + 1) % 4) * 2 + k, ctx)
        self.dn = (dp, ((y + 3) % 4) * 2 + k, ctx)
        self.sib = (dp, y * 2 + 1 - k, ctx)

    def block(self, dy, other=False):
        return ((self.y + dy) % 4) * 2 + ((1 - self.k) if other else self.k)

    def copy(self, i):
        half = self.cbuf.shape[1] // 2
        lo, hi = pl.ds(0, half), pl.ds(half, half)
        s, r = self.send, self.recv
        if i < 4:
            away = self.block((2, 1, 3, 0)[i], True)
            return remote(self.part.at[away], self.cbuf.at[i], s.at[i], r.at[i], self.sib)
        src, dst, device = (
            (self.cbuf.at[0, lo], self.fbuf.at[0], self.up),
            (self.cbuf.at[0, hi], self.fbuf.at[1], self.dn),
            (self.cbuf.at[1], self.gbuf.at[0], self.up),
            (self.cbuf.at[2], self.gbuf.at[1], self.dn),
        )[i - 4]
        return remote(src, dst, s.at[i], r.at[i], device)

    def start(self):
        for i in range(4):
            self.copy(i).start()

    def far(self):
        self.copy(0).wait_recv()
        self.cbuf[0] = (self.cbuf[0].astype(F32) + self.part[self.block(2)].astype(F32)).astype(BF16)
        self.copy(4).start()
        self.copy(5).start()

    def near(self):
        half = self.cbuf.shape[1] // 2
        for slot, dy, far, rows, rest in ((1, 1, 0, pl.ds(0, half), pl.ds(half, half)), (2, 3, 1, pl.ds(half, half), pl.ds(0, half))):
            b = self.block(dy)
            self.copy(slot).wait_recv()
            self.copy(4 + far).wait_recv()
            self.cbuf[slot, rows] = (
                self.cbuf[slot, rows].astype(F32) + self.part[b, rows].astype(F32) + self.fbuf[far].astype(F32)
            ).astype(BF16)
            self.cbuf[slot, rest] = (self.cbuf[slot, rest].astype(F32) + self.part[b, rest].astype(F32)).astype(BF16)
            self.copy(6 + far).start()

    def last(self):
        for i in (3, 6, 7):
            self.copy(i).wait_recv()
        return (
            self.part[self.block(0)].astype(F32) + self.cbuf[3].astype(F32)
            + self.gbuf[0].astype(F32) + self.gbuf[1].astype(F32)
        )

    def sent(self):
        for i in range(self.COUNT):
            self.copy(i).wait_send()


def scatter_sum_scratch():
    return [
        pltpu.VMEM((4, TOK, 1024), BF16),
        pltpu.VMEM((2, TOK // 2, 1024), BF16),
        pltpu.VMEM((2, TOK, 1024), BF16),
        pltpu.SemaphoreType.DMA((8,)),
        pltpu.SemaphoreType.DMA((8,)),
    ]


def repeat(first, last, work):
    def each(i, carry):
        work(i)
        return carry

    lax.fori_loop(first, last, each, 0)


def exchange(src, dst, send, recv, place, wait):
    dp, ep, ctx = place

    def one(r):
        to, source = (ep + r) % 8, (ep + 8 - r) % 8
        if not wait:
            remote(src.at[to], dst.at[ep], send.at[r], recv.at[r], (dp, to, ctx)).start()
        else:
            remote(src.at[to], dst.at[source], send.at[r], recv.at[r], (dp, to, ctx)).wait_recv()

    repeat(1, 8, one)


def exchange_sent(src, dst, send, recv, place):
    dp, ep, ctx = place

    def one(r):
        to = (ep + r) % 8
        remote(src.at[to], dst.at[ep], send.at[r], recv.at[r], (dp, to, ctx)).wait_send()

    repeat(1, 8, one)


def starts_of(docs):
    rows = lax.broadcasted_iota(jnp.int32, docs.shape, 0)
    lane = lax.broadcasted_iota(jnp.int32, docs.shape, 1)
    docs = docs.astype(F32)
    turned = pltpu.roll(docs, 1, 1)
    before = jnp.where(lane == 0, pltpu.roll(turned, 1, 0), turned)
    place = rows * 128 + lane
    fresh = (docs != before) | (place == 0)
    value = jnp.where(fresh, place.astype(F32), 0.0)
    for shift in (1, 2, 4, 8, 16, 32, 64):
        value = jnp.maximum(value, jnp.where(lane >= shift, pltpu.roll(value, shift, 1), 0.0))
    carry = jnp.broadcast_to(jnp.max(value, axis=1, keepdims=True), value.shape)
    for shift in (1, 2, 4, 8, 16):
        carry = jnp.maximum(carry, jnp.where(rows >= shift, pltpu.roll(carry, shift, 0), 0.0))
    above = jnp.where(rows >= 1, pltpu.roll(carry, 1, 0), 0.0)
    return jnp.maximum(value, above)


def priorities(order):
    def spread(part):
        return mm(part.astype(F32).astype(BF16), from_rows, TN)

    r = lax.broadcasted_iota(jnp.int32, (8, 128), 0)
    t = lax.broadcasted_iota(jnp.int32, (8, 128), 1)
    from_rows = jnp.where(t // 16 == r, 1.0, 0.0).astype(BF16)
    of_k = jnp.where(t % 8 == r, 1.0, 0.0).astype(BF16)
    l = lax.broadcasted_iota(jnp.int32, (128, 128), 0)
    t = lax.broadcasted_iota(jnp.int32, (128, 128), 1)
    meets = l // 8 == t % 16
    high = jnp.where(meets, spread(order // 32), 0.0).astype(BF16)
    low = jnp.where(meets, spread(order % 32), 0.0).astype(BF16)
    return mm(of_k, high) * 32.0 + mm(of_k, low)


def slots_of(eidT_ref, order_ref, slot_scr, sel_ref):
    def expert(index):
        return jnp.where(index % 8 < 4, (index // 8) * 4 + index % 8, -1)

    row_expert = expert(lax.broadcasted_iota(jnp.int32, (64, TOK), 0))
    by_row = jnp.full((64, TOK), BIG, F32)
    ranks = priorities(order_ref[...])
    for k in range(8):
        by_row = jnp.where(eidT_ref[k : k + 1, :] == row_expert, ranks[k : k + 1, :], by_row)
    by_lane = by_row.T
    sel_ref[...] = jnp.where(by_row < BIG, 1.0, 0.0)
    for g in range(8):
        for j in range(4):
            r = 8 * g + j
            row = by_row[r : r + 1, :]
            less = jnp.where(by_lane[:, r : r + 1] < row, 1.0, 0.0)
            rank = jnp.sum(less, axis=0, keepdims=True)
            slot_scr[g, j : j + 1, :] = jnp.where((row < BIG) & (rank < CAP), rank, -1.0)
        slot_scr[g, 4:8, :] = jnp.full((4, TOK), -1.0, F32)


CHUNK = 512


def key_mask(step, start_row, place_row):
    keys = (lax.broadcasted_iota(jnp.int32, (2 * CHUNK, 256), 0) + step * (2 * CHUNK)).astype(F32)
    return (keys >= start_row) & (keys <= place_row)


def query_rows(j, ctx, start_ref):
    block = 4 * j + ctx
    start = start_ref[pl.ds(block, 1), :]
    places = (lax.broadcasted_iota(jnp.int32, (1, 128), 1) + block * 128).astype(F32)
    return jnp.concatenate([start, start], axis=1), jnp.concatenate([places, places], axis=1)


def turned(block):
    return block.astype(F32).T.astype(BF16)


def heads_wide(tall):
    return jnp.concatenate([tall[:HD], tall[HD:]], axis=1)


def head_kernel(
    x_ref, gain_one_ref, gain_two_ref, og_ref, ca_ref, sa_ref, cb_ref, sb_ref, eidT_ref, order_ref, doc_ref, wr_ref,
    wq_hbm, wk_hbm, wv_hbm, wp_hbm,
    nall_ref, ogall_ref, q_ref, kv_ref, slot_ref, start_ref, attT_ref, lse_ref, res_ref, nf_ref, gin_ref, gates_ref,
    wq, wk, wv, w_own, wp, slot_scr, sel, att, abuf, kv_rows, kvT, gscr,
    wsem, nsend, nrecv, osend, orecv, ssend, srecv, ksend, krecv, asend, arecv, fsend, frecv, gsend, grecv,
):
    place = where_am_i()
    dp, ep, ctx = place
    y = ep // 2
    pair = pl.ds(pl.multiple_of(y * 128, 128), 128)
    loads = [
        pltpu.make_async_copy(src, dst, wsem.at[i])
        for i, (src, dst) in enumerate(
            (
                (wq_hbm.at[:, pl.ds(pl.multiple_of(ep * 128, 128), 128)], wq),
                (wk_hbm.at[:, pair], wk),
                (wv_hbm.at[:, pair], wv),
                (wp_hbm, wp),
            )
        )
    ]
    for f in loads:
        f.start()
    barrier = pltpu.get_barrier_semaphore()
    repeat(1, 8, lambda r: greet(barrier, (dp, (ep + r) % 8, ctx)))

    @pl.when(ctx > 0)
    def _():
        greet(barrier, (dp, ep, ctx - 1))

    @pl.when(ctx < 3)
    def _():
        greet(barrier, (dp, ep, ctx + 1))

    x = x_ref[...].astype(F32)
    normed = x * lax.rsqrt(jnp.mean(x * x, axis=-1, keepdims=True) + EPSILON) * gain_one_ref[...]
    nall_ref[ep] = normed.astype(BF16)
    ogall_ref[ep] = og_ref[...]
    edges = jnp.where(ctx > 0, 1, 0) + jnp.where(ctx < 3, 1, 0)
    pl.semaphore_wait(barrier, 7 + edges)

    gather = EpGather(nall_ref, nsend, nrecv, place)
    grads = EpGather(ogall_ref, osend, orecv, place)
    gather.go(0, 1, 3, 2, 4)
    for f in loads[:3]:
        f.wait()
    lane = lax.broadcasted_iota(jnp.int32, (1024, 128), 1)
    even = ep % 2 == 0
    k_pair, v_pair = wk[...].astype(F32), wv[...].astype(F32)
    k_half = jnp.where(even, k_pair, pltpu.roll(k_pair, HD, 1))
    v_half = jnp.where(even, pltpu.roll(v_pair, HD, 1), v_pair)
    w_own[:, 0:128] = wq[...]
    w_own[:, 128:256] = jnp.where(lane < HD, k_half, v_half).astype(BF16)
    lane = lax.broadcasted_iota(jnp.int32, (TOK, 128), 1)

    def project(dy):
        chip = (y + dy) % 4
        rows = jnp.concatenate([nall_ref[2 * chip], nall_ref[2 * chip + 1]], axis=0)
        out = mm(rows, w_own[...])
        for i in range(2):
            b = 2 * chip + i
            cosine, sine = rope_block(4 * b + ctx, ca_ref, sa_ref, cb_ref, sb_ref)
            q = out[i * TOK : (i + 1) * TOK, :128]
            kv = out[i * TOK : (i + 1) * TOK, 128:]
            q_rot = (q * cosine + rotate_half(q) * sine).astype(BF16)
            q_ref[b] = (q_rot.astype(F32) * (HD**-0.5)).astype(BF16)
            cosine = jnp.where(lane < HD, cosine, 1.0)
            sine = jnp.where(lane < HD, sine, 0.0)
            kv_ref[b, ctx] = (kv * cosine + rotate_half(kv) * sine).astype(BF16)

    offsets = (0, 3, 1, 2)

    def hop(direction, h, g, action):
        chip = (y + offsets[g]) % 4
        back = h - 1
        own = ctx - back if direction == 0 else ctx + back
        come = ctx - h if direction == 0 else ctx + h
        to = ctx + 1 if direction == 0 else ctx - 1
        index = (direction * 3 + back) * 4 + g
        send, recv = ksend.at[index], krecv.at[index]
        if action == "recv":
            ok = come >= 0 if direction == 0 else come <= 3

            @pl.when(ok)
            def _():
                v = kv_ref.at[pl.ds(2 * chip, 2), come]
                remote(v, v, send, recv, (dp, ep, ctx)).wait_recv()

        else:
            ok = (own >= 0) & (ctx < 3) if direction == 0 else (own <= 3) & (ctx > 0)

            @pl.when(ok)
            def _():
                v = kv_ref.at[pl.ds(2 * chip, 2), own]
                c = remote(v, v, send, recv, (dp, ep, to))
                c.start() if action == "send" else c.wait_send()

    def hops(h, g):
        for direction in (0, 1):
            if h > 1:
                hop(direction, h - 1, g, "recv")
            hop(direction, h, g, "send")

    gather.got(0)
    project(0)
    hops(1, 0)
    start_ref[...] = starts_of(doc_ref[...])
    slots_of(eidT_ref, order_ref, slot_scr, sel)
    gather.got(1)
    gather.go(5, 6)
    gather.got(3)
    gather.go(7, 8)
    gather.got(2)
    gather.go(9)
    gather.got(4)
    gather.go(10)
    slot_ref[ep] = slot_scr[ep]
    exchange(slot_scr, slot_ref, ssend, srecv, place, False)
    hops(2, 0)
    gather.got(6, 9)
    project(3)
    hops(1, 1)
    gather.got(8, 10)
    project(1)
    hops(1, 2)
    hops(3, 0)
    hops(2, 1)
    gather.got(5)
    gather.go(11)
    gather.got(7)
    gather.go(12)
    grads.go(0, 1, 3, 2, 4)
    gather.got(11, 12)
    project(2)
    hops(1, 3)
    hops(2, 2)
    hops(3, 1)
    hops(2, 3)
    hops(3, 2)
    hops(3, 3)
    grads.got(1)
    grads.go(5, 6)
    grads.got(3)
    grads.go(7, 8)
    for g in range(4):
        for direction in (0, 1):
            hop(direction, 3, g, "recv")

    def turn_keys(chunk):
        rows = kv_ref[chunk].reshape(CHUNK, 128)
        at = pl.ds(pl.multiple_of(chunk * CHUNK, CHUNK), CHUNK)
        kv_rows[at, :] = rows
        part = rows.astype(F32).T
        row = lax.broadcasted_iota(jnp.int32, part.shape, 0)
        kvT[:, at] = jnp.where(row < HD, 1.0, part).astype(BF16)

    repeat(0, 8, turn_keys)

    def piece_copy(m):
        return remote(att.at[m], abuf.at[ep], asend.at[m], arecv.at[ep], (dp, m, ctx))

    def block(j):
        start_row, place_row = query_rows(j, ctx, start_ref)
        wide = heads_wide(turned(q_ref[j]))
        q_pad = jnp.concatenate([wide, jnp.zeros_like(wide)], axis=0)

        def step(i, carry):
            top, total = carry
            rows = pl.ds(pl.multiple_of(i * (2 * CHUNK), 2 * CHUNK), 2 * CHUNK)
            scores = mm(kv_rows[rows, :], q_pad)
            scores = jnp.where(key_mask(i, start_row, place_row), scores, MASKED)
            new_top = jnp.maximum(top, jnp.max(scores, axis=0, keepdims=True))
            probs = jnp.exp(scores - new_top).astype(BF16)
            total = total * jnp.exp(top - new_top) + mm(kvT[:, rows], probs)
            return new_top, total

        top, total = lax.fori_loop(0, j // 2 + 1, step, (jnp.full((1, 256), MASKED, F32), jnp.zeros((128, 256), F32)))
        norm = total[0:1]
        out = total[HD:] / norm
        tall = jnp.concatenate([out[:, :128], out[:, 128:]], axis=0)
        attT_ref[j] = tall
        att[j] = tall.T.astype(BF16)
        lse_ref[j] = jnp.broadcast_to(top + jnp.log(norm), (8, 256))

        @pl.when(ep != j)
        def _():
            piece_copy(j).start()

        @pl.when(ep == j)
        def _():
            abuf[ep] = att[j]

    repeat(0, 6, block)
    grads.got(2)
    grads.go(9)
    grads.got(4)
    grads.go(10)
    grads.got(5)
    grads.go(11)
    grads.got(7)
    grads.go(12)
    repeat(6, 8, block)

    loads[3].wait()

    def piece_got(r):
        p = (ep + r) % 8
        remote(att.at[p], abuf.at[p], asend.at[p], arecv.at[p], (dp, p, ctx)).wait_recv()

    repeat(1, 8, piece_got)
    attended = jnp.concatenate([abuf[p] for p in range(8)], axis=1)
    res = x_ref[...].astype(F32) + mm(attended, wp[...])
    res_ref[...] = res
    normed = res * lax.rsqrt(jnp.mean(res * res, axis=-1, keepdims=True) + EPSILON) * gain_two_ref[...]
    normed = normed.astype(BF16)
    nf_ref[ep] = normed
    rows = EpGather(nf_ref, fsend, frecv, place)
    rows.go(0, 1, 3, 2, 4)
    to = lax.broadcasted_iota(jnp.int32, (64, 32), 0)
    source = lax.broadcasted_iota(jnp.int32, (64, 32), 1)
    spread = jnp.where((to % 8 < 4) & (source == (to // 8) * 4 + to % 8), 1.0, 0.0).astype(BF16)
    logits = mm(mm(spread, wr_ref[...]).astype(BF16), normed, NT)
    chosen = sel[...] > 0.5
    top = jnp.max(jnp.where(chosen, logits, MASKED), axis=0, keepdims=True)
    weight = jnp.where(chosen, jnp.exp(jnp.where(chosen, logits, MASKED) - top), 0.0)
    gates = weight / jnp.sum(weight, axis=0, keepdims=True)
    gates_ref[...] = gates
    for g in range(8):
        gscr[g] = gates[8 * g : 8 * g + 8, :]
    gin_ref[ep] = gscr[ep]
    exchange(gscr, gin_ref, gsend, grecv, place, False)
    exchange(slot_scr, slot_ref, ssend, srecv, place, True)
    grads.got(0, 6, 8, 9, 10, 11, 12)
    rows.whole()
    exchange(gscr, gin_ref, gsend, grecv, place, True)
    for g in (gather, grads, rows):
        g.sent()
    exchange_sent(slot_scr, slot_ref, ssend, srecv, place)
    exchange_sent(gscr, gin_ref, gsend, grecv, place)
    repeat(1, 8, lambda r: piece_copy((ep + r) % 8).wait_send())
    for g in range(4):
        for h in (1, 2, 3):
            for direction in (0, 1):
                hop(direction, h, g, "sent")


def each_slab(lead, work):
    count = 1
    for size in lead:
        count *= size

    def each(i, carry):
        work((i,) if len(lead) == 1 else (i // lead[1], i % lead[1]))
        return carry

    lax.fori_loop(0, count, each, 0)


class Arc:
    def __init__(self, n, pos, own, half, slots, devices, send, recv):
        self.n, self.pos, self.own, self.half, self.slots = n, pos, own, half, slots
        self.devices, self.send, self.recv = devices, send, recv
        self.steps = n // 2

    def chunk(self, way, s):
        reach = self.steps - s + 1
        return (self.pos + reach) % self.n if way == 0 else (self.pos + self.n - reach) % self.n

    def copy(self, way, s):
        dst = self.slots.at[way, s - 1]
        src = self.own(self.chunk(way, s)) if s == 1 else self.slots.at[way, s - 2]
        if s == 1:
            src, dst = self.half(src, way), self.half(dst, way)
        return remote(src, dst, self.send.at[way, s - 1], self.recv.at[way, s - 1], self.devices[way])

    def start(self):
        for way in (0, 1):
            self.copy(way, 1).start()

    def slabs(self, work):
        each_slab(self.slots.shape[2:-2], work)

    def advance(self, s):
        for way in (0, 1):
            self.copy(way, s - 1).wait_recv()
            held, own = self.slots.at[way, s - 2], self.own(self.chunk(way, s))
            if s == 2:
                self.merge(way, held, own)
            else:

                def add(index):
                    held[index] = (held[index].astype(F32) + own[index].astype(F32)).astype(BF16)

                self.slabs(add)
            self.copy(way, s).start()

    def merge(self, way, held, own):
        mine, its = self.half(held, way), self.half(own, way)
        other, from_own = self.half(held, 1 - way), self.half(own, 1 - way)

        def add(index):
            mine[index] = (mine[index].astype(F32) + its[index].astype(F32)).astype(BF16)

        def take(index):
            other[index] = from_own[index]

        each_slab(mine.shape[:-2], add)
        each_slab(other.shape[:-2], take)

    def finish(self, put):
        for way in (0, 1):
            self.copy(way, self.steps).wait_recv()
        own, up, down = self.own(self.pos), self.slots.at[0, self.steps - 1], self.slots.at[1, self.steps - 1]

        def add(index):
            put(index, own[index].astype(F32) + up[index].astype(F32) + down[index].astype(F32))

        self.slabs(add)

    def sent(self):
        for way in (0, 1):
            for s in range(1, self.steps + 1):
                self.copy(way, s).wait_send()


class Torus:
    def __init__(self, place):
        self.dp, self.ep, self.ctx = place
        self.zh, self.x = self.dp // 4, self.dp % 4
        self.z = self.zh * 4 + self.ctx

    def at_x(self, v):
        return (self.zh * 4 + v % 4, self.ep, self.ctx)

    def at_z(self, v):
        v = v % 8
        return ((v // 4) * 4 + self.x, self.ep, v % 4)

    def x_ways(self):
        return self.at_x(self.x + 1), self.at_x(self.x + 3)

    def z_ways(self):
        return self.at_z(self.z + 1), self.at_z(self.z + 7)

    def x_arc(self, own, half, slots, send, recv):
        return Arc(4, self.x, own, half, slots, self.x_ways(), send, recv)

    def z_arc(self, own, half, slots, send, recv):
        return Arc(8, self.z, own, half, slots, self.z_ways(), send, recv)


def first_or_last(sizes):
    def half(view, h):
        return view.at[pl.ds(0, sizes[0])] if h == 0 else view.at[pl.ds(sizes[0], sizes[1])]

    return half


X_FIRST, Z_FIRST = (0, 1), (2,)
KEPT = 3
X_UNITS, Z_UNITS = (3, 4, 5, 6, 7, 8), (9, 10, 11)


def unit_arcs(torus, own, x_units, z_units, x_slots, z_slots, xs, xr, zs, zr):
    xa = [
        torus.x_arc(
            lambda t, i=i: own.at[i, :, t], first_or_last((1, 1)), x_slots.at[i], xs.at[i], xr.at[i]
        )
        for i in range(len(x_units))
    ]
    za = [
        torus.z_arc(
            lambda t, i=i: own.at[len(x_units) + i, t // 4, :, t % 4], first_or_last((2, 2)), z_slots.at[i], zs.at[i], zr.at[i]
        )
        for i in range(len(z_units))
    ]
    return xa, za


def expert_kernel(
    slot_ref, gate_ref, nf_hbm, og_hbm, win_hbm, wout_hbm,
    y_ref, d_ref, dg_ref, rx_ref, rz_ref, gw_hbm,
    nf, og, win, wout, rows_scr, grad_scr, units, x_slots, z_slots,
    fsem, wsem, gsem, xs, xr, zs, zr,
):
    torus = Torus(where_am_i())
    loads = [pltpu.make_async_copy(nf_hbm, nf, fsem.at[0]), pltpu.make_async_copy(og_hbm, og, fsem.at[1])]

    def weights(j):
        return (
            pltpu.make_async_copy(win_hbm.at[j], win.at[j % 2], wsem.at[j, 0]),
            pltpu.make_async_copy(wout_hbm.at[j], wout.at[j % 2], wsem.at[j, 1]),
        )

    for f in loads + list(weights(0)) + list(weights(1)):
        f.start()
    barrier = pltpu.get_barrier_semaphore()
    for device in torus.x_ways() + torus.z_ways():
        greet(barrier, device)
    slot = lax.broadcasted_iota(jnp.int32, (CAP, TOK), 0).astype(F32)

    def picks(s, e):
        return slot == slot_ref[s, pl.ds(e, 1), :]

    for f in loads:
        f.wait()

    def load(s, carry):
        pick = jnp.concatenate([jnp.where(picks(s, e), 1.0, 0.0) for e in range(4)], axis=0).astype(BF16)
        got = mm(pick, nf[s])
        grad = mm(pick, og[s])
        for e in range(4):
            rows = pl.ds(pl.multiple_of(s * CAP, 8), CAP)
            rows_scr[e, rows, :] = got[e * CAP : (e + 1) * CAP]
            grad_scr[e, rows, :] = grad[e * CAP : (e + 1) * CAP]
        return carry

    lax.fori_loop(0, 8, load, 0)

    xa, za = unit_arcs(torus, units, X_FIRST, Z_FIRST, x_slots, z_slots, xs, xr, zs, zr)
    views = (2, 4, 4, 16, 1024)

    def back_weights(j, received, grad_gu):
        grad_in = mm(received, grad_gu, TN).astype(BF16).reshape(32, 32, 1024)
        units[3 * j] = grad_in[:, 0:16].reshape(views)
        units[3 * j + 1] = grad_in[:, 16:32].reshape(views)

    def expert(j, carry):
        gates = jnp.concatenate(
            [
                jnp.sum(jnp.where(picks(s, j), gate_ref[s, pl.ds(j, 1), :], 0.0), axis=1, keepdims=True)
                for s in range(8)
            ],
            axis=0,
        )
        for f in weights(j):
            f.wait()
        w_in, w_out = win[j % 2], wout[j % 2]
        received = rows_scr[j].astype(BF16)
        grad_tok = grad_scr[j]
        gate_up = mm(received, w_in)
        gating, up = gate_up[:, :512], gate_up[:, 512:]
        sig = 1.0 / (1.0 + jnp.exp(-gating))
        silu = gating * sig
        act = (silu * up).astype(BF16)
        result = mm(act, w_out).astype(BF16).astype(F32)
        dots = jnp.sum(grad_tok * result, axis=1, keepdims=True)
        grad_res = (grad_tok * gates).astype(BF16)
        grad_scr[j] = result * gates
        for s in range(8):
            dg_ref[s, pl.ds(j, 1), :] = jnp.sum(
                jnp.where(picks(s, j), dots[s * CAP : (s + 1) * CAP], 0.0), axis=0, keepdims=True
            )
        units[3 * j + 2] = mm(act, grad_res, TN).astype(BF16).reshape(views)
        grad_act = mm(grad_res, w_out, NT)
        grad_up = (grad_act * silu).astype(BF16)
        grad_gate = (grad_act * up * sig * (1.0 + gating * (1.0 - sig))).astype(BF16)
        grad_gu = jnp.concatenate([grad_gate, grad_up], axis=1)
        between(j)
        back_weights(j, received, grad_gu)
        rows_scr[j] = mm(grad_gu, w_in, NT)
        after(j)
        return carry

    def keep(first, last):
        return [pltpu.make_async_copy(units.at[u], gw_hbm.at[u - KEPT], gsem.at[u - KEPT]) for u in range(first, last)]

    def between(j):
        @pl.when(j == 1)
        def _():
            za[0].advance(2)
            xa[0].advance(2)

        @pl.when(j == 2)
        def _():
            za[0].advance(3)

        @pl.when(j == 3)
        def _():
            za[0].advance(4)

    def after(j):
        @pl.when(j < 2)
        def _():
            for f in weights(j + 2):
                f.start()

        @pl.when(j == 0)
        def _():
            for arc in za + xa:
                arc.start()

        @pl.when(j == 1)
        def _():
            xa[1].advance(2)
            for f in keep(KEPT, 6):
                f.start()

        @pl.when(j == 2)
        def _():
            for f in keep(6, 9):
                f.start()

    pl.semaphore_wait(barrier, 4)
    lax.fori_loop(0, 4, expert, 0)
    for f in keep(9, 12):
        f.start()

    def store(s, carry):
        pick = jnp.concatenate([jnp.where(picks(s, e), 1.0, 0.0) for e in range(4)], axis=0).astype(BF16)
        rows = pl.ds(pl.multiple_of(s * CAP, 8), CAP)
        weighted = jnp.concatenate([grad_scr[e, rows, :] for e in range(4)], axis=0).astype(BF16)
        y_ref[s] = mm(pick, weighted, TN).astype(BF16)
        back = jnp.concatenate([rows_scr[e, rows, :] for e in range(4)], axis=0).astype(BF16)
        d_ref[s] = mm(pick, back, TN).astype(BF16)
        dg_ref[s, 4:8, :] = jnp.zeros((4, TOK), F32)
        return carry

    lax.fori_loop(0, 8, store, 0)

    def put_z(index, value):
        for h in (0, 1):
            rz_ref[index[0], h] = value[:, 512 * h : 512 * h + 512].astype(BF16)

    za[0].finish(put_z)
    for i, arc in enumerate(xa):

        def put_x(index, value, i=i):
            rx_ref[index[0] * 4 + index[1], i] = value.astype(BF16)

        arc.finish(put_x)
    for f in keep(KEPT, 12):
        f.wait()
    for arc in xa + za:
        arc.sent()


class Direct:
    def __init__(self, torus, part, x_slots, result, z_slots, send, recv):
        self.t, self.part, self.x_slots, self.result, self.z_slots = torus, part, x_slots, result, z_slots
        self.send, self.recv = send, recv

    def x_copy(self, r):
        to = (self.t.x + r) % 4
        return remote(
            self.part.at[:, to], self.x_slots.at[r - 1], self.send.at[r], self.recv.at[r], self.t.at_x(to)
        )

    def z_copy(self, r):
        to = (self.t.z + r) % 8
        return remote(
            self.result.at[to], self.z_slots.at[r - 1], self.send.at[3 + r], self.recv.at[3 + r], self.t.at_z(to)
        )

    def start(self):
        for r in (2, 1, 3):
            self.x_copy(r).start()

    def turn(self):
        for r in (1, 2, 3):
            self.x_copy(r).wait_recv()

        def add(i, carry):
            h, l = i // 4, i % 4
            value = self.part[h, self.t.x, l].astype(F32)
            for r in range(3):
                value = value + self.x_slots[r, h, l].astype(F32)
            self.result[i] = value.astype(BF16)
            return carry

        lax.fori_loop(0, 8, add, 0)
        repeat(0, 7, lambda i: self.z_copy(4 + (2 * (i % 2) - 1) * ((i + 1) // 2)).start())

    def finish(self):
        repeat(1, 8, lambda r: self.z_copy(r).wait_recv())
        value = self.result[self.t.z].astype(F32)
        for r in range(7):
            value = value + self.z_slots[r].astype(F32)
        return value

    def sent(self):
        repeat(1, 4, lambda r: self.x_copy(r).wait_send())
        repeat(1, 8, lambda r: self.z_copy(r).wait_send())


def prepare_queries(j, ctx, start_ref, q_ref, lse_ref, both, stack, rows):
    lane = lax.broadcasted_iota(jnp.int32, (256, 128), 1)
    start_row, place_row = query_rows(j, ctx, start_ref)
    q_blk = q_ref[j]
    zero = jnp.zeros((HD, 256), BF16)
    both[j, 0:HD, 0:256] = heads_wide(turned(q_blk))
    both[j, HD:128, 0:256] = zero
    both[j, 0:HD, 256:512] = zero
    q_f = q_blk.astype(F32)
    q_rows = jnp.concatenate([q_f, pltpu.roll(q_f, HD, 1)], axis=0)
    stack[j, 0:256] = jnp.where(lane < HD, q_rows, 0.0).astype(BF16)
    rows[j, 0:1, :] = lse_ref[j, 0:1, :]
    rows[j, 2:3, :] = start_row
    rows[j, 3:4, :] = place_row


def prepare_grads(j, attT_ref, gm_ref, w_ref, both, stack, rows):
    lane = lax.broadcasted_iota(jnp.int32, (256, 128), 1)
    tall = mm(w_ref[...], gm_ref[j], NT).astype(BF16).astype(F32)
    rows[j, 1:2, :] = jnp.sum(heads_wide(tall) * heads_wide(attT_ref[j]), axis=0, keepdims=True)
    both[j, HD:128, 256:512] = heads_wide(tall).astype(BF16)
    g_f = tall.T
    g_rows = jnp.concatenate([pltpu.roll(g_f, HD, 1), g_f], axis=0)
    stack[j, 256:512] = jnp.where(lane < HD, 0.0, g_rows).astype(BF16)


def attend_pair(m, j, kv, kT, both, stack, rows):
    row = rows[j]
    chunk = pl.ds(pl.multiple_of(m * CHUNK, CHUNK), CHUNK)
    pair = mm(kv[chunk, :], both[j])
    keys = (lax.broadcasted_iota(jnp.int32, (CHUNK, 256), 0) + m * CHUNK).astype(F32)
    allowed = (keys >= row[2:3]) & (keys <= row[3:4])
    probs = jnp.exp(jnp.where(allowed, pair[:, :256], MASKED) - row[0:1])
    grad = (probs * (pair[:, 256:] - row[1:2])).astype(BF16)
    return mm(jnp.concatenate([grad, probs.astype(BF16)], axis=1), stack[j]), mm(kT[:, chunk], grad)


def tail_kernel(
    dg_ref, gates_ref, gain_two_ref, wr_ref, x_ref, gain_one_ref, ca_ref, sa_ref, cb_ref, sb_ref, start_ref, lse_ref,
    rx0, rz0,
    back_hbm, nf_hbm, res_hbm, og_hbm, q_hbm, kv_hbm, attT_hbm, wp_hbm, y_hbm, nall_hbm, wq_hbm, wk_hbm, wv_hbm, gw_hbm,
    out_ref, ing_ref, gin_ref, gout_ref, gq_ref, gk_ref, gv_ref, gproj_out, gside_ref, gains_ref,
    back, nf, res, og, q_ref, kv, attT, wp, y_part, wq, wk, wv, own,
    dbuf, cbuf, fbuf, gbuf, cbuf2, fbuf2, gbuf2, gm, gres,
    kT, both, stack, rows, dqs, acc, dkv, dqb, dkvb, kbuf, qpieces, kpieces,
    x_slots, z_slots, g0_slots, g1_slots, g2_slots, h0_slots, h1_slots, rx1, rx2, rz1,
    early, late_q, late_k, e_x, e_res, e_z, q_x, q_res, q_z, k_x, k_res, k_z,
    gain_own, gain_e, gain_x, gain_z, fin, fin_late, rs, rp, rq,
    fsem, usem, csend, crecv, c2send, c2recv, dsend, drecv, msend, mrecv, ksend, krecv, qsend, qrecv, psend, precv,
    xs, xr, zs, zr, g0s, g0r, g1s, g1r, g2s, g2r, h0s, h0r, h1s, h1r, es, er, lqs, lqr, lks, lkr, gs, gr,
    fsend, frecv,
):
    place = where_am_i()
    dp, ep, ctx = place
    torus = Torus(place)
    nall = back
    sources = dict(
        back=(back_hbm, back), nf=(nf_hbm.at[ep], nf), res=(res_hbm, res), og=(og_hbm, og), q=(q_hbm, q_ref),
        kv=(kv_hbm, kv), attT=(attT_hbm, attT), wp=(wp_hbm.at[pl.ds(pl.multiple_of(ep * 128, 128), 128)], wp), y=(y_hbm, y_part),
        nall=(nall_hbm, nall), wq=(wq_hbm, wq), wk=(wk_hbm, wk), wv=(wv_hbm, wv),
    )
    loads = {
        name: pltpu.make_async_copy(src, dst, fsem.at[i]) for i, (name, (src, dst)) in enumerate(sources.items())
    }
    units = {u: pltpu.make_async_copy(gw_hbm.at[u - KEPT], own.at[i], usem.at[i]) for i, u in enumerate(X_UNITS + Z_UNITS)}
    loads["back"].start()
    for u in (3, 9, 4, 10, 5, 11, 6, 7, 8):
        units[u].start()
    for name in ("nf", "res", "og", "kv", "q", "attT", "wp"):
        loads[name].start()
    for name in ("y", "wq", "wk", "wv"):
        loads[name].start()

    def send_to(g, h):
        return (dp, 2 * ctx + g // 2, 2 * (g % 2) + h), (ep, 2 * ctx + g // 2, 2 * (g % 2) + h)

    def is_me(device):
        return (device[0] == dp) & (device[1] == ep) & (device[2] == ctx)

    barrier = pltpu.get_barrier_semaphore()

    def greet_peers(r):
        greet(barrier, (dp, (ep + r) % 8, ctx))
        greet(barrier, torus.at_z(torus.z + r))

    repeat(1, 8, greet_peers)
    repeat(1, 4, lambda r: greet(barrier, torus.at_x(torus.x + r)))

    def greet_senders(i):
        for device in ((dp, i, ep // 2), (i, dp, ep // 2)):

            @pl.when(jnp.logical_not(is_me(device)))
            def _():
                greet(barrier, device)

    repeat(0, 8, greet_senders)
    waits = 17
    for g in range(4):
        for h in range(2):
            for device in send_to(g, h):
                waits = waits + jnp.where(is_me(device), 0, 1)
    pl.semaphore_wait(barrier, waits)

    xa, za = unit_arcs(torus, own, X_UNITS, Z_UNITS, x_slots, z_slots, xs, xr, zs, zr)
    g0 = torus.z_arc(lambda t: rx0.at[t], first_or_last((1, 1)), g0_slots, g0s, g0r)
    g1 = torus.z_arc(lambda t: rx1.at[t], first_or_last((2, 2)), g1_slots, g1s, g1r)
    g2 = torus.z_arc(lambda t: rx2.at[t], first_or_last((1, 1)), g2_slots, g2s, g2r)
    h0 = torus.x_arc(lambda t: rz0.at[t], first_or_last((1, 1)), h0_slots, h0s, h0r)
    h1 = torus.x_arc(lambda t: rz1.at[t], first_or_last((1, 2)), h1_slots, h1s, h1r)

    def finish_x(i):
        target = rx1 if i < 4 else rx2

        def put(index, value):
            target[index[0] * 4 + index[1], i % 4] = value.astype(BF16)

        xa[i].finish(put)

    def finish_z(i):
        def put(index, value):
            rz1[index[0], i] = value.astype(BF16)

        za[i].finish(put)

    total = EpScatterSum(back, cbuf, fbuf, gbuf, csend, crecv, place)
    loads["back"].wait()
    total.start()
    exchange(dg_ref, dbuf, dsend, drecv, place, False)
    dbuf[ep] = dg_ref[ep]
    h0.start()
    for i in range(4):
        units[X_UNITS[i]].wait()
        xa[i].start()
        if i < 3:
            units[Z_UNITS[i]].wait()
            za[i].start()
    g0.start()
    total.far()
    za[0].advance(2)
    xa[0].advance(2)
    za[1].advance(2)
    total.near()
    h0.advance(2)
    xa[1].advance(2)
    za[2].advance(2)
    g0.advance(2)
    exchange(dg_ref, dbuf, dsend, drecv, place, True)
    for name in ("nf", "res", "og"):
        loads[name].wait()
    gates = gates_ref[...]
    grad_gates = jnp.concatenate([dbuf[p] for p in range(8)], axis=0)
    grad_logits = gates * (grad_gates - jnp.sum(gates * grad_gates, axis=0, keepdims=True))
    high = grad_logits.astype(BF16)
    low = (grad_logits - high.astype(F32)).astype(BF16)
    to = lax.broadcasted_iota(jnp.int32, (32, 64), 0)
    source = lax.broadcasted_iota(jnp.int32, (32, 64), 1)
    squeeze = jnp.where(source == (to // 4) * 8 + to % 4, 1.0, 0.0).astype(BF16)
    high, low = mm(squeeze, high).astype(BF16), mm(squeeze, low).astype(BF16)
    from_router = mm(high, wr_ref[...], TN) + mm(low, wr_ref[...], TN)
    resid = res[...]
    scale = lax.rsqrt(jnp.mean(resid * resid, axis=-1, keepdims=True) + EPSILON)
    scaled = resid * scale
    za[0].advance(3)
    xa[2].advance(2)
    za[1].advance(3)
    grad_normed = total.last() + from_router
    gain_two = jnp.sum(grad_normed * scaled, axis=0, keepdims=True)
    grad_normed = grad_normed * gain_two_ref[...]
    mean = jnp.mean(grad_normed * scaled, axis=-1, keepdims=True)
    grad_res = og[...].astype(F32) + scale * (grad_normed - scaled * mean)
    gm[ep] = grad_res.astype(BF16)
    gather = EpGather(gm, msend, mrecv, place)
    gather.go(0, 1, 3, 2, 4)
    gres[...] = grad_res
    for t in range(8):
        gain_own[0, 8 + t : 9 + t, :] = gain_two[:, 128 * t : 128 * t + 128]
    xa[3].advance(2)
    za[2].advance(3)
    g0.advance(3)

    for name in ("kv", "q"):
        loads[name].wait()
    for chunk in range(4):
        part = kv[chunk * CHUNK : (chunk + 1) * CHUNK, :].astype(F32).T
        kT[:, chunk * CHUNK : (chunk + 1) * CHUNK] = part[:HD].astype(BF16)
    gather.got(1)
    gather.go(5, 6)
    gather.got(3)
    gather.go(7, 8)
    za[0].advance(4)
    for chunk in range(4, 8):
        part = kv[chunk * CHUNK : (chunk + 1) * CHUNK, :].astype(F32).T
        kT[:, chunk * CHUNK : (chunk + 1) * CHUNK] = part[:HD].astype(BF16)
    gather.got(2)
    gather.go(9)
    gather.got(4)
    gather.go(10)
    za[1].advance(4)
    repeat(0, 8, lambda j: prepare_queries(j, ctx, start_ref, q_ref, lse_ref, both, stack, rows))
    gather.got(5)
    gather.go(11)
    gather.got(7)
    gather.go(12)
    za[2].advance(4)
    g0.advance(4)
    grad_router = mm(high, nf[...]) + mm(low, nf[...])
    side = jnp.concatenate([grad_router, jnp.zeros((96, 1024), F32)], axis=0)
    for d in range(8):
        tile = side[:, d * 128 : (d + 1) * 128].T.astype(BF16)
        for c in range(4):
            early[d // 4, d % 4, c, :, 128:256] = tile[32 * c : 32 * c + 32]
    for i in (4, 5):
        units[X_UNITS[i]].wait()
        xa[i].start()
    for name in ("attT", "wp"):
        loads[name].wait()
    gather.got(0, 6, 8, 9, 10, 11, 12)

    total.sent()
    loads["nall"].start()
    results = EpScatterSum(y_part, cbuf2, fbuf2, gbuf2, c2send, c2recv, place)
    loads["y"].wait()
    results.start()
    repeat(0, 8, lambda j: prepare_grads(j, attT, gm, wp, both, stack, rows))
    grad_proj = mm(attT[0].astype(BF16), gm[0])
    for j in range(1, 8):
        grad_proj = grad_proj + mm(attT[j].astype(BF16), gm[j])
    grad_proj = grad_proj.astype(BF16)
    for d in range(8):
        for c in range(4):
            early[d // 4, d % 4, c, :, 0:128] = grad_proj[32 * c : 32 * c + 32, 128 * d : 128 * d + 128]
    sums_early = Direct(torus, early, e_x, e_res, e_z, es, er)
    sums_q = Direct(torus, late_q, q_x, q_res, q_z, lqs, lqr)
    sums_k = Direct(torus, late_k, k_x, k_res, k_z, lks, lkr)
    sums_early.start()

    lane = lax.broadcasted_iota(jnp.int32, (TOK, 128), 1)

    def chunk_copy(r, m):
        shard = (ctx + r) % 4
        return remote(dkv.at[m, shard], kbuf.at[m, ctx], ksend.at[m, r], krecv.at[m, r], (dp, ep, shard))

    def chunk_go(m):
        for r in (2, 1, 3):
            chunk_copy(r, m).start()
        kbuf[m, ctx] = dkv[m, ctx]

    def piece_copy(src, dst, send, recv, m):
        return remote(src.at[m], dst.at[ep], send.at[m], recv.at[ep], (dp, m, ctx))

    def piece_go(src, dst, send, recv, m):
        @pl.when(ep != m)
        def _():
            piece_copy(src, dst, send, recv, m).start()

        @pl.when(ep == m)
        def _():
            dst[ep] = src[m]

    def pieces_got(src, dst, send, recv):
        def one(r):
            p = (ep + r) % 8
            remote(src.at[p], dst.at[p], send.at[p], recv.at[p], (dp, p, ctx)).wait_recv()

        repeat(1, 8, one)

    def pieces_sent(src, dst, send, recv):
        repeat(1, 8, lambda r: piece_copy(src, dst, send, recv, (ep + r) % 8).wait_send())

    def chunk_done(m):
        for r in (1, 2, 3):
            v = kbuf.at[m, (ctx + 4 - r) % 4]
            remote(v, v, ksend.at[m, r], krecv.at[m, r], (dp, ep, (ctx + r) % 4)).wait_recv()
        grad = kbuf[m, 0].astype(F32) + kbuf[m, 1].astype(F32) + kbuf[m, 2].astype(F32) + kbuf[m, 3].astype(F32)
        cosine, sine = rope_block(4 * m + ctx, ca_ref, sa_ref, cb_ref, sb_ref)
        cosine = jnp.where(lane < HD, cosine, 1.0)
        sine = jnp.where(lane < HD, sine, 0.0)
        dkvb[m] = (grad * cosine - rotate_half(grad) * sine).astype(BF16)
        piece_go(dkvb, kpieces, psend, precv, m)

    def progress(m):
        @pl.when(m == 0)
        def _():
            finish_x(0)
            finish_z(0)
            results.far()

        @pl.when(m == 1)
        def _():
            finish_x(1)
            finish_z(1)
            finish_z(2)
            results.near()

        @pl.when(m == 2)
        def _():
            finish_x(2)
            xa[4].advance(2)
            h1.start()

        @pl.when(m == 3)
        def _():
            finish_x(3)
            g1.start()
            xa[5].advance(2)
            sums_early.turn()

        @pl.when(m == 4)
        def _():
            h1.advance(2)
            out_ref[...] = (res[...] + results.last()).astype(BF16)

        @pl.when(m == 6)
        def _():
            g1.advance(2)

    dqs[...] = jnp.zeros((8, HD, 256), F32)

    def key_chunk(m):
        acc[...] = jnp.zeros((CHUNK, 128), F32)

        def pair(j):
            both_grads, query_grad = attend_pair(m, j, kv, kT, both, stack, rows)
            acc[...] += both_grads
            dqs[j] += query_grad

        repeat(m, 8, pair)
        dkv[m] = acc[...].astype(BF16).reshape(4, TOK, 128)
        chunk_go(m)
        dq = dqs[m] * (HD**-0.5)
        dq = jnp.concatenate([dq[:, :128], dq[:, 128:]], axis=0).T
        cosine, sine = rope_block(4 * m + ctx, ca_ref, sa_ref, cb_ref, sb_ref)
        dqb[m] = (dq * cosine - rotate_half(dq) * sine).astype(BF16)
        piece_go(dqb, qpieces, qsend, qrecv, m)

        @pl.when(m >= 2)
        def _():
            chunk_done(m - 2)

        progress(m)

    repeat(0, 8, key_chunk)
    chunk_done(6)
    for name in ("nall", "wq"):
        loads[name].wait()

    def weights(grad, late):
        out = mm(nall[...].reshape(1024, 1024), grad.reshape(1024, 128), TN).astype(BF16)
        for d in range(8):
            for c in range(4):
                at = d * 128 + c * 32
                late[d // 4, d % 4, c] = out[at : at + 32]

    weights(dqb[...], late_q)
    sums_q.start()
    chunk_done(7)
    weights(dkvb[...], late_k)
    sums_k.start()
    for i in (4, 5):
        finish_x(i)
    g2.start()
    pieces_got(dqb, qpieces, qsend, qrecv)
    grad_q = jnp.concatenate([qpieces[p] for p in range(8)], axis=1)
    grad_normed = mm(grad_q, wq[...], NT)
    sums_q.turn()

    def piece(g, h, kind, device):
        index = (kind * 4 + g) * 2 + h
        src = (fin.at[g, :, pl.ds(128, 128)], fin.at[g, :, pl.ds(0, 128)], fin_late.at[g])[kind]
        mine = dp if kind == 1 else ep
        return remote(src, (rs, rp, rq)[kind].at[mine], fsend.at[index], frecv.at[kind, mine], device)

    def each_piece(kinds, act, local):
        def one(i):
            g, h = i // 2, i % 2
            for kind in kinds:
                device = send_to(g, h)[kind % 2]

                @pl.when(jnp.logical_not(is_me(device)))
                def _():
                    act(piece(g, h, kind, device))

                if local:

                    @pl.when(is_me(device))
                    def _():
                        if kind == 0:
                            rs[ep] = fin[g, :, 128:256]
                        elif kind == 1:
                            rp[dp] = fin[g, :, 0:128]
                        else:
                            rq[ep] = fin_late[g]

        repeat(0, 8, one)

    def pieces_in(kind):
        def one(i):
            device = (i, dp, ep // 2) if kind == 1 else (dp, i, ep // 2)

            @pl.when(jnp.logical_not(is_me(device)))
            def _():
                dst = (rs, rp, rq)[kind].at[i]
                remote(dst, dst, fsend.at[kind * 8], frecv.at[kind, i], device).wait_recv()

        repeat(0, 8, one)

    for name in ("wk", "wv"):
        loads[name].wait()
    pieces_got(dkvb, kpieces, psend, precv)
    grad_k = jnp.concatenate([kpieces[p, :, 0:HD] for p in range(8)], axis=1)
    grad_v = jnp.concatenate([kpieces[p, :, HD:128] for p in range(8)], axis=1)
    grad_normed = grad_normed + mm(grad_k, wk[...], NT) + mm(grad_v, wv[...], NT)
    x = x_ref[...].astype(F32)
    scale = lax.rsqrt(jnp.mean(x * x, axis=-1, keepdims=True) + EPSILON)
    scaled = x * scale
    gain_one = jnp.sum(grad_normed * scaled, axis=0, keepdims=True)
    for t in range(8):
        gain_own[0, t : t + 1, :] = gain_one[:, 128 * t : 128 * t + 128]

    def gain_copy(stage, r):
        src = gain_own.at[stage]
        if stage == 0:
            dst, device, base = gain_e.at[r - 1], (dp, (ep + r) % 8, ctx), 0
        elif stage == 1:
            dst, device, base = gain_x.at[r - 1], torus.at_x(torus.x + r), 7
        else:
            dst, device, base = gain_z.at[r - 1], torus.at_z(torus.z + r), 10
        return remote(src, dst, gs.at[base + r], gr.at[base + r], device)

    def gain_stage(stage, count):
        if stage > 0:
            last, slots = ((7, gain_e), (3, gain_x), (7, gain_z))[stage - 1]
            repeat(1, last + 1, lambda r: gain_copy(stage - 1, r).wait_recv())
            value = gain_own[stage - 1]
            for r in range(1, last + 1):
                value = value + slots[r - 1]
            gain_own[stage] = value
        repeat(1, count + 1, lambda r: gain_copy(stage, r).start())

    gain_stage(0, 7)
    sums_k.turn()
    g2.advance(2)
    grad_normed = grad_normed * gain_one_ref[...]
    mean = jnp.mean(grad_normed * scaled, axis=-1, keepdims=True)
    ing_ref[...] = (gres[...] + scale * (grad_normed - scaled * mean)).astype(BF16)

    gain_stage(1, 3)
    g1.advance(3)
    done_early = sums_early.finish()
    for g in range(4):
        fin[g] = done_early[8 * g : 8 * g + 8]
    each_piece((0, 1), lambda c: c.start(), True)
    g2.advance(3)

    done_q, done_k = sums_q.finish(), sums_k.finish()
    for g in range(4):
        at = slice(8 * g, 8 * g + 8)
        fin_late[g, :, 0:128] = done_q[at]
        fin_late[g, :, 128:256] = done_k[at]
    each_piece((2,), lambda c: c.start(), True)
    gain_stage(2, 7)
    g1.advance(4)
    g2.advance(4)


    def put_unit(unit, value):
        j, u = unit // 3, unit % 3
        if u < 2:
            gin_ref[j, 16 * u : 16 * u + 16, :] = value
        else:
            gout_ref[j] = value

    def finish_units(arc, units):
        for way in (0, 1):
            arc.copy(way, arc.steps).wait_recv()
        mine = arc.own(arc.pos)
        up, down = arc.slots.at[0, arc.steps - 1], arc.slots.at[1, arc.steps - 1]
        for i, unit in enumerate(units):
            put_unit(unit, mine[i].astype(F32) + up[i].astype(F32) + down[i].astype(F32))

    for way in (0, 1):
        h0.copy(way, 2).wait_recv()
    for h in (0, 1):
        value = rz0[torus.x, h].astype(F32) + h0_slots[0, 1, h].astype(F32) + h0_slots[1, 1, h].astype(F32)
        gout_ref[0, :, 512 * h : 512 * h + 512] = value
    finish_units(h1, Z_UNITS)
    finish_units(g0, X_FIRST)
    finish_units(g1, X_UNITS[:4])
    pieces_in(0)
    pieces_in(1)
    last = gain_own[2]
    repeat(1, 8, lambda r: gain_copy(2, r).wait_recv())
    for r in range(7):
        last = last + gain_z[r]
    gain_own[3] = last

    pieces_in(2)
    odd = ctx % 2 == 1

    def mine(v):
        return jnp.where(odd, v[4:8], v[0:4])

    gq_ref[...] = mine(jnp.concatenate([rq[i, :, 0:128] for i in range(8)], axis=1))
    gk_ref[...] = mine(jnp.concatenate([rq[i, :, 128:192] for i in range(8)], axis=1))
    gv_ref[...] = mine(jnp.concatenate([rq[i, :, 192:256] for i in range(8)], axis=1))
    side = rs[0]
    for i in range(1, 8):
        side = side + rs[i]
    gside_ref[...] = mine(side)
    gproj_out[...] = mine(jnp.concatenate([rp[i] for i in range(8)], axis=1))
    for which in (0, 1):
        row = jnp.broadcast_to(gain_own[3, pl.ds(8 * which + dp, 1), :], (8, 128))
        gains_ref[8 * which : 8 * which + 8, :] = pltpu.roll(row, (128 - 16 * ep - 4 * ctx) % 128, 1)

    finish_units(g2, X_UNITS[4:])

    results.sent()
    gather.sent()
    exchange_sent(dg_ref, dbuf, dsend, drecv, place)
    pieces_sent(dqb, qpieces, qsend, qrecv)
    pieces_sent(dkvb, kpieces, psend, precv)

    def chunk_sent(m):
        for r in (1, 2, 3):
            chunk_copy(r, m).wait_send()

    repeat(0, 8, chunk_sent)
    for arc in xa + za + [g0, g1, g2, h0, h1]:
        arc.sent()
    for sums in (sums_early, sums_q, sums_k):
        sums.sent()
    for stage, count in ((0, 7), (1, 3), (2, 7)):
        repeat(1, count + 1, lambda r: gain_copy(stage, r).wait_send())
    each_piece((0, 1, 2), lambda c: c.wait_send(), False)


def pack_kernel(*refs):
    count = (len(refs) - 1) // 2
    for src, dst in zip(refs[: count - 2], refs[count:]):
        dst[...] = src[...]
    side, gains = refs[count - 2 : count]
    router, one, two = refs[-3:]
    router[...] = side[:, 0:32]
    one[...] = gains[0, 0:4]
    two[...] = gains[8, 0:4]


def call(kernel, outs, scratch, args, name, collective=None, **more):
    params = dict(vmem_limit_bytes=VMEM_LIMIT)
    if collective is not None:
        params.update(collective_id=collective, has_side_effects=True)
    space = pl.BlockSpec(memory_space=pltpu.VMEM)
    return pl.pallas_call(
        kernel,
        out_shape=[jax.ShapeDtypeStruct(shape, kind) for shape, kind in outs],
        in_specs=more.pop("in_specs", [space] * len(args)),
        out_specs=more.pop("out_specs", [space] * len(outs)),
        scratch_shapes=scratch,
        compiler_params=pltpu.CompilerParams(**params),
        name=name,
        **more,
    )(*args)


def sems(*sizes):
    return [pltpu.SemaphoreType.DMA(s if isinstance(s, tuple) else (s,)) for s in sizes]


def body(
    layer_input, gain_attn, w_query, w_key, w_value, w_proj, gain_ffn, w_router,
    w_expert_in, w_expert_out, segment_ids, expert_ids, slot_order, out_grad,
):
    gain_one, gain_two = gain_attn.reshape(1, 1024), gain_ffn.reshape(1, 1024)
    tables = [jnp.asarray(t) for t in rope_tables()]
    wr_rows = w_router.T
    order = slot_order.reshape(8, 128)
    docs = segment_ids.reshape(32, 128)

    vm, hbm = pl.BlockSpec(memory_space=pltpu.VMEM), pl.BlockSpec(memory_space=pl.ANY)
    wide, block = pltpu.VMEM((8, TOK, 1024), BF16), pltpu.VMEM((8, TOK, 128), BF16)
    (
        normed_all, grad_all, query, kv, slots, starts, attended_tall, log_sums, residual, ffn_all, gates_in, gates,
    ) = call(
        head_kernel,
        [
            ((8, TOK, 1024), BF16), ((8, TOK, 1024), BF16), ((8, TOK, 128), BF16), ((8, 4, TOK, 128), BF16),
            ((8, 8, TOK), F32), ((32, 128), F32), ((8, 128, TOK), F32), ((8, 8, 256), F32),
            ((TOK, 1024), F32), ((8, TOK, 1024), BF16), ((8, 8, TOK), F32), ((64, TOK), F32),
        ],
        [
            pltpu.VMEM((1024, 128), BF16), pltpu.VMEM((1024, 128), BF16), pltpu.VMEM((1024, 128), BF16),
            pltpu.VMEM((1024, 256), BF16), pltpu.VMEM((1024, 1024), BF16), pltpu.VMEM((8, 8, TOK), F32),
            pltpu.VMEM((64, TOK), F32), block, block, pltpu.VMEM((4096, 128), BF16), pltpu.VMEM((128, 4096), BF16),
            pltpu.VMEM((8, 8, TOK), F32),
        ]
        + sems(4, 13, 13, 13, 13, 8, 8, 24, 24, 8, 8, 13, 13, 8, 8),
        [
            layer_input, gain_one, gain_two, out_grad, *tables, expert_ids.T, order, docs, wr_rows,
            w_query, w_key, w_value, w_proj,
        ],
        "head", 1, in_specs=[vm] * 12 + [hbm] * 4,
    )
    kv_rows = kv.reshape(4096, 128)
    ex, ez = len(X_FIRST), len(Z_FIRST)
    sums, back, grad_gates, sums_x, sums_z, units = call(
        expert_kernel,
        [
            ((8, TOK, 1024), BF16), ((8, TOK, 1024), BF16), ((8, 8, TOK), F32), ((8, ex, 16, 1024), BF16),
            ((4, 2, 16, 512), BF16), ((12 - KEPT, 2, 4, 4, 16, 1024), BF16),
        ],
        [
            wide, wide, pltpu.VMEM((2, 1024, 1024), BF16), pltpu.VMEM((2, 512, 1024), BF16),
            pltpu.VMEM((4, 8 * CAP, 1024), F32), pltpu.VMEM((4, 8 * CAP, 1024), F32),
            pltpu.VMEM((12, 2, 4, 4, 16, 1024), BF16),
            pltpu.VMEM((ex, 2, 2, 2, 4, 16, 1024), BF16), pltpu.VMEM((ez, 2, 4, 4, 16, 1024), BF16),
        ]
        + sems(2, (4, 2), 12 - KEPT, (ex, 2, 2), (ex, 2, 2), (ez, 2, 4), (ez, 2, 4)),
        [slots, gates_in, ffn_all, grad_all, w_expert_in, w_expert_out],
        "experts", 4, in_specs=[vm, vm] + [hbm] * 4, out_specs=[vm] * 5 + [hbm],
    )
    nx, nz = len(X_UNITS), len(Z_UNITS)

    def direct(lanes):
        return [
            pltpu.VMEM((3, 2, 4, 32, lanes), BF16), pltpu.VMEM((8, 32, lanes), BF16), pltpu.VMEM((7, 32, lanes), BF16)
        ]

    results = call(
        tail_kernel,
        [
            ((TOK, 1024), BF16), ((TOK, 1024), BF16), ((4, 32, 1024), F32), ((4, 16, 1024), F32), ((4, 1024), F32),
            ((4, 512), F32), ((4, 512), F32), ((4, 1024), F32), ((4, 128), F32), ((16, 128), F32),
        ],
        [
            wide, pltpu.VMEM((TOK, 1024), BF16), pltpu.VMEM((TOK, 1024), F32), pltpu.VMEM((TOK, 1024), BF16), block,
            pltpu.VMEM((4096, 128), BF16), pltpu.VMEM((8, 128, TOK), F32), pltpu.VMEM((128, 1024), BF16), wide,
            pltpu.VMEM((1024, 1024), BF16), pltpu.VMEM((1024, 512), BF16), pltpu.VMEM((1024, 512), BF16),
            pltpu.VMEM((nx + nz, 2, 4, 4, 16, 1024), BF16),
            pltpu.VMEM((8, 8, TOK), F32),
        ]
        + scatter_sum_scratch()[:3] * 2
        + [
            wide, pltpu.VMEM((TOK, 1024), F32),
            pltpu.VMEM((HD, 4096), BF16), pltpu.VMEM((8, 128, 512), BF16), pltpu.VMEM((8, 512, 128), BF16),
            pltpu.VMEM((8, 8, 256), F32), pltpu.VMEM((8, HD, 256), F32), pltpu.VMEM((CHUNK, 128), F32),
            pltpu.VMEM((8, 4, TOK, 128), BF16),
            block, block, pltpu.VMEM((8, 4, TOK, 128), BF16), block, block,
            pltpu.VMEM((nx, 2, 2, 2, 4, 16, 1024), BF16), pltpu.VMEM((nz, 2, 4, 4, 16, 1024), BF16),
            pltpu.VMEM((2, 4, ex, 16, 1024), BF16), pltpu.VMEM((2, 4, 4, 16, 1024), BF16), pltpu.VMEM((2, 4, 2, 16, 1024), BF16),
            pltpu.VMEM((2, 2, 2, 16, 512), BF16), pltpu.VMEM((2, 2, nz, 16, 1024), BF16),
            pltpu.VMEM((8, 4, 16, 1024), BF16), pltpu.VMEM((8, 2, 16, 1024), BF16), pltpu.VMEM((4, nz, 16, 1024), BF16),
            pltpu.VMEM((2, 4, 4, 32, 256), BF16), pltpu.VMEM((2, 4, 4, 32, 128), BF16), pltpu.VMEM((2, 4, 4, 32, 128), BF16),
        ]
        + direct(256) + direct(128) + direct(128)
        + [
            pltpu.VMEM((4, 16, 128), F32), pltpu.VMEM((7, 16, 128), F32), pltpu.VMEM((3, 16, 128), F32),
            pltpu.VMEM((7, 16, 128), F32),
            pltpu.VMEM((4, 8, 256), F32), pltpu.VMEM((4, 8, 256), F32), pltpu.VMEM((8, 8, 128), F32),
            pltpu.VMEM((8, 8, 128), F32), pltpu.VMEM((8, 8, 256), F32),
        ]
        + sems(
            13, nx + nz, 8, 8, 8, 8, 8, 8, 13, 13, (8, 4), (8, 4), 8, 8, 8, 8,
            (nx, 2, 2), (nx, 2, 2), (nz, 2, 4), (nz, 2, 4),
            (2, 4), (2, 4), (2, 4), (2, 4), (2, 4), (2, 4), (2, 2), (2, 2), (2, 2), (2, 2), 11, 11, 11, 11, 11, 11, 18, 18,
            24, (3, 8),
        ),
        [
            grad_gates, gates, gain_two, wr_rows, layer_input, gain_one, *tables, starts, log_sums,
            sums_x, sums_z, back, ffn_all, residual, out_grad, query, kv_rows, attended_tall, w_proj, sums, normed_all,
            w_query, w_key, w_value, units,
        ],
        "tail", 3, in_specs=[vm] * 14 + [hbm] * 14,
    )
    layer_output, input_grad, grad_in, grad_out, out_q, out_k, out_v, out_proj, router, gain_a, gain_b = call(
        pack_kernel,
        [(r.shape, r.dtype) for r in results[:8]] + [((4, 32), F32), ((4,), F32), ((4,), F32)], [], results, "pack",
    )
    return layer_output, input_grad, gain_a, out_q, out_k, out_v, out_proj, gain_b, router, grad_in, grad_out


def solution(mesh):
    tokens = P(("dp", "ep", "ctx"), None)
    in_specs = (
        tokens, P(), P(), P(), P(), P(), P(), P(),
        P("ep", None, None), P("ep", None, None), P("dp", None), tokens, tokens, tokens,
    )
    out_specs = (
        tokens, tokens, P(("dp", "ep", "ctx")), tokens, tokens, tokens, tokens, P(("dp", "ep", "ctx")), tokens,
        P("ep", ("dp", "ctx"), None), P("ep", ("dp", "ctx"), None),
    )
    return jax.shard_map(body, mesh=mesh, in_specs=in_specs, out_specs=out_specs, check_vma=False)
```
